32 devices in a mesh: batch: 8 (over y, x, core), ctx: 4 (over z).
Axes of the slice: x: 2, y: 2, z: 4, core: 2. Of those that a mesh axis runs over, the one named last changes fastest.
Arguments:
- block_in: bfloat16 [8, 8, 128, 768], P('batch', 'ctx'), may hold values from -6 to 6
- cotangent: bfloat16 [8, 8, 128, 768], P('batch', 'ctx'), may hold values from -6 to 6
- w_qkv: float32 [768, 2304], P('batch', 'ctx'), may hold values from -0.21875 to 0.21875
- w_out: float32 [768, 768], P('batch', 'ctx'), may hold values from -0.875 to 0.875
- w_fc: float32 [768, 3072], P('batch', 'ctx'), may hold values from -0.21875 to 0.21875
- w_proj: float32 [3072, 768], P('batch', 'ctx'), may hold values from -0.109375 to 0.109375
- vectors: float32 [12, 768], P(None, 'ctx'), may hold values from -0.5 to 1.5, as said below
- qkv_first: float32 [768, 2304], P('batch', 'ctx'), may hold values from -16 to 16
- qkv_second: float32 [768, 2304], P('batch', 'ctx'), may hold values from 0.73728 to 2.94912
- out_first: float32 [768, 768], P('batch', 'ctx'), may hold values from -28 to 28
- out_second: float32 [768, 768], P('batch', 'ctx'), may hold values from 2.048 to 8.192
- fc_first: float32 [768, 3072], P('batch', 'ctx'), may hold values from -28 to 28
- fc_second: float32 [768, 3072], P('batch', 'ctx'), may hold values from 2.048 to 8.192
- proj_first: float32 [3072, 768], P('batch', 'ctx'), may hold values from -28 to 28
- proj_second: float32 [3072, 768], P('batch', 'ctx'), may hold values from 2.048 to 8.192
- vec_first: float32 [12, 768], P(None, 'ctx'), may hold values from -56 to 56
- vec_second: float32 [12, 768], P(None, 'ctx'), may hold values from 8.192 to 32.768
Outputs:
- out_block: bfloat16 [8, 8, 128, 768], P('batch', 'ctx')
- grad_input: float32 [8, 8, 128, 768], P('batch', 'ctx')
- qkv_first_new: float32 [768, 2304], P('batch', 'ctx')
- qkv_second_new: float32 [768, 2304], P('batch', 'ctx')
- qkv_new: float32 [768, 2304], P('batch', 'ctx')
- out_first_new: float32 [768, 768], P('batch', 'ctx')
- out_second_new: float32 [768, 768], P('batch', 'ctx')
- out_new: float32 [768, 768], P('batch', 'ctx')
- fc_first_new: float32 [768, 3072], P('batch', 'ctx')
- fc_second_new: float32 [768, 3072], P('batch', 'ctx')
- fc_new: float32 [768, 3072], P('batch', 'ctx')
- proj_first_new: float32 [3072, 768], P('batch', 'ctx')
- proj_second_new: float32 [3072, 768], P('batch', 'ctx')
- proj_new: float32 [3072, 768], P('batch', 'ctx')
- vec_first_new: float32 [12, 768], P(None, 'ctx')
- vec_second_new: float32 [12, 768], P(None, 'ctx')
- vec_new: float32 [12, 768], P(None, 'ctx')
The draws below stay inside these ranges and needn't reach their ends.
Inputs may be any that keep to these rules, and one draw needn't show every extreme that they name: `vectors`: rows 0 and 2 are gains between 0.5 and 1.5; the other rows are biases between -0.5 and 0.5.
All inputs are finite; a program needn't handle non-finite values.
Results may differ from the reference program's by a relative error of at most 0.0085.
The reference program's roundings to bfloat16 on the way count: a program that leaves them out, or rounds other values in their place, can miss the bound.
Values may be sent and summed in bfloat16 or wider, within the bound.
No kernel may reach another device: no remote copies, remote signals or barrier semaphores. Data moves between devices by JAX's collectives and lax.ppermute only.
A program may use at most 128 MiB of HBM per device.

```python
import math
import jax
import jax.numpy as jnp
from jax import lax

D = 768
HEADS = 12
HEAD = 64
FF = 3072
HALF = 128
STEP = 10
BLOCKS = 8
LEN = 1024
SEQS = 8
TOKENS = 8192


def draw_vectors(key, part):
    key = jax.random.fold_in(key, 7)
    gain_key, shift_key = jax.random.split(key)
    gains = jnp.clip(1.0 + 0.2 * jax.random.normal(gain_key, (12, D), jnp.float32), 0.5, 1.5)
    shifts = jnp.clip(0.25 * jax.random.normal(shift_key, (12, D), jnp.float32), -0.5, 0.5)
    which = jnp.arange(12, dtype=jnp.int32)[:, None]
    is_gain = (which == 0) | (which == 2)
    return jnp.where(is_gain, gains, shifts)


def level_of(key, shape, cuts, smallest, top_value):
    factor_of = 1.0
    for position, blocks in cuts:
        draws = jax.random.uniform(jax.random.fold_in(jax.random.fold_in(key, 6), position), (blocks,), jnp.float32, smallest / len(cuts), top_value / len(cuts))
        factor_of = factor_of * jnp.repeat(jnp.exp(draws), shape[position] // blocks).reshape((-1,) + (1,) * (len(shape) - 1 - position))
    return factor_of


def normal_values(key, dims, scale, most, pieces=(), held_as=jnp.bfloat16):
    values = scale * jax.random.normal(key, dims, jnp.float32)
    if pieces:
        values = values * level_of(key, dims, pieces, -0.22, 0.18)
    return jnp.clip(values, -most, most).astype(held_as)


def setup_inputs(seed: int = 0) -> dict:
    seeds = jax.random.split(jax.random.key(seed), 18)
    return {
        "block_in": normal_values(seeds[0], (SEQS, BLOCKS, HALF, D), 1.0, 6.0, ((0, 8), (1, 4))),
        "cotangent": normal_values(seeds[1], (SEQS, BLOCKS, HALF, D), 1.0, 6.0, ((0, 8), (1, 4))),
        "w_qkv": normal_values(seeds[2], (D, 3 * D), D ** -0.5, 0.21875, ((0, 8), (1, 4)), jnp.float32),
        "w_out": normal_values(seeds[3], (D, D), (D // 16) ** -0.5, 0.875, ((0, 8), (1, 4)), jnp.float32),
        "w_fc": normal_values(seeds[4], (D, FF), D ** -0.5, 0.21875, ((0, 8), (1, 4)), jnp.float32),
        "w_proj": normal_values(seeds[5], (FF, D), FF ** -0.5, 0.109375, ((0, 8), (1, 4)), jnp.float32),
        "vectors": draw_vectors(jax.random.fold_in(seeds[17], 71), 0),
        "qkv_first": normal_values(seeds[7], (D, 3 * D), (0.03 * TOKENS ** 0.5), 16.0, ((0, 8), (1, 4)), jnp.float32),
        "qkv_second": jnp.clip(jnp.exp(math.log(2.94912) - 1.3862944 * jax.random.uniform(seeds[8], (D, 3 * D), jnp.float32) ** level_of(seeds[8], (D, 3 * D), ((0, 8), (1, 4)), -0.2, 0.2)), 0.73728, 2.94912),
        "out_first": normal_values(seeds[9], (D, D), (0.05 * TOKENS ** 0.5), 28.0, ((0, 8), (1, 4)), jnp.float32),
        "out_second": jnp.clip(jnp.exp(math.log(8.192) - 1.3862944 * jax.random.uniform(seeds[10], (D, D), jnp.float32) ** level_of(seeds[10], (D, D), ((0, 8), (1, 4)), -0.2, 0.2)), 2.048, 8.192),
        "fc_first": normal_values(seeds[11], (D, FF), (0.05 * TOKENS ** 0.5), 28.0, ((0, 8), (1, 4)), jnp.float32),
        "fc_second": jnp.clip(jnp.exp(math.log(8.192) - 1.3862944 * jax.random.uniform(seeds[12], (D, FF), jnp.float32) ** level_of(seeds[12], (D, FF), ((0, 8), (1, 4)), -0.2, 0.2)), 2.048, 8.192),
        "proj_first": normal_values(seeds[13], (FF, D), (0.05 * TOKENS ** 0.5), 28.0, ((0, 8), (1, 4)), jnp.float32),
        "proj_second": jnp.clip(jnp.exp(math.log(8.192) - 1.3862944 * jax.random.uniform(seeds[14], (FF, D), jnp.float32) ** level_of(seeds[14], (FF, D), ((0, 8), (1, 4)), -0.2, 0.2)), 2.048, 8.192),
        "vec_first": normal_values(seeds[15], (12, D), (0.1 * TOKENS ** 0.5), 56.0, ((1, 4),), jnp.float32),
        "vec_second": jnp.clip(jnp.exp(math.log(32.768) - 1.3862944 * jax.random.uniform(seeds[16], (12, D), jnp.float32) ** level_of(seeds[16], (12, D), ((1, 4),), -0.2, 0.2)), 8.192, 32.768),
    }


@jax.custom_vjp
def low(v):
    return lax.optimization_barrier(v.astype(jnp.bfloat16)).astype(jnp.float32)

@jax.custom_vjp
def low_back(v):
    return v

def low_keep(v):
    return (low(v), None)

def low_pass(kept, grad):
    return (grad,)

def back_keep(v):
    return (v, None)

def back_low(kept, grad):
    return (low(grad),)
low.defvjp(low_keep, low_pass)
low_back.defvjp(back_keep, back_low)

def layer_norm(value, gain, shift):
    mean = lax.optimization_barrier(jnp.mean(value, axis=-1, keepdims=True))
    centred = value - mean
    spread = lax.optimization_barrier(jnp.mean(centred * centred, axis=-1, keepdims=True))
    return centred * lax.rsqrt(spread + 1e-05) * gain + shift

def gelu_tanh(value):
    return 0.5 * value * (1.0 + jnp.tanh(0.7978845608028654 * (value + 0.044715 * value * value * value)))

def matmul(left, right):
    return jnp.dot(left, right, precision=lax.Precision.HIGHEST)

def token_places():
    block = jnp.arange(BLOCKS, dtype=jnp.int32)
    pair = block // 2
    place = jnp.where(block % 2 == 0, pair, BLOCKS - 1 - pair)
    return (place[:, None] * HALF + jnp.arange(HALF, dtype=jnp.int32)[None, :]).reshape(-1)

def forward(inputs, w_qkv, w_out, w_fc, w_proj, vectors):
    params = low(vectors)
    full_qkv = low(w_qkv)
    full_out = low(w_out)
    full_fc = low(w_fc)
    full_proj = low(w_proj)
    places = token_places()
    scale = 1.0 / HEAD ** 0.5
    block_rows = min(512, LEN)

    def one_sequence(sequence):
        rows = sequence.reshape(LEN, D)
        normed_one = low(layer_norm(rows, params[0], params[1]))
        mixed = matmul(normed_one, full_qkv)
        queries = low(low_back(mixed[:, :D] + params[4])).reshape(LEN, HEADS, HEAD)
        keys = low(low_back(mixed[:, D:2 * D])).reshape(LEN, HEADS, HEAD)
        values = low(low_back(mixed[:, 2 * D:] + params[5])).reshape(LEN, HEADS, HEAD)

        def attend(start):
            query_block = lax.dynamic_slice_in_dim(queries, start, block_rows, 0)
            query_places = lax.dynamic_slice_in_dim(places, start, block_rows, 0)
            raw = jnp.einsum('qhd,khd->hqk', query_block, keys, precision=lax.Precision.HIGHEST)
            score = low_back(raw * scale)
            allowed = query_places[None, :, None] >= places[None, None, :]
            score = jnp.where(allowed, score, -1e+30)
            top = lax.optimization_barrier(jnp.max(score, axis=-1, keepdims=True))
            expo = jnp.exp(score - top)
            prob = low(expo / lax.optimization_barrier(jnp.sum(expo, axis=-1, keepdims=True)))
            result = jnp.einsum('hqk,khd->qhd', prob, values, precision=lax.Precision.HIGHEST)
            return low(low_back(result)).reshape(block_rows, D)
        starts = jnp.arange(LEN // block_rows, dtype=jnp.int32) * block_rows
        attended = lax.map(jax.checkpoint(attend), starts).reshape(LEN, D)
        branch = low_back(matmul(attended, full_out) + params[6])
        mid = rows + branch
        normed_two = low(layer_norm(mid, params[2], params[3]))
        pre = low_back(matmul(normed_two, full_fc) + params[8:12].reshape(FF))
        act = low(gelu_tanh(pre))
        result = mid + matmul(act, full_proj) + params[7]
        return result.reshape(BLOCKS, HALF, D)
    return lax.map(jax.checkpoint(one_sequence), inputs)

def adamw(weight, grad, first, second, rate, decay):
    first = 0.9 * first + 0.1 * grad
    second = 0.999 * second + 0.001 * grad * grad
    first_hat = first / (1.0 - 0.9 ** STEP)
    second_hat = second / (1.0 - 0.999 ** STEP)
    weight = weight - rate * (first_hat / (jnp.sqrt(second_hat) + 1e-08) + decay * weight)
    return (first, second, weight)

def reference(block_in, cotangent, w_qkv, w_out, w_fc, w_proj, vectors, qkv_first, qkv_second, out_first, out_second, fc_first, fc_second, proj_first, proj_second, vec_first, vec_second):
    inputs = block_in.astype(jnp.float32)
    result, pullback = jax.vjp(forward, inputs, w_qkv, w_out, w_fc, w_proj, vectors)
    grads = pullback(cotangent.astype(jnp.float32))
    qkv_m, qkv_s, qkv_w = adamw(w_qkv, grads[1], qkv_first, qkv_second, 0.06, 0.1)
    out_m, out_s, out_w = adamw(w_out, grads[2], out_first, out_second, 0.06, 0.1)
    fc_m, fc_s, fc_w = adamw(w_fc, grads[3], fc_first, fc_second, 0.06, 0.1)
    proj_m, proj_s, proj_w = adamw(w_proj, grads[4], proj_first, proj_second, 0.06, 0.1)
    vec_m, vec_s, vec_w = adamw(vectors, grads[5], vec_first, vec_second, 0.2, 0.0)
    return (result.astype(jnp.bfloat16), grads[0], qkv_m, qkv_s, qkv_w, out_m, out_s, out_w, fc_m, fc_s, fc_w, proj_m, proj_s, proj_w, vec_m, vec_s, vec_w)
```

```python
import functools
import math

import jax
import jax.numpy as jnp
from jax import lax
from jax.experimental import pallas as pl
from jax.experimental.pallas import tpu as pltpu
from jax.sharding import PartitionSpec as P

HEADS = 12
STEP = 10


def layer_norm(value, gain, shift):
    mean = jnp.mean(value, axis=-1, keepdims=True)
    centred = value - mean
    spread = jnp.mean(centred * centred, axis=-1, keepdims=True)
    return centred * lax.rsqrt(spread + 1e-05) * gain + shift


def gelu_tanh(value):
    return (
        0.5
        * value
        * (1.0 + jnp.tanh(0.7978845608028654 * (value + 0.044715 * value * value * value)))
    )


def block_places(index, count, half):
    offsets = jnp.arange(half, dtype=jnp.int32)
    first = index * half + offsets
    second = (2 * count - 1 - index) * half + offsets
    return jnp.concatenate([first, second])


def scores_of(queries, keys, scale, allowed):
    raw = jnp.einsum("sqhd,skhd->shqk", queries, keys, preferred_element_type=jnp.float32) * scale
    return jnp.where(allowed[None, None], raw, -1e30)


def pair_grads(queries, grads, keys, values, top, total, delta, scale, allowed):
    score = scores_of(queries, keys, scale, allowed)
    weights = jnp.exp(score - top[..., None]) / total[..., None]
    back_weights = jnp.einsum("sqhd,skhd->shqk", grads, values, preferred_element_type=jnp.float32)
    grad_score = (weights * (back_weights - delta[..., None])).astype(jnp.bfloat16)
    return (weights.astype(jnp.bfloat16), grad_score)


def rows_product(left, right):
    return jnp.einsum("ra,rb->ab", left, right, preferred_element_type=jnp.float32)


def back_product(grad, weight):
    return jnp.einsum("rb,ab->ra", grad, weight, preferred_element_type=jnp.float32)


def adamw(weight, grad, first, second, rate, decay):
    first = 0.9 * first + 0.1 * grad
    second = 0.999 * second + 0.001 * grad * grad
    first_hat = first / (1.0 - 0.9**STEP)
    second_hat = second / (1.0 - 0.999**STEP)
    weight = weight - rate * (first_hat / (jnp.sqrt(second_hat) + 1e-08) + decay * weight)
    return (first, second, weight)


def local_any(
    block_in,
    cotangent,
    w_qkv,
    w_out,
    w_fc,
    w_proj,
    vectors,
    qkv_first,
    qkv_second,
    out_first,
    out_second,
    fc_first,
    fc_second,
    proj_first,
    proj_second,
    vec_first,
    vec_second,
):
    low_type = jnp.bfloat16
    wide = jnp.float32
    row_parts = (
        lax.all_gather(w_qkv.astype(low_type), "batch", axis=0, tiled=True),
        lax.all_gather(w_out.astype(low_type), "batch", axis=0, tiled=True),
        lax.all_gather(w_fc.astype(low_type), "batch", axis=0, tiled=True),
        lax.all_gather(w_proj.astype(low_type), "batch", axis=0, tiled=True),
    )
    full_qkv, full_out, full_fc, full_proj, full_vec = (
        lax.all_gather(row_parts[0], "ctx", axis=1, tiled=True),
        lax.all_gather(row_parts[1], "ctx", axis=1, tiled=True),
        lax.all_gather(row_parts[2], "ctx", axis=1, tiled=True),
        lax.all_gather(row_parts[3], "ctx", axis=1, tiled=True),
        lax.all_gather(vectors.astype(low_type), "ctx", axis=1, tiled=True),
    )
    params = full_vec.astype(wide)
    seqs, pair, half, width = block_in.shape
    heads = HEADS
    head = width // heads
    rows = seqs * pair * half
    span = pair * half
    count = lax.axis_size("ctx")
    index = lax.axis_index("ctx")
    scale = 1.0 / math.sqrt(head)
    inputs = block_in.astype(wide).reshape(rows, width)
    normed_one = layer_norm(inputs, params[0], params[1]).astype(low_type)
    mixed = jnp.dot(normed_one, full_qkv, preferred_element_type=wide)
    queries = (mixed[:, :width] + params[4]).astype(low_type)
    keys = mixed[:, width : 2 * width].astype(low_type)
    values = (mixed[:, 2 * width :] + params[5]).astype(low_type)
    key_all, value_all = (
        lax.all_gather(keys.reshape(seqs, pair, half, width), "ctx", axis=1, tiled=True),
        lax.all_gather(values.reshape(seqs, pair, half, width), "ctx", axis=1, tiled=True),
    )
    query_heads = queries.reshape(seqs, span, heads, head)
    own_places = block_places(index, count, half)

    def piece_of(source, piece):
        return lax.dynamic_slice_in_dim(source, 2 * piece, 2, 1).reshape(seqs, span, heads, head)

    def allowed_for(piece):
        return own_places[:, None] >= block_places(piece, count, half)[None, :]

    def stats_step(piece, carry):
        top, total = carry
        score = scores_of(query_heads, piece_of(key_all, piece), scale, allowed_for(piece))
        new_top = jnp.maximum(top, jnp.max(score, axis=-1))
        total = total * jnp.exp(top - new_top) + jnp.sum(
            jnp.exp(score - new_top[..., None]), axis=-1
        )
        return (new_top, total)

    start_stats = (jnp.full((seqs, heads, span), -1e30, wide), jnp.zeros((seqs, heads, span), wide))
    top, total = lax.fori_loop(0, count, stats_step, start_stats)

    def output_step(piece, acc):
        score = scores_of(query_heads, piece_of(key_all, piece), scale, allowed_for(piece))
        weights = (jnp.exp(score - top[..., None]) / total[..., None]).astype(low_type)
        return acc + jnp.einsum(
            "shqk,skhd->sqhd", weights, piece_of(value_all, piece), preferred_element_type=wide
        )

    attended = lax.fori_loop(0, count, output_step, jnp.zeros((seqs, span, heads, head), wide))
    att_low = attended.reshape(rows, width).astype(low_type)
    mid = inputs + jnp.dot(att_low, full_out, preferred_element_type=wide) + params[6]
    normed_two = layer_norm(mid, params[2], params[3]).astype(low_type)
    pre = jnp.dot(normed_two, full_fc, preferred_element_type=wide) + params[8:12].reshape(-1)
    act_low = gelu_tanh(pre).astype(low_type)
    result = mid + jnp.dot(act_low, full_proj, preferred_element_type=wide) + params[7]
    out_block = result.astype(low_type).reshape(block_in.shape)
    grad_low = cotangent.reshape(rows, width)
    grad_out = grad_low.astype(wide)
    grad_wproj = rows_product(act_low, grad_low)
    back_act = back_product(grad_low, full_proj)
    grad_pre = jax.vjp(gelu_tanh, pre)[1](back_act)[0].astype(low_type)
    grad_wfc = rows_product(normed_two, grad_pre)
    back_two = back_product(grad_pre, full_fc)
    back_mid, grad_gain_two, grad_shift_two = jax.vjp(layer_norm, mid, params[2], params[3])[1](
        back_two
    )
    grad_mid = grad_out + back_mid
    grad_att_low = grad_mid.astype(low_type)
    grad_wout = rows_product(att_low, grad_att_low)
    back_att = back_product(grad_att_low, full_out)
    grad_heads = back_att.astype(low_type).reshape(seqs, span, heads, head)
    delta = jnp.einsum("sqhd,sqhd->shq", grad_heads.astype(wide), attended)
    query_all, grad_all = (
        lax.all_gather(queries.reshape(seqs, pair, half, width), "ctx", axis=1, tiled=True),
        lax.all_gather(grad_heads.reshape(seqs, pair, half, width), "ctx", axis=1, tiled=True),
    )
    top_all, total_all, delta_all = (
        lax.all_gather(top.reshape(seqs, heads, pair, half), "ctx", axis=2, tiled=True),
        lax.all_gather(total.reshape(seqs, heads, pair, half), "ctx", axis=2, tiled=True),
        lax.all_gather(delta.reshape(seqs, heads, pair, half), "ctx", axis=2, tiled=True),
    )

    def query_step(piece, grad_query):
        key_part = piece_of(key_all, piece)
        value_part = piece_of(value_all, piece)
        weights_low, grad_score = pair_grads(
            query_heads,
            grad_heads,
            key_part,
            value_part,
            top,
            total,
            delta,
            scale,
            allowed_for(piece),
        )
        return grad_query + jnp.einsum(
            "shqk,skhd->sqhd", grad_score, key_part, preferred_element_type=wide
        )

    grad_query = lax.fori_loop(0, count, query_step, jnp.zeros((seqs, span, heads, head), wide))
    key_heads = keys.reshape(seqs, span, heads, head)
    value_heads = values.reshape(seqs, span, heads, head)

    def stat_piece(source, piece):
        return lax.dynamic_slice_in_dim(source, 2 * piece, 2, 2).reshape(seqs, heads, span)

    def key_step(piece, carry):
        grad_key, grad_value = carry
        query_part = piece_of(query_all, piece)
        grad_part = piece_of(grad_all, piece)
        allowed = block_places(piece, count, half)[:, None] >= own_places[None, :]
        weights_low, grad_score = pair_grads(
            query_part,
            grad_part,
            key_heads,
            value_heads,
            stat_piece(top_all, piece),
            stat_piece(total_all, piece),
            stat_piece(delta_all, piece),
            scale,
            allowed,
        )
        grad_key = grad_key + jnp.einsum(
            "shqk,sqhd->skhd", grad_score, query_part, preferred_element_type=wide
        )
        grad_value = grad_value + jnp.einsum(
            "shqk,sqhd->skhd", weights_low, grad_part, preferred_element_type=wide
        )
        return (grad_key, grad_value)

    start_keys = (
        jnp.zeros((seqs, span, heads, head), wide),
        jnp.zeros((seqs, span, heads, head), wide),
    )
    grad_key, grad_value = lax.fori_loop(0, count, key_step, start_keys)
    grad_keys = (grad_key * scale).reshape(seqs, pair, half, width)
    grad_values = grad_value.reshape(seqs, pair, half, width)
    grad_q_low = (grad_query * scale).reshape(rows, width).astype(low_type)
    grad_k_low = grad_keys.reshape(rows, width).astype(low_type)
    grad_v_low = grad_values.reshape(rows, width).astype(low_type)
    grad_mixed = jnp.concatenate([grad_q_low, grad_k_low, grad_v_low], axis=1)
    grad_wqkv = rows_product(normed_one, grad_mixed)
    back_one = back_product(grad_mixed, full_qkv)
    back_in, grad_gain_one, grad_shift_one = jax.vjp(layer_norm, inputs, params[0], params[1])[1](
        back_one
    )
    grad_input = (grad_mid + back_in).reshape(block_in.shape)
    grad_bias_q = jnp.sum(grad_q_low.astype(wide), axis=0)
    grad_bias_v = jnp.sum(grad_v_low.astype(wide), axis=0)
    grad_bias_out = jnp.sum(grad_att_low.astype(wide), axis=0)
    grad_bias_proj = jnp.sum(grad_out, axis=0)
    grad_bias_fc = jnp.sum(grad_pre.astype(wide), axis=0).reshape(4, width)
    small_rows = jnp.stack(
        [
            grad_gain_one,
            grad_shift_one,
            grad_gain_two,
            grad_shift_two,
            grad_bias_q,
            grad_bias_v,
            grad_bias_out,
            grad_bias_proj,
        ]
    )
    grad_vectors = jnp.concatenate([small_rows, grad_bias_fc], axis=0)
    col_sums = (
        lax.psum_scatter(grad_wqkv, "ctx", scatter_dimension=1, tiled=True),
        lax.psum_scatter(grad_wout, "ctx", scatter_dimension=1, tiled=True),
        lax.psum_scatter(grad_wfc, "ctx", scatter_dimension=1, tiled=True),
        lax.psum_scatter(grad_wproj, "ctx", scatter_dimension=1, tiled=True),
        lax.psum_scatter(grad_vectors, "ctx", scatter_dimension=1, tiled=True),
    )
    qkv_grad, out_grad, fc_grad, proj_grad = (
        lax.psum_scatter(col_sums[0], "batch", scatter_dimension=0, tiled=True),
        lax.psum_scatter(col_sums[1], "batch", scatter_dimension=0, tiled=True),
        lax.psum_scatter(col_sums[2], "batch", scatter_dimension=0, tiled=True),
        lax.psum_scatter(col_sums[3], "batch", scatter_dimension=0, tiled=True),
    )
    vec_grad = lax.psum(col_sums[4], "batch")
    qkv_m, qkv_s, qkv_w = adamw(w_qkv, qkv_grad, qkv_first, qkv_second, 0.06, 0.1)
    out_m, out_s, out_w = adamw(w_out, out_grad, out_first, out_second, 0.06, 0.1)
    fc_m, fc_s, fc_w = adamw(w_fc, fc_grad, fc_first, fc_second, 0.06, 0.1)
    proj_m, proj_s, proj_w = adamw(w_proj, proj_grad, proj_first, proj_second, 0.06, 0.1)
    vec_m, vec_s, vec_w = adamw(vectors, vec_grad, vec_first, vec_second, 0.2, 0.0)
    return (
        out_block,
        grad_input,
        qkv_m,
        qkv_s,
        qkv_w,
        out_m,
        out_s,
        out_w,
        fc_m,
        fc_s,
        fc_w,
        proj_m,
        proj_s,
        proj_w,
        vec_m,
        vec_s,
        vec_w,
    )


BATCH = 8
CTX = 4
WIDTH = 768
HEAD = 64
GROUP = WIDTH // CTX
TOKENS = 256
HALF = 128
FF_SIDE = 384
SPAN = TOKENS * CTX
TILE = 256
LOW = jnp.bfloat16
WIDE = jnp.float32
CORE, XBIT, YBIT = 1, 2, 4
SOURCES = (0, 0, 2, 2, 4, 4, 6, 6, 1, 1, 3, 3, 5, 5, 7, 7)
VMEM_LIMIT = 56 * 1024 * 1024


def swap(value, axis, bit):
    size = BATCH if axis == "batch" else CTX
    return lax.ppermute(value, axis, [(i, i ^ bit) for i in range(size)])


def mm(left, right):
    return lax.dot_general(left, right, (((1,), (0,)), ((), ())), preferred_element_type=WIDE)


def mt(left, right):
    return lax.dot_general(left, right, (((1,), (1,)), ((), ())), preferred_element_type=WIDE)


def tm(left, right):
    return lax.dot_general(left, right, (((0,), (0,)), ((), ())), preferred_element_type=WIDE)


def turned(value):
    return value.astype(WIDE).T.astype(LOW)


def moments(value):
    mean = jnp.mean(value, axis=-1, keepdims=True)
    centred = value - mean
    spread = jnp.mean(centred * centred, axis=-1, keepdims=True)
    return centred, lax.rsqrt(spread + 1e-05)


def norm_back(grad, normed, inverse, gain):
    part = grad * gain
    mean = jnp.mean(part, axis=-1, keepdims=True)
    cross = jnp.mean(part * normed, axis=-1, keepdims=True)
    return inverse * (part - mean - normed * cross)


def gather_weight(piece):
    near, far, last = swap(piece, "ctx", 1), swap(piece, "ctx", 2), swap(piece, "ctx", 3)
    one, two = jnp.stack([piece, near]), jnp.stack([far, last])
    one_x, two_y = swap(one, "batch", XBIT), swap(two, "batch", YBIT)
    one_y, two_x = swap(one, "batch", YBIT), swap(two, "batch", XBIT)
    one_xy, two_xy = swap(one_x, "batch", YBIT), swap(two_y, "batch", XBIT)
    held = [one, two, one_x, two_x, one_y, two_y, one_xy, two_xy]
    return held + [swap(part, "batch", CORE) for part in held]


def scatter_grad(mine, theirs):
    came = swap(theirs, "batch", CORE)
    total = mine.astype(WIDE) + came.astype(WIDE)
    total = total.reshape((2, 2) + total.shape[1:])
    one, two = total[:, :, 0:2], total[:, :, 2:4]
    one_back = swap(one[1].astype(LOW), "batch", YBIT)
    two_back = swap(two[:, 1].astype(LOW), "batch", XBIT)
    one = one[0] + one_back.astype(WIDE)
    two = two[:, 0] + two_back.astype(WIDE)
    one_back = swap(one[1].astype(LOW), "batch", XBIT)
    two_back = swap(two[1].astype(LOW), "batch", YBIT)
    one = one[0] + one_back.astype(WIDE)
    two = two[0] + two_back.astype(WIDE)
    near = swap(one[1].astype(LOW), "ctx", 1)
    far = swap(two[0].astype(LOW), "ctx", 2)
    last = swap(two[1].astype(LOW), "ctx", 3)
    return one[0] + near.astype(WIDE) + (far.astype(WIDE) + last.astype(WIDE))


def rows_place(held, batch, ctx):
    size = WIDTH // BATCH
    return held.at[ctx, pl.ds(pl.multiple_of(batch * size, 16), size), :]


def columns_place(held, batch, ctx):
    return held.at[batch, pl.ds(pl.multiple_of(ctx * GROUP, 16), GROUP), :]


def load_weight(meta, parts, held, place, sems, lanes=None):
    copies = []
    for index, (part, source) in enumerate(zip(parts, SOURCES)):
        for half in range(2):
            ctx = meta[1] ^ (2 * (index % 2) + half)
            origin = part.at[half] if lanes is None else part.at[half, :, lanes]
            copy = pltpu.make_async_copy(
                origin, place(held, meta[0] ^ source, ctx), sems.at[2 * index + half]
            )
            copy.start()
            copies.append(copy)
    return copies


def store_grad(meta, held, place, mine, theirs, sems):
    copies = []
    for batch in range(BATCH):
        for ctx in range(CTX):
            target = theirs if batch % 2 else mine
            copy = pltpu.make_async_copy(
                place(held, meta[0] ^ batch, meta[1] ^ ctx),
                target.at[batch // 2, ctx],
                sems.at[batch * CTX + ctx],
            )
            copy.start()
            copies.append(copy)
    for copy in copies:
        copy.wait()


def wait_all(copies):
    for copy in copies:
        copy.wait()


def in_place(ctx, block):
    first = ctx if block == 0 else 2 * CTX - 1 - ctx
    return pl.ds(pl.multiple_of(first * HALF, HALF), HALF)


def qkv_kernel(meta, x_ref, vec_ref, bias_ref, *refs):
    parts, (h_ref, own, near, far, last, held, units, sems) = refs[:16], refs[16:]
    copies = load_weight(meta, parts, held, rows_place, sems)
    centred, inverse = moments(x_ref[...].astype(WIDE))
    normed = (centred * inverse * vec_ref[0:1] + vec_ref[1:2]).astype(LOW)
    h_ref[...] = normed
    wait_all(copies)
    for chunk in range(CTX):
        mixed = mm(normed, held[chunk, :, : 3 * GROUP]) + bias_ref[chunk]
        mixed = mixed.astype(LOW)
        for part in range(3):
            unit = 3 * chunk + part
            units[unit % CTX, :, (unit // CTX) * GROUP : (unit // CTX + 1) * GROUP] = mixed[
                :, part * GROUP : (part + 1) * GROUP
            ]
    for ctx, target in enumerate((own, near, far, last)):
        target[...] = units[meta[1] ^ ctx]


def read_sequence(meta, pieces, targets):
    for ctx, piece in enumerate(pieces):
        for block in range(2):
            place = in_place(meta[1] ^ ctx, block)
            rows = piece[block * HALF : (block + 1) * HALF, :]
            for index, target in enumerate(targets):
                target[place, :] = rows[:, index * GROUP : (index + 1) * GROUP]


def write_sequence(meta, pieces, sources):
    for ctx, piece in enumerate(pieces):
        for block in range(2):
            place = in_place(meta[1] ^ ctx, block)
            for index, source in enumerate(sources):
                piece[
                    block * HALF : (block + 1) * HALF, index * GROUP : (index + 1) * GROUP
                ] = source[place, :].astype(LOW)


def head_mask(head, scale=1.0):
    lane = lax.broadcasted_iota(jnp.int32, (1, GROUP), 1)
    inside = (lane >= head * HEAD) & (lane < (head + 1) * HEAD)
    return jnp.where(inside, scale, 0.0).astype(LOW)


def tile_of(index):
    return slice(index * TILE, (index + 1) * TILE)


def weights_of(queries, k_seq, tile, causal):
    scores = [mt(queries, k_seq[tile_of(other), :]) for other in range(tile + 1)]
    scores[tile] = jnp.where(causal, scores[tile], -1e30)
    top = jnp.max(functools.reduce(jnp.maximum, scores), axis=-1, keepdims=True)
    expo = [jnp.exp(score - top) for score in scores]
    total = jnp.sum(functools.reduce(jnp.add, expo), axis=-1, keepdims=True)
    inverse = 1.0 / total
    return [value * inverse for value in expo]


def causal_tile():
    row = lax.broadcasted_iota(jnp.int32, (TILE, TILE), 0)
    column = lax.broadcasted_iota(jnp.int32, (TILE, TILE), 1)
    return row >= column


def attend_kernel(meta, *refs):
    pieces, results, (q_seq, k_seq, v_seq, out) = refs[:4], refs[4:8], refs[8:]
    read_sequence(meta, pieces, (q_seq, k_seq, v_seq))
    causal = causal_tile()
    scale = 1.0 / math.sqrt(HEAD)
    for tile in range(SPAN // TILE):

        def one_head(head, total, tile=tile):
            mask = head_mask(head)
            queries = q_seq[tile_of(tile), :] * head_mask(head, scale)
            weights = weights_of(queries, k_seq, tile, causal)
            for other, weight in enumerate(weights):
                total = total + mm(weight.astype(LOW), v_seq[tile_of(other), :] * mask)
            return total

        out[tile_of(tile), :] = lax.fori_loop(
            0, GROUP // HEAD, one_head, jnp.zeros((TILE, GROUP), WIDE)
        )
    write_sequence(meta, results, (out,))


def attend_back_kernel(meta, *refs):
    pieces, grads, results = refs[:4], refs[4:8], refs[8:12]
    q_seq, k_seq, v_seq, g_seq, dq, dk, dv = refs[12:]
    read_sequence(meta, pieces, (q_seq, k_seq, v_seq))
    read_sequence(meta, grads, (g_seq,))
    causal = causal_tile()
    scale = 1.0 / math.sqrt(HEAD)
    dk[...] = jnp.zeros_like(dk)
    dv[...] = jnp.zeros_like(dv)
    for tile in range(SPAN // TILE):

        def one_head(head, total, tile=tile):
            mask = head_mask(head)
            scaled = head_mask(head, scale)
            queries = q_seq[tile_of(tile), :] * scaled
            grad = g_seq[tile_of(tile), :] * mask
            weights = weights_of(queries, k_seq, tile, causal)
            backs = [mt(grad, v_seq[tile_of(other), :]) for other in range(tile + 1)]
            products = [weight * back for weight, back in zip(weights, backs)]
            delta = jnp.sum(functools.reduce(jnp.add, products), axis=-1, keepdims=True)
            for other, (weight, back) in enumerate(zip(weights, backs)):
                step = (weight * (back - delta)).astype(LOW)
                total = total + mm(step, k_seq[tile_of(other), :] * scaled)
                dk[tile_of(other), :] += tm(step, queries)
                dv[tile_of(other), :] += tm(weight.astype(LOW), grad)
            return total

        dq[tile_of(tile), :] = lax.fori_loop(
            0, GROUP // HEAD, one_head, jnp.zeros((TILE, GROUP), WIDE)
        )
    write_sequence(meta, results, (dq, dk, dv))


def middle_kernel(meta, x_ref, dy_ref, vec_ref, bias_ref, *refs):
    pieces, refs = refs[:4], refs[4:]
    parts_one, parts_two, parts_three, refs = refs[:16], refs[16:32], refs[32:48], refs[48:]
    (out_ref, att_ref, h_ref, act_ref, dpre_ref, datt_ref, dmid_ref), refs = refs[:7], refs[7:]
    results, (rows_ref, dbias_ref), refs = refs[:4], refs[4:6], refs[6:]
    out_parts, held_out, held_fc, held_proj, units, total, back, sem_one, sem_two, sem_three = refs
    lanes = pl.ds(2 * TILE, TILE)
    copies_one = load_weight(meta, parts_one, out_parts, rows_place, sem_one, lanes)
    copies_two = load_weight(meta, parts_two, held_fc, rows_place, sem_two)
    copies_three = load_weight(meta, parts_three, held_proj, columns_place, sem_three)
    for ctx, piece in enumerate(pieces):
        units[meta[1] ^ ctx] = piece[...]
    att = jnp.concatenate([units[index] for index in range(CTX)], axis=1)
    att_ref[...] = att
    wait_all(copies_one)
    for chunk in range(CTX):
        held_out[:, chunk * GROUP : (chunk + 1) * GROUP] = out_parts[chunk, :, TILE - GROUP :]
    mid = x_ref[...].astype(WIDE) + mm(att, held_out[...]) + vec_ref[6:7]
    centred, inverse = moments(mid)
    normed = centred * inverse
    h_ref[...] = (normed * vec_ref[2:3] + vec_ref[3:4]).astype(LOW)
    total[...] = mid + vec_ref[7:8]
    back[...] = jnp.zeros_like(back)
    wait_all(copies_two)
    wait_all(copies_three)
    side = FF_SIDE

    def chunk_step(chunk, carry):
        pre = mm(h_ref[...], held_fc[chunk]) + bias_ref[chunk]
        square = pre * pre
        tanh = jnp.tanh(0.7978845608028654 * (pre + 0.044715 * square * pre))
        act = (0.5 * pre * (1.0 + tanh)).astype(LOW)
        slope = 0.5 * (1.0 + tanh) + 0.5 * pre * (1.0 - tanh * tanh) * (
            0.7978845608028654 * (1.0 + 3.0 * 0.044715 * square)
        )
        act_ref[chunk] = act
        grads = []
        for half in range(2):
            weight = held_proj[2 * chunk + half]
            total[...] += mt(act[:, half * side : (half + 1) * side], weight)
            grads.append(mm(dy_ref[...], weight))
        dpre = (jnp.concatenate(grads, axis=1) * slope).astype(LOW)
        dpre_ref[chunk] = dpre
        dbias_ref[chunk] = jnp.sum(dpre.astype(WIDE), axis=0, keepdims=True)
        back[...] += mt(dpre, held_fc[chunk])
        return carry

    lax.fori_loop(0, CTX, chunk_step, 0)
    out_ref[...] = total[...].astype(LOW)
    grad = back[...]
    dy = dy_ref[...].astype(WIDE)
    dmid = dy + norm_back(grad, normed, inverse, vec_ref[2:3])
    dmid_ref[...] = dmid
    datt = dmid.astype(LOW)
    datt_ref[...] = datt
    rows_ref[0:1] = jnp.sum(grad * normed, axis=0, keepdims=True)
    rows_ref[1:2] = jnp.sum(grad, axis=0, keepdims=True)
    rows_ref[2:3] = jnp.sum(datt.astype(WIDE), axis=0, keepdims=True)
    rows_ref[3:4] = jnp.sum(dy, axis=0, keepdims=True)
    rows_ref[4:8] = jnp.zeros((4, WIDTH), WIDE)
    dout = mt(datt, held_out[...]).astype(LOW)
    for index in range(CTX):
        units[index] = dout[:, index * GROUP : (index + 1) * GROUP]
    for ctx, target in enumerate(results):
        target[...] = units[meta[1] ^ ctx]


def proj_grad_kernel(meta, dy_ref, act_ref, mine, theirs, held, sems):
    left = turned(dy_ref[...])
    for chunk in range(CTX):
        for half in range(2):
            held[2 * chunk + half] = mm(
                left, act_ref[chunk, :, half * FF_SIDE : (half + 1) * FF_SIDE]
            ).astype(LOW)
    store_grad(meta, held, columns_place, mine, theirs, sems)


def fc_grad_kernel(meta, h_ref, dpre_ref, mine, theirs, held, sems):
    left = turned(h_ref[...])
    for chunk in range(CTX):
        held[chunk] = mm(left, dpre_ref[chunk]).astype(LOW)
    store_grad(meta, held, rows_place, mine, theirs, sems)


def qkv_grad_kernel(meta, h_ref, att_ref, datt_ref, *refs):
    pieces, (mine, theirs, mixed_ref, dbias_ref, held, units, sems) = refs[:4], refs[4:]
    for ctx, piece in enumerate(pieces):
        for part in range(3):
            units[CTX * part + (meta[1] ^ ctx)] = piece[:, part * GROUP : (part + 1) * GROUP]
    left, att = turned(h_ref[...]), turned(att_ref[...])
    for chunk in range(CTX):
        mixed = jnp.concatenate([units[3 * chunk + part] for part in range(3)], axis=1)
        mixed_ref[chunk] = mixed
        dbias_ref[chunk] = jnp.sum(mixed.astype(WIDE), axis=0, keepdims=True)
        held[chunk, :, : 3 * GROUP] = mm(left, mixed).astype(LOW)
        held[chunk, :, 3 * GROUP :] = mm(
            att, datt_ref[:, chunk * GROUP : (chunk + 1) * GROUP]
        ).astype(LOW)
    store_grad(meta, held, rows_place, mine, theirs, sems)


def input_grad_kernel(meta, x_ref, vec_ref, dmid_ref, mixed_ref, *refs):
    parts, (grad_ref, rows_ref, held, sems) = refs[:16], refs[16:]
    copies = load_weight(meta, parts, held, rows_place, sems)
    centred, inverse = moments(x_ref[...].astype(WIDE))
    normed = centred * inverse
    wait_all(copies)
    grad = jnp.zeros((TOKENS, WIDTH), WIDE)
    for chunk in range(CTX):
        grad = grad + mt(mixed_ref[chunk], held[chunk, :, : 3 * GROUP])
    grad_ref[...] = dmid_ref[...] + norm_back(grad, normed, inverse, vec_ref[0:1])
    rows_ref[0:1] = jnp.sum(grad * normed, axis=0, keepdims=True)
    rows_ref[1:2] = jnp.sum(grad, axis=0, keepdims=True)
    rows_ref[2:8] = jnp.zeros((6, WIDTH), WIDE)


def shape_of(dtype, *dims):
    return jax.ShapeDtypeStruct(dims, dtype)


def call(kernel, arguments, kinds, outputs, out_kinds, scratch, flops):
    spec = {
        "v": pl.BlockSpec(memory_space=pltpu.VMEM),
        "s": pl.BlockSpec(memory_space=pltpu.SMEM),
        "a": pl.BlockSpec(memory_space=pl.ANY),
    }
    moved = sum(math.prod(value.shape) * value.dtype.itemsize for value in arguments)
    moved += sum(math.prod(value.shape) * value.dtype.itemsize for value in outputs)
    return pl.pallas_call(
        kernel,
        out_shape=tuple(outputs),
        in_specs=[spec[kind] for kind in kinds],
        out_specs=tuple(spec[kind] for kind in out_kinds),
        scratch_shapes=scratch,
        cost_estimate=pl.CostEstimate(
            flops=int(flops), bytes_accessed=int(moved), transcendentals=0
        ),
        compiler_params=pltpu.CompilerParams(vmem_limit_bytes=VMEM_LIMIT),
    )(*arguments)


def local_fast(
    block_in,
    cotangent,
    w_qkv,
    w_out,
    w_fc,
    w_proj,
    vectors,
    qkv_first,
    qkv_second,
    out_first,
    out_second,
    fc_first,
    fc_second,
    proj_first,
    proj_second,
    vec_first,
    vec_second,
):
    batch, ctx = lax.axis_index("batch"), lax.axis_index("ctx")
    meta = jnp.stack([batch, ctx]).astype(jnp.int32)
    inputs = block_in.reshape(TOKENS, WIDTH)
    grad_low = cotangent.reshape(TOKENS, WIDTH)
    order = ctx ^ jnp.arange(CTX, dtype=jnp.int32)
    rows = WIDTH // BATCH
    dma = pltpu.SemaphoreType.DMA((BATCH * CTX,))
    held_shape = pltpu.VMEM((CTX, WIDTH, WIDTH), LOW)
    proj_shape = pltpu.VMEM((BATCH, WIDTH, FF_SIDE), LOW)

    low_vec = vectors.astype(LOW)
    vec_parts = jnp.stack([low_vec] + [swap(low_vec, "ctx", bit) for bit in (1, 2, 3)])
    params = vec_parts[order].astype(WIDE).transpose(1, 0, 2).reshape(12, WIDTH)
    qkv_bias = jnp.concatenate([params[4], jnp.zeros((WIDTH,), WIDE), params[5]])
    qkv_bias = qkv_bias.reshape(CTX, 1, 3 * GROUP)
    fc_bias = params[8:12].reshape(CTX, 1, WIDTH)

    piece_one = jnp.concatenate([w_qkv.astype(LOW), w_out.astype(LOW)], axis=1)
    parts_one = gather_weight(piece_one)
    parts_two = gather_weight(w_fc.astype(LOW))
    parts_three = gather_weight(w_proj.astype(LOW).T)

    packed = shape_of(LOW, TOKENS, 3 * GROUP)
    single = shape_of(LOW, TOKENS, GROUP)
    square = WIDTH * WIDTH
    h_one, own, *sent = call(
        qkv_kernel,
        (meta, inputs, params, qkv_bias, *parts_one),
        "svvv" + "a" * 16,
        [shape_of(LOW, TOKENS, WIDTH)] + [packed] * 4,
        "v" * 5,
        [held_shape, pltpu.VMEM((CTX, TOKENS, 3 * GROUP), LOW), dma],
        2 * TOKENS * 3 * square,
    )
    qkv_pieces = [own] + [swap(part, "ctx", bit) for bit, part in zip((1, 2, 3), sent)]

    sequence_low = pltpu.VMEM((SPAN, GROUP), LOW)
    sequence_wide = pltpu.VMEM((SPAN, GROUP), WIDE)
    own, *sent = call(
        attend_kernel,
        (meta, *qkv_pieces),
        "s" + "v" * 4,
        [single] * 4,
        "v" * 4,
        [sequence_low] * 3 + [sequence_wide],
        2 * SPAN * SPAN * GROUP * 2,
    )
    att_pieces = [own] + [swap(part, "ctx", bit) for bit, part in zip((1, 2, 3), sent)]

    tokens_low = shape_of(LOW, TOKENS, WIDTH)
    hidden_low = shape_of(LOW, CTX, TOKENS, WIDTH)
    out, att, h_two, act, dpre, datt, dmid, own, *sent = call(
        middle_kernel,
        (
            meta,
            inputs,
            grad_low,
            params,
            fc_bias,
            *att_pieces,
            *parts_one,
            *parts_two,
            *parts_three,
        ),
        "svvvv" + "v" * 4 + "a" * 48,
        [
            tokens_low,
            tokens_low,
            tokens_low,
            hidden_low,
            hidden_low,
            tokens_low,
            shape_of(WIDE, TOKENS, WIDTH),
        ]
        + [single] * 4
        + [shape_of(WIDE, 8, WIDTH), shape_of(WIDE, CTX, 1, WIDTH)],
        "v" * 13,
        [
            pltpu.VMEM((CTX, WIDTH, TILE), LOW),
            pltpu.VMEM((WIDTH, WIDTH), LOW),
            held_shape,
            proj_shape,
            pltpu.VMEM((CTX, TOKENS, GROUP), LOW),
            pltpu.VMEM((TOKENS, WIDTH), WIDE),
            pltpu.VMEM((TOKENS, WIDTH), WIDE),
            dma,
            dma,
            dma,
        ],
        2 * TOKENS * 18 * square,
    )
    sent, (rows_two, dbias_fc) = sent[:3], sent[3:]
    grad_pieces = [own] + [swap(part, "ctx", bit) for bit, part in zip((1, 2, 3), sent)]

    row_parts = [shape_of(LOW, BATCH // 2, CTX, rows, WIDTH)] * 2
    column_parts = [shape_of(LOW, BATCH // 2, CTX, GROUP, FF_SIDE)] * 2
    proj_parts = call(
        proj_grad_kernel,
        (meta, grad_low, act),
        "svv",
        column_parts,
        "aa",
        [proj_shape, dma],
        2 * TOKENS * 4 * square,
    )
    proj_grad = scatter_grad(*proj_parts)
    fc_parts = call(
        fc_grad_kernel,
        (meta, h_two, dpre),
        "svv",
        row_parts,
        "aa",
        [held_shape, dma],
        2 * TOKENS * 4 * square,
    )
    fc_grad = scatter_grad(*fc_parts)

    own, *sent = call(
        attend_back_kernel,
        (meta, *qkv_pieces, *grad_pieces),
        "s" + "v" * 8,
        [packed] * 4,
        "v" * 4,
        [sequence_low] * 4 + [sequence_wide] * 3,
        2 * SPAN * SPAN * GROUP * 5,
    )
    mixed_pieces = [own] + [swap(part, "ctx", bit) for bit, part in zip((1, 2, 3), sent)]

    mine, theirs, mixed, dbias_qkv = call(
        qkv_grad_kernel,
        (meta, h_one, att, datt, *mixed_pieces),
        "svvv" + "v" * 4,
        row_parts + [shape_of(LOW, CTX, TOKENS, 3 * GROUP), shape_of(WIDE, CTX, 1, 3 * GROUP)],
        "aavv",
        [held_shape, pltpu.VMEM((3 * CTX, TOKENS, GROUP), LOW), dma],
        2 * TOKENS * 4 * square,
    )
    one_grad = scatter_grad(mine, theirs)
    grad_input, rows_one = call(
        input_grad_kernel,
        (meta, inputs, params, dmid, mixed, *parts_one),
        "svvvv" + "a" * 16,
        [shape_of(WIDE, TOKENS, WIDTH), shape_of(WIDE, 8, WIDTH)],
        "vv",
        [held_shape, dma],
        2 * TOKENS * 3 * square,
    )

    dbias_qkv = dbias_qkv.reshape(3, WIDTH)
    vec_rows = jnp.concatenate(
        [
            rows_one[0:2],
            rows_two[0:2],
            dbias_qkv[0:1],
            dbias_qkv[2:3],
            rows_two[2:4],
            dbias_fc.reshape(4, WIDTH),
        ],
        axis=0,
    )
    vec_rows = vec_rows.reshape(12, CTX, GROUP).transpose(1, 0, 2)[order]
    vec_grad = vec_rows[0] + sum(swap(vec_rows[bit], "ctx", bit) for bit in (1, 2, 3))
    for bit in (CORE, XBIT, YBIT):
        vec_grad = vec_grad + swap(vec_grad, "batch", bit)

    qkv_grad, out_grad = one_grad[:, : 3 * GROUP], one_grad[:, 3 * GROUP :]
    qkv_m, qkv_s, qkv_w = adamw(w_qkv, qkv_grad, qkv_first, qkv_second, 0.06, 0.1)
    out_m, out_s, out_w = adamw(w_out, out_grad, out_first, out_second, 0.06, 0.1)
    fc_m, fc_s, fc_w = adamw(w_fc, fc_grad, fc_first, fc_second, 0.06, 0.1)
    proj_m, proj_s, proj_w = adamw(w_proj, proj_grad.T, proj_first, proj_second, 0.06, 0.1)
    vec_m, vec_s, vec_w = adamw(vectors, vec_grad, vec_first, vec_second, 0.2, 0.0)
    return (
        out.reshape(block_in.shape),
        grad_input.reshape(block_in.shape),
        qkv_m,
        qkv_s,
        qkv_w,
        out_m,
        out_s,
        out_w,
        fc_m,
        fc_s,
        fc_w,
        proj_m,
        proj_s,
        proj_w,
        vec_m,
        vec_s,
        vec_w,
    )


def solution(mesh):
    in_specs = (
        P("batch", "ctx", None, None),
        P("batch", "ctx", None, None),
        P("batch", "ctx"),
        P("batch", "ctx"),
        P("batch", "ctx"),
        P("batch", "ctx"),
        P(None, "ctx"),
        P("batch", "ctx"),
        P("batch", "ctx"),
        P("batch", "ctx"),
        P("batch", "ctx"),
        P("batch", "ctx"),
        P("batch", "ctx"),
        P("batch", "ctx"),
        P("batch", "ctx"),
        P(None, "ctx"),
        P(None, "ctx"),
    )
    out_specs = (
        P("batch", "ctx", None, None),
        P("batch", "ctx", None, None),
        P("batch", "ctx"),
        P("batch", "ctx"),
        P("batch", "ctx"),
        P("batch", "ctx"),
        P("batch", "ctx"),
        P("batch", "ctx"),
        P("batch", "ctx"),
        P("batch", "ctx"),
        P("batch", "ctx"),
        P("batch", "ctx"),
        P("batch", "ctx"),
        P("batch", "ctx"),
        P(None, "ctx"),
        P(None, "ctx"),
        P(None, "ctx"),
    )
    sizes = (mesh.shape["batch"], mesh.shape["ctx"])
    local = local_fast if sizes == (BATCH, CTX) else local_any
    return jax.shard_map(local, mesh=mesh, in_specs=in_specs, out_specs=out_specs, check_vma=False)
```

```python
import functools
import math

import jax
import jax.numpy as jnp
from jax import lax
from jax.experimental import pallas as pl
from jax.experimental.pallas import tpu as pltpu
from jax.sharding import PartitionSpec as P

HEADS = 12
STEP = 10


def layer_norm(value, gain, shift):
    mean = jnp.mean(value, axis=-1, keepdims=True)
    centred = value - mean
    spread = jnp.mean(centred * centred, axis=-1, keepdims=True)
    return centred * lax.rsqrt(spread + 1e-05) * gain + shift


def gelu_tanh(value):
    return (
        0.5
        * value
        * (1.0 + jnp.tanh(0.7978845608028654 * (value + 0.044715 * value * value * value)))
    )


def block_places(index, count, half):
    offsets = jnp.arange(half, dtype=jnp.int32)
    first = index * half + offsets
    second = (2 * count - 1 - index) * half + offsets
    return jnp.concatenate([first, second])


def scores_of(queries, keys, scale, allowed):
    raw = jnp.einsum("sqhd,skhd->shqk", queries, keys, preferred_element_type=jnp.float32) * scale
    return jnp.where(allowed[None, None], raw, -1e30)


def pair_grads(queries, grads, keys, values, top, total, delta, scale, allowed):
    score = scores_of(queries, keys, scale, allowed)
    weights = jnp.exp(score - top[..., None]) / total[..., None]
    back_weights = jnp.einsum("sqhd,skhd->shqk", grads, values, preferred_element_type=jnp.float32)
    grad_score = (weights * (back_weights - delta[..., None])).astype(jnp.bfloat16)
    return (weights.astype(jnp.bfloat16), grad_score)


def rows_product(left, right):
    return jnp.einsum("ra,rb->ab", left, right, preferred_element_type=jnp.float32)


def back_product(grad, weight):
    return jnp.einsum("rb,ab->ra", grad, weight, preferred_element_type=jnp.float32)


def adamw(weight, grad, first, second, rate, decay):
    first = 0.9 * first + 0.1 * grad
    second = 0.999 * second + 0.001 * grad * grad
    first_hat = first / (1.0 - 0.9**STEP)
    second_hat = second / (1.0 - 0.999**STEP)
    weight = weight - rate * (first_hat / (jnp.sqrt(second_hat) + 1e-08) + decay * weight)
    return (first, second, weight)


def local_any(
    block_in,
    cotangent,
    w_qkv,
    w_out,
    w_fc,
    w_proj,
    vectors,
    qkv_first,
    qkv_second,
    out_first,
    out_second,
    fc_first,
    fc_second,
    proj_first,
    proj_second,
    vec_first,
    vec_second,
):
    low_type = jnp.bfloat16
    wide = jnp.float32
    row_parts = (
        lax.all_gather(w_qkv.astype(low_type), "batch", axis=0, tiled=True),
        lax.all_gather(w_out.astype(low_type), "batch", axis=0, tiled=True),
        lax.all_gather(w_fc.astype(low_type), "batch", axis=0, tiled=True),
        lax.all_gather(w_proj.astype(low_type), "batch", axis=0, tiled=True),
    )
    full_qkv, full_out, full_fc, full_proj, full_vec = (
        lax.all_gather(row_parts[0], "ctx", axis=1, tiled=True),
        lax.all_gather(row_parts[1], "ctx", axis=1, tiled=True),
        lax.all_gather(row_parts[2], "ctx", axis=1, tiled=True),
        lax.all_gather(row_parts[3], "ctx", axis=1, tiled=True),
        lax.all_gather(vectors.astype(low_type), "ctx", axis=1, tiled=True),
    )
    params = full_vec.astype(wide)
    seqs, pair, half, width = block_in.shape
    heads = HEADS
    head = width // heads
    rows = seqs * pair * half
    span = pair * half
    count = lax.axis_size("ctx")
    index = lax.axis_index("ctx")
    scale = 1.0 / math.sqrt(head)
    inputs = block_in.astype(wide).reshape(rows, width)
    normed_one = layer_norm(inputs, params[0], params[1]).astype(low_type)
    mixed = jnp.dot(normed_one, full_qkv, preferred_element_type=wide)
    queries = (mixed[:, :width] + params[4]).astype(low_type)
    keys = mixed[:, width : 2 * width].astype(low_type)
    values = (mixed[:, 2 * width :] + params[5]).astype(low_type)
    key_all, value_all = (
        lax.all_gather(keys.reshape(seqs, pair, half, width), "ctx", axis=1, tiled=True),
        lax.all_gather(values.reshape(seqs, pair, half, width), "ctx", axis=1, tiled=True),
    )
    query_heads = queries.reshape(seqs, span, heads, head)
    own_places = block_places(index, count, half)

    def piece_of(source, piece):
        return lax.dynamic_slice_in_dim(source, 2 * piece, 2, 1).reshape(seqs, span, heads, head)

    def allowed_for(piece):
        return own_places[:, None] >= block_places(piece, count, half)[None, :]

    def stats_step(piece, carry):
        top, total = carry
        score = scores_of(query_heads, piece_of(key_all, piece), scale, allowed_for(piece))
        new_top = jnp.maximum(top, jnp.max(score, axis=-1))
        total = total * jnp.exp(top - new_top) + jnp.sum(
            jnp.exp(score - new_top[..., None]), axis=-1
        )
        return (new_top, total)

    start_stats = (jnp.full((seqs, heads, span), -1e30, wide), jnp.zeros((seqs, heads, span), wide))
    top, total = lax.fori_loop(0, count, stats_step, start_stats)

    def output_step(piece, acc):
        score = scores_of(query_heads, piece_of(key_all, piece), scale, allowed_for(piece))
        weights = (jnp.exp(score - top[..., None]) / total[..., None]).astype(low_type)
        return acc + jnp.einsum(
            "shqk,skhd->sqhd", weights, piece_of(value_all, piece), preferred_element_type=wide
        )

    attended = lax.fori_loop(0, count, output_step, jnp.zeros((seqs, span, heads, head), wide))
    att_low = attended.reshape(rows, width).astype(low_type)
    mid = inputs + jnp.dot(att_low, full_out, preferred_element_type=wide) + params[6]
    normed_two = layer_norm(mid, params[2], params[3]).astype(low_type)
    pre = jnp.dot(normed_two, full_fc, preferred_element_type=wide) + params[8:12].reshape(-1)
    act_low = gelu_tanh(pre).astype(low_type)
    result = mid + jnp.dot(act_low, full_proj, preferred_element_type=wide) + params[7]
    out_block = result.astype(low_type).reshape(block_in.shape)
    grad_low = cotangent.reshape(rows, width)
    grad_out = grad_low.astype(wide)
    grad_wproj = rows_product(act_low, grad_low)
    back_act = back_product(grad_low, full_proj)
    grad_pre = jax.vjp(gelu_tanh, pre)[1](back_act)[0].astype(low_type)
    grad_wfc = rows_product(normed_two, grad_pre)
    back_two = back_product(grad_pre, full_fc)
    back_mid, grad_gain_two, grad_shift_two = jax.vjp(layer_norm, mid, params[2], params[3])[1](
        back_two
    )
    grad_mid = grad_out + back_mid
    grad_att_low = grad_mid.astype(low_type)
    grad_wout = rows_product(att_low, grad_att_low)
    back_att = back_product(grad_att_low, full_out)
    grad_heads = back_att.astype(low_type).reshape(seqs, span, heads, head)
    delta = jnp.einsum("sqhd,sqhd->shq", grad_heads.astype(wide), attended)
    query_all, grad_all = (
        lax.all_gather(queries.reshape(seqs, pair, half, width), "ctx", axis=1, tiled=True),
        lax.all_gather(grad_heads.reshape(seqs, pair, half, width), "ctx", axis=1, tiled=True),
    )
    top_all, total_all, delta_all = (
        lax.all_gather(top.reshape(seqs, heads, pair, half), "ctx", axis=2, tiled=True),
        lax.all_gather(total.reshape(seqs, heads, pair, half), "ctx", axis=2, tiled=True),
        lax.all_gather(delta.reshape(seqs, heads, pair, half), "ctx", axis=2, tiled=True),
    )

    def query_step(piece, grad_query):
        key_part = piece_of(key_all, piece)
        value_part = piece_of(value_all, piece)
        weights_low, grad_score = pair_grads(
            query_heads,
            grad_heads,
            key_part,
            value_part,
            top,
            total,
            delta,
            scale,
            allowed_for(piece),
        )
        return grad_query + jnp.einsum(
            "shqk,skhd->sqhd", grad_score, key_part, preferred_element_type=wide
        )

    grad_query = lax.fori_loop(0, count, query_step, jnp.zeros((seqs, span, heads, head), wide))
    key_heads = keys.reshape(seqs, span, heads, head)
    value_heads = values.reshape(seqs, span, heads, head)

    def stat_piece(source, piece):
        return lax.dynamic_slice_in_dim(source, 2 * piece, 2, 2).reshape(seqs, heads, span)

    def key_step(piece, carry):
        grad_key, grad_value = carry
        query_part = piece_of(query_all, piece)
        grad_part = piece_of(grad_all, piece)
        allowed = block_places(piece, count, half)[:, None] >= own_places[None, :]
        weights_low, grad_score = pair_grads(
            query_part,
            grad_part,
            key_heads,
            value_heads,
            stat_piece(top_all, piece),
            stat_piece(total_all, piece),
            stat_piece(delta_all, piece),
            scale,
            allowed,
        )
        grad_key = grad_key + jnp.einsum(
            "shqk,sqhd->skhd", grad_score, query_part, preferred_element_type=wide
        )
        grad_value = grad_value + jnp.einsum(
            "shqk,sqhd->skhd", weights_low, grad_part, preferred_element_type=wide
        )
        return (grad_key, grad_value)

    start_keys = (
        jnp.zeros((seqs, span, heads, head), wide),
        jnp.zeros((seqs, span, heads, head), wide),
    )
    grad_key, grad_value = lax.fori_loop(0, count, key_step, start_keys)
    grad_keys = (grad_key * scale).reshape(seqs, pair, half, width)
    grad_values = grad_value.reshape(seqs, pair, half, width)
    grad_q_low = (grad_query * scale).reshape(rows, width).astype(low_type)
    grad_k_low = grad_keys.reshape(rows, width).astype(low_type)
    grad_v_low = grad_values.reshape(rows, width).astype(low_type)
    grad_mixed = jnp.concatenate([grad_q_low, grad_k_low, grad_v_low], axis=1)
    grad_wqkv = rows_product(normed_one, grad_mixed)
    back_one = back_product(grad_mixed, full_qkv)
    back_in, grad_gain_one, grad_shift_one = jax.vjp(layer_norm, inputs, params[0], params[1])[1](
        back_one
    )
    grad_input = (grad_mid + back_in).reshape(block_in.shape)
    grad_bias_q = jnp.sum(grad_q_low.astype(wide), axis=0)
    grad_bias_v = jnp.sum(grad_v_low.astype(wide), axis=0)
    grad_bias_out = jnp.sum(grad_att_low.astype(wide), axis=0)
    grad_bias_proj = jnp.sum(grad_out, axis=0)
    grad_bias_fc = jnp.sum(grad_pre.astype(wide), axis=0).reshape(4, width)
    small_rows = jnp.stack(
        [
            grad_gain_one,
            grad_shift_one,
            grad_gain_two,
            grad_shift_two,
            grad_bias_q,
            grad_bias_v,
            grad_bias_out,
            grad_bias_proj,
        ]
    )
    grad_vectors = jnp.concatenate([small_rows, grad_bias_fc], axis=0)
    col_sums = (
        lax.psum_scatter(grad_wqkv, "ctx", scatter_dimension=1, tiled=True),
        lax.psum_scatter(grad_wout, "ctx", scatter_dimension=1, tiled=True),
        lax.psum_scatter(grad_wfc, "ctx", scatter_dimension=1, tiled=True),
        lax.psum_scatter(grad_wproj, "ctx", scatter_dimension=1, tiled=True),
        lax.psum_scatter(grad_vectors, "ctx", scatter_dimension=1, tiled=True),
    )
    qkv_grad, out_grad, fc_grad, proj_grad = (
        lax.psum_scatter(col_sums[0], "batch", scatter_dimension=0, tiled=True),
        lax.psum_scatter(col_sums[1], "batch", scatter_dimension=0, tiled=True),
        lax.psum_scatter(col_sums[2], "batch", scatter_dimension=0, tiled=True),
        lax.psum_scatter(col_sums[3], "batch", scatter_dimension=0, tiled=True),
    )
    vec_grad = lax.psum(col_sums[4], "batch")
    qkv_m, qkv_s, qkv_w = adamw(w_qkv, qkv_grad, qkv_first, qkv_second, 0.06, 0.1)
    out_m, out_s, out_w = adamw(w_out, out_grad, out_first, out_second, 0.06, 0.1)
    fc_m, fc_s, fc_w = adamw(w_fc, fc_grad, fc_first, fc_second, 0.06, 0.1)
    proj_m, proj_s, proj_w = adamw(w_proj, proj_grad, proj_first, proj_second, 0.06, 0.1)
    vec_m, vec_s, vec_w = adamw(vectors, vec_grad, vec_first, vec_second, 0.2, 0.0)
    return (
        out_block,
        grad_input,
        qkv_m,
        qkv_s,
        qkv_w,
        out_m,
        out_s,
        out_w,
        fc_m,
        fc_s,
        fc_w,
        proj_m,
        proj_s,
        proj_w,
        vec_m,
        vec_s,
        vec_w,
    )


BATCH = 8
CTX = 4
WIDTH = 768
HEAD = 64
GROUP = WIDTH // CTX
TOKENS = 256
HALF = 128
FF_SIDE = 384
ROWS = WIDTH // BATCH
MLP = WIDTH + 2 * FF_SIDE + 256
SPAN = TOKENS * CTX
TILE = 256
LOW = jnp.bfloat16
WIDE = jnp.float32
CORE, XBIT, YBIT = 1, 2, 4
SOURCES = (0, 2, 0, 4, 4, 6, 2, 6, 1, 3, 1, 5, 5, 7, 3, 7)
VMEM_LIMIT = 56 * 1024 * 1024


def swap(value, axis, bit):
    size = BATCH if axis == "batch" else CTX
    return lax.ppermute(value, axis, [(i, i ^ bit) for i in range(size)])


def mm(left, right):
    return lax.dot_general(left, right, (((1,), (0,)), ((), ())), preferred_element_type=WIDE)


def mt(left, right):
    return lax.dot_general(left, right, (((1,), (1,)), ((), ())), preferred_element_type=WIDE)


def tm(left, right):
    return lax.dot_general(left, right, (((0,), (0,)), ((), ())), preferred_element_type=WIDE)


def turned(value):
    return value.astype(WIDE).T.astype(LOW)


def moments(value):
    mean = jnp.mean(value, axis=-1, keepdims=True)
    centred = value - mean
    spread = jnp.mean(centred * centred, axis=-1, keepdims=True)
    return centred, lax.rsqrt(spread + 1e-05)


def norm_back(grad, normed, inverse, gain):
    part = grad * gain
    mean = jnp.mean(part, axis=-1, keepdims=True)
    cross = jnp.mean(part * normed, axis=-1, keepdims=True)
    return inverse * (part - mean - normed * cross)


def exchange(value):
    return swap(value, "ctx", 1), swap(value, "ctx", 2), swap(value, "ctx", 3)


def gather_first(piece, parts):
    near, far, last = parts
    one, two = jnp.stack([piece, near]), jnp.stack([far, last])
    return (one, two), (swap(one, "batch", XBIT), swap(two, "batch", YBIT))


def gather_second(kept, came):
    one, two = jnp.stack([kept[0], came[0]]), jnp.stack([kept[1], came[1]])
    return [one, two, swap(one, "batch", YBIT), swap(two, "batch", XBIT)]


def gather_last(held):
    return held + [swap(part, "batch", CORE) for part in held]


def scatter_first(mine, came):
    total = mine.astype(WIDE) + came.astype(WIDE)
    total = total.reshape((2, 2) + total.shape[1:])
    one, two = total[:, :, 0:2], total[:, :, 2:4]
    return (one[0], two[:, 0]), (one[1].astype(LOW), two[:, 1].astype(LOW))


def swap_pair(pair, first, second):
    return swap(pair[0], "batch", first), swap(pair[1], "batch", second)


def scatter_second(kept, back):
    one = kept[0] + back[0].astype(WIDE)
    two = kept[1] + back[1].astype(WIDE)
    return (one[0], two[0]), (one[1].astype(LOW), two[1].astype(LOW))


def scatter_third(kept, back):
    one = kept[0] + back[0].astype(WIDE)
    two = kept[1] + back[1].astype(WIDE)
    return one[0], (one[1].astype(LOW), two[0].astype(LOW), two[1].astype(LOW))


def scatter_last(kept, sent):
    near, far, last = (swap(part, "ctx", bit) for bit, part in zip((1, 2, 3), sent))
    return kept + near.astype(WIDE) + (far.astype(WIDE) + last.astype(WIDE))


def rows_of(index, size):
    return pl.ds(pl.multiple_of(index * size, 16), size)


def qkv_place(held, batch, ctx):
    return [(pl.ds(0, 3 * GROUP), held.at[ctx, rows_of(batch, ROWS), :])]


def mlp_place(held_out, held_fc, held_proj, batch, ctx):
    return [
        (pl.ds(WIDTH + 2 * FF_SIDE, TILE), held_out.at[ctx, rows_of(batch, ROWS), :]),
        (pl.ds(0, WIDTH), held_fc.at[ctx, rows_of(batch, ROWS), :]),
        (pl.ds(WIDTH, FF_SIDE), held_proj.at[batch, rows_of(2 * ctx, ROWS), :]),
        (pl.ds(WIDTH + FF_SIDE, FF_SIDE), held_proj.at[batch, rows_of(2 * ctx + 1, ROWS), :]),
    ]


def load_weight(meta, parts, place, sems):
    copies = []
    for index, part in enumerate(parts):
        for first in range(2):
            for second in range(2):
                batch = meta[0] ^ SOURCES[2 * index + first]
                ctx = meta[1] ^ (2 * (index % 2) + second)
                copies.append(
                    [
                        (part.at[first, second, :, lanes], target)
                        for lanes, target in place(batch, ctx)
                    ]
                )
    started = []
    for kind in range(len(copies[0])):
        group = []
        for number, copy in enumerate(copies):
            group.append(pltpu.make_async_copy(*copy[kind], sems.at[kind, number]))
            group[-1].start()
        started.append(group)
    return started


def store_grad(meta, place, mine, theirs, sems):
    copies = []
    for batch in range(BATCH):
        for ctx in range(CTX):
            target = theirs if batch % 2 else mine
            ranges = place(meta[0] ^ batch, meta[1] ^ ctx)
            for kind, (lanes, source) in enumerate(ranges):
                copies.append(
                    pltpu.make_async_copy(
                        source,
                        target.at[batch // 2, ctx, :, lanes],
                        sems.at[kind, batch * CTX + ctx],
                    )
                )
                copies[-1].start()
    wait_all(copies)


def wait_all(copies):
    for copy in copies:
        copy.wait()


def in_place(ctx, block):
    first = ctx if block == 0 else 2 * CTX - 1 - ctx
    return pl.ds(pl.multiple_of(first * HALF, HALF), HALF)


def read_vectors(meta, parts, chunks):
    for ctx, part in enumerate(parts):
        chunks[meta[1] ^ ctx] = part[...].astype(WIDE)
    return jnp.concatenate([chunks[index] for index in range(CTX)], axis=1)


def qkv_kernel(meta, x_ref, *refs):
    vectors, parts, refs = refs[:4], refs[4:12], refs[12:]
    h_ref, own, near, far, last, held, units, chunks, sems = refs
    (copies,) = load_weight(meta, parts, functools.partial(qkv_place, held), sems)
    params = read_vectors(meta, vectors, chunks)
    bias = jnp.concatenate([params[4:5], jnp.zeros((1, WIDTH), WIDE), params[5:6]], axis=1)
    centred, inverse = moments(x_ref[...].astype(WIDE))
    normed = (centred * inverse * params[0:1] + params[1:2]).astype(LOW)
    h_ref[...] = normed
    wait_all(copies)
    for chunk in range(CTX):
        mixed = mm(normed, held[chunk]) + bias[:, 3 * GROUP * chunk : 3 * GROUP * (chunk + 1)]
        mixed = mixed.astype(LOW)
        for part in range(3):
            unit = 3 * chunk + part
            units[unit % CTX, :, (unit // CTX) * GROUP : (unit // CTX + 1) * GROUP] = mixed[
                :, part * GROUP : (part + 1) * GROUP
            ]
    for ctx, target in enumerate((own, near, far, last)):
        target[...] = units[meta[1] ^ ctx]


def read_sequence(meta, pieces, targets):
    for ctx, piece in enumerate(pieces):
        for block in range(2):
            place = in_place(meta[1] ^ ctx, block)
            rows = piece[block * HALF : (block + 1) * HALF, :]
            for index, target in enumerate(targets):
                target[place, :] = rows[:, index * GROUP : (index + 1) * GROUP]


def write_sequence(meta, pieces, sources):
    for ctx, piece in enumerate(pieces):
        for block in range(2):
            place = in_place(meta[1] ^ ctx, block)
            for index, source in enumerate(sources):
                piece[
                    block * HALF : (block + 1) * HALF, index * GROUP : (index + 1) * GROUP
                ] = source[place, :].astype(LOW)


def head_mask(head, scale=1.0):
    lane = lax.broadcasted_iota(jnp.int32, (1, GROUP), 1)
    inside = (lane >= head * HEAD) & (lane < (head + 1) * HEAD)
    return jnp.where(inside, scale, 0.0).astype(LOW)


def tile_of(index):
    return slice(index * TILE, (index + 1) * TILE)


def weights_of(queries, k_seq, tile, causal):
    scores = [mt(queries, k_seq[tile_of(other), :]) for other in range(tile + 1)]
    scores[tile] = jnp.where(causal, scores[tile], -1e30)
    top = jnp.max(functools.reduce(jnp.maximum, scores), axis=-1, keepdims=True)
    expo = [jnp.exp(score - top) for score in scores]
    total = jnp.sum(functools.reduce(jnp.add, expo), axis=-1, keepdims=True)
    inverse = 1.0 / total
    return [value * inverse for value in expo]


def causal_tile():
    row = lax.broadcasted_iota(jnp.int32, (TILE, TILE), 0)
    column = lax.broadcasted_iota(jnp.int32, (TILE, TILE), 1)
    return row >= column


def attend_kernel(meta, *refs):
    pieces, results, (q_seq, k_seq, v_seq, out) = refs[:4], refs[4:8], refs[8:]
    read_sequence(meta, pieces, (q_seq, k_seq, v_seq))
    causal = causal_tile()
    scale = 1.0 / math.sqrt(HEAD)
    for tile in range(SPAN // TILE):

        def one_head(head, total, tile=tile):
            mask = head_mask(head)
            queries = q_seq[tile_of(tile), :] * head_mask(head, scale)
            weights = weights_of(queries, k_seq, tile, causal)
            for other, weight in enumerate(weights):
                total = total + mm(weight.astype(LOW), v_seq[tile_of(other), :] * mask)
            return total

        out[tile_of(tile), :] = lax.fori_loop(
            0, GROUP // HEAD, one_head, jnp.zeros((TILE, GROUP), WIDE)
        )
    write_sequence(meta, results, (out,))


def attend_back_kernel(meta, *refs):
    pieces, grads, results = refs[:4], refs[4:8], refs[8:12]
    q_seq, k_seq, v_seq, g_seq, dq, dk, dv = refs[12:]
    read_sequence(meta, pieces, (q_seq, k_seq, v_seq))
    read_sequence(meta, grads, (g_seq,))
    causal = causal_tile()
    scale = 1.0 / math.sqrt(HEAD)
    dk[...] = jnp.zeros_like(dk)
    dv[...] = jnp.zeros_like(dv)
    for tile in range(SPAN // TILE):

        def one_head(head, total, tile=tile):
            mask = head_mask(head)
            scaled = head_mask(head, scale)
            queries = q_seq[tile_of(tile), :] * scaled
            grad = g_seq[tile_of(tile), :] * mask
            weights = weights_of(queries, k_seq, tile, causal)
            backs = [mt(grad, v_seq[tile_of(other), :]) for other in range(tile + 1)]
            products = [weight * back for weight, back in zip(weights, backs)]
            delta = jnp.sum(functools.reduce(jnp.add, products), axis=-1, keepdims=True)
            for other, (weight, back) in enumerate(zip(weights, backs)):
                step = (weight * (back - delta)).astype(LOW)
                total = total + mm(step, k_seq[tile_of(other), :] * scaled)
                dk[tile_of(other), :] += tm(step, queries)
                dv[tile_of(other), :] += tm(weight.astype(LOW), grad)
            return total

        dq[tile_of(tile), :] = lax.fori_loop(
            0, GROUP // HEAD, one_head, jnp.zeros((TILE, GROUP), WIDE)
        )
    write_sequence(meta, results, (dq, dk, dv))


def middle_kernel(meta, x_ref, dy_ref, *refs):
    vectors, pieces, parts, refs = refs[:4], refs[4:8], refs[8:16], refs[16:]
    (out_ref, att_ref, h_ref, act_ref, dpre_ref, datt_ref, dmid_ref), refs = refs[:7], refs[7:]
    results, (rows_ref, dbias_ref), refs = refs[:4], refs[4:6], refs[6:]
    out_parts, held_out, held_fc, held_proj, units, total, back, chunks, bias, sems = refs
    place = functools.partial(mlp_place, out_parts, held_fc, held_proj)
    copies = load_weight(meta, parts, place, sems)
    vec = read_vectors(meta, vectors, chunks)
    for chunk in range(CTX):
        bias[chunk] = vec[8 + chunk : 9 + chunk]
    for ctx, piece in enumerate(pieces):
        units[meta[1] ^ ctx] = piece[...]
    att = jnp.concatenate([units[index] for index in range(CTX)], axis=1)
    att_ref[...] = att
    wait_all(copies[0])
    for chunk in range(CTX):
        held_out[:, chunk * GROUP : (chunk + 1) * GROUP] = out_parts[chunk, :, :GROUP]
    mid = x_ref[...].astype(WIDE) + mm(att, held_out[...]) + vec[6:7]
    centred, inverse = moments(mid)
    normed = centred * inverse
    h_ref[...] = (normed * vec[2:3] + vec[3:4]).astype(LOW)
    total[...] = mid + vec[7:8]
    back[...] = jnp.zeros_like(back)
    for group in copies[1:]:
        wait_all(group)
    side = FF_SIDE

    def chunk_step(chunk, carry):
        pre = mm(h_ref[...], held_fc[chunk]) + bias[chunk]
        square = pre * pre
        tanh = jnp.tanh(0.7978845608028654 * (pre + 0.044715 * square * pre))
        act = (0.5 * pre * (1.0 + tanh)).astype(LOW)
        slope = 0.5 * (1.0 + tanh) + 0.5 * pre * (1.0 - tanh * tanh) * (
            0.7978845608028654 * (1.0 + 3.0 * 0.044715 * square)
        )
        act_ref[chunk] = act
        grads = []
        for half in range(2):
            weight = held_proj[2 * chunk + half]
            total[...] += mt(act[:, half * side : (half + 1) * side], weight)
            grads.append(mm(dy_ref[...], weight))
        dpre = (jnp.concatenate(grads, axis=1) * slope).astype(LOW)
        dpre_ref[chunk] = dpre
        dbias_ref[chunk] = jnp.sum(dpre.astype(WIDE), axis=0, keepdims=True)
        back[...] += mt(dpre, held_fc[chunk])
        return carry

    lax.fori_loop(0, CTX, chunk_step, 0)
    out_ref[...] = total[...].astype(LOW)
    grad = back[...]
    dy = dy_ref[...].astype(WIDE)
    dmid = dy + norm_back(grad, normed, inverse, vec[2:3])
    dmid_ref[...] = dmid
    datt = dmid.astype(LOW)
    datt_ref[...] = datt
    rows_ref[0:1] = jnp.sum(grad * normed, axis=0, keepdims=True)
    rows_ref[1:2] = jnp.sum(grad, axis=0, keepdims=True)
    rows_ref[2:3] = jnp.sum(datt.astype(WIDE), axis=0, keepdims=True)
    rows_ref[3:4] = jnp.sum(dy, axis=0, keepdims=True)
    rows_ref[4:8] = jnp.zeros((4, WIDTH), WIDE)
    dout = mt(datt, held_out[...]).astype(LOW)
    for index in range(CTX):
        units[index] = dout[:, index * GROUP : (index + 1) * GROUP]
    for ctx, target in enumerate(results):
        target[...] = units[meta[1] ^ ctx]


def mlp_grad_kernel(meta, dy_ref, act_ref, h_ref, dpre_ref, att_ref, datt_ref, *refs):
    mine, theirs, held_out, held_fc, held_proj, sems = refs
    dy, h_two, att = turned(dy_ref[...]), turned(h_ref[...]), turned(att_ref[...])
    for chunk in range(CTX):
        proj = mm(dy, act_ref[chunk]).astype(LOW)
        for half in range(2):
            held_proj[2 * chunk + half] = proj[:, half * FF_SIDE : (half + 1) * FF_SIDE]
        held_fc[chunk] = mm(h_two, dpre_ref[chunk]).astype(LOW)
    grad = mm(att, datt_ref[...]).astype(LOW)
    for chunk in range(CTX):
        held_out[chunk, :, :GROUP] = grad[:, chunk * GROUP : (chunk + 1) * GROUP]
        held_out[chunk, :, GROUP:] = jnp.zeros((WIDTH, TILE - GROUP), LOW)
    place = functools.partial(mlp_place, held_out, held_fc, held_proj)
    store_grad(meta, place, mine, theirs, sems)


def qkv_grad_kernel(meta, h_ref, *refs):
    pieces, (mine, theirs, mixed_ref, dbias_ref, held, units, sems) = refs[:4], refs[4:]
    for ctx, piece in enumerate(pieces):
        for part in range(3):
            units[CTX * part + (meta[1] ^ ctx)] = piece[:, part * GROUP : (part + 1) * GROUP]
    left = turned(h_ref[...])
    for chunk in range(CTX):
        mixed = jnp.concatenate([units[3 * chunk + part] for part in range(3)], axis=1)
        mixed_ref[chunk] = mixed
        bias = jnp.sum(mixed.astype(WIDE), axis=0, keepdims=True)
        for part in range(3):
            dbias_ref[3 * chunk + part] = bias[:, part * GROUP : (part + 1) * GROUP]
        held[chunk] = mm(left, mixed).astype(LOW)
    store_grad(meta, functools.partial(qkv_place, held), mine, theirs, sems)


def input_grad_kernel(meta, x_ref, dmid_ref, mixed_ref, rows_ref, dfc_ref, dqkv_ref, *refs):
    vectors, parts, refs = refs[:4], refs[4:12], refs[12:]
    grad_ref, results, (held, chunks, rows, sums, sems) = refs[0], refs[1:5], refs[5:]
    (copies,) = load_weight(meta, parts, functools.partial(qkv_place, held), sems)
    params = read_vectors(meta, vectors, chunks)
    centred, inverse = moments(x_ref[...].astype(WIDE))
    normed = centred * inverse
    wait_all(copies)
    grad = jnp.zeros((TOKENS, WIDTH), WIDE)
    for chunk in range(CTX):
        grad = grad + mt(mixed_ref[chunk], held[chunk])
    grad_ref[...] = dmid_ref[...] + norm_back(grad, normed, inverse, params[0:1])
    rows[0:1] = jnp.sum(grad * normed, axis=0, keepdims=True)
    rows[1:2] = jnp.sum(grad, axis=0, keepdims=True)
    rows[2:4] = rows_ref[0:2]
    for chunk in range(CTX):
        lanes = slice(chunk * GROUP, (chunk + 1) * GROUP)
        rows[4:5, lanes] = dqkv_ref[chunk]
        rows[5:6, lanes] = dqkv_ref[2 * CTX + chunk]
        rows[8 + chunk : 9 + chunk] = dfc_ref[chunk]
    rows[6:8] = rows_ref[2:4]
    rows[12:16] = jnp.zeros((4, WIDTH), WIDE)
    for chunk in range(CTX):
        sums[chunk] = rows[:, chunk * GROUP : (chunk + 1) * GROUP]
    for ctx, target in enumerate(results):
        target[...] = sums[meta[1] ^ ctx]


def shape_of(dtype, *dims):
    return jax.ShapeDtypeStruct(dims, dtype)


def call(kernel, arguments, kinds, outputs, out_kinds, scratch, flops):
    spec = {
        "v": pl.BlockSpec(memory_space=pltpu.VMEM),
        "s": pl.BlockSpec(memory_space=pltpu.SMEM),
        "a": pl.BlockSpec(memory_space=pl.ANY),
    }
    moved = sum(math.prod(value.shape) * value.dtype.itemsize for value in arguments)
    moved += sum(math.prod(value.shape) * value.dtype.itemsize for value in outputs)
    return pl.pallas_call(
        kernel,
        out_shape=tuple(outputs),
        in_specs=[spec[kind] for kind in kinds],
        out_specs=tuple(spec[kind] for kind in out_kinds),
        scratch_shapes=scratch,
        cost_estimate=pl.CostEstimate(
            flops=int(flops), bytes_accessed=int(moved), transcendentals=0
        ),
        compiler_params=pltpu.CompilerParams(vmem_limit_bytes=VMEM_LIMIT),
    )(*arguments)


def local_fast(
    block_in,
    cotangent,
    w_qkv,
    w_out,
    w_fc,
    w_proj,
    vectors,
    qkv_first,
    qkv_second,
    out_first,
    out_second,
    fc_first,
    fc_second,
    proj_first,
    proj_second,
    vec_first,
    vec_second,
):
    batch, ctx = lax.axis_index("batch"), lax.axis_index("ctx")
    meta = jnp.stack([batch, ctx]).astype(jnp.int32)
    inputs = block_in.reshape(TOKENS, WIDTH)
    grad_low = cotangent.reshape(TOKENS, WIDTH)
    tie = lax.optimization_barrier

    qkv_sems = pltpu.SemaphoreType.DMA((1, BATCH * CTX))
    mlp_sems = pltpu.SemaphoreType.DMA((4, BATCH * CTX))
    qkv_held = pltpu.VMEM((CTX, WIDTH, 3 * GROUP), LOW)
    mlp_held = [
        pltpu.VMEM((CTX, WIDTH, TILE), LOW),
        pltpu.VMEM((CTX, WIDTH, WIDTH), LOW),
        pltpu.VMEM((BATCH, WIDTH, FF_SIDE), LOW),
    ]
    vec_held = pltpu.VMEM((CTX, 16, GROUP), WIDE)

    piece_one = w_qkv.astype(LOW)
    low_proj = w_proj.astype(LOW).T
    piece_two = jnp.concatenate(
        [
            w_fc.astype(LOW),
            low_proj[:ROWS],
            low_proj[ROWS:],
            w_out.astype(LOW),
            jnp.zeros((ROWS, TILE - GROUP), LOW),
        ],
        axis=1,
    )
    low_vec = jnp.pad(vectors.astype(LOW), ((0, 4), (0, 0)))
    parts_one = exchange(piece_one)
    vec_parts = (low_vec,) + exchange(low_vec)
    piece_two, _ = tie((piece_two, parts_one))
    parts_two = exchange(piece_two)
    parts_one = gather_second(*gather_first(piece_one, parts_one))
    parts_two, _ = tie((parts_two, parts_one))
    parts_one = gather_last(parts_one)
    kept_two, came_two = gather_first(piece_two, parts_two)

    packed = shape_of(LOW, TOKENS, 3 * GROUP)
    single = shape_of(LOW, TOKENS, GROUP)
    tokens_low = shape_of(LOW, TOKENS, WIDTH)
    hidden_low = shape_of(LOW, CTX, TOKENS, WIDTH)
    square = WIDTH * WIDTH
    h_one, own, *sent = call(
        qkv_kernel,
        (meta, inputs, *vec_parts, *parts_one),
        "s" + "v" * 5 + "a" * 8,
        [tokens_low] + [packed] * 4,
        "v" * 5,
        [qkv_held, pltpu.VMEM((CTX, TOKENS, 3 * GROUP), LOW), vec_held, qkv_sems],
        2 * TOKENS * 3 * square,
    )
    qkv_pieces = [own] + [swap(part, "ctx", bit) for bit, part in zip((1, 2, 3), sent)]

    qkv_pieces, came_two = tie((qkv_pieces, came_two))
    parts_two = gather_second(kept_two, came_two)

    sequence_low = pltpu.VMEM((SPAN, GROUP), LOW)
    sequence_wide = pltpu.VMEM((SPAN, GROUP), WIDE)
    own, *sent = call(
        attend_kernel,
        (meta, *qkv_pieces),
        "s" + "v" * 4,
        [single] * 4,
        "v" * 4,
        [sequence_low] * 3 + [sequence_wide],
        2 * SPAN * SPAN * GROUP * 2,
    )
    parts_two, _ = tie((parts_two, own))
    parts_two = gather_last(parts_two)
    att_pieces = [own] + [swap(part, "ctx", bit) for bit, part in zip((1, 2, 3), sent)]

    out, att, h_two, act, dpre, datt, dmid, own, *sent = call(
        middle_kernel,
        (meta, inputs, grad_low, *vec_parts, *att_pieces, *parts_two),
        "s" + "v" * 10 + "a" * 8,
        [tokens_low] * 3
        + [hidden_low] * 2
        + [tokens_low, shape_of(WIDE, TOKENS, WIDTH)]
        + [single] * 4
        + [shape_of(WIDE, 8, WIDTH), shape_of(WIDE, CTX, 1, WIDTH)],
        "v" * 13,
        mlp_held[:1]
        + [pltpu.VMEM((WIDTH, WIDTH), LOW)]
        + mlp_held[1:]
        + [
            pltpu.VMEM((CTX, TOKENS, GROUP), LOW),
            pltpu.VMEM((TOKENS, WIDTH), WIDE),
            pltpu.VMEM((TOKENS, WIDTH), WIDE),
            vec_held,
            pltpu.VMEM((CTX, 1, WIDTH), WIDE),
            mlp_sems,
        ],
        2 * TOKENS * 18 * square,
    )
    sent, (rows_two, dbias_fc) = sent[:3], sent[3:]
    grad_pieces = [own] + [swap(part, "ctx", bit) for bit, part in zip((1, 2, 3), sent)]

    mlp_mine, mlp_theirs = call(
        mlp_grad_kernel,
        (meta, grad_low, act, h_two, dpre, att, datt),
        "s" + "v" * 6,
        [shape_of(LOW, BATCH // 2, CTX, ROWS, MLP)] * 2,
        "aa",
        mlp_held + [mlp_sems],
        2 * TOKENS * 9 * square,
    )
    mlp_mine, mlp_theirs, grad_pieces = tie((mlp_mine, mlp_theirs, grad_pieces))
    mlp_came = swap(mlp_theirs, "batch", CORE)
    own, *sent = call(
        attend_back_kernel,
        (meta, *qkv_pieces, *grad_pieces),
        "s" + "v" * 8,
        [packed] * 4,
        "v" * 4,
        [sequence_low] * 4 + [sequence_wide] * 3,
        2 * SPAN * SPAN * GROUP * 5,
    )
    mlp_came, own, sent = tie((mlp_came, own, sent))
    mixed_pieces = [own] + [swap(part, "ctx", bit) for bit, part in zip((1, 2, 3), sent)]
    mlp_kept, mlp_sent = scatter_first(mlp_mine, mlp_came)
    mlp_kept, mlp_sent, mixed_pieces = tie((mlp_kept, mlp_sent, mixed_pieces))
    mlp_back = swap_pair(mlp_sent, YBIT, XBIT)

    qkv_mine, qkv_theirs, mixed, dbias_qkv = call(
        qkv_grad_kernel,
        (meta, h_one, *mixed_pieces),
        "s" + "v" * 5,
        [shape_of(LOW, BATCH // 2, CTX, ROWS, 3 * GROUP)] * 2
        + [shape_of(LOW, CTX, TOKENS, 3 * GROUP), shape_of(WIDE, 3 * CTX, 1, GROUP)],
        "aavv",
        [qkv_held, pltpu.VMEM((3 * CTX, TOKENS, GROUP), LOW), qkv_sems],
        2 * TOKENS * 3 * square,
    )
    qkv_came = swap(qkv_theirs, "batch", CORE)
    grad_input, own, *sent = call(
        input_grad_kernel,
        (meta, inputs, dmid, mixed, rows_two, dbias_fc, dbias_qkv, *vec_parts, *parts_one),
        "s" + "v" * 10 + "a" * 8,
        [shape_of(WIDE, TOKENS, WIDTH)] + [shape_of(WIDE, 16, GROUP)] * 4,
        "v" * 5,
        [qkv_held, vec_held, pltpu.VMEM((16, WIDTH), WIDE), vec_held, qkv_sems],
        2 * TOKENS * 3 * square,
    )
    mlp_back, own = tie((mlp_back, own))
    mlp_kept, mlp_sent = scatter_second(mlp_kept, mlp_back)
    mlp_back = swap_pair(mlp_sent, XBIT, YBIT)
    qkv_kept, qkv_sent = scatter_first(qkv_mine, qkv_came)
    qkv_back = swap_pair(qkv_sent, YBIT, XBIT)
    mlp_back, qkv_back = tie((mlp_back, qkv_back))
    mlp_kept, mlp_sent = scatter_third(mlp_kept, mlp_back)
    qkv_kept, qkv_sent = scatter_second(qkv_kept, qkv_back)
    qkv_back = swap_pair(qkv_sent, XBIT, YBIT)
    mlp_grad = scatter_last(mlp_kept, mlp_sent)
    qkv_kept, qkv_sent = scatter_third(qkv_kept, qkv_back)
    qkv_grad = scatter_last(qkv_kept, qkv_sent)

    vec_grad = own + sum(swap(part, "ctx", bit) for bit, part in zip((1, 2, 3), sent))
    for bit in (CORE, XBIT, YBIT):
        vec_grad = vec_grad + swap(vec_grad, "batch", bit)
    vec_grad = vec_grad[:12]
    fc_grad = mlp_grad[:, :WIDTH]
    proj_grad = jnp.concatenate(
        [mlp_grad[:, WIDTH : WIDTH + FF_SIDE], mlp_grad[:, WIDTH + FF_SIDE : WIDTH + 2 * FF_SIDE]],
        axis=0,
    )
    out_grad = mlp_grad[:, WIDTH + 2 * FF_SIDE : WIDTH + 2 * FF_SIDE + GROUP]

    qkv_m, qkv_s, qkv_w = adamw(w_qkv, qkv_grad, qkv_first, qkv_second, 0.06, 0.1)
    out_m, out_s, out_w = adamw(w_out, out_grad, out_first, out_second, 0.06, 0.1)
    fc_m, fc_s, fc_w = adamw(w_fc, fc_grad, fc_first, fc_second, 0.06, 0.1)
    proj_m, proj_s, proj_w = adamw(w_proj, proj_grad.T, proj_first, proj_second, 0.06, 0.1)
    vec_m, vec_s, vec_w = adamw(vectors, vec_grad, vec_first, vec_second, 0.2, 0.0)
    return (
        out.reshape(block_in.shape),
        grad_input.reshape(block_in.shape),
        qkv_m,
        qkv_s,
        qkv_w,
        out_m,
        out_s,
        out_w,
        fc_m,
        fc_s,
        fc_w,
        proj_m,
        proj_s,
        proj_w,
        vec_m,
        vec_s,
        vec_w,
    )


def solution(mesh):
    in_specs = (
        P("batch", "ctx", None, None),
        P("batch", "ctx", None, None),
        P("batch", "ctx"),
        P("batch", "ctx"),
        P("batch", "ctx"),
        P("batch", "ctx"),
        P(None, "ctx"),
        P("batch", "ctx"),
        P("batch", "ctx"),
        P("batch", "ctx"),
        P("batch", "ctx"),
        P("batch", "ctx"),
        P("batch", "ctx"),
        P("batch", "ctx"),
        P("batch", "ctx"),
        P(None, "ctx"),
        P(None, "ctx"),
    )
    out_specs = (
        P("batch", "ctx", None, None),
        P("batch", "ctx", None, None),
        P("batch", "ctx"),
        P("batch", "ctx"),
        P("batch", "ctx"),
        P("batch", "ctx"),
        P("batch", "ctx"),
        P("batch", "ctx"),
        P("batch", "ctx"),
        P("batch", "ctx"),
        P("batch", "ctx"),
        P("batch", "ctx"),
        P("batch", "ctx"),
        P("batch", "ctx"),
        P(None, "ctx"),
        P(None, "ctx"),
        P(None, "ctx"),
    )
    sizes = (mesh.shape["batch"], mesh.shape["ctx"])
    local = local_fast if sizes == (BATCH, CTX) else local_any
    return jax.shard_map(local, mesh=mesh, in_specs=in_specs, out_specs=out_specs, check_vma=False)
```

```python
import functools
import math

import jax
import jax.numpy as jnp
from jax import lax
from jax.experimental import pallas as pl
from jax.experimental.pallas import tpu as pltpu
from jax.sharding import PartitionSpec as P

HEADS = 12
STEP = 10


def layer_norm(value, gain, shift):
    mean = jnp.mean(value, axis=-1, keepdims=True)
    centred = value - mean
    spread = jnp.mean(centred * centred, axis=-1, keepdims=True)
    return centred * lax.rsqrt(spread + 1e-05) * gain + shift


def gelu_tanh(value):
    return (
        0.5
        * value
        * (1.0 + jnp.tanh(0.7978845608028654 * (value + 0.044715 * value * value * value)))
    )


def block_places(index, count, half):
    offsets = jnp.arange(half, dtype=jnp.int32)
    first = index * half + offsets
    second = (2 * count - 1 - index) * half + offsets
    return jnp.concatenate([first, second])


def scores_of(queries, keys, scale, allowed):
    raw = jnp.einsum("sqhd,skhd->shqk", queries, keys, preferred_element_type=jnp.float32) * scale
    return jnp.where(allowed[None, None], raw, -1e30)


def pair_grads(queries, grads, keys, values, top, total, delta, scale, allowed):
    score = scores_of(queries, keys, scale, allowed)
    weights = jnp.exp(score - top[..., None]) / total[..., None]
    back_weights = jnp.einsum("sqhd,skhd->shqk", grads, values, preferred_element_type=jnp.float32)
    grad_score = (weights * (back_weights - delta[..., None])).astype(jnp.bfloat16)
    return (weights.astype(jnp.bfloat16), grad_score)


def rows_product(left, right):
    return jnp.einsum("ra,rb->ab", left, right, preferred_element_type=jnp.float32)


def back_product(grad, weight):
    return jnp.einsum("rb,ab->ra", grad, weight, preferred_element_type=jnp.float32)


def adamw(weight, grad, first, second, rate, decay):
    first = 0.9 * first + 0.1 * grad
    second = 0.999 * second + 0.001 * grad * grad
    first_hat = first / (1.0 - 0.9**STEP)
    second_hat = second / (1.0 - 0.999**STEP)
    weight = weight - rate * (first_hat / (jnp.sqrt(second_hat) + 1e-08) + decay * weight)
    return (first, second, weight)


def local_any(
    block_in,
    cotangent,
    w_qkv,
    w_out,
    w_fc,
    w_proj,
    vectors,
    qkv_first,
    qkv_second,
    out_first,
    out_second,
    fc_first,
    fc_second,
    proj_first,
    proj_second,
    vec_first,
    vec_second,
):
    low_type = jnp.bfloat16
    wide = jnp.float32
    row_parts = (
        lax.all_gather(w_qkv.astype(low_type), "batch", axis=0, tiled=True),
        lax.all_gather(w_out.astype(low_type), "batch", axis=0, tiled=True),
        lax.all_gather(w_fc.astype(low_type), "batch", axis=0, tiled=True),
        lax.all_gather(w_proj.astype(low_type), "batch", axis=0, tiled=True),
    )
    full_qkv, full_out, full_fc, full_proj, full_vec = (
        lax.all_gather(row_parts[0], "ctx", axis=1, tiled=True),
        lax.all_gather(row_parts[1], "ctx", axis=1, tiled=True),
        lax.all_gather(row_parts[2], "ctx", axis=1, tiled=True),
        lax.all_gather(row_parts[3], "ctx", axis=1, tiled=True),
        lax.all_gather(vectors.astype(low_type), "ctx", axis=1, tiled=True),
    )
    params = full_vec.astype(wide)
    seqs, pair, half, width = block_in.shape
    heads = HEADS
    head = width // heads
    rows = seqs * pair * half
    span = pair * half
    count = lax.axis_size("ctx")
    index = lax.axis_index("ctx")
    scale = 1.0 / math.sqrt(head)
    inputs = block_in.astype(wide).reshape(rows, width)
    normed_one = layer_norm(inputs, params[0], params[1]).astype(low_type)
    mixed = jnp.dot(normed_one, full_qkv, preferred_element_type=wide)
    queries = (mixed[:, :width] + params[4]).astype(low_type)
    keys = mixed[:, width : 2 * width].astype(low_type)
    values = (mixed[:, 2 * width :] + params[5]).astype(low_type)
    key_all, value_all = (
        lax.all_gather(keys.reshape(seqs, pair, half, width), "ctx", axis=1, tiled=True),
        lax.all_gather(values.reshape(seqs, pair, half, width), "ctx", axis=1, tiled=True),
    )
    query_heads = queries.reshape(seqs, span, heads, head)
    own_places = block_places(index, count, half)

    def piece_of(source, piece):
        return lax.dynamic_slice_in_dim(source, 2 * piece, 2, 1).reshape(seqs, span, heads, head)

    def allowed_for(piece):
        return own_places[:, None] >= block_places(piece, count, half)[None, :]

    def stats_step(piece, carry):
        top, total = carry
        score = scores_of(query_heads, piece_of(key_all, piece), scale, allowed_for(piece))
        new_top = jnp.maximum(top, jnp.max(score, axis=-1))
        total = total * jnp.exp(top - new_top) + jnp.sum(
            jnp.exp(score - new_top[..., None]), axis=-1
        )
        return (new_top, total)

    start_stats = (jnp.full((seqs, heads, span), -1e30, wide), jnp.zeros((seqs, heads, span), wide))
    top, total = lax.fori_loop(0, count, stats_step, start_stats)

    def output_step(piece, acc):
        score = scores_of(query_heads, piece_of(key_all, piece), scale, allowed_for(piece))
        weights = (jnp.exp(score - top[..., None]) / total[..., None]).astype(low_type)
        return acc + jnp.einsum(
            "shqk,skhd->sqhd", weights, piece_of(value_all, piece), preferred_element_type=wide
        )

    attended = lax.fori_loop(0, count, output_step, jnp.zeros((seqs, span, heads, head), wide))
    att_low = attended.reshape(rows, width).astype(low_type)
    mid = inputs + jnp.dot(att_low, full_out, preferred_element_type=wide) + params[6]
    normed_two = layer_norm(mid, params[2], params[3]).astype(low_type)
    pre = jnp.dot(normed_two, full_fc, preferred_element_type=wide) + params[8:12].reshape(-1)
    act_low = gelu_tanh(pre).astype(low_type)
    result = mid + jnp.dot(act_low, full_proj, preferred_element_type=wide) + params[7]
    out_block = result.astype(low_type).reshape(block_in.shape)
    grad_low = cotangent.reshape(rows, width)
    grad_out = grad_low.astype(wide)
    grad_wproj = rows_product(act_low, grad_low)
    back_act = back_product(grad_low, full_proj)
    grad_pre = jax.vjp(gelu_tanh, pre)[1](back_act)[0].astype(low_type)
    grad_wfc = rows_product(normed_two, grad_pre)
    back_two = back_product(grad_pre, full_fc)
    back_mid, grad_gain_two, grad_shift_two = jax.vjp(layer_norm, mid, params[2], params[3])[1](
        back_two
    )
    grad_mid = grad_out + back_mid
    grad_att_low = grad_mid.astype(low_type)
    grad_wout = rows_product(att_low, grad_att_low)
    back_att = back_product(grad_att_low, full_out)
    grad_heads = back_att.astype(low_type).reshape(seqs, span, heads, head)
    delta = jnp.einsum("sqhd,sqhd->shq", grad_heads.astype(wide), attended)
    query_all, grad_all = (
        lax.all_gather(queries.reshape(seqs, pair, half, width), "ctx", axis=1, tiled=True),
        lax.all_gather(grad_heads.reshape(seqs, pair, half, width), "ctx", axis=1, tiled=True),
    )
    top_all, total_all, delta_all = (
        lax.all_gather(top.reshape(seqs, heads, pair, half), "ctx", axis=2, tiled=True),
        lax.all_gather(total.reshape(seqs, heads, pair, half), "ctx", axis=2, tiled=True),
        lax.all_gather(delta.reshape(seqs, heads, pair, half), "ctx", axis=2, tiled=True),
    )

    def query_step(piece, grad_query):
        key_part = piece_of(key_all, piece)
        value_part = piece_of(value_all, piece)
        weights_low, grad_score = pair_grads(
            query_heads,
            grad_heads,
            key_part,
            value_part,
            top,
            total,
            delta,
            scale,
            allowed_for(piece),
        )
        return grad_query + jnp.einsum(
            "shqk,skhd->sqhd", grad_score, key_part, preferred_element_type=wide
        )

    grad_query = lax.fori_loop(0, count, query_step, jnp.zeros((seqs, span, heads, head), wide))
    key_heads = keys.reshape(seqs, span, heads, head)
    value_heads = values.reshape(seqs, span, heads, head)

    def stat_piece(source, piece):
        return lax.dynamic_slice_in_dim(source, 2 * piece, 2, 2).reshape(seqs, heads, span)

    def key_step(piece, carry):
        grad_key, grad_value = carry
        query_part = piece_of(query_all, piece)
        grad_part = piece_of(grad_all, piece)
        allowed = block_places(piece, count, half)[:, None] >= own_places[None, :]
        weights_low, grad_score = pair_grads(
            query_part,
            grad_part,
            key_heads,
            value_heads,
            stat_piece(top_all, piece),
            stat_piece(total_all, piece),
            stat_piece(delta_all, piece),
            scale,
            allowed,
        )
        grad_key = grad_key + jnp.einsum(
            "shqk,sqhd->skhd", grad_score, query_part, preferred_element_type=wide
        )
        grad_value = grad_value + jnp.einsum(
            "shqk,sqhd->skhd", weights_low, grad_part, preferred_element_type=wide
        )
        return (grad_key, grad_value)

    start_keys = (
        jnp.zeros((seqs, span, heads, head), wide),
        jnp.zeros((seqs, span, heads, head), wide),
    )
    grad_key, grad_value = lax.fori_loop(0, count, key_step, start_keys)
    grad_keys = (grad_key * scale).reshape(seqs, pair, half, width)
    grad_values = grad_value.reshape(seqs, pair, half, width)
    grad_q_low = (grad_query * scale).reshape(rows, width).astype(low_type)
    grad_k_low = grad_keys.reshape(rows, width).astype(low_type)
    grad_v_low = grad_values.reshape(rows, width).astype(low_type)
    grad_mixed = jnp.concatenate([grad_q_low, grad_k_low, grad_v_low], axis=1)
    grad_wqkv = rows_product(normed_one, grad_mixed)
    back_one = back_product(grad_mixed, full_qkv)
    back_in, grad_gain_one, grad_shift_one = jax.vjp(layer_norm, inputs, params[0], params[1])[1](
        back_one
    )
    grad_input = (grad_mid + back_in).reshape(block_in.shape)
    grad_bias_q = jnp.sum(grad_q_low.astype(wide), axis=0)
    grad_bias_v = jnp.sum(grad_v_low.astype(wide), axis=0)
    grad_bias_out = jnp.sum(grad_att_low.astype(wide), axis=0)
    grad_bias_proj = jnp.sum(grad_out, axis=0)
    grad_bias_fc = jnp.sum(grad_pre.astype(wide), axis=0).reshape(4, width)
    small_rows = jnp.stack(
        [
            grad_gain_one,
            grad_shift_one,
            grad_gain_two,
            grad_shift_two,
            grad_bias_q,
            grad_bias_v,
            grad_bias_out,
            grad_bias_proj,
        ]
    )
    grad_vectors = jnp.concatenate([small_rows, grad_bias_fc], axis=0)
    col_sums = (
        lax.psum_scatter(grad_wqkv, "ctx", scatter_dimension=1, tiled=True),
        lax.psum_scatter(grad_wout, "ctx", scatter_dimension=1, tiled=True),
        lax.psum_scatter(grad_wfc, "ctx", scatter_dimension=1, tiled=True),
        lax.psum_scatter(grad_wproj, "ctx", scatter_dimension=1, tiled=True),
        lax.psum_scatter(grad_vectors, "ctx", scatter_dimension=1, tiled=True),
    )
    qkv_grad, out_grad, fc_grad, proj_grad = (
        lax.psum_scatter(col_sums[0], "batch", scatter_dimension=0, tiled=True),
        lax.psum_scatter(col_sums[1], "batch", scatter_dimension=0, tiled=True),
        lax.psum_scatter(col_sums[2], "batch", scatter_dimension=0, tiled=True),
        lax.psum_scatter(col_sums[3], "batch", scatter_dimension=0, tiled=True),
    )
    vec_grad = lax.psum(col_sums[4], "batch")
    qkv_m, qkv_s, qkv_w = adamw(w_qkv, qkv_grad, qkv_first, qkv_second, 0.06, 0.1)
    out_m, out_s, out_w = adamw(w_out, out_grad, out_first, out_second, 0.06, 0.1)
    fc_m, fc_s, fc_w = adamw(w_fc, fc_grad, fc_first, fc_second, 0.06, 0.1)
    proj_m, proj_s, proj_w = adamw(w_proj, proj_grad, proj_first, proj_second, 0.06, 0.1)
    vec_m, vec_s, vec_w = adamw(vectors, vec_grad, vec_first, vec_second, 0.2, 0.0)
    return (
        out_block,
        grad_input,
        qkv_m,
        qkv_s,
        qkv_w,
        out_m,
        out_s,
        out_w,
        fc_m,
        fc_s,
        fc_w,
        proj_m,
        proj_s,
        proj_w,
        vec_m,
        vec_s,
        vec_w,
    )


BATCH = 8
CTX = 4
WIDTH = 768
HEAD = 64
GROUP = WIDTH // CTX
TOKENS = 256
HALF = 128
FF_SIDE = 384
ROWS = WIDTH // BATCH
MLP = WIDTH + 2 * FF_SIDE + 256
SPAN = TOKENS * CTX
TILE = 256
LOW = jnp.bfloat16
WIDE = jnp.float32
CORE, XBIT, YBIT = 1, 2, 4
SOURCES = (0, 2, 0, 4, 4, 6, 2, 6, 1, 3, 1, 5, 5, 7, 3, 7)
VMEM_LIMIT = 56 * 1024 * 1024


def swap(value, axis, bit):
    size = BATCH if axis == "batch" else CTX
    return lax.ppermute(value, axis, [(i, i ^ bit) for i in range(size)])


def mm(left, right):
    return lax.dot_general(left, right, (((1,), (0,)), ((), ())), preferred_element_type=WIDE)


def mt(left, right):
    return lax.dot_general(left, right, (((1,), (1,)), ((), ())), preferred_element_type=WIDE)


def tm(left, right):
    return lax.dot_general(left, right, (((0,), (0,)), ((), ())), preferred_element_type=WIDE)


def turned(value):
    return value.astype(WIDE).T.astype(LOW)


def moments(value):
    mean = jnp.mean(value, axis=-1, keepdims=True)
    centred = value - mean
    spread = jnp.mean(centred * centred, axis=-1, keepdims=True)
    return centred, lax.rsqrt(spread + 1e-05)


def norm_back(grad, normed, inverse, gain):
    part = grad * gain
    mean = jnp.mean(part, axis=-1, keepdims=True)
    cross = jnp.mean(part * normed, axis=-1, keepdims=True)
    return inverse * (part - mean - normed * cross)


def exchange(value):
    return swap(value, "ctx", 1), swap(value, "ctx", 2), swap(value, "ctx", 3)


def gather_first(piece, parts):
    near, far, last = parts
    one, two = jnp.stack([piece, near]), jnp.stack([far, last])
    return (one, two), (swap(one, "batch", XBIT), swap(two, "batch", YBIT))


def gather_second(kept, came):
    one, two = jnp.stack([kept[0], came[0]]), jnp.stack([kept[1], came[1]])
    return [one, two, swap(one, "batch", YBIT), swap(two, "batch", XBIT)]


def gather_last(held):
    return held + [swap(part, "batch", CORE) for part in held]


def swap_pair(pair, first, second):
    return swap(pair[0], "batch", first), swap(pair[1], "batch", second)


def scatter_second(kept, back):
    one = kept[0].astype(WIDE) + back[0].astype(WIDE)
    two = kept[1].astype(WIDE) + back[1].astype(WIDE)
    return (one[0], two[0]), (one[1].astype(LOW), two[1].astype(LOW))


def scatter_third(kept, back):
    one = kept[0] + back[0].astype(WIDE)
    two = kept[1] + back[1].astype(WIDE)
    return one[0], (one[1].astype(LOW), two[0].astype(LOW), two[1].astype(LOW))


def scatter_last(kept, sent):
    near, far, last = (swap(part, "ctx", bit) for bit, part in zip((1, 2, 3), sent))
    return kept + near.astype(WIDE) + (far.astype(WIDE) + last.astype(WIDE))


def rows_of(index, size):
    return pl.ds(pl.multiple_of(index * size, 16), size)


def qkv_place(held, batch, ctx):
    return [(pl.ds(0, 3 * GROUP), held.at[ctx, rows_of(batch, ROWS), :])]


def mlp_place(held_out, held_fc, held_proj, batch, ctx):
    return [
        (pl.ds(WIDTH + 2 * FF_SIDE, TILE), held_out.at[ctx, rows_of(batch, ROWS), :]),
        (pl.ds(0, WIDTH), held_fc.at[ctx, rows_of(batch, ROWS), :]),
        (pl.ds(WIDTH, FF_SIDE), held_proj.at[batch, rows_of(2 * ctx, ROWS), :]),
        (pl.ds(WIDTH + FF_SIDE, FF_SIDE), held_proj.at[batch, rows_of(2 * ctx + 1, ROWS), :]),
    ]


def load_weight(meta, parts, place, sems):
    copies = []
    for index, part in enumerate(parts):
        for first in range(2):
            for second in range(2):
                batch = meta[0] ^ SOURCES[2 * index + first]
                ctx = meta[1] ^ (2 * (index % 2) + second)
                copies.append(
                    [
                        (part.at[first, second, :, lanes], target)
                        for lanes, target in place(batch, ctx)
                    ]
                )
    started = []
    for kind in range(len(copies[0])):
        group = []
        for number, copy in enumerate(copies):
            group.append(pltpu.make_async_copy(*copy[kind], sems.at[kind, number]))
            group[-1].start()
        started.append(group)
    return started


def store_grad(held, targets, sems):
    one_kept, one_sent, two_kept, two_sent = targets
    copies = []
    for y in range(2):
        for x in range(2):
            for ctx in range(CTX):
                if ctx < 2:
                    target = (one_sent if y else one_kept).at[x, ctx]
                else:
                    target = (two_sent if x else two_kept).at[y, ctx - 2]
                for kind, (lanes, source) in enumerate(held(2 * y + x, ctx)):
                    number = (2 * y + x) * CTX + ctx
                    copies.append(
                        pltpu.make_async_copy(source, target.at[:, lanes], sems.at[kind, number])
                    )
                    copies[-1].start()
    wait_all(copies)


def half_rows(meta, pair, held):
    for index, value in enumerate(pair):
        held[index] = turned(value)
    parts = []
    for index in range(2):
        rows = [held[index, rows_of(meta[0] ^ (2 * part), ROWS), :] for part in range(BATCH // 2)]
        parts.append(jnp.concatenate(rows, axis=0))
    return parts


def over_both(left, right):
    return mm(left[0], right[0]) + mm(left[1], right[1])


def wait_all(copies):
    for copy in copies:
        copy.wait()


def in_place(ctx, block):
    first = ctx if block == 0 else 2 * CTX - 1 - ctx
    return pl.ds(pl.multiple_of(first * HALF, HALF), HALF)


def read_vectors(meta, parts, chunks):
    for ctx, part in enumerate(parts):
        chunks[meta[1] ^ ctx] = part[...].astype(WIDE)
    return jnp.concatenate([chunks[index] for index in range(CTX)], axis=1)


def qkv_kernel(meta, x_ref, *refs):
    vectors, parts, refs = refs[:4], refs[4:12], refs[12:]
    h_ref, own, near, far, last, held, units, chunks, sems = refs
    (copies,) = load_weight(meta, parts, functools.partial(qkv_place, held), sems)
    params = read_vectors(meta, vectors, chunks)
    bias = jnp.concatenate([params[4:5], jnp.zeros((1, WIDTH), WIDE), params[5:6]], axis=1)
    centred, inverse = moments(x_ref[...].astype(WIDE))
    normed = (centred * inverse * params[0:1] + params[1:2]).astype(LOW)
    h_ref[...] = normed
    wait_all(copies)
    for chunk in range(CTX):
        mixed = mm(normed, held[chunk]) + bias[:, 3 * GROUP * chunk : 3 * GROUP * (chunk + 1)]
        mixed = mixed.astype(LOW)
        for part in range(3):
            unit = 3 * chunk + part
            units[unit % CTX, :, (unit // CTX) * GROUP : (unit // CTX + 1) * GROUP] = mixed[
                :, part * GROUP : (part + 1) * GROUP
            ]
    for ctx, target in enumerate((own, near, far, last)):
        target[...] = units[meta[1] ^ ctx]


def read_sequence(meta, pieces, targets):
    for ctx, piece in enumerate(pieces):
        for block in range(2):
            place = in_place(meta[1] ^ ctx, block)
            rows = piece[block * HALF : (block + 1) * HALF, :]
            for index, target in enumerate(targets):
                target[place, :] = rows[:, index * GROUP : (index + 1) * GROUP]


def write_sequence(meta, pieces, sources):
    for ctx, piece in enumerate(pieces):
        for block in range(2):
            place = in_place(meta[1] ^ ctx, block)
            for index, source in enumerate(sources):
                piece[
                    block * HALF : (block + 1) * HALF, index * GROUP : (index + 1) * GROUP
                ] = source[place, :].astype(LOW)


def head_mask(head, scale=1.0):
    lane = lax.broadcasted_iota(jnp.int32, (1, GROUP), 1)
    inside = (lane >= head * HEAD) & (lane < (head + 1) * HEAD)
    return jnp.where(inside, scale, 0.0).astype(LOW)


def tile_of(index):
    return slice(index * TILE, (index + 1) * TILE)


def weights_of(queries, k_seq, tile, causal):
    scores = [mt(queries, k_seq[tile_of(other), :]) for other in range(tile + 1)]
    scores[tile] = jnp.where(causal, scores[tile], -1e30)
    top = jnp.max(functools.reduce(jnp.maximum, scores), axis=-1, keepdims=True)
    expo = [jnp.exp(score - top) for score in scores]
    total = jnp.sum(functools.reduce(jnp.add, expo), axis=-1, keepdims=True)
    inverse = 1.0 / total
    return [value * inverse for value in expo]


def causal_tile():
    row = lax.broadcasted_iota(jnp.int32, (TILE, TILE), 0)
    column = lax.broadcasted_iota(jnp.int32, (TILE, TILE), 1)
    return row >= column


def attend_kernel(meta, *refs):
    pieces, results, (q_seq, k_seq, v_seq, out) = refs[:4], refs[4:8], refs[8:]
    read_sequence(meta, pieces, (q_seq, k_seq, v_seq))
    causal = causal_tile()
    scale = 1.0 / math.sqrt(HEAD)
    for tile in range(SPAN // TILE):

        def one_head(head, total, tile=tile):
            mask = head_mask(head)
            queries = q_seq[tile_of(tile), :] * head_mask(head, scale)
            weights = weights_of(queries, k_seq, tile, causal)
            for other, weight in enumerate(weights):
                total = total + mm(weight.astype(LOW), v_seq[tile_of(other), :] * mask)
            return total

        out[tile_of(tile), :] = lax.fori_loop(
            0, GROUP // HEAD, one_head, jnp.zeros((TILE, GROUP), WIDE)
        )
    write_sequence(meta, results, (out,))


def attend_back_kernel(meta, *refs):
    pieces, grads, results = refs[:4], refs[4:8], refs[8:12]
    q_seq, k_seq, v_seq, g_seq, dq, dk, dv = refs[12:]
    read_sequence(meta, pieces, (q_seq, k_seq, v_seq))
    read_sequence(meta, grads, (g_seq,))
    causal = causal_tile()
    scale = 1.0 / math.sqrt(HEAD)
    dk[...] = jnp.zeros_like(dk)
    dv[...] = jnp.zeros_like(dv)
    for tile in range(SPAN // TILE):

        def one_head(head, total, tile=tile):
            mask = head_mask(head)
            scaled = head_mask(head, scale)
            queries = q_seq[tile_of(tile), :] * scaled
            grad = g_seq[tile_of(tile), :] * mask
            weights = weights_of(queries, k_seq, tile, causal)
            backs = [mt(grad, v_seq[tile_of(other), :]) for other in range(tile + 1)]
            products = [weight * back for weight, back in zip(weights, backs)]
            delta = jnp.sum(functools.reduce(jnp.add, products), axis=-1, keepdims=True)
            for other, (weight, back) in enumerate(zip(weights, backs)):
                step = (weight * (back - delta)).astype(LOW)
                total = total + mm(step, k_seq[tile_of(other), :] * scaled)
                dk[tile_of(other), :] += tm(step, queries)
                dv[tile_of(other), :] += tm(weight.astype(LOW), grad)
            return total

        dq[tile_of(tile), :] = lax.fori_loop(
            0, GROUP // HEAD, one_head, jnp.zeros((TILE, GROUP), WIDE)
        )
    write_sequence(meta, results, (dq, dk, dv))


def middle_kernel(meta, x_ref, dy_ref, h_one_ref, *refs):
    vectors, pieces, parts, refs = refs[:4], refs[4:8], refs[8:16], refs[16:]
    (out_ref, pack_ref, mine, theirs, dmid_ref), refs = refs[:5], refs[5:]
    results, (rows_ref, dbias_ref), refs = refs[:4], refs[4:6], refs[6:]
    out_parts, held_out, held_fc, held_proj, units, total, back, chunks, bias, acts, sems = refs
    place = functools.partial(mlp_place, out_parts, held_fc, held_proj)
    copies = load_weight(meta, parts, place, sems)
    vec = read_vectors(meta, vectors, chunks)
    for chunk in range(CTX):
        bias[chunk] = vec[8 + chunk : 9 + chunk]
    for ctx, piece in enumerate(pieces):
        units[meta[1] ^ ctx] = piece[...]
    att = jnp.concatenate([units[index] for index in range(CTX)], axis=1)
    pack_ref[CTX + 1] = att
    pack_ref[CTX + 3] = dy_ref[...]
    pack_ref[CTX + 4] = h_one_ref[...]
    wait_all(copies[0])
    for chunk in range(CTX):
        held_out[:, chunk * GROUP : (chunk + 1) * GROUP] = out_parts[chunk, :, :GROUP]
    mid = x_ref[...].astype(WIDE) + mm(att, held_out[...]) + vec[6:7]
    centred, inverse = moments(mid)
    normed = centred * inverse
    pack_ref[CTX] = (normed * vec[2:3] + vec[3:4]).astype(LOW)
    total[...] = mid + vec[7:8]
    back[...] = jnp.zeros_like(back)
    for group in copies[1:]:
        wait_all(group)
    side = FF_SIDE

    def chunk_step(chunk, carry):
        pre = mm(pack_ref[CTX], held_fc[chunk]) + bias[chunk]
        square = pre * pre
        tanh = jnp.tanh(0.7978845608028654 * (pre + 0.044715 * square * pre))
        act = (0.5 * pre * (1.0 + tanh)).astype(LOW)
        slope = 0.5 * (1.0 + tanh) + 0.5 * pre * (1.0 - tanh * tanh) * (
            0.7978845608028654 * (1.0 + 3.0 * 0.044715 * square)
        )
        grads = []
        for half in range(2):
            weight = held_proj[2 * chunk + half]
            part = act[:, half * side : (half + 1) * side]
            acts[2 * chunk + half] = part
            total[...] += mt(part, weight)
            grads.append(mm(dy_ref[...], weight))
        dpre = (jnp.concatenate(grads, axis=1) * slope).astype(LOW)
        pack_ref[chunk] = dpre
        dbias_ref[chunk] = jnp.sum(dpre.astype(WIDE), axis=0, keepdims=True)
        back[...] += mt(dpre, held_fc[chunk])
        return carry

    lax.fori_loop(0, CTX, chunk_step, 0)
    out_ref[...] = total[...].astype(LOW)
    core = meta[0] & 1
    for chunk in range(CTX):
        mine[chunk] = acts[2 * chunk + core]
        theirs[chunk] = acts[2 * chunk + 1 - core]
    grad = back[...]
    dy = dy_ref[...].astype(WIDE)
    dmid = dy + norm_back(grad, normed, inverse, vec[2:3])
    dmid_ref[...] = dmid
    datt = dmid.astype(LOW)
    pack_ref[CTX + 2] = datt
    rows_ref[0:1] = jnp.sum(grad * normed, axis=0, keepdims=True)
    rows_ref[1:2] = jnp.sum(grad, axis=0, keepdims=True)
    rows_ref[2:3] = jnp.sum(datt.astype(WIDE), axis=0, keepdims=True)
    rows_ref[3:4] = jnp.sum(dy, axis=0, keepdims=True)
    rows_ref[4:8] = jnp.zeros((4, WIDTH), WIDE)
    dout = mt(datt, held_out[...]).astype(LOW)
    for index in range(CTX):
        units[index] = dout[:, index * GROUP : (index + 1) * GROUP]
    for ctx, target in enumerate(results):
        target[...] = units[meta[1] ^ ctx]


def mlp_grad_kernel(meta, *refs):
    acts, packs, targets = refs[:2], refs[2:4], refs[4:8]
    held_out, held_fc, held_proj, turn, sems = refs[8:]
    dy = [turned(pack[CTX + 3]) for pack in packs]
    for chunk in range(CTX):
        held_proj[chunk] = over_both(dy, [act[chunk] for act in acts]).astype(LOW)
    left = half_rows(meta, [pack[CTX] for pack in packs], turn)
    for chunk in range(CTX):
        held_fc[chunk] = over_both(left, [pack[chunk] for pack in packs]).astype(LOW)
    left = half_rows(meta, [pack[CTX + 1] for pack in packs], turn)
    grad = over_both(left, [pack[CTX + 2] for pack in packs]).astype(LOW)
    for chunk in range(CTX):
        held_out[chunk, :, :GROUP] = grad[:, chunk * GROUP : (chunk + 1) * GROUP]
        held_out[chunk, :, GROUP:] = jnp.zeros((WIDTH // 2, TILE - GROUP), LOW)

    def place(part, ctx):
        ctx = meta[1] ^ ctx
        chunk = (meta[0] ^ (2 * part)) // 2
        rows = pl.ds(part * ROWS, ROWS)
        return [
            (pl.ds(WIDTH + 2 * FF_SIDE, TILE), held_out.at[ctx, rows, :]),
            (pl.ds(0, WIDTH), held_fc.at[ctx, rows, :]),
            (pl.ds(WIDTH, FF_SIDE), held_proj.at[chunk, rows_of(2 * ctx, ROWS), :]),
            (pl.ds(WIDTH + FF_SIDE, FF_SIDE), held_proj.at[chunk, rows_of(2 * ctx + 1, ROWS), :]),
        ]

    store_grad(place, targets, sems)


def qkv_grad_kernel(meta, *refs):
    pack, pieces, targets = refs[:2], (refs[2:6], refs[6:10]), refs[10:14]
    mixed_ref, dbias_ref, held, units, turn, sems = refs[14:]
    for core in range(2):
        for ctx, piece in enumerate(pieces[core]):
            for part in range(3):
                units[core, CTX * part + (meta[1] ^ ctx)] = piece[
                    :, part * GROUP : (part + 1) * GROUP
                ]
    left = half_rows(meta, [pack[0][...], pack[1][...]], turn)
    for chunk in range(CTX):
        mixed = [
            jnp.concatenate([units[core, 3 * chunk + part] for part in range(3)], axis=1)
            for core in range(2)
        ]
        mixed_ref[chunk] = mixed[0]
        bias = jnp.sum(mixed[0].astype(WIDE), axis=0, keepdims=True)
        for part in range(3):
            dbias_ref[3 * chunk + part] = bias[:, part * GROUP : (part + 1) * GROUP]
        held[chunk] = over_both(left, mixed).astype(LOW)

    def place(part, ctx):
        return [(pl.ds(0, 3 * GROUP), held.at[meta[1] ^ ctx, pl.ds(part * ROWS, ROWS), :])]

    store_grad(place, targets, sems)


def input_grad_kernel(meta, x_ref, dmid_ref, mixed_ref, rows_ref, dfc_ref, dqkv_ref, *refs):
    vectors, parts, refs = refs[:4], refs[4:12], refs[12:]
    grad_ref, results, (held, chunks, rows, sums, sems) = refs[0], refs[1:5], refs[5:]
    (copies,) = load_weight(meta, parts, functools.partial(qkv_place, held), sems)
    params = read_vectors(meta, vectors, chunks)
    centred, inverse = moments(x_ref[...].astype(WIDE))
    normed = centred * inverse
    wait_all(copies)
    grad = jnp.zeros((TOKENS, WIDTH), WIDE)
    for chunk in range(CTX):
        grad = grad + mt(mixed_ref[chunk], held[chunk])
    grad_ref[...] = dmid_ref[...] + norm_back(grad, normed, inverse, params[0:1])
    rows[0:1] = jnp.sum(grad * normed, axis=0, keepdims=True)
    rows[1:2] = jnp.sum(grad, axis=0, keepdims=True)
    rows[2:4] = rows_ref[0:2]
    for chunk in range(CTX):
        lanes = slice(chunk * GROUP, (chunk + 1) * GROUP)
        rows[4:5, lanes] = dqkv_ref[chunk]
        rows[5:6, lanes] = dqkv_ref[2 * CTX + chunk]
        rows[8 + chunk : 9 + chunk] = dfc_ref[chunk]
    rows[6:8] = rows_ref[2:4]
    rows[12:16] = jnp.zeros((4, WIDTH), WIDE)
    for chunk in range(CTX):
        sums[chunk] = rows[:, chunk * GROUP : (chunk + 1) * GROUP]
    for ctx, target in enumerate(results):
        target[...] = sums[meta[1] ^ ctx]


def shape_of(dtype, *dims):
    return jax.ShapeDtypeStruct(dims, dtype)


def call(kernel, arguments, kinds, outputs, out_kinds, scratch, flops):
    spec = {
        "v": pl.BlockSpec(memory_space=pltpu.VMEM),
        "s": pl.BlockSpec(memory_space=pltpu.SMEM),
        "a": pl.BlockSpec(memory_space=pl.ANY),
    }
    moved = sum(math.prod(value.shape) * value.dtype.itemsize for value in arguments)
    moved += sum(math.prod(value.shape) * value.dtype.itemsize for value in outputs)
    return pl.pallas_call(
        kernel,
        out_shape=tuple(outputs),
        in_specs=[spec[kind] for kind in kinds],
        out_specs=tuple(spec[kind] for kind in out_kinds),
        scratch_shapes=scratch,
        cost_estimate=pl.CostEstimate(
            flops=int(flops), bytes_accessed=int(moved), transcendentals=0
        ),
        compiler_params=pltpu.CompilerParams(vmem_limit_bytes=VMEM_LIMIT),
    )(*arguments)


def local_fast(
    block_in,
    cotangent,
    w_qkv,
    w_out,
    w_fc,
    w_proj,
    vectors,
    qkv_first,
    qkv_second,
    out_first,
    out_second,
    fc_first,
    fc_second,
    proj_first,
    proj_second,
    vec_first,
    vec_second,
):
    batch, ctx = lax.axis_index("batch"), lax.axis_index("ctx")
    meta = jnp.stack([batch, ctx]).astype(jnp.int32)
    inputs = block_in.reshape(TOKENS, WIDTH)
    grad_low = cotangent.reshape(TOKENS, WIDTH)
    tie = lax.optimization_barrier

    qkv_sems = pltpu.SemaphoreType.DMA((1, BATCH * CTX))
    mlp_sems = pltpu.SemaphoreType.DMA((4, BATCH * CTX))
    qkv_held = pltpu.VMEM((CTX, WIDTH, 3 * GROUP), LOW)
    vec_held = pltpu.VMEM((CTX, 16, GROUP), WIDE)

    piece_one = w_qkv.astype(LOW)
    low_proj = w_proj.astype(LOW).T
    piece_two = jnp.concatenate(
        [
            w_fc.astype(LOW),
            low_proj[:ROWS],
            low_proj[ROWS:],
            w_out.astype(LOW),
            jnp.zeros((ROWS, TILE - GROUP), LOW),
        ],
        axis=1,
    )
    low_vec = jnp.pad(vectors.astype(LOW), ((0, 4), (0, 0)))
    parts_one = exchange(piece_one)
    vec_parts = (low_vec,) + exchange(low_vec)
    piece_two, _ = tie((piece_two, parts_one))
    parts_two = exchange(piece_two)
    parts_one = gather_second(*gather_first(piece_one, parts_one))
    parts_one = gather_last(parts_one)

    packed = shape_of(LOW, TOKENS, 3 * GROUP)
    single = shape_of(LOW, TOKENS, GROUP)
    tokens_low = shape_of(LOW, TOKENS, WIDTH)
    hidden_low = shape_of(LOW, CTX, TOKENS, WIDTH)
    square = WIDTH * WIDTH
    h_one, own, *sent = call(
        qkv_kernel,
        (meta, inputs, *vec_parts, *parts_one),
        "s" + "v" * 5 + "a" * 8,
        [tokens_low] + [packed] * 4,
        "v" * 5,
        [qkv_held, pltpu.VMEM((CTX, TOKENS, 3 * GROUP), LOW), vec_held, qkv_sems],
        2 * TOKENS * 3 * square,
    )
    parts_two, _ = tie((parts_two, own))
    kept_two, came_two = gather_first(piece_two, parts_two)
    qkv_pieces = [own] + [swap(part, "ctx", bit) for bit, part in zip((1, 2, 3), sent)]

    qkv_pieces, came_two = tie((qkv_pieces, came_two))
    parts_two = gather_second(kept_two, came_two)

    sequence_low = pltpu.VMEM((SPAN, GROUP), LOW)
    sequence_wide = pltpu.VMEM((SPAN, GROUP), WIDE)
    own, *sent = call(
        attend_kernel,
        (meta, *qkv_pieces),
        "s" + "v" * 4,
        [single] * 4,
        "v" * 4,
        [sequence_low] * 3 + [sequence_wide],
        2 * SPAN * SPAN * GROUP * 2,
    )
    att_pieces = [own] + [swap(part, "ctx", bit) for bit, part in zip((1, 2, 3), sent)]
    last_two, _ = tie((parts_two[2:], att_pieces[1]))
    parts_two = gather_last(parts_two[:2] + last_two)

    pack_shape = shape_of(LOW, CTX + 5, TOKENS, WIDTH)
    act_shape = shape_of(LOW, BATCH // 2, TOKENS, FF_SIDE)
    out, pack, act_mine, act_theirs, dmid, own, *sent = call(
        middle_kernel,
        (meta, inputs, grad_low, h_one, *vec_parts, *att_pieces, *parts_two),
        "s" + "v" * 11 + "a" * 8,
        [tokens_low, pack_shape, act_shape, act_shape, shape_of(WIDE, TOKENS, WIDTH)]
        + [single] * 4
        + [shape_of(WIDE, 8, WIDTH), shape_of(WIDE, CTX, 1, WIDTH)],
        "v" * 11,
        [
            pltpu.VMEM((CTX, WIDTH, TILE), LOW),
            pltpu.VMEM((WIDTH, WIDTH), LOW),
            pltpu.VMEM((CTX, WIDTH, WIDTH), LOW),
            pltpu.VMEM((BATCH, WIDTH, FF_SIDE), LOW),
            pltpu.VMEM((CTX, TOKENS, GROUP), LOW),
            pltpu.VMEM((TOKENS, WIDTH), WIDE),
            pltpu.VMEM((TOKENS, WIDTH), WIDE),
            vec_held,
            pltpu.VMEM((CTX, 1, WIDTH), WIDE),
            pltpu.VMEM((BATCH, TOKENS, FF_SIDE), LOW),
            mlp_sems,
        ],
        2 * TOKENS * 18 * square,
    )
    sent, (rows_two, dbias_fc) = sent[:3], sent[3:]
    grad_pieces = [own] + [swap(part, "ctx", bit) for bit, part in zip((1, 2, 3), sent)]
    act_came, pack_came = swap(act_theirs, "batch", CORE), swap(pack, "batch", CORE)

    half_sems = BATCH * CTX // 2
    turn_held = pltpu.VMEM((2, WIDTH, TOKENS), LOW)
    mlp_parts = call(
        mlp_grad_kernel,
        (meta, act_mine, act_came, pack, pack_came),
        "s" + "v" * 4,
        [shape_of(LOW, 2, 2, ROWS, MLP)] * 4,
        "aaaa",
        [
            pltpu.VMEM((CTX, WIDTH // 2, TILE), LOW),
            pltpu.VMEM((CTX, WIDTH // 2, WIDTH), LOW),
            pltpu.VMEM((BATCH // 2, WIDTH, FF_SIDE), LOW),
            turn_held,
            pltpu.SemaphoreType.DMA((4, half_sems)),
        ],
        2 * TOKENS * 9 * square,
    )
    mlp_parts, grad_pieces = tie((mlp_parts, grad_pieces))
    mlp_kept = mlp_parts[0], mlp_parts[2]
    mlp_back = swap_pair((mlp_parts[1], mlp_parts[3]), YBIT, XBIT)
    own, *sent = call(
        attend_back_kernel,
        (meta, *qkv_pieces, *grad_pieces),
        "s" + "v" * 8,
        [packed] * 4,
        "v" * 4,
        [sequence_low] * 4 + [sequence_wide] * 3,
        2 * SPAN * SPAN * GROUP * 5,
    )
    mixed_pieces = [own] + [swap(part, "ctx", bit) for bit, part in zip((1, 2, 3), sent)]
    mixed_came = [swap(part, "batch", CORE) for part in mixed_pieces]
    mlp_back, mixed_pieces, mixed_came = tie((mlp_back, mixed_pieces, mixed_came))
    mlp_kept, mlp_sent = scatter_second(mlp_kept, mlp_back)
    mlp_back = swap_pair(mlp_sent, XBIT, YBIT)

    *qkv_parts, mixed, dbias_qkv = call(
        qkv_grad_kernel,
        (meta, pack[CTX + 4], pack_came[CTX + 4], *mixed_pieces, *mixed_came),
        "s" + "v" * 10,
        [shape_of(LOW, 2, 2, ROWS, 3 * GROUP)] * 4
        + [shape_of(LOW, CTX, TOKENS, 3 * GROUP), shape_of(WIDE, 3 * CTX, 1, GROUP)],
        "aaaavv",
        [
            pltpu.VMEM((CTX, WIDTH // 2, 3 * GROUP), LOW),
            pltpu.VMEM((2, 3 * CTX, TOKENS, GROUP), LOW),
            turn_held,
            pltpu.SemaphoreType.DMA((1, half_sems)),
        ],
        2 * TOKENS * 3 * square,
    )
    qkv_kept = qkv_parts[0], qkv_parts[2]
    qkv_back = swap_pair((qkv_parts[1], qkv_parts[3]), YBIT, XBIT)
    grad_input, own, *sent = call(
        input_grad_kernel,
        (meta, inputs, dmid, mixed, rows_two, dbias_fc, dbias_qkv, *vec_parts, *parts_one),
        "s" + "v" * 10 + "a" * 8,
        [shape_of(WIDE, TOKENS, WIDTH)] + [shape_of(WIDE, 16, GROUP)] * 4,
        "v" * 5,
        [qkv_held, vec_held, pltpu.VMEM((16, WIDTH), WIDE), vec_held, qkv_sems],
        2 * TOKENS * 3 * square,
    )
    mlp_back, own, sent = tie((mlp_back, own, sent))
    mlp_kept, mlp_sent = scatter_third(mlp_kept, mlp_back)
    qkv_kept, qkv_sent = scatter_second(qkv_kept, qkv_back)
    qkv_back = swap_pair(qkv_sent, XBIT, YBIT)
    mlp_grad = scatter_last(mlp_kept, mlp_sent)
    qkv_kept, qkv_sent = scatter_third(qkv_kept, qkv_back)
    qkv_grad = scatter_last(qkv_kept, qkv_sent)

    vec_grad = own + sum(swap(part, "ctx", bit) for bit, part in zip((1, 2, 3), sent))
    for bit in (CORE, XBIT, YBIT):
        vec_grad = vec_grad + swap(vec_grad, "batch", bit)
    vec_grad = vec_grad[:12]
    fc_grad = mlp_grad[:, :WIDTH]
    proj_grad = jnp.concatenate(
        [mlp_grad[:, WIDTH : WIDTH + FF_SIDE], mlp_grad[:, WIDTH + FF_SIDE : WIDTH + 2 * FF_SIDE]],
        axis=0,
    )
    out_grad = mlp_grad[:, WIDTH + 2 * FF_SIDE : WIDTH + 2 * FF_SIDE + GROUP]

    qkv_m, qkv_s, qkv_w = adamw(w_qkv, qkv_grad, qkv_first, qkv_second, 0.06, 0.1)
    out_m, out_s, out_w = adamw(w_out, out_grad, out_first, out_second, 0.06, 0.1)
    fc_m, fc_s, fc_w = adamw(w_fc, fc_grad, fc_first, fc_second, 0.06, 0.1)
    proj_m, proj_s, proj_w = adamw(w_proj, proj_grad.T, proj_first, proj_second, 0.06, 0.1)
    vec_m, vec_s, vec_w = adamw(vectors, vec_grad, vec_first, vec_second, 0.2, 0.0)
    return (
        out.reshape(block_in.shape),
        grad_input.reshape(block_in.shape),
        qkv_m,
        qkv_s,
        qkv_w,
        out_m,
        out_s,
        out_w,
        fc_m,
        fc_s,
        fc_w,
        proj_m,
        proj_s,
        proj_w,
        vec_m,
        vec_s,
        vec_w,
    )


def solution(mesh):
    in_specs = (
        P("batch", "ctx", None, None),
        P("batch", "ctx", None, None),
        P("batch", "ctx"),
        P("batch", "ctx"),
        P("batch", "ctx"),
        P("batch", "ctx"),
        P(None, "ctx"),
        P("batch", "ctx"),
        P("batch", "ctx"),
        P("batch", "ctx"),
        P("batch", "ctx"),
        P("batch", "ctx"),
        P("batch", "ctx"),
        P("batch", "ctx"),
        P("batch", "ctx"),
        P(None, "ctx"),
        P(None, "ctx"),
    )
    out_specs = (
        P("batch", "ctx", None, None),
        P("batch", "ctx", None, None),
        P("batch", "ctx"),
        P("batch", "ctx"),
        P("batch", "ctx"),
        P("batch", "ctx"),
        P("batch", "ctx"),
        P("batch", "ctx"),
        P("batch", "ctx"),
        P("batch", "ctx"),
        P("batch", "ctx"),
        P("batch", "ctx"),
        P("batch", "ctx"),
        P("batch", "ctx"),
        P(None, "ctx"),
        P(None, "ctx"),
        P(None, "ctx"),
    )
    sizes = (mesh.shape["batch"], mesh.shape["ctx"])
    local = local_fast if sizes == (BATCH, CTX) else local_any
    return jax.shard_map(local, mesh=mesh, in_specs=in_specs, out_specs=out_specs, check_vma=False)
```

```python
import functools
import math

import jax
import jax.numpy as jnp
from jax import lax
from jax.experimental import pallas as pl
from jax.experimental.pallas import tpu as pltpu
from jax.sharding import PartitionSpec as P

HEADS = 12
STEP = 10


def layer_norm(value, gain, shift):
    mean = jnp.mean(value, axis=-1, keepdims=True)
    centred = value - mean
    spread = jnp.mean(centred * centred, axis=-1, keepdims=True)
    return centred * lax.rsqrt(spread + 1e-05) * gain + shift


def gelu_tanh(value):
    return (
        0.5
        * value
        * (1.0 + jnp.tanh(0.7978845608028654 * (value + 0.044715 * value * value * value)))
    )


def block_places(index, count, half):
    offsets = jnp.arange(half, dtype=jnp.int32)
    first = index * half + offsets
    second = (2 * count - 1 - index) * half + offsets
    return jnp.concatenate([first, second])


def scores_of(queries, keys, scale, allowed):
    raw = jnp.einsum("sqhd,skhd->shqk", queries, keys, preferred_element_type=jnp.float32) * scale
    return jnp.where(allowed[None, None], raw, -1e30)


def pair_grads(queries, grads, keys, values, top, total, delta, scale, allowed):
    score = scores_of(queries, keys, scale, allowed)
    weights = jnp.exp(score - top[..., None]) / total[..., None]
    back_weights = jnp.einsum("sqhd,skhd->shqk", grads, values, preferred_element_type=jnp.float32)
    grad_score = (weights * (back_weights - delta[..., None])).astype(jnp.bfloat16)
    return (weights.astype(jnp.bfloat16), grad_score)


def rows_product(left, right):
    return jnp.einsum("ra,rb->ab", left, right, preferred_element_type=jnp.float32)


def back_product(grad, weight):
    return jnp.einsum("rb,ab->ra", grad, weight, preferred_element_type=jnp.float32)


def adamw(weight, grad, first, second, rate, decay):
    first = 0.9 * first + 0.1 * grad
    second = 0.999 * second + 0.001 * grad * grad
    first_hat = first / (1.0 - 0.9**STEP)
    second_hat = second / (1.0 - 0.999**STEP)
    weight = weight - rate * (first_hat / (jnp.sqrt(second_hat) + 1e-08) + decay * weight)
    return (first, second, weight)


def local_any(
    block_in,
    cotangent,
    w_qkv,
    w_out,
    w_fc,
    w_proj,
    vectors,
    qkv_first,
    qkv_second,
    out_first,
    out_second,
    fc_first,
    fc_second,
    proj_first,
    proj_second,
    vec_first,
    vec_second,
):
    low_type = jnp.bfloat16
    wide = jnp.float32
    row_parts = (
        lax.all_gather(w_qkv.astype(low_type), "batch", axis=0, tiled=True),
        lax.all_gather(w_out.astype(low_type), "batch", axis=0, tiled=True),
        lax.all_gather(w_fc.astype(low_type), "batch", axis=0, tiled=True),
        lax.all_gather(w_proj.astype(low_type), "batch", axis=0, tiled=True),
    )
    full_qkv, full_out, full_fc, full_proj, full_vec = (
        lax.all_gather(row_parts[0], "ctx", axis=1, tiled=True),
        lax.all_gather(row_parts[1], "ctx", axis=1, tiled=True),
        lax.all_gather(row_parts[2], "ctx", axis=1, tiled=True),
        lax.all_gather(row_parts[3], "ctx", axis=1, tiled=True),
        lax.all_gather(vectors.astype(low_type), "ctx", axis=1, tiled=True),
    )
    params = full_vec.astype(wide)
    seqs, pair, half, width = block_in.shape
    heads = HEADS
    head = width // heads
    rows = seqs * pair * half
    span = pair * half
    count = lax.axis_size("ctx")
    index = lax.axis_index("ctx")
    scale = 1.0 / math.sqrt(head)
    inputs = block_in.astype(wide).reshape(rows, width)
    normed_one = layer_norm(inputs, params[0], params[1]).astype(low_type)
    mixed = jnp.dot(normed_one, full_qkv, preferred_element_type=wide)
    queries = (mixed[:, :width] + params[4]).astype(low_type)
    keys = mixed[:, width : 2 * width].astype(low_type)
    values = (mixed[:, 2 * width :] + params[5]).astype(low_type)
    key_all, value_all = (
        lax.all_gather(keys.reshape(seqs, pair, half, width), "ctx", axis=1, tiled=True),
        lax.all_gather(values.reshape(seqs, pair, half, width), "ctx", axis=1, tiled=True),
    )
    query_heads = queries.reshape(seqs, span, heads, head)
    own_places = block_places(index, count, half)

    def piece_of(source, piece):
        return lax.dynamic_slice_in_dim(source, 2 * piece, 2, 1).reshape(seqs, span, heads, head)

    def allowed_for(piece):
        return own_places[:, None] >= block_places(piece, count, half)[None, :]

    def stats_step(piece, carry):
        top, total = carry
        score = scores_of(query_heads, piece_of(key_all, piece), scale, allowed_for(piece))
        new_top = jnp.maximum(top, jnp.max(score, axis=-1))
        total = total * jnp.exp(top - new_top) + jnp.sum(
            jnp.exp(score - new_top[..., None]), axis=-1
        )
        return (new_top, total)

    start_stats = (jnp.full((seqs, heads, span), -1e30, wide), jnp.zeros((seqs, heads, span), wide))
    top, total = lax.fori_loop(0, count, stats_step, start_stats)

    def output_step(piece, acc):
        score = scores_of(query_heads, piece_of(key_all, piece), scale, allowed_for(piece))
        weights = (jnp.exp(score - top[..., None]) / total[..., None]).astype(low_type)
        return acc + jnp.einsum(
            "shqk,skhd->sqhd", weights, piece_of(value_all, piece), preferred_element_type=wide
        )

    attended = lax.fori_loop(0, count, output_step, jnp.zeros((seqs, span, heads, head), wide))
    att_low = attended.reshape(rows, width).astype(low_type)
    mid = inputs + jnp.dot(att_low, full_out, preferred_element_type=wide) + params[6]
    normed_two = layer_norm(mid, params[2], params[3]).astype(low_type)
    pre = jnp.dot(normed_two, full_fc, preferred_element_type=wide) + params[8:12].reshape(-1)
    act_low = gelu_tanh(pre).astype(low_type)
    result = mid + jnp.dot(act_low, full_proj, preferred_element_type=wide) + params[7]
    out_block = result.astype(low_type).reshape(block_in.shape)
    grad_low = cotangent.reshape(rows, width)
    grad_out = grad_low.astype(wide)
    grad_wproj = rows_product(act_low, grad_low)
    back_act = back_product(grad_low, full_proj)
    grad_pre = jax.vjp(gelu_tanh, pre)[1](back_act)[0].astype(low_type)
    grad_wfc = rows_product(normed_two, grad_pre)
    back_two = back_product(grad_pre, full_fc)
    back_mid, grad_gain_two, grad_shift_two = jax.vjp(layer_norm, mid, params[2], params[3])[1](
        back_two
    )
    grad_mid = grad_out + back_mid
    grad_att_low = grad_mid.astype(low_type)
    grad_wout = rows_product(att_low, grad_att_low)
    back_att = back_product(grad_att_low, full_out)
    grad_heads = back_att.astype(low_type).reshape(seqs, span, heads, head)
    delta = jnp.einsum("sqhd,sqhd->shq", grad_heads.astype(wide), attended)
    query_all, grad_all = (
        lax.all_gather(queries.reshape(seqs, pair, half, width), "ctx", axis=1, tiled=True),
        lax.all_gather(grad_heads.reshape(seqs, pair, half, width), "ctx", axis=1, tiled=True),
    )
    top_all, total_all, delta_all = (
        lax.all_gather(top.reshape(seqs, heads, pair, half), "ctx", axis=2, tiled=True),
        lax.all_gather(total.reshape(seqs, heads, pair, half), "ctx", axis=2, tiled=True),
        lax.all_gather(delta.reshape(seqs, heads, pair, half), "ctx", axis=2, tiled=True),
    )

    def query_step(piece, grad_query):
        key_part = piece_of(key_all, piece)
        value_part = piece_of(value_all, piece)
        weights_low, grad_score = pair_grads(
            query_heads,
            grad_heads,
            key_part,
            value_part,
            top,
            total,
            delta,
            scale,
            allowed_for(piece),
        )
        return grad_query + jnp.einsum(
            "shqk,skhd->sqhd", grad_score, key_part, preferred_element_type=wide
        )

    grad_query = lax.fori_loop(0, count, query_step, jnp.zeros((seqs, span, heads, head), wide))
    key_heads = keys.reshape(seqs, span, heads, head)
    value_heads = values.reshape(seqs, span, heads, head)

    def stat_piece(source, piece):
        return lax.dynamic_slice_in_dim(source, 2 * piece, 2, 2).reshape(seqs, heads, span)

    def key_step(piece, carry):
        grad_key, grad_value = carry
        query_part = piece_of(query_all, piece)
        grad_part = piece_of(grad_all, piece)
        allowed = block_places(piece, count, half)[:, None] >= own_places[None, :]
        weights_low, grad_score = pair_grads(
            query_part,
            grad_part,
            key_heads,
            value_heads,
            stat_piece(top_all, piece),
            stat_piece(total_all, piece),
            stat_piece(delta_all, piece),
            scale,
            allowed,
        )
        grad_key = grad_key + jnp.einsum(
            "shqk,sqhd->skhd", grad_score, query_part, preferred_element_type=wide
        )
        grad_value = grad_value + jnp.einsum(
            "shqk,sqhd->skhd", weights_low, grad_part, preferred_element_type=wide
        )
        return (grad_key, grad_value)

    start_keys = (
        jnp.zeros((seqs, span, heads, head), wide),
        jnp.zeros((seqs, span, heads, head), wide),
    )
    grad_key, grad_value = lax.fori_loop(0, count, key_step, start_keys)
    grad_keys = (grad_key * scale).reshape(seqs, pair, half, width)
    grad_values = grad_value.reshape(seqs, pair, half, width)
    grad_q_low = (grad_query * scale).reshape(rows, width).astype(low_type)
    grad_k_low = grad_keys.reshape(rows, width).astype(low_type)
    grad_v_low = grad_values.reshape(rows, width).astype(low_type)
    grad_mixed = jnp.concatenate([grad_q_low, grad_k_low, grad_v_low], axis=1)
    grad_wqkv = rows_product(normed_one, grad_mixed)
    back_one = back_product(grad_mixed, full_qkv)
    back_in, grad_gain_one, grad_shift_one = jax.vjp(layer_norm, inputs, params[0], params[1])[1](
        back_one
    )
    grad_input = (grad_mid + back_in).reshape(block_in.shape)
    grad_bias_q = jnp.sum(grad_q_low.astype(wide), axis=0)
    grad_bias_v = jnp.sum(grad_v_low.astype(wide), axis=0)
    grad_bias_out = jnp.sum(grad_att_low.astype(wide), axis=0)
    grad_bias_proj = jnp.sum(grad_out, axis=0)
    grad_bias_fc = jnp.sum(grad_pre.astype(wide), axis=0).reshape(4, width)
    small_rows = jnp.stack(
        [
            grad_gain_one,
            grad_shift_one,
            grad_gain_two,
            grad_shift_two,
            grad_bias_q,
            grad_bias_v,
            grad_bias_out,
            grad_bias_proj,
        ]
    )
    grad_vectors = jnp.concatenate([small_rows, grad_bias_fc], axis=0)
    col_sums = (
        lax.psum_scatter(grad_wqkv, "ctx", scatter_dimension=1, tiled=True),
        lax.psum_scatter(grad_wout, "ctx", scatter_dimension=1, tiled=True),
        lax.psum_scatter(grad_wfc, "ctx", scatter_dimension=1, tiled=True),
        lax.psum_scatter(grad_wproj, "ctx", scatter_dimension=1, tiled=True),
        lax.psum_scatter(grad_vectors, "ctx", scatter_dimension=1, tiled=True),
    )
    qkv_grad, out_grad, fc_grad, proj_grad = (
        lax.psum_scatter(col_sums[0], "batch", scatter_dimension=0, tiled=True),
        lax.psum_scatter(col_sums[1], "batch", scatter_dimension=0, tiled=True),
        lax.psum_scatter(col_sums[2], "batch", scatter_dimension=0, tiled=True),
        lax.psum_scatter(col_sums[3], "batch", scatter_dimension=0, tiled=True),
    )
    vec_grad = lax.psum(col_sums[4], "batch")
    qkv_m, qkv_s, qkv_w = adamw(w_qkv, qkv_grad, qkv_first, qkv_second, 0.06, 0.1)
    out_m, out_s, out_w = adamw(w_out, out_grad, out_first, out_second, 0.06, 0.1)
    fc_m, fc_s, fc_w = adamw(w_fc, fc_grad, fc_first, fc_second, 0.06, 0.1)
    proj_m, proj_s, proj_w = adamw(w_proj, proj_grad, proj_first, proj_second, 0.06, 0.1)
    vec_m, vec_s, vec_w = adamw(vectors, vec_grad, vec_first, vec_second, 0.2, 0.0)
    return (
        out_block,
        grad_input,
        qkv_m,
        qkv_s,
        qkv_w,
        out_m,
        out_s,
        out_w,
        fc_m,
        fc_s,
        fc_w,
        proj_m,
        proj_s,
        proj_w,
        vec_m,
        vec_s,
        vec_w,
    )


BATCH = 8
CTX = 4
WIDTH = 768
HEAD = 64
GROUP = WIDTH // CTX
TOKENS = 256
HALF = 128
FF_SIDE = 384
ROWS = WIDTH // BATCH
MLP = WIDTH + 2 * FF_SIDE + 256
SPAN = TOKENS * CTX
TILE = 256
LOW = jnp.bfloat16
WIDE = jnp.float32
CORE, XBIT, YBIT = 1, 2, 4
SOURCES = (
    (0, (0, 1, 2, 3)),
    (XBIT, (0, 1, 2, 3)),
    (YBIT, (0, 1, 2, 3)),
    (XBIT + YBIT, (0, 1)),
    (XBIT + YBIT, (2, 3)),
    (CORE, (0, 1, 2, 3)),
    (CORE + XBIT, (0, 1, 2, 3)),
    (CORE + YBIT, (0, 1, 2, 3)),
    (CORE + XBIT + YBIT, (0, 1)),
    (CORE + XBIT + YBIT, (2, 3)),
)
PARTS = len(SOURCES)
VMEM_LIMIT = 56 * 1024 * 1024


def swap(value, axis, bit):
    size = BATCH if axis == "batch" else CTX
    return lax.ppermute(value, axis, [(i, i ^ bit) for i in range(size)])


def mm(left, right):
    return lax.dot_general(left, right, (((1,), (0,)), ((), ())), preferred_element_type=WIDE)


def mt(left, right):
    return lax.dot_general(left, right, (((1,), (1,)), ((), ())), preferred_element_type=WIDE)


def tm(left, right):
    return lax.dot_general(left, right, (((0,), (0,)), ((), ())), preferred_element_type=WIDE)


def turned(value):
    return value.astype(WIDE).T.astype(LOW)


def moments(value):
    mean = jnp.mean(value, axis=-1, keepdims=True)
    centred = value - mean
    spread = jnp.mean(centred * centred, axis=-1, keepdims=True)
    return centred, lax.rsqrt(spread + 1e-05)


def norm_back(grad, normed, inverse, gain):
    part = grad * gain
    mean = jnp.mean(part, axis=-1, keepdims=True)
    cross = jnp.mean(part * normed, axis=-1, keepdims=True)
    return inverse * (part - mean - normed * cross)


def exchange(value):
    return swap(value, "ctx", 1), swap(value, "ctx", 2), swap(value, "ctx", 3)


def gather_first(own):
    return swap(own, "batch", XBIT), swap(own, "batch", YBIT)


def gather_second(from_x, from_y):
    return swap(from_x[:2], "batch", YBIT), swap(from_y[2:], "batch", XBIT)


def to_core(parts):
    return [swap(part, "batch", CORE) for part in parts]


def swap_pair(pair, first, second):
    return swap(pair[0], "batch", first), swap(pair[1], "batch", second)


def scatter_second(kept, back):
    one = kept[0].astype(WIDE) + back[0].astype(WIDE)
    two = kept[1].astype(WIDE) + back[1].astype(WIDE)
    return (one[0], two[0]), (one[1].astype(LOW), two[1].astype(LOW))


def scatter_third(kept, back):
    one = kept[0] + back[0].astype(WIDE)
    two = kept[1] + back[1].astype(WIDE)
    return one[0], (one[1].astype(LOW), two[0].astype(LOW), two[1].astype(LOW))


def scatter_last(kept, sent):
    near, far, last = (swap(part, "ctx", bit) for bit, part in zip((1, 2, 3), sent))
    return kept + near.astype(WIDE) + (far.astype(WIDE) + last.astype(WIDE))


def rows_of(index, size):
    return pl.ds(pl.multiple_of(index * size, 16), size)


def qkv_place(held, batch, ctx):
    return [(pl.ds(0, 3 * GROUP), held.at[ctx, rows_of(batch, ROWS), :])]


def mlp_place(held_out, held_fc, held_proj, batch, ctx):
    return [
        (pl.ds(WIDTH + 2 * FF_SIDE, TILE), held_out.at[ctx, rows_of(batch, ROWS), :]),
        (pl.ds(0, WIDTH), held_fc.at[ctx, rows_of(batch, ROWS), :]),
        (pl.ds(WIDTH, FF_SIDE), held_proj.at[batch, rows_of(2 * ctx, ROWS), :]),
        (pl.ds(WIDTH + FF_SIDE, FF_SIDE), held_proj.at[batch, rows_of(2 * ctx + 1, ROWS), :]),
    ]


def load_weight(meta, parts, place, sems, shift):
    copies = []
    for part, (source, places) in zip(parts, SOURCES):
        for index, ctx in enumerate(places):
            ranges = place(meta[0] ^ source, ctx ^ shift)
            copies.append([(part.at[index, :, lanes], target) for lanes, target in ranges])
    started = []
    for kind in range(len(copies[0])):
        group = []
        for number, copy in enumerate(copies):
            group.append(pltpu.make_async_copy(*copy[kind], sems.at[kind, number]))
            group[-1].start()
        started.append(group)
    return started


def store_grad(held, targets, sems):
    one_kept, one_sent, two_kept, two_sent = targets
    copies = []
    for y in range(2):
        for x in range(2):
            for ctx in range(CTX):
                if ctx < 2:
                    target = (one_sent if y else one_kept).at[x, ctx]
                else:
                    target = (two_sent if x else two_kept).at[y, ctx - 2]
                for kind, (lanes, source) in enumerate(held(2 * y + x, ctx)):
                    number = (2 * y + x) * CTX + ctx
                    copies.append(
                        pltpu.make_async_copy(source, target.at[:, lanes], sems.at[kind, number])
                    )
                    copies[-1].start()
    wait_all(copies)


def half_rows(meta, pair, held):
    for index, value in enumerate(pair):
        held[index] = turned(value)
    parts = []
    for index in range(2):
        rows = [held[index, rows_of(meta[0] ^ (2 * part), ROWS), :] for part in range(BATCH // 2)]
        parts.append(jnp.concatenate(rows, axis=0))
    return parts


def over_both(left, right):
    return mm(left[0], right[0]) + mm(left[1], right[1])


def wait_all(copies):
    for copy in copies:
        copy.wait()


def in_place(ctx, block):
    first = ctx if block == 0 else 2 * CTX - 1 - ctx
    return pl.ds(pl.multiple_of(first * HALF, HALF), HALF)


def read_vectors(meta, parts, chunks):
    for ctx, part in enumerate(parts):
        rows = [part[16 * index : 16 * (index + 1), :] for index in range(GROUP // HEAD)]
        chunks[meta[1] ^ ctx] = jnp.concatenate(rows, axis=1).astype(WIDE)
    return jnp.concatenate([chunks[index] for index in range(CTX)], axis=1)


def qkv_kernel(meta, x_ref, *refs):
    vectors, parts, refs = refs[:4], refs[4 : 4 + PARTS], refs[4 + PARTS :]
    h_ref, own, near, far, last, held, units, chunks, sems = refs
    (copies,) = load_weight(meta, parts, functools.partial(qkv_place, held), sems, meta[1])
    params = read_vectors(meta, vectors, chunks)
    bias = jnp.concatenate([params[4:5], jnp.zeros((1, WIDTH), WIDE), params[5:6]], axis=1)
    centred, inverse = moments(x_ref[...].astype(WIDE))
    normed = (centred * inverse * params[0:1] + params[1:2]).astype(LOW)
    h_ref[...] = normed
    wait_all(copies)
    for chunk in range(CTX):
        mixed = mm(normed, held[chunk]) + bias[:, 3 * GROUP * chunk : 3 * GROUP * (chunk + 1)]
        mixed = mixed.astype(LOW)
        for part in range(3):
            unit = 3 * chunk + part
            units[unit % CTX, :, (unit // CTX) * GROUP : (unit // CTX + 1) * GROUP] = mixed[
                :, part * GROUP : (part + 1) * GROUP
            ]
    for ctx, target in enumerate((own, near, far, last)):
        target[...] = units[meta[1] ^ ctx]


def read_sequence(meta, pieces, targets):
    for ctx, piece in enumerate(pieces):
        for block in range(2):
            place = in_place(meta[1] ^ ctx, block)
            rows = piece[block * HALF : (block + 1) * HALF, :]
            for index, target in enumerate(targets):
                target[place, :] = rows[:, index * GROUP : (index + 1) * GROUP]


def write_sequence(meta, pieces, sources):
    for ctx, piece in enumerate(pieces):
        for block in range(2):
            place = in_place(meta[1] ^ ctx, block)
            for index, source in enumerate(sources):
                piece[
                    block * HALF : (block + 1) * HALF, index * GROUP : (index + 1) * GROUP
                ] = source[place, :].astype(LOW)


def head_mask(head, scale=1.0):
    lane = lax.broadcasted_iota(jnp.int32, (1, GROUP), 1)
    inside = (lane >= head * HEAD) & (lane < (head + 1) * HEAD)
    return jnp.where(inside, scale, 0.0).astype(LOW)


def tile_of(index):
    return slice(index * TILE, (index + 1) * TILE)


def weights_of(queries, k_seq, tile, causal):
    scores = [mt(queries, k_seq[tile_of(other), :]) for other in range(tile + 1)]
    scores[tile] = jnp.where(causal, scores[tile], -1e30)
    top = jnp.max(functools.reduce(jnp.maximum, scores), axis=-1, keepdims=True)
    expo = [jnp.exp(score - top) for score in scores]
    total = jnp.sum(functools.reduce(jnp.add, expo), axis=-1, keepdims=True)
    inverse = 1.0 / total
    return [value * inverse for value in expo]


def causal_tile():
    row = lax.broadcasted_iota(jnp.int32, (TILE, TILE), 0)
    column = lax.broadcasted_iota(jnp.int32, (TILE, TILE), 1)
    return row >= column


def attend_kernel(meta, *refs):
    pieces, results, (q_seq, k_seq, v_seq, out) = refs[:4], refs[4:8], refs[8:]
    read_sequence(meta, pieces, (q_seq, k_seq, v_seq))
    causal = causal_tile()
    scale = 1.0 / math.sqrt(HEAD)
    for tile in range(SPAN // TILE):

        def one_head(head, total, tile=tile):
            mask = head_mask(head)
            queries = q_seq[tile_of(tile), :] * head_mask(head, scale)
            weights = weights_of(queries, k_seq, tile, causal)
            for other, weight in enumerate(weights):
                total = total + mm(weight.astype(LOW), v_seq[tile_of(other), :] * mask)
            return total

        out[tile_of(tile), :] = lax.fori_loop(
            0, GROUP // HEAD, one_head, jnp.zeros((TILE, GROUP), WIDE)
        )
    write_sequence(meta, results, (out,))


def attend_back_kernel(meta, *refs):
    pieces, grads, results = refs[:4], refs[4:8], refs[8:12]
    q_seq, k_seq, v_seq, g_seq, dq, dk, dv = refs[12:]
    read_sequence(meta, pieces, (q_seq, k_seq, v_seq))
    read_sequence(meta, grads, (g_seq,))
    causal = causal_tile()
    scale = 1.0 / math.sqrt(HEAD)
    dk[...] = jnp.zeros_like(dk)
    dv[...] = jnp.zeros_like(dv)
    for tile in range(SPAN // TILE):

        def one_head(head, total, tile=tile):
            mask = head_mask(head)
            scaled = head_mask(head, scale)
            queries = q_seq[tile_of(tile), :] * scaled
            grad = g_seq[tile_of(tile), :] * mask
            weights = weights_of(queries, k_seq, tile, causal)
            backs = [mt(grad, v_seq[tile_of(other), :]) for other in range(tile + 1)]
            products = [weight * back for weight, back in zip(weights, backs)]
            delta = jnp.sum(functools.reduce(jnp.add, products), axis=-1, keepdims=True)
            for other, (weight, back) in enumerate(zip(weights, backs)):
                step = (weight * (back - delta)).astype(LOW)
                total = total + mm(step, k_seq[tile_of(other), :] * scaled)
                dk[tile_of(other), :] += tm(step, queries)
                dv[tile_of(other), :] += tm(weight.astype(LOW), grad)
            return total

        dq[tile_of(tile), :] = lax.fori_loop(
            0, GROUP // HEAD, one_head, jnp.zeros((TILE, GROUP), WIDE)
        )
    write_sequence(meta, results, (dq, dk, dv))


def middle_kernel(meta, x_ref, dy_ref, h_one_ref, *refs):
    vectors, pieces, parts, refs = refs[:4], refs[4:8], refs[8 : 8 + PARTS], refs[8 + PARTS :]
    (out_ref, pack_ref, mine, theirs, dmid_ref), refs = refs[:5], refs[5:]
    results, (rows_ref, dbias_ref), refs = refs[:4], refs[4:6], refs[6:]
    out_parts, held_out, held_fc, held_proj, units, total, back, chunks, bias, acts, sems = refs
    place = functools.partial(mlp_place, out_parts, held_fc, held_proj)
    copies = load_weight(meta, parts, place, sems, 0)
    vec = read_vectors(meta, vectors, chunks)
    for chunk in range(CTX):
        bias[chunk] = vec[8 + chunk : 9 + chunk]
    for ctx, piece in enumerate(pieces):
        units[meta[1] ^ ctx] = piece[...]
    att = jnp.concatenate([units[index] for index in range(CTX)], axis=1)
    pack_ref[CTX + 1] = att
    pack_ref[CTX + 3] = dy_ref[...]
    pack_ref[CTX + 4] = h_one_ref[...]
    wait_all(copies[0])
    for chunk in range(CTX):
        held_out[:, chunk * GROUP : (chunk + 1) * GROUP] = out_parts[chunk, :, :GROUP]
    mid = x_ref[...].astype(WIDE) + mm(att, held_out[...]) + vec[6:7]
    centred, inverse = moments(mid)
    normed = centred * inverse
    pack_ref[CTX] = (normed * vec[2:3] + vec[3:4]).astype(LOW)
    total[...] = mid + vec[7:8]
    back[...] = jnp.zeros_like(back)
    for group in copies[1:]:
        wait_all(group)
    side = FF_SIDE

    def chunk_step(chunk, carry):
        pre = mm(pack_ref[CTX], held_fc[chunk]) + bias[chunk]
        square = pre * pre
        tanh = jnp.tanh(0.7978845608028654 * (pre + 0.044715 * square * pre))
        act = (0.5 * pre * (1.0 + tanh)).astype(LOW)
        slope = 0.5 * (1.0 + tanh) + 0.5 * pre * (1.0 - tanh * tanh) * (
            0.7978845608028654 * (1.0 + 3.0 * 0.044715 * square)
        )
        grads = []
        for half in range(2):
            weight = held_proj[2 * chunk + half]
            part = act[:, half * side : (half + 1) * side]
            acts[2 * chunk + half] = part
            total[...] += mt(part, weight)
            grads.append(mm(dy_ref[...], weight))
        dpre = (jnp.concatenate(grads, axis=1) * slope).astype(LOW)
        pack_ref[chunk] = dpre
        dbias_ref[chunk] = jnp.sum(dpre.astype(WIDE), axis=0, keepdims=True)
        back[...] += mt(dpre, held_fc[chunk])
        return carry

    lax.fori_loop(0, CTX, chunk_step, 0)
    out_ref[...] = total[...].astype(LOW)
    core = meta[0] & 1
    for chunk in range(CTX):
        mine[chunk] = acts[2 * chunk + core]
        theirs[chunk] = acts[2 * chunk + 1 - core]
    grad = back[...]
    dy = dy_ref[...].astype(WIDE)
    dmid = dy + norm_back(grad, normed, inverse, vec[2:3])
    dmid_ref[...] = dmid
    datt = dmid.astype(LOW)
    pack_ref[CTX + 2] = datt
    rows_ref[0:1] = jnp.sum(grad * normed, axis=0, keepdims=True)
    rows_ref[1:2] = jnp.sum(grad, axis=0, keepdims=True)
    rows_ref[2:3] = jnp.sum(datt.astype(WIDE), axis=0, keepdims=True)
    rows_ref[3:4] = jnp.sum(dy, axis=0, keepdims=True)
    rows_ref[4:8] = jnp.zeros((4, WIDTH), WIDE)
    dout = mt(datt, held_out[...]).astype(LOW)
    for index in range(CTX):
        units[index] = dout[:, index * GROUP : (index + 1) * GROUP]
    for ctx, target in enumerate(results):
        target[...] = units[meta[1] ^ ctx]


def mlp_grad_kernel(meta, *refs):
    acts, packs, targets = refs[:2], refs[2:4], refs[4:8]
    held_out, held_fc, held_proj, turn, sems = refs[8:]
    dy = [turned(pack[CTX + 3]) for pack in packs]
    for chunk in range(CTX):
        held_proj[chunk] = over_both(dy, [act[chunk] for act in acts]).astype(LOW)
    left = half_rows(meta, [pack[CTX] for pack in packs], turn)
    for chunk in range(CTX):
        held_fc[chunk] = over_both(left, [pack[chunk] for pack in packs]).astype(LOW)
    left = half_rows(meta, [pack[CTX + 1] for pack in packs], turn)
    grad = over_both(left, [pack[CTX + 2] for pack in packs]).astype(LOW)
    for chunk in range(CTX):
        held_out[chunk, :, :GROUP] = grad[:, chunk * GROUP : (chunk + 1) * GROUP]
        held_out[chunk, :, GROUP:] = jnp.zeros((WIDTH // 2, TILE - GROUP), LOW)

    def place(part, ctx):
        ctx = meta[1] ^ ctx
        chunk = (meta[0] ^ (2 * part)) // 2
        rows = pl.ds(part * ROWS, ROWS)
        return [
            (pl.ds(WIDTH + 2 * FF_SIDE, TILE), held_out.at[ctx, rows, :]),
            (pl.ds(0, WIDTH), held_fc.at[ctx, rows, :]),
            (pl.ds(WIDTH, FF_SIDE), held_proj.at[chunk, rows_of(2 * ctx, ROWS), :]),
            (pl.ds(WIDTH + FF_SIDE, FF_SIDE), held_proj.at[chunk, rows_of(2 * ctx + 1, ROWS), :]),
        ]

    store_grad(place, targets, sems)


def qkv_grad_kernel(meta, *refs):
    pack, pieces, targets = refs[:2], (refs[2:6], refs[6:10]), refs[10:14]
    mixed_ref, dbias_ref, held, units, turn, sems = refs[14:]
    for core in range(2):
        for ctx, piece in enumerate(pieces[core]):
            for part in range(3):
                units[core, CTX * part + (meta[1] ^ ctx)] = piece[
                    :, part * GROUP : (part + 1) * GROUP
                ]
    left = half_rows(meta, [pack[0][...], pack[1][...]], turn)
    for chunk in range(CTX):
        mixed = [
            jnp.concatenate([units[core, 3 * chunk + part] for part in range(3)], axis=1)
            for core in range(2)
        ]
        mixed_ref[chunk] = mixed[0]
        bias = jnp.sum(mixed[0].astype(WIDE), axis=0, keepdims=True)
        for part in range(3):
            dbias_ref[3 * chunk + part] = bias[:, part * GROUP : (part + 1) * GROUP]
        held[chunk] = over_both(left, mixed).astype(LOW)

    def place(part, ctx):
        return [(pl.ds(0, 3 * GROUP), held.at[meta[1] ^ ctx, pl.ds(part * ROWS, ROWS), :])]

    store_grad(place, targets, sems)


def input_grad_kernel(meta, x_ref, dmid_ref, mixed_ref, rows_ref, dfc_ref, dqkv_ref, *refs):
    vectors, parts, refs = refs[:4], refs[4 : 4 + PARTS], refs[4 + PARTS :]
    grad_ref, results, (held, chunks, rows, sums, sems) = refs[0], refs[1:5], refs[5:]
    (copies,) = load_weight(meta, parts, functools.partial(qkv_place, held), sems, meta[1])
    params = read_vectors(meta, vectors, chunks)
    centred, inverse = moments(x_ref[...].astype(WIDE))
    normed = centred * inverse
    wait_all(copies)
    grad = jnp.zeros((TOKENS, WIDTH), WIDE)
    for chunk in range(CTX):
        grad = grad + mt(mixed_ref[chunk], held[chunk])
    grad_ref[...] = dmid_ref[...] + norm_back(grad, normed, inverse, params[0:1])
    rows[0:1] = jnp.sum(grad * normed, axis=0, keepdims=True)
    rows[1:2] = jnp.sum(grad, axis=0, keepdims=True)
    rows[2:4] = rows_ref[0:2]
    for chunk in range(CTX):
        lanes = slice(chunk * GROUP, (chunk + 1) * GROUP)
        rows[4:5, lanes] = dqkv_ref[chunk]
        rows[5:6, lanes] = dqkv_ref[2 * CTX + chunk]
        rows[8 + chunk : 9 + chunk] = dfc_ref[chunk]
    rows[6:8] = rows_ref[2:4]
    rows[12:16] = jnp.zeros((4, WIDTH), WIDE)
    for chunk in range(CTX):
        sums[chunk] = rows[:, chunk * GROUP : (chunk + 1) * GROUP]
    for ctx, target in enumerate(results):
        target[...] = sums[meta[1] ^ ctx]


def shape_of(dtype, *dims):
    return jax.ShapeDtypeStruct(dims, dtype)


def call(kernel, arguments, kinds, outputs, out_kinds, scratch, flops):
    spec = {
        "v": pl.BlockSpec(memory_space=pltpu.VMEM),
        "s": pl.BlockSpec(memory_space=pltpu.SMEM),
        "a": pl.BlockSpec(memory_space=pl.ANY),
        "h": pl.BlockSpec((None, TOKENS, WIDTH), lambda step: (CTX + 4, 0, 0)),
    }
    moved = sum(math.prod(value.shape) * value.dtype.itemsize for value in arguments)
    moved += sum(math.prod(value.shape) * value.dtype.itemsize for value in outputs)
    return pl.pallas_call(
        kernel,
        grid=(1,),
        out_shape=tuple(outputs),
        in_specs=[spec[kind] for kind in kinds],
        out_specs=tuple(spec[kind] for kind in out_kinds),
        scratch_shapes=scratch,
        cost_estimate=pl.CostEstimate(
            flops=int(flops), bytes_accessed=int(moved), transcendentals=0
        ),
        compiler_params=pltpu.CompilerParams(vmem_limit_bytes=VMEM_LIMIT),
    )(*arguments)


def local_fast(
    block_in,
    cotangent,
    w_qkv,
    w_out,
    w_fc,
    w_proj,
    vectors,
    qkv_first,
    qkv_second,
    out_first,
    out_second,
    fc_first,
    fc_second,
    proj_first,
    proj_second,
    vec_first,
    vec_second,
):
    batch, ctx = lax.axis_index("batch"), lax.axis_index("ctx")
    meta = jnp.stack([batch, ctx]).astype(jnp.int32)
    inputs = block_in.reshape(TOKENS, WIDTH)
    grad_low = cotangent.reshape(TOKENS, WIDTH)
    tie = lax.optimization_barrier

    qkv_sems = pltpu.SemaphoreType.DMA((1, BATCH * CTX))
    mlp_sems = pltpu.SemaphoreType.DMA((4, BATCH * CTX))
    qkv_held = pltpu.VMEM((CTX, WIDTH, 3 * GROUP), LOW)
    vec_held = pltpu.VMEM((CTX, 16, GROUP), WIDE)

    low_vec = jnp.pad(vectors.astype(LOW), ((0, 4), (0, 0)))
    low_vec = [low_vec[:, start : start + HEAD] for start in range(0, GROUP, HEAD)]
    low_vec = jnp.concatenate(low_vec + [jnp.zeros((ROWS - 48, HEAD), LOW)], axis=0)
    piece_one = jnp.concatenate([w_qkv.astype(LOW), low_vec], axis=1)
    low_proj = w_proj.astype(LOW).T
    piece_two = jnp.concatenate(
        [
            w_fc.astype(LOW),
            low_proj[:ROWS],
            low_proj[ROWS:],
            w_out.astype(LOW),
            jnp.zeros((ROWS, TILE - GROUP), LOW),
        ],
        axis=1,
    )
    parts_one = (piece_one,) + exchange(piece_one)
    vec_parts = [part[:48, 3 * GROUP :] for part in parts_one]
    parts_one = [part[:, : 3 * GROUP] for part in parts_one]
    own_one = jnp.stack(parts_one)
    piece_two, late_vec = tie((piece_two, vec_parts))
    own_two = lax.all_gather(piece_two, "ctx", axis=0)
    x_one, y_one = gather_first(own_one)
    parts_one = [own_one, x_one, y_one, *gather_second(x_one, y_one)]
    parts_one = parts_one + to_core(parts_one)

    packed = shape_of(LOW, TOKENS, 3 * GROUP)
    single = shape_of(LOW, TOKENS, GROUP)
    tokens_low = shape_of(LOW, TOKENS, WIDTH)
    hidden_low = shape_of(LOW, CTX, TOKENS, WIDTH)
    square = WIDTH * WIDTH
    h_one, own, *sent = call(
        qkv_kernel,
        (meta, inputs, *vec_parts, *parts_one),
        "s" + "v" * 5 + "a" * PARTS,
        [tokens_low] + [packed] * 4,
        "v" * 5,
        [qkv_held, pltpu.VMEM((CTX, TOKENS, 3 * GROUP), LOW), vec_held, qkv_sems],
        2 * TOKENS * 3 * square,
    )
    qkv_pieces = [own] + [swap(part, "ctx", bit) for bit, part in zip((1, 2, 3), sent)]

    own_two, late_h = tie((own_two, h_one))
    x_two, y_two = gather_first(own_two)
    qkv_pieces, x_two, y_two = tie((qkv_pieces, x_two, y_two))
    across_two = gather_second(x_two, y_two)
    parts_two = [own_two, x_two, y_two]
    swapped_two = to_core(parts_two)

    sequence_low = pltpu.VMEM((SPAN, GROUP), LOW)
    sequence_wide = pltpu.VMEM((SPAN, GROUP), WIDE)
    own, *sent = call(
        attend_kernel,
        (meta, *qkv_pieces),
        "s" + "v" * 4,
        [single] * 4,
        "v" * 4,
        [sequence_low] * 3 + [sequence_wide],
        2 * SPAN * SPAN * GROUP * 2,
    )
    sent, swapped_two = tie((sent, swapped_two))
    att_pieces = [own] + [swap(part, "ctx", bit) for bit, part in zip((1, 2, 3), sent)]
    across_two, att_pieces = tie((across_two, att_pieces))
    parts_two = parts_two + list(across_two) + swapped_two + to_core(across_two)

    pack_shape = shape_of(LOW, CTX + 5, TOKENS, WIDTH)
    act_shape = shape_of(LOW, BATCH // 2, TOKENS, FF_SIDE)
    out, pack, act_mine, act_theirs, dmid, own, *sent = call(
        middle_kernel,
        (meta, inputs, grad_low, late_h, *vec_parts, *att_pieces, *parts_two),
        "s" + "v" * 11 + "a" * PARTS,
        [tokens_low, pack_shape, act_shape, act_shape, shape_of(WIDE, TOKENS, WIDTH)]
        + [single] * 4
        + [shape_of(WIDE, 8, WIDTH), shape_of(WIDE, CTX, 1, WIDTH)],
        "v" * 11,
        [
            pltpu.VMEM((CTX, WIDTH, TILE), LOW),
            pltpu.VMEM((WIDTH, WIDTH), LOW),
            pltpu.VMEM((CTX, WIDTH, WIDTH), LOW),
            pltpu.VMEM((BATCH, WIDTH, FF_SIDE), LOW),
            pltpu.VMEM((CTX, TOKENS, GROUP), LOW),
            pltpu.VMEM((TOKENS, WIDTH), WIDE),
            pltpu.VMEM((TOKENS, WIDTH), WIDE),
            vec_held,
            pltpu.VMEM((CTX, 1, WIDTH), WIDE),
            pltpu.VMEM((BATCH, TOKENS, FF_SIDE), LOW),
            mlp_sems,
        ],
        2 * TOKENS * 18 * square,
    )
    sent, (rows_two, dbias_fc) = sent[:3], sent[3:]
    grad_pieces = [own] + [swap(part, "ctx", bit) for bit, part in zip((1, 2, 3), sent)]
    act_came, pack_came = swap(act_theirs, "batch", CORE), swap(pack, "batch", CORE)

    half_sems = BATCH * CTX // 2
    turn_held = pltpu.VMEM((2, WIDTH, TOKENS), LOW)
    mlp_parts = call(
        mlp_grad_kernel,
        (meta, act_mine, act_came, pack, pack_came),
        "s" + "v" * 4,
        [shape_of(LOW, 2, 2, ROWS, MLP)] * 4,
        "aaaa",
        [
            pltpu.VMEM((CTX, WIDTH // 2, TILE), LOW),
            pltpu.VMEM((CTX, WIDTH // 2, WIDTH), LOW),
            pltpu.VMEM((BATCH // 2, WIDTH, FF_SIDE), LOW),
            turn_held,
            pltpu.SemaphoreType.DMA((4, half_sems)),
        ],
        2 * TOKENS * 9 * square,
    )
    mlp_parts, grad_pieces = tie((mlp_parts, grad_pieces))
    mlp_kept = mlp_parts[0], mlp_parts[2]
    mlp_back = swap_pair((mlp_parts[1], mlp_parts[3]), YBIT, XBIT)
    own, *sent = call(
        attend_back_kernel,
        (meta, *qkv_pieces, *grad_pieces),
        "s" + "v" * 8,
        [packed] * 4,
        "v" * 4,
        [sequence_low] * 4 + [sequence_wide] * 3,
        2 * SPAN * SPAN * GROUP * 5,
    )
    mixed_pieces = [own] + [swap(part, "ctx", bit) for bit, part in zip((1, 2, 3), sent)]
    came = to_core(mixed_pieces[:1])
    mlp_back, received = tie((mlp_back, mixed_pieces[1:]))
    mixed_pieces = mixed_pieces[:1] + received
    mixed_came = came + to_core(received)
    mlp_kept, mlp_sent = scatter_second(mlp_kept, mlp_back)
    mlp_sent, mixed_came = tie((mlp_sent, mixed_came))
    mlp_back = swap_pair(mlp_sent, XBIT, YBIT)

    *qkv_parts, mixed, dbias_qkv = call(
        qkv_grad_kernel,
        (meta, pack, pack_came, *mixed_pieces, *mixed_came),
        "shh" + "v" * 8,
        [shape_of(LOW, 2, 2, ROWS, 3 * GROUP)] * 4
        + [shape_of(LOW, CTX, TOKENS, 3 * GROUP), shape_of(WIDE, 3 * CTX, 1, GROUP)],
        "aaaavv",
        [
            pltpu.VMEM((CTX, WIDTH // 2, 3 * GROUP), LOW),
            pltpu.VMEM((2, 3 * CTX, TOKENS, GROUP), LOW),
            turn_held,
            pltpu.SemaphoreType.DMA((1, half_sems)),
        ],
        2 * TOKENS * 3 * square,
    )
    qkv_kept = qkv_parts[0], qkv_parts[2]
    qkv_back = swap_pair((qkv_parts[1], qkv_parts[3]), YBIT, XBIT)
    grad_input, own, *sent = call(
        input_grad_kernel,
        (meta, inputs, dmid, mixed, rows_two, dbias_fc, dbias_qkv, *late_vec, *parts_one),
        "s" + "v" * 10 + "a" * PARTS,
        [shape_of(WIDE, TOKENS, WIDTH)] + [shape_of(WIDE, 16, GROUP)] * 4,
        "v" * 5,
        [qkv_held, vec_held, pltpu.VMEM((16, WIDTH), WIDE), vec_held, qkv_sems],
        2 * TOKENS * 3 * square,
    )
    mlp_back, qkv_back = tie((mlp_back, qkv_back))
    mlp_one = mlp_kept[0].astype(WIDE) + mlp_back[0].astype(WIDE)
    mlp_two = (mlp_kept[1].astype(WIDE) + mlp_back[1].astype(WIDE)).astype(LOW)
    mlp_two = swap(mlp_two, "ctx", 2)
    mlp_one = mlp_one + mlp_two.astype(WIDE)
    mlp_grad = mlp_one[0] + swap(mlp_one[1].astype(LOW), "ctx", 1).astype(WIDE)
    qkv_kept, qkv_sent = scatter_second(qkv_kept, qkv_back)
    qkv_back = swap_pair(qkv_sent, XBIT, YBIT)
    qkv_kept, qkv_sent = scatter_third(qkv_kept, qkv_back)
    qkv_grad = scatter_last(qkv_kept, qkv_sent)

    vec_grad = own + sum(swap(part, "ctx", bit) for bit, part in zip((1, 2, 3), sent))
    for bit in (CORE, XBIT, YBIT):
        vec_grad = vec_grad + swap(vec_grad, "batch", bit)
    vec_grad = vec_grad[:12]
    fc_grad = mlp_grad[:, :WIDTH]
    proj_grad = jnp.concatenate(
        [mlp_grad[:, WIDTH : WIDTH + FF_SIDE], mlp_grad[:, WIDTH + FF_SIDE : WIDTH + 2 * FF_SIDE]],
        axis=0,
    )
    out_grad = mlp_grad[:, WIDTH + 2 * FF_SIDE : WIDTH + 2 * FF_SIDE + GROUP]

    qkv_m, qkv_s, qkv_w = adamw(w_qkv, qkv_grad, qkv_first, qkv_second, 0.06, 0.1)
    out_m, out_s, out_w = adamw(w_out, out_grad, out_first, out_second, 0.06, 0.1)
    fc_m, fc_s, fc_w = adamw(w_fc, fc_grad, fc_first, fc_second, 0.06, 0.1)
    proj_m, proj_s, proj_w = adamw(w_proj, proj_grad.T, proj_first, proj_second, 0.06, 0.1)
    vec_m, vec_s, vec_w = adamw(vectors, vec_grad, vec_first, vec_second, 0.2, 0.0)
    return (
        out.reshape(block_in.shape),
        grad_input.reshape(block_in.shape),
        qkv_m,
        qkv_s,
        qkv_w,
        out_m,
        out_s,
        out_w,
        fc_m,
        fc_s,
        fc_w,
        proj_m,
        proj_s,
        proj_w,
        vec_m,
        vec_s,
        vec_w,
    )


def solution(mesh):
    in_specs = (
        P("batch", "ctx", None, None),
        P("batch", "ctx", None, None),
        P("batch", "ctx"),
        P("batch", "ctx"),
        P("batch", "ctx"),
        P("batch", "ctx"),
        P(None, "ctx"),
        P("batch", "ctx"),
        P("batch", "ctx"),
        P("batch", "ctx"),
        P("batch", "ctx"),
        P("batch", "ctx"),
        P("batch", "ctx"),
        P("batch", "ctx"),
        P("batch", "ctx"),
        P(None, "ctx"),
        P(None, "ctx"),
    )
    out_specs = (
        P("batch", "ctx", None, None),
        P("batch", "ctx", None, None),
        P("batch", "ctx"),
        P("batch", "ctx"),
        P("batch", "ctx"),
        P("batch", "ctx"),
        P("batch", "ctx"),
        P("batch", "ctx"),
        P("batch", "ctx"),
        P("batch", "ctx"),
        P("batch", "ctx"),
        P("batch", "ctx"),
        P("batch", "ctx"),
        P("batch", "ctx"),
        P(None, "ctx"),
        P(None, "ctx"),
        P(None, "ctx"),
    )
    sizes = (mesh.shape["batch"], mesh.shape["ctx"])
    local = local_fast if sizes == (BATCH, CTX) else local_any
    return jax.shard_map(local, mesh=mesh, in_specs=in_specs, out_specs=out_specs, check_vma=False)
```

```python
import functools
import math

import jax
import jax.numpy as jnp
from jax import lax
from jax.experimental import pallas as pl
from jax.experimental.pallas import tpu as pltpu
from jax.sharding import PartitionSpec as P

HEADS = 12
STEP = 10


def layer_norm(value, gain, shift):
    mean = jnp.mean(value, axis=-1, keepdims=True)
    centred = value - mean
    spread = jnp.mean(centred * centred, axis=-1, keepdims=True)
    return centred * lax.rsqrt(spread + 1e-05) * gain + shift


def gelu_tanh(value):
    return (
        0.5
        * value
        * (1.0 + jnp.tanh(0.7978845608028654 * (value + 0.044715 * value * value * value)))
    )


def block_places(index, count, half):
    offsets = jnp.arange(half, dtype=jnp.int32)
    first = index * half + offsets
    second = (2 * count - 1 - index) * half + offsets
    return jnp.concatenate([first, second])


def scores_of(queries, keys, scale, allowed):
    raw = jnp.einsum("sqhd,skhd->shqk", queries, keys, preferred_element_type=jnp.float32) * scale
    return jnp.where(allowed[None, None], raw, -1e30)


def pair_grads(queries, grads, keys, values, top, total, delta, scale, allowed):
    score = scores_of(queries, keys, scale, allowed)
    weights = jnp.exp(score - top[..., None]) / total[..., None]
    back_weights = jnp.einsum("sqhd,skhd->shqk", grads, values, preferred_element_type=jnp.float32)
    grad_score = (weights * (back_weights - delta[..., None])).astype(jnp.bfloat16)
    return (weights.astype(jnp.bfloat16), grad_score)


def rows_product(left, right):
    return jnp.einsum("ra,rb->ab", left, right, preferred_element_type=jnp.float32)


def back_product(grad, weight):
    return jnp.einsum("rb,ab->ra", grad, weight, preferred_element_type=jnp.float32)


def adamw(weight, grad, first, second, rate, decay):
    first = 0.9 * first + 0.1 * grad
    second = 0.999 * second + 0.001 * grad * grad
    first_hat = first / (1.0 - 0.9**STEP)
    second_hat = second / (1.0 - 0.999**STEP)
    weight = weight - rate * (first_hat / (jnp.sqrt(second_hat) + 1e-08) + decay * weight)
    return (first, second, weight)


def local_any(
    block_in,
    cotangent,
    w_qkv,
    w_out,
    w_fc,
    w_proj,
    vectors,
    qkv_first,
    qkv_second,
    out_first,
    out_second,
    fc_first,
    fc_second,
    proj_first,
    proj_second,
    vec_first,
    vec_second,
):
    low_type = jnp.bfloat16
    wide = jnp.float32
    row_parts = (
        lax.all_gather(w_qkv.astype(low_type), "batch", axis=0, tiled=True),
        lax.all_gather(w_out.astype(low_type), "batch", axis=0, tiled=True),
        lax.all_gather(w_fc.astype(low_type), "batch", axis=0, tiled=True),
        lax.all_gather(w_proj.astype(low_type), "batch", axis=0, tiled=True),
    )
    full_qkv, full_out, full_fc, full_proj, full_vec = (
        lax.all_gather(row_parts[0], "ctx", axis=1, tiled=True),
        lax.all_gather(row_parts[1], "ctx", axis=1, tiled=True),
        lax.all_gather(row_parts[2], "ctx", axis=1, tiled=True),
        lax.all_gather(row_parts[3], "ctx", axis=1, tiled=True),
        lax.all_gather(vectors.astype(low_type), "ctx", axis=1, tiled=True),
    )
    params = full_vec.astype(wide)
    seqs, pair, half, width = block_in.shape
    heads = HEADS
    head = width // heads
    rows = seqs * pair * half
    span = pair * half
    count = lax.axis_size("ctx")
    index = lax.axis_index("ctx")
    scale = 1.0 / math.sqrt(head)
    inputs = block_in.astype(wide).reshape(rows, width)
    normed_one = layer_norm(inputs, params[0], params[1]).astype(low_type)
    mixed = jnp.dot(normed_one, full_qkv, preferred_element_type=wide)
    queries = (mixed[:, :width] + params[4]).astype(low_type)
    keys = mixed[:, width : 2 * width].astype(low_type)
    values = (mixed[:, 2 * width :] + params[5]).astype(low_type)
    key_all, value_all = (
        lax.all_gather(keys.reshape(seqs, pair, half, width), "ctx", axis=1, tiled=True),
        lax.all_gather(values.reshape(seqs, pair, half, width), "ctx", axis=1, tiled=True),
    )
    query_heads = queries.reshape(seqs, span, heads, head)
    own_places = block_places(index, count, half)

    def piece_of(source, piece):
        return lax.dynamic_slice_in_dim(source, 2 * piece, 2, 1).reshape(seqs, span, heads, head)

    def allowed_for(piece):
        return own_places[:, None] >= block_places(piece, count, half)[None, :]

    def stats_step(piece, carry):
        top, total = carry
        score = scores_of(query_heads, piece_of(key_all, piece), scale, allowed_for(piece))
        new_top = jnp.maximum(top, jnp.max(score, axis=-1))
        total = total * jnp.exp(top - new_top) + jnp.sum(
            jnp.exp(score - new_top[..., None]), axis=-1
        )
        return (new_top, total)

    start_stats = (jnp.full((seqs, heads, span), -1e30, wide), jnp.zeros((seqs, heads, span), wide))
    top, total = lax.fori_loop(0, count, stats_step, start_stats)

    def output_step(piece, acc):
        score = scores_of(query_heads, piece_of(key_all, piece), scale, allowed_for(piece))
        weights = (jnp.exp(score - top[..., None]) / total[..., None]).astype(low_type)
        return acc + jnp.einsum(
            "shqk,skhd->sqhd", weights, piece_of(value_all, piece), preferred_element_type=wide
        )

    attended = lax.fori_loop(0, count, output_step, jnp.zeros((seqs, span, heads, head), wide))
    att_low = attended.reshape(rows, width).astype(low_type)
    mid = inputs + jnp.dot(att_low, full_out, preferred_element_type=wide) + params[6]
    normed_two = layer_norm(mid, params[2], params[3]).astype(low_type)
    pre = jnp.dot(normed_two, full_fc, preferred_element_type=wide) + params[8:12].reshape(-1)
    act_low = gelu_tanh(pre).astype(low_type)
    result = mid + jnp.dot(act_low, full_proj, preferred_element_type=wide) + params[7]
    out_block = result.astype(low_type).reshape(block_in.shape)
    grad_low = cotangent.reshape(rows, width)
    grad_out = grad_low.astype(wide)
    grad_wproj = rows_product(act_low, grad_low)
    back_act = back_product(grad_low, full_proj)
    grad_pre = jax.vjp(gelu_tanh, pre)[1](back_act)[0].astype(low_type)
    grad_wfc = rows_product(normed_two, grad_pre)
    back_two = back_product(grad_pre, full_fc)
    back_mid, grad_gain_two, grad_shift_two = jax.vjp(layer_norm, mid, params[2], params[3])[1](
        back_two
    )
    grad_mid = grad_out + back_mid
    grad_att_low = grad_mid.astype(low_type)
    grad_wout = rows_product(att_low, grad_att_low)
    back_att = back_product(grad_att_low, full_out)
    grad_heads = back_att.astype(low_type).reshape(seqs, span, heads, head)
    delta = jnp.einsum("sqhd,sqhd->shq", grad_heads.astype(wide), attended)
    query_all, grad_all = (
        lax.all_gather(queries.reshape(seqs, pair, half, width), "ctx", axis=1, tiled=True),
        lax.all_gather(grad_heads.reshape(seqs, pair, half, width), "ctx", axis=1, tiled=True),
    )
    top_all, total_all, delta_all = (
        lax.all_gather(top.reshape(seqs, heads, pair, half), "ctx", axis=2, tiled=True),
        lax.all_gather(total.reshape(seqs, heads, pair, half), "ctx", axis=2, tiled=True),
        lax.all_gather(delta.reshape(seqs, heads, pair, half), "ctx", axis=2, tiled=True),
    )

    def query_step(piece, grad_query):
        key_part = piece_of(key_all, piece)
        value_part = piece_of(value_all, piece)
        weights_low, grad_score = pair_grads(
            query_heads,
            grad_heads,
            key_part,
            value_part,
            top,
            total,
            delta,
            scale,
            allowed_for(piece),
        )
        return grad_query + jnp.einsum(
            "shqk,skhd->sqhd", grad_score, key_part, preferred_element_type=wide
        )

    grad_query = lax.fori_loop(0, count, query_step, jnp.zeros((seqs, span, heads, head), wide))
    key_heads = keys.reshape(seqs, span, heads, head)
    value_heads = values.reshape(seqs, span, heads, head)

    def stat_piece(source, piece):
        return lax.dynamic_slice_in_dim(source, 2 * piece, 2, 2).reshape(seqs, heads, span)

    def key_step(piece, carry):
        grad_key, grad_value = carry
        query_part = piece_of(query_all, piece)
        grad_part = piece_of(grad_all, piece)
        allowed = block_places(piece, count, half)[:, None] >= own_places[None, :]
        weights_low, grad_score = pair_grads(
            query_part,
            grad_part,
            key_heads,
            value_heads,
            stat_piece(top_all, piece),
            stat_piece(total_all, piece),
            stat_piece(delta_all, piece),
            scale,
            allowed,
        )
        grad_key = grad_key + jnp.einsum(
            "shqk,sqhd->skhd", grad_score, query_part, preferred_element_type=wide
        )
        grad_value = grad_value + jnp.einsum(
            "shqk,sqhd->skhd", weights_low, grad_part, preferred_element_type=wide
        )
        return (grad_key, grad_value)

    start_keys = (
        jnp.zeros((seqs, span, heads, head), wide),
        jnp.zeros((seqs, span, heads, head), wide),
    )
    grad_key, grad_value = lax.fori_loop(0, count, key_step, start_keys)
    grad_keys = (grad_key * scale).reshape(seqs, pair, half, width)
    grad_values = grad_value.reshape(seqs, pair, half, width)
    grad_q_low = (grad_query * scale).reshape(rows, width).astype(low_type)
    grad_k_low = grad_keys.reshape(rows, width).astype(low_type)
    grad_v_low = grad_values.reshape(rows, width).astype(low_type)
    grad_mixed = jnp.concatenate([grad_q_low, grad_k_low, grad_v_low], axis=1)
    grad_wqkv = rows_product(normed_one, grad_mixed)
    back_one = back_product(grad_mixed, full_qkv)
    back_in, grad_gain_one, grad_shift_one = jax.vjp(layer_norm, inputs, params[0], params[1])[1](
        back_one
    )
    grad_input = (grad_mid + back_in).reshape(block_in.shape)
    grad_bias_q = jnp.sum(grad_q_low.astype(wide), axis=0)
    grad_bias_v = jnp.sum(grad_v_low.astype(wide), axis=0)
    grad_bias_out = jnp.sum(grad_att_low.astype(wide), axis=0)
    grad_bias_proj = jnp.sum(grad_out, axis=0)
    grad_bias_fc = jnp.sum(grad_pre.astype(wide), axis=0).reshape(4, width)
    small_rows = jnp.stack(
        [
            grad_gain_one,
            grad_shift_one,
            grad_gain_two,
            grad_shift_two,
            grad_bias_q,
            grad_bias_v,
            grad_bias_out,
            grad_bias_proj,
        ]
    )
    grad_vectors = jnp.concatenate([small_rows, grad_bias_fc], axis=0)
    col_sums = (
        lax.psum_scatter(grad_wqkv, "ctx", scatter_dimension=1, tiled=True),
        lax.psum_scatter(grad_wout, "ctx", scatter_dimension=1, tiled=True),
        lax.psum_scatter(grad_wfc, "ctx", scatter_dimension=1, tiled=True),
        lax.psum_scatter(grad_wproj, "ctx", scatter_dimension=1, tiled=True),
        lax.psum_scatter(grad_vectors, "ctx", scatter_dimension=1, tiled=True),
    )
    qkv_grad, out_grad, fc_grad, proj_grad = (
        lax.psum_scatter(col_sums[0], "batch", scatter_dimension=0, tiled=True),
        lax.psum_scatter(col_sums[1], "batch", scatter_dimension=0, tiled=True),
        lax.psum_scatter(col_sums[2], "batch", scatter_dimension=0, tiled=True),
        lax.psum_scatter(col_sums[3], "batch", scatter_dimension=0, tiled=True),
    )
    vec_grad = lax.psum(col_sums[4], "batch")
    qkv_m, qkv_s, qkv_w = adamw(w_qkv, qkv_grad, qkv_first, qkv_second, 0.06, 0.1)
    out_m, out_s, out_w = adamw(w_out, out_grad, out_first, out_second, 0.06, 0.1)
    fc_m, fc_s, fc_w = adamw(w_fc, fc_grad, fc_first, fc_second, 0.06, 0.1)
    proj_m, proj_s, proj_w = adamw(w_proj, proj_grad, proj_first, proj_second, 0.06, 0.1)
    vec_m, vec_s, vec_w = adamw(vectors, vec_grad, vec_first, vec_second, 0.2, 0.0)
    return (
        out_block,
        grad_input,
        qkv_m,
        qkv_s,
        qkv_w,
        out_m,
        out_s,
        out_w,
        fc_m,
        fc_s,
        fc_w,
        proj_m,
        proj_s,
        proj_w,
        vec_m,
        vec_s,
        vec_w,
    )


BATCH = 8
CTX = 4
WIDTH = 768
HEAD = 64
GROUP = WIDTH // CTX
TOKENS = 256
HALF = 128
FF_SIDE = 384
ROWS = WIDTH // BATCH
MLP = WIDTH + 2 * FF_SIDE + 256
SPAN = TOKENS * CTX
TILE = 256
LOW = jnp.bfloat16
WIDE = jnp.float32
CORE, XBIT, YBIT = 1, 2, 4
PLACES = (0, 2, 1, 3)
SOURCES = (
    (0, PLACES),
    (XBIT, PLACES),
    (YBIT, PLACES),
    (XBIT + YBIT, PLACES[:2]),
    (XBIT + YBIT, PLACES[2:]),
    (CORE, PLACES),
    (CORE + XBIT, PLACES),
    (CORE + YBIT, PLACES),
    (CORE + XBIT + YBIT, PLACES[:2]),
    (CORE + XBIT + YBIT, PLACES[2:]),
)
PARTS = len(SOURCES)
VMEM_LIMIT = 56 * 1024 * 1024


def swap(value, axis, bit):
    size = BATCH if axis == "batch" else CTX
    return lax.ppermute(value, axis, [(i, i ^ bit) for i in range(size)])


def mm(left, right):
    return lax.dot_general(left, right, (((1,), (0,)), ((), ())), preferred_element_type=WIDE)


def mt(left, right):
    return lax.dot_general(left, right, (((1,), (1,)), ((), ())), preferred_element_type=WIDE)


def tm(left, right):
    return lax.dot_general(left, right, (((0,), (0,)), ((), ())), preferred_element_type=WIDE)


def turned(value):
    return value.astype(WIDE).T.astype(LOW)


def moments(value):
    mean = jnp.mean(value, axis=-1, keepdims=True)
    centred = value - mean
    spread = jnp.mean(centred * centred, axis=-1, keepdims=True)
    return centred, lax.rsqrt(spread + 1e-05)


def norm_back(grad, normed, inverse, gain):
    part = grad * gain
    mean = jnp.mean(part, axis=-1, keepdims=True)
    cross = jnp.mean(part * normed, axis=-1, keepdims=True)
    return inverse * (part - mean - normed * cross)


def gather_ctx(piece):
    two = jnp.stack([piece, swap(piece, "ctx", 2)])
    return two, swap(two, "ctx", 1)


def gather_first(own):
    return swap(own, "batch", XBIT), swap(own, "batch", YBIT)


def gather_second(from_x, from_y):
    return swap(from_x[:2], "batch", YBIT), swap(from_y[2:], "batch", XBIT)


def to_core(parts):
    return [swap(part, "batch", CORE) for part in parts]


def swap_pair(pair, first, second):
    return swap(pair[0], "batch", first), swap(pair[1], "batch", second)


def scatter_second(kept, back):
    one = kept[0].astype(WIDE) + back[0].astype(WIDE)
    two = kept[1].astype(WIDE) + back[1].astype(WIDE)
    return (one[0], two[0]), (one[1].astype(LOW), two[1].astype(LOW))


def scatter_ctx(kept, back):
    one = kept[0].astype(WIDE) + back[0].astype(WIDE)
    two = (kept[1].astype(WIDE) + back[1].astype(WIDE)).astype(LOW)
    one = one + swap(two, "ctx", 1).astype(WIDE)
    return one[0] + swap(one[1].astype(LOW), "ctx", 2).astype(WIDE)


def rows_of(index, size):
    return pl.ds(pl.multiple_of(index * size, 16), size)


def qkv_place(held, batch, ctx):
    return [(pl.ds(0, 3 * GROUP), held.at[ctx, rows_of(batch, ROWS), :])]


def mlp_place(held_out, held_fc, held_proj, batch, ctx):
    return [
        (pl.ds(WIDTH + 2 * FF_SIDE, TILE), held_out.at[ctx, rows_of(batch, ROWS), :]),
        (pl.ds(0, WIDTH), held_fc.at[ctx, rows_of(batch, ROWS), :]),
        (pl.ds(WIDTH, FF_SIDE), held_proj.at[batch, rows_of(2 * ctx, ROWS), :]),
        (pl.ds(WIDTH + FF_SIDE, FF_SIDE), held_proj.at[batch, rows_of(2 * ctx + 1, ROWS), :]),
    ]


def load_weight(meta, parts, place, sems):
    copies = []
    for part, (source, places) in zip(parts, SOURCES):
        for index, ctx in enumerate(places):
            ranges = place(meta[0] ^ source, meta[1] ^ ctx)
            copies.append([(part.at[index, :, lanes], target) for lanes, target in ranges])
    started = []
    for kind in range(len(copies[0])):
        group = []
        for number, copy in enumerate(copies):
            group.append(pltpu.make_async_copy(*copy[kind], sems.at[kind, number]))
            group[-1].start()
        started.append(group)
    return started


def store_grad(held, targets, sems):
    one_kept, one_sent, two_kept, two_sent = targets
    copies = []
    for y in range(2):
        for x in range(2):
            for index, ctx in enumerate(PLACES):
                if index < 2:
                    target = (one_sent if y else one_kept).at[x, index]
                else:
                    target = (two_sent if x else two_kept).at[y, index - 2]
                for kind, (lanes, source) in enumerate(held(2 * y + x, ctx)):
                    number = (2 * y + x) * CTX + ctx
                    copies.append(
                        pltpu.make_async_copy(source, target.at[:, lanes], sems.at[kind, number])
                    )
                    copies[-1].start()
    wait_all(copies)


def half_rows(meta, pair, held):
    for index, value in enumerate(pair):
        held[index] = turned(value)
    parts = []
    for index in range(2):
        rows = [held[index, rows_of(meta[0] ^ (2 * part), ROWS), :] for part in range(BATCH // 2)]
        parts.append(jnp.concatenate(rows, axis=0))
    return parts


def over_both(left, right):
    return mm(left[0], right[0]) + mm(left[1], right[1])


def wait_all(copies):
    for copy in copies:
        copy.wait()


def in_place(ctx, block):
    first = ctx if block == 0 else 2 * CTX - 1 - ctx
    return pl.ds(pl.multiple_of(first * HALF, HALF), HALF)


def read_vectors(meta, parts, chunks):
    for ctx, part in enumerate(parts):
        rows = [part[16 * index : 16 * (index + 1), :] for index in range(GROUP // HEAD)]
        chunks[meta[1] ^ ctx] = jnp.concatenate(rows, axis=1).astype(WIDE)
    return jnp.concatenate([chunks[index] for index in range(CTX)], axis=1)


def qkv_kernel(meta, x_ref, *refs):
    vectors, parts, refs = refs[:4], refs[4 : 4 + PARTS], refs[4 + PARTS :]
    h_ref, own, near, far, last, held, units, chunks, sems = refs
    (copies,) = load_weight(meta, parts, functools.partial(qkv_place, held), sems)
    params = read_vectors(meta, vectors, chunks)
    bias = jnp.concatenate([params[4:5], jnp.zeros((1, WIDTH), WIDE), params[5:6]], axis=1)
    centred, inverse = moments(x_ref[...].astype(WIDE))
    normed = (centred * inverse * params[0:1] + params[1:2]).astype(LOW)
    h_ref[...] = normed
    wait_all(copies)
    for chunk in range(CTX):
        mixed = mm(normed, held[chunk]) + bias[:, 3 * GROUP * chunk : 3 * GROUP * (chunk + 1)]
        mixed = mixed.astype(LOW)
        for part in range(3):
            unit = 3 * chunk + part
            units[unit % CTX, :, (unit // CTX) * GROUP : (unit // CTX + 1) * GROUP] = mixed[
                :, part * GROUP : (part + 1) * GROUP
            ]
    for ctx, target in enumerate((own, near, far, last)):
        target[...] = units[meta[1] ^ ctx]


def read_sequence(meta, pieces, targets):
    for ctx, piece in enumerate(pieces):
        for block in range(2):
            place = in_place(meta[1] ^ ctx, block)
            rows = piece[block * HALF : (block + 1) * HALF, :]
            for index, target in enumerate(targets):
                target[place, :] = rows[:, index * GROUP : (index + 1) * GROUP]


def write_sequence(meta, pieces, sources):
    for ctx, piece in enumerate(pieces):
        for block in range(2):
            place = in_place(meta[1] ^ ctx, block)
            for index, source in enumerate(sources):
                piece[
                    block * HALF : (block + 1) * HALF, index * GROUP : (index + 1) * GROUP
                ] = source[place, :].astype(LOW)


def head_mask(head, scale=1.0):
    lane = lax.broadcasted_iota(jnp.int32, (1, GROUP), 1)
    inside = (lane >= head * HEAD) & (lane < (head + 1) * HEAD)
    return jnp.where(inside, scale, 0.0).astype(LOW)


def tile_of(index):
    return slice(index * TILE, (index + 1) * TILE)


def weights_of(queries, k_seq, tile, causal):
    scores = [mt(queries, k_seq[tile_of(other), :]) for other in range(tile + 1)]
    scores[tile] = jnp.where(causal, scores[tile], -1e30)
    top = jnp.max(functools.reduce(jnp.maximum, scores), axis=-1, keepdims=True)
    expo = [jnp.exp(score - top) for score in scores]
    total = jnp.sum(functools.reduce(jnp.add, expo), axis=-1, keepdims=True)
    inverse = 1.0 / total
    return [value * inverse for value in expo]


def causal_tile():
    row = lax.broadcasted_iota(jnp.int32, (TILE, TILE), 0)
    column = lax.broadcasted_iota(jnp.int32, (TILE, TILE), 1)
    return row >= column


def attend_kernel(meta, *refs):
    pieces, results, (q_seq, k_seq, v_seq, out) = refs[:4], refs[4:8], refs[8:]
    read_sequence(meta, pieces, (q_seq, k_seq, v_seq))
    causal = causal_tile()
    scale = 1.0 / math.sqrt(HEAD)
    for tile in range(SPAN // TILE):

        def one_head(head, total, tile=tile):
            mask = head_mask(head)
            queries = q_seq[tile_of(tile), :] * head_mask(head, scale)
            weights = weights_of(queries, k_seq, tile, causal)
            for other, weight in enumerate(weights):
                total = total + mm(weight.astype(LOW), v_seq[tile_of(other), :] * mask)
            return total

        out[tile_of(tile), :] = lax.fori_loop(
            0, GROUP // HEAD, one_head, jnp.zeros((TILE, GROUP), WIDE), unroll=True
        )
    write_sequence(meta, results, (out,))


def attend_back_kernel(meta, *refs):
    pieces, grads, results = refs[:4], refs[4:8], refs[8:12]
    q_seq, k_seq, v_seq, g_seq, dq, dk, dv = refs[12:]
    read_sequence(meta, pieces, (q_seq, k_seq, v_seq))
    read_sequence(meta, grads, (g_seq,))
    causal = causal_tile()
    scale = 1.0 / math.sqrt(HEAD)
    dk[...] = jnp.zeros_like(dk)
    dv[...] = jnp.zeros_like(dv)
    for tile in range(SPAN // TILE):

        def one_head(head, total, tile=tile):
            mask = head_mask(head)
            scaled = head_mask(head, scale)
            queries = q_seq[tile_of(tile), :] * scaled
            grad = g_seq[tile_of(tile), :] * mask
            weights = weights_of(queries, k_seq, tile, causal)
            backs = [mt(grad, v_seq[tile_of(other), :]) for other in range(tile + 1)]
            products = [weight * back for weight, back in zip(weights, backs)]
            delta = jnp.sum(functools.reduce(jnp.add, products), axis=-1, keepdims=True)
            for other, (weight, back) in enumerate(zip(weights, backs)):
                step = (weight * (back - delta)).astype(LOW)
                total = total + mm(step, k_seq[tile_of(other), :] * scaled)
                dk[tile_of(other), :] += tm(step, queries)
                dv[tile_of(other), :] += tm(weight.astype(LOW), grad)
            return total

        dq[tile_of(tile), :] = lax.fori_loop(
            0, GROUP // HEAD, one_head, jnp.zeros((TILE, GROUP), WIDE), unroll=True
        )
    write_sequence(meta, results, (dq, dk, dv))


def middle_kernel(meta, x_ref, dy_ref, h_one_ref, *refs):
    vectors, pieces, parts, refs = refs[:4], refs[4:8], refs[8 : 8 + PARTS], refs[8 + PARTS :]
    (out_ref, pack_ref, mine, theirs, dmid_ref), refs = refs[:5], refs[5:]
    results, (rows_ref, dbias_ref), refs = refs[:4], refs[4:6], refs[6:]
    out_parts, held_out, held_fc, held_proj, units, total, back, chunks, bias, acts, sems = refs
    place = functools.partial(mlp_place, out_parts, held_fc, held_proj)
    copies = load_weight(meta, parts, place, sems)
    vec = read_vectors(meta, vectors, chunks)
    for chunk in range(CTX):
        bias[chunk] = vec[8 + chunk : 9 + chunk]
    for ctx, piece in enumerate(pieces):
        units[meta[1] ^ ctx] = piece[...]
    att = jnp.concatenate([units[index] for index in range(CTX)], axis=1)
    pack_ref[CTX + 1] = att
    pack_ref[CTX + 3] = dy_ref[...]
    pack_ref[CTX + 4] = h_one_ref[...]
    wait_all(copies[0])
    for chunk in range(CTX):
        held_out[:, chunk * GROUP : (chunk + 1) * GROUP] = out_parts[chunk, :, :GROUP]
    mid = x_ref[...].astype(WIDE) + mm(att, held_out[...]) + vec[6:7]
    centred, inverse = moments(mid)
    normed = centred * inverse
    pack_ref[CTX] = (normed * vec[2:3] + vec[3:4]).astype(LOW)
    total[...] = mid + vec[7:8]
    back[...] = jnp.zeros_like(back)
    for group in copies[1:]:
        wait_all(group)
    side = FF_SIDE

    def chunk_step(chunk, carry):
        pre = mm(pack_ref[CTX], held_fc[chunk]) + bias[chunk]
        square = pre * pre
        tanh = jnp.tanh(0.7978845608028654 * (pre + 0.044715 * square * pre))
        act = (0.5 * pre * (1.0 + tanh)).astype(LOW)
        slope = 0.5 * (1.0 + tanh) + 0.5 * pre * (1.0 - tanh * tanh) * (
            0.7978845608028654 * (1.0 + 3.0 * 0.044715 * square)
        )
        grads = []
        for half in range(2):
            weight = held_proj[2 * chunk + half]
            part = act[:, half * side : (half + 1) * side]
            acts[2 * chunk + half] = part
            total[...] += mt(part, weight)
            grads.append(mm(dy_ref[...], weight))
        dpre = (jnp.concatenate(grads, axis=1) * slope).astype(LOW)
        pack_ref[chunk] = dpre
        dbias_ref[chunk] = jnp.sum(dpre.astype(WIDE), axis=0, keepdims=True)
        back[...] += mt(dpre, held_fc[chunk])
        return carry

    lax.fori_loop(0, CTX, chunk_step, 0)
    out_ref[...] = total[...].astype(LOW)
    core = meta[0] & 1
    for chunk in range(CTX):
        mine[chunk] = acts[2 * chunk + core]
        theirs[chunk] = acts[2 * chunk + 1 - core]
    grad = back[...]
    dy = dy_ref[...].astype(WIDE)
    dmid = dy + norm_back(grad, normed, inverse, vec[2:3])
    dmid_ref[...] = dmid
    datt = dmid.astype(LOW)
    pack_ref[CTX + 2] = datt
    rows_ref[0:1] = jnp.sum(grad * normed, axis=0, keepdims=True)
    rows_ref[1:2] = jnp.sum(grad, axis=0, keepdims=True)
    rows_ref[2:3] = jnp.sum(datt.astype(WIDE), axis=0, keepdims=True)
    rows_ref[3:4] = jnp.sum(dy, axis=0, keepdims=True)
    rows_ref[4:8] = jnp.zeros((4, WIDTH), WIDE)
    dout = mt(datt, held_out[...]).astype(LOW)
    for index in range(CTX):
        units[index] = dout[:, index * GROUP : (index + 1) * GROUP]
    for ctx, target in enumerate(results):
        target[...] = units[meta[1] ^ ctx]


def mlp_grad_kernel(meta, *refs):
    acts, packs, targets = refs[:2], refs[2:4], refs[4:8]
    held_out, held_fc, held_proj, turn, sems = refs[8:]
    dy = [turned(pack[CTX + 3]) for pack in packs]
    for chunk in range(CTX):
        held_proj[chunk] = over_both(dy, [act[chunk] for act in acts]).astype(LOW)
    left = half_rows(meta, [pack[CTX] for pack in packs], turn)
    for chunk in range(CTX):
        held_fc[chunk] = over_both(left, [pack[chunk] for pack in packs]).astype(LOW)
    left = half_rows(meta, [pack[CTX + 1] for pack in packs], turn)
    grad = over_both(left, [pack[CTX + 2] for pack in packs]).astype(LOW)
    for chunk in range(CTX):
        held_out[chunk, :, :GROUP] = grad[:, chunk * GROUP : (chunk + 1) * GROUP]
        held_out[chunk, :, GROUP:] = jnp.zeros((WIDTH // 2, TILE - GROUP), LOW)

    def place(part, ctx):
        ctx = meta[1] ^ ctx
        chunk = (meta[0] ^ (2 * part)) // 2
        rows = pl.ds(part * ROWS, ROWS)
        return [
            (pl.ds(WIDTH + 2 * FF_SIDE, TILE), held_out.at[ctx, rows, :]),
            (pl.ds(0, WIDTH), held_fc.at[ctx, rows, :]),
            (pl.ds(WIDTH, FF_SIDE), held_proj.at[chunk, rows_of(2 * ctx, ROWS), :]),
            (pl.ds(WIDTH + FF_SIDE, FF_SIDE), held_proj.at[chunk, rows_of(2 * ctx + 1, ROWS), :]),
        ]

    store_grad(place, targets, sems)


def qkv_grad_kernel(meta, *refs):
    pack, pieces, targets = refs[:2], (refs[2:6], refs[6:10]), refs[10:14]
    mixed_ref, dbias_ref, held, units, turn, sems = refs[14:]
    for core in range(2):
        for ctx, piece in enumerate(pieces[core]):
            for part in range(3):
                units[core, CTX * part + (meta[1] ^ ctx)] = piece[
                    :, part * GROUP : (part + 1) * GROUP
                ]
    left = half_rows(meta, [pack[0][...], pack[1][...]], turn)
    for chunk in range(CTX):
        mixed = [
            jnp.concatenate([units[core, 3 * chunk + part] for part in range(3)], axis=1)
            for core in range(2)
        ]
        mixed_ref[chunk] = mixed[0]
        bias = jnp.sum(mixed[0].astype(WIDE), axis=0, keepdims=True)
        for part in range(3):
            dbias_ref[3 * chunk + part] = bias[:, part * GROUP : (part + 1) * GROUP]
        held[chunk] = over_both(left, mixed).astype(LOW)

    def place(part, ctx):
        return [(pl.ds(0, 3 * GROUP), held.at[meta[1] ^ ctx, pl.ds(part * ROWS, ROWS), :])]

    store_grad(place, targets, sems)


def input_grad_kernel(meta, x_ref, dmid_ref, mixed_ref, rows_ref, dfc_ref, dqkv_ref, *refs):
    vectors, parts, refs = refs[:4], refs[4 : 4 + PARTS], refs[4 + PARTS :]
    grad_ref, results, (held, chunks, rows, sums, sems) = refs[0], refs[1:5], refs[5:]
    (copies,) = load_weight(meta, parts, functools.partial(qkv_place, held), sems)
    params = read_vectors(meta, vectors, chunks)
    centred, inverse = moments(x_ref[...].astype(WIDE))
    normed = centred * inverse
    wait_all(copies)
    grad = jnp.zeros((TOKENS, WIDTH), WIDE)
    for chunk in range(CTX):
        grad = grad + mt(mixed_ref[chunk], held[chunk])
    grad_ref[...] = dmid_ref[...] + norm_back(grad, normed, inverse, params[0:1])
    rows[0:1] = jnp.sum(grad * normed, axis=0, keepdims=True)
    rows[1:2] = jnp.sum(grad, axis=0, keepdims=True)
    rows[2:4] = rows_ref[0:2]
    for chunk in range(CTX):
        lanes = slice(chunk * GROUP, (chunk + 1) * GROUP)
        rows[4:5, lanes] = dqkv_ref[chunk]
        rows[5:6, lanes] = dqkv_ref[2 * CTX + chunk]
        rows[8 + chunk : 9 + chunk] = dfc_ref[chunk]
    rows[6:8] = rows_ref[2:4]
    rows[12:16] = jnp.zeros((4, WIDTH), WIDE)
    for chunk in range(CTX):
        sums[chunk] = rows[:, chunk * GROUP : (chunk + 1) * GROUP]
    for ctx, target in enumerate(results):
        target[...] = sums[meta[1] ^ ctx]


def shape_of(dtype, *dims):
    return jax.ShapeDtypeStruct(dims, dtype)


def call(kernel, arguments, kinds, outputs, out_kinds, scratch, flops):
    spec = {
        "v": pl.BlockSpec(memory_space=pltpu.VMEM),
        "s": pl.BlockSpec(memory_space=pltpu.SMEM),
        "a": pl.BlockSpec(memory_space=pl.ANY),
        "h": pl.BlockSpec((None, TOKENS, WIDTH), lambda step: (CTX + 4, 0, 0)),
    }
    moved = sum(math.prod(value.shape) * value.dtype.itemsize for value in arguments)
    moved += sum(math.prod(value.shape) * value.dtype.itemsize for value in outputs)
    return pl.pallas_call(
        kernel,
        grid=(1,),
        out_shape=tuple(outputs),
        in_specs=[spec[kind] for kind in kinds],
        out_specs=tuple(spec[kind] for kind in out_kinds),
        scratch_shapes=scratch,
        cost_estimate=pl.CostEstimate(
            flops=int(flops), bytes_accessed=int(moved), transcendentals=0
        ),
        compiler_params=pltpu.CompilerParams(vmem_limit_bytes=VMEM_LIMIT),
    )(*arguments)


def local_fast(
    block_in,
    cotangent,
    w_qkv,
    w_out,
    w_fc,
    w_proj,
    vectors,
    qkv_first,
    qkv_second,
    out_first,
    out_second,
    fc_first,
    fc_second,
    proj_first,
    proj_second,
    vec_first,
    vec_second,
):
    batch, ctx = lax.axis_index("batch"), lax.axis_index("ctx")
    meta = jnp.stack([batch, ctx]).astype(jnp.int32)
    inputs = block_in.reshape(TOKENS, WIDTH)
    grad_low = cotangent.reshape(TOKENS, WIDTH)
    tie = lax.optimization_barrier

    qkv_sems = pltpu.SemaphoreType.DMA((1, BATCH * CTX))
    mlp_sems = pltpu.SemaphoreType.DMA((4, BATCH * CTX))
    qkv_held = pltpu.VMEM((CTX, WIDTH, 3 * GROUP), LOW)
    vec_held = pltpu.VMEM((CTX, 16, GROUP), WIDE)

    low_vec = jnp.pad(vectors.astype(LOW), ((0, 4), (0, 0)))
    low_vec = [low_vec[:, start : start + HEAD] for start in range(0, GROUP, HEAD)]
    low_vec = jnp.concatenate(low_vec + [jnp.zeros((ROWS - 48, HEAD), LOW)], axis=0)
    piece_one = jnp.concatenate([w_qkv.astype(LOW), low_vec], axis=1)
    low_proj = w_proj.astype(LOW).T
    piece_two = jnp.concatenate(
        [
            w_fc.astype(LOW),
            low_proj[:ROWS],
            low_proj[ROWS:],
            w_out.astype(LOW),
            jnp.zeros((ROWS, TILE - GROUP), LOW),
        ],
        axis=1,
    )
    near, far = gather_ctx(piece_one)
    vec_parts = [part[:48, 3 * GROUP :] for part in (near[0], far[0], near[1], far[1])]
    own_one = jnp.concatenate([near, far], axis=0)[:, :, : 3 * GROUP]
    piece_two, late_vec = tie((piece_two, vec_parts))
    far = swap(piece_two, "ctx", 2)
    x_one, y_one = gather_first(own_one)
    far, x_one, y_one = tie((far, x_one, y_one))
    near = jnp.stack([piece_two, far])
    far = swap(near, "ctx", 1)
    parts_one = [own_one, x_one, y_one, *gather_second(x_one, y_one)]
    parts_one = parts_one + to_core(parts_one)
    far, parts_one = tie((far, parts_one))
    own_two = jnp.concatenate([near, far], axis=0)

    packed = shape_of(LOW, TOKENS, 3 * GROUP)
    single = shape_of(LOW, TOKENS, GROUP)
    tokens_low = shape_of(LOW, TOKENS, WIDTH)
    hidden_low = shape_of(LOW, CTX, TOKENS, WIDTH)
    square = WIDTH * WIDTH
    h_one, own, *sent = call(
        qkv_kernel,
        (meta, inputs, *vec_parts, *parts_one),
        "s" + "v" * 5 + "a" * PARTS,
        [tokens_low] + [packed] * 4,
        "v" * 5,
        [qkv_held, pltpu.VMEM((CTX, TOKENS, 3 * GROUP), LOW), vec_held, qkv_sems],
        2 * TOKENS * 3 * square,
    )
    qkv_pieces = [own] + [swap(part, "ctx", bit) for bit, part in zip((1, 2, 3), sent)]

    x_two, y_two = gather_first(own_two)
    qkv_pieces, x_two, y_two = tie((qkv_pieces, x_two, y_two))
    across_two = gather_second(x_two, y_two)
    parts_two = [own_two, x_two, y_two]
    swapped_two = to_core(parts_two)

    sequence_low = pltpu.VMEM((SPAN, GROUP), LOW)
    sequence_wide = pltpu.VMEM((SPAN, GROUP), WIDE)
    own, *sent = call(
        attend_kernel,
        (meta, *qkv_pieces),
        "s" + "v" * 4,
        [single] * 4,
        "v" * 4,
        [sequence_low] * 3 + [sequence_wide],
        2 * SPAN * SPAN * GROUP * 2,
    )
    sent, swapped_two = tie((sent, swapped_two))
    att_pieces = [own] + [swap(part, "ctx", bit) for bit, part in zip((1, 2, 3), sent)]
    across_two, att_pieces = tie((across_two, att_pieces))
    parts_two = parts_two + list(across_two) + swapped_two + to_core(across_two)

    pack_shape = shape_of(LOW, CTX + 5, TOKENS, WIDTH)
    act_shape = shape_of(LOW, BATCH // 2, TOKENS, FF_SIDE)
    out, pack, act_mine, act_theirs, dmid, own, *sent = call(
        middle_kernel,
        (meta, inputs, grad_low, h_one, *vec_parts, *att_pieces, *parts_two),
        "s" + "v" * 11 + "a" * PARTS,
        [tokens_low, pack_shape, act_shape, act_shape, shape_of(WIDE, TOKENS, WIDTH)]
        + [single] * 4
        + [shape_of(WIDE, 8, WIDTH), shape_of(WIDE, CTX, 1, WIDTH)],
        "v" * 11,
        [
            pltpu.VMEM((CTX, WIDTH, TILE), LOW),
            pltpu.VMEM((WIDTH, WIDTH), LOW),
            pltpu.VMEM((CTX, WIDTH, WIDTH), LOW),
            pltpu.VMEM((BATCH, WIDTH, FF_SIDE), LOW),
            pltpu.VMEM((CTX, TOKENS, GROUP), LOW),
            pltpu.VMEM((TOKENS, WIDTH), WIDE),
            pltpu.VMEM((TOKENS, WIDTH), WIDE),
            vec_held,
            pltpu.VMEM((CTX, 1, WIDTH), WIDE),
            pltpu.VMEM((BATCH, TOKENS, FF_SIDE), LOW),
            mlp_sems,
        ],
        2 * TOKENS * 18 * square,
    )
    sent, (rows_two, dbias_fc) = sent[:3], sent[3:]
    grad_pieces = [own] + [swap(part, "ctx", bit) for bit, part in zip((1, 2, 3), sent)]
    act_came, pack_came = swap(act_theirs, "batch", CORE), swap(pack, "batch", CORE)

    half_sems = BATCH * CTX // 2
    turn_held = pltpu.VMEM((2, WIDTH, TOKENS), LOW)
    mlp_parts = call(
        mlp_grad_kernel,
        (meta, act_mine, act_came, pack, pack_came),
        "s" + "v" * 4,
        [shape_of(LOW, 2, 2, ROWS, MLP)] * 4,
        "aaaa",
        [
            pltpu.VMEM((CTX, WIDTH // 2, TILE), LOW),
            pltpu.VMEM((CTX, WIDTH // 2, WIDTH), LOW),
            pltpu.VMEM((BATCH // 2, WIDTH, FF_SIDE), LOW),
            turn_held,
            pltpu.SemaphoreType.DMA((4, half_sems)),
        ],
        2 * TOKENS * 9 * square,
    )
    mlp_parts, grad_pieces = tie((mlp_parts, grad_pieces))
    mlp_kept = mlp_parts[0], mlp_parts[2]
    mlp_back = swap_pair((mlp_parts[1], mlp_parts[3]), YBIT, XBIT)
    own, *sent = call(
        attend_back_kernel,
        (meta, *qkv_pieces, *grad_pieces),
        "s" + "v" * 8,
        [packed] * 4,
        "v" * 4,
        [sequence_low] * 4 + [sequence_wide] * 3,
        2 * SPAN * SPAN * GROUP * 5,
    )
    mixed_pieces = [own] + [swap(part, "ctx", bit) for bit, part in zip((1, 2, 3), sent)]
    came = to_core(mixed_pieces[:1])
    mlp_back, received = tie((mlp_back, mixed_pieces[1:]))
    mixed_pieces = mixed_pieces[:1] + received
    mixed_came = came + to_core(received)
    mlp_kept, mlp_sent = scatter_second(mlp_kept, mlp_back)
    mlp_sent, mixed_came = tie((mlp_sent, mixed_came))
    mlp_back = swap_pair(mlp_sent, XBIT, YBIT)

    *qkv_parts, mixed, dbias_qkv = call(
        qkv_grad_kernel,
        (meta, pack, pack_came, *mixed_pieces, *mixed_came),
        "shh" + "v" * 8,
        [shape_of(LOW, 2, 2, ROWS, 3 * GROUP)] * 4
        + [shape_of(LOW, CTX, TOKENS, 3 * GROUP), shape_of(WIDE, 3 * CTX, 1, GROUP)],
        "aaaavv",
        [
            pltpu.VMEM((CTX, WIDTH // 2, 3 * GROUP), LOW),
            pltpu.VMEM((2, 3 * CTX, TOKENS, GROUP), LOW),
            turn_held,
            pltpu.SemaphoreType.DMA((1, half_sems)),
        ],
        2 * TOKENS * 3 * square,
    )
    qkv_kept = qkv_parts[0], qkv_parts[2]
    qkv_back = swap_pair((qkv_parts[1], qkv_parts[3]), YBIT, XBIT)
    grad_input, own, *sent = call(
        input_grad_kernel,
        (meta, inputs, dmid, mixed, rows_two, dbias_fc, dbias_qkv, *late_vec, *parts_one),
        "s" + "v" * 10 + "a" * PARTS,
        [shape_of(WIDE, TOKENS, WIDTH)] + [shape_of(WIDE, 16, GROUP)] * 4,
        "v" * 5,
        [qkv_held, vec_held, pltpu.VMEM((16, WIDTH), WIDE), vec_held, qkv_sems],
        2 * TOKENS * 3 * square,
    )
    mlp_back, qkv_back = tie((mlp_back, qkv_back))
    mlp_grad = scatter_ctx(mlp_kept, mlp_back)
    qkv_kept, qkv_sent = scatter_second(qkv_kept, qkv_back)
    qkv_sent, own, sent = tie((qkv_sent, own, sent))
    qkv_back = swap_pair(qkv_sent, XBIT, YBIT)
    qkv_grad = scatter_ctx(qkv_kept, qkv_back)

    vec_grad = own + sum(swap(part, "ctx", bit) for bit, part in zip((1, 2, 3), sent))
    for bit in (CORE, XBIT, YBIT):
        vec_grad = vec_grad + swap(vec_grad, "batch", bit)
    vec_grad = vec_grad[:12]
    fc_grad = mlp_grad[:, :WIDTH]
    proj_grad = jnp.concatenate(
        [mlp_grad[:, WIDTH : WIDTH + FF_SIDE], mlp_grad[:, WIDTH + FF_SIDE : WIDTH + 2 * FF_SIDE]],
        axis=0,
    )
    out_grad = mlp_grad[:, WIDTH + 2 * FF_SIDE : WIDTH + 2 * FF_SIDE + GROUP]

    qkv_m, qkv_s, qkv_w = adamw(w_qkv, qkv_grad, qkv_first, qkv_second, 0.06, 0.1)
    out_m, out_s, out_w = adamw(w_out, out_grad, out_first, out_second, 0.06, 0.1)
    fc_m, fc_s, fc_w = adamw(w_fc, fc_grad, fc_first, fc_second, 0.06, 0.1)
    proj_m, proj_s, proj_w = adamw(w_proj, proj_grad.T, proj_first, proj_second, 0.06, 0.1)
    vec_m, vec_s, vec_w = adamw(vectors, vec_grad, vec_first, vec_second, 0.2, 0.0)
    return (
        out.reshape(block_in.shape),
        grad_input.reshape(block_in.shape),
        qkv_m,
        qkv_s,
        qkv_w,
        out_m,
        out_s,
        out_w,
        fc_m,
        fc_s,
        fc_w,
        proj_m,
        proj_s,
        proj_w,
        vec_m,
        vec_s,
        vec_w,
    )


def solution(mesh):
    in_specs = (
        P("batch", "ctx", None, None),
        P("batch", "ctx", None, None),
        P("batch", "ctx"),
        P("batch", "ctx"),
        P("batch", "ctx"),
        P("batch", "ctx"),
        P(None, "ctx"),
        P("batch", "ctx"),
        P("batch", "ctx"),
        P("batch", "ctx"),
        P("batch", "ctx"),
        P("batch", "ctx"),
        P("batch", "ctx"),
        P("batch", "ctx"),
        P("batch", "ctx"),
        P(None, "ctx"),
        P(None, "ctx"),
    )
    out_specs = (
        P("batch", "ctx", None, None),
        P("batch", "ctx", None, None),
        P("batch", "ctx"),
        P("batch", "ctx"),
        P("batch", "ctx"),
        P("batch", "ctx"),
        P("batch", "ctx"),
        P("batch", "ctx"),
        P("batch", "ctx"),
        P("batch", "ctx"),
        P("batch", "ctx"),
        P("batch", "ctx"),
        P("batch", "ctx"),
        P("batch", "ctx"),
        P(None, "ctx"),
        P(None, "ctx"),
        P(None, "ctx"),
    )
    sizes = (mesh.shape["batch"], mesh.shape["ctx"])
    local = local_fast if sizes == (BATCH, CTX) else local_any
    return jax.shard_map(local, mesh=mesh, in_specs=in_specs, out_specs=out_specs, check_vma=False)
```

```python
import functools
import math

import jax
import jax.numpy as jnp
from jax import lax
from jax.experimental import pallas as pl
from jax.experimental.pallas import tpu as pltpu
from jax.sharding import PartitionSpec as P

HEADS = 12
STEP = 10


def layer_norm(value, gain, shift):
    mean = jnp.mean(value, axis=-1, keepdims=True)
    centred = value - mean
    spread = jnp.mean(centred * centred, axis=-1, keepdims=True)
    return centred * lax.rsqrt(spread + 1e-05) * gain + shift


def gelu_tanh(value):
    return (
        0.5
        * value
        * (1.0 + jnp.tanh(0.7978845608028654 * (value + 0.044715 * value * value * value)))
    )


def block_places(index, count, half):
    offsets = jnp.arange(half, dtype=jnp.int32)
    first = index * half + offsets
    second = (2 * count - 1 - index) * half + offsets
    return jnp.concatenate([first, second])


def scores_of(queries, keys, scale, allowed):
    raw = jnp.einsum("sqhd,skhd->shqk", queries, keys, preferred_element_type=jnp.float32) * scale
    return jnp.where(allowed[None, None], raw, -1e30)


def pair_grads(queries, grads, keys, values, top, total, delta, scale, allowed):
    score = scores_of(queries, keys, scale, allowed)
    weights = jnp.exp(score - top[..., None]) / total[..., None]
    back_weights = jnp.einsum("sqhd,skhd->shqk", grads, values, preferred_element_type=jnp.float32)
    grad_score = (weights * (back_weights - delta[..., None])).astype(jnp.bfloat16)
    return (weights.astype(jnp.bfloat16), grad_score)


def rows_product(left, right):
    return jnp.einsum("ra,rb->ab", left, right, preferred_element_type=jnp.float32)


def back_product(grad, weight):
    return jnp.einsum("rb,ab->ra", grad, weight, preferred_element_type=jnp.float32)


def adamw(weight, grad, first, second, rate, decay):
    first = 0.9 * first + 0.1 * grad
    second = 0.999 * second + 0.001 * grad * grad
    first_hat = first / (1.0 - 0.9**STEP)
    second_hat = second / (1.0 - 0.999**STEP)
    weight = weight - rate * (first_hat / (jnp.sqrt(second_hat) + 1e-08) + decay * weight)
    return (first, second, weight)


def local_any(
    block_in,
    cotangent,
    w_qkv,
    w_out,
    w_fc,
    w_proj,
    vectors,
    qkv_first,
    qkv_second,
    out_first,
    out_second,
    fc_first,
    fc_second,
    proj_first,
    proj_second,
    vec_first,
    vec_second,
):
    low_type = jnp.bfloat16
    wide = jnp.float32
    row_parts = (
        lax.all_gather(w_qkv.astype(low_type), "batch", axis=0, tiled=True),
        lax.all_gather(w_out.astype(low_type), "batch", axis=0, tiled=True),
        lax.all_gather(w_fc.astype(low_type), "batch", axis=0, tiled=True),
        lax.all_gather(w_proj.astype(low_type), "batch", axis=0, tiled=True),
    )
    full_qkv, full_out, full_fc, full_proj, full_vec = (
        lax.all_gather(row_parts[0], "ctx", axis=1, tiled=True),
        lax.all_gather(row_parts[1], "ctx", axis=1, tiled=True),
        lax.all_gather(row_parts[2], "ctx", axis=1, tiled=True),
        lax.all_gather(row_parts[3], "ctx", axis=1, tiled=True),
        lax.all_gather(vectors.astype(low_type), "ctx", axis=1, tiled=True),
    )
    params = full_vec.astype(wide)
    seqs, pair, half, width = block_in.shape
    heads = HEADS
    head = width // heads
    rows = seqs * pair * half
    span = pair * half
    count = lax.axis_size("ctx")
    index = lax.axis_index("ctx")
    scale = 1.0 / math.sqrt(head)
    inputs = block_in.astype(wide).reshape(rows, width)
    normed_one = layer_norm(inputs, params[0], params[1]).astype(low_type)
    mixed = jnp.dot(normed_one, full_qkv, preferred_element_type=wide)
    queries = (mixed[:, :width] + params[4]).astype(low_type)
    keys = mixed[:, width : 2 * width].astype(low_type)
    values = (mixed[:, 2 * width :] + params[5]).astype(low_type)
    key_all, value_all = (
        lax.all_gather(keys.reshape(seqs, pair, half, width), "ctx", axis=1, tiled=True),
        lax.all_gather(values.reshape(seqs, pair, half, width), "ctx", axis=1, tiled=True),
    )
    query_heads = queries.reshape(seqs, span, heads, head)
    own_places = block_places(index, count, half)

    def piece_of(source, piece):
        return lax.dynamic_slice_in_dim(source, 2 * piece, 2, 1).reshape(seqs, span, heads, head)

    def allowed_for(piece):
        return own_places[:, None] >= block_places(piece, count, half)[None, :]

    def stats_step(piece, carry):
        top, total = carry
        score = scores_of(query_heads, piece_of(key_all, piece), scale, allowed_for(piece))
        new_top = jnp.maximum(top, jnp.max(score, axis=-1))
        total = total * jnp.exp(top - new_top) + jnp.sum(
            jnp.exp(score - new_top[..., None]), axis=-1
        )
        return (new_top, total)

    start_stats = (jnp.full((seqs, heads, span), -1e30, wide), jnp.zeros((seqs, heads, span), wide))
    top, total = lax.fori_loop(0, count, stats_step, start_stats)

    def output_step(piece, acc):
        score = scores_of(query_heads, piece_of(key_all, piece), scale, allowed_for(piece))
        weights = (jnp.exp(score - top[..., None]) / total[..., None]).astype(low_type)
        return acc + jnp.einsum(
            "shqk,skhd->sqhd", weights, piece_of(value_all, piece), preferred_element_type=wide
        )

    attended = lax.fori_loop(0, count, output_step, jnp.zeros((seqs, span, heads, head), wide))
    att_low = attended.reshape(rows, width).astype(low_type)
    mid = inputs + jnp.dot(att_low, full_out, preferred_element_type=wide) + params[6]
    normed_two = layer_norm(mid, params[2], params[3]).astype(low_type)
    pre = jnp.dot(normed_two, full_fc, preferred_element_type=wide) + params[8:12].reshape(-1)
    act_low = gelu_tanh(pre).astype(low_type)
    result = mid + jnp.dot(act_low, full_proj, preferred_element_type=wide) + params[7]
    out_block = result.astype(low_type).reshape(block_in.shape)
    grad_low = cotangent.reshape(rows, width)
    grad_out = grad_low.astype(wide)
    grad_wproj = rows_product(act_low, grad_low)
    back_act = back_product(grad_low, full_proj)
    grad_pre = jax.vjp(gelu_tanh, pre)[1](back_act)[0].astype(low_type)
    grad_wfc = rows_product(normed_two, grad_pre)
    back_two = back_product(grad_pre, full_fc)
    back_mid, grad_gain_two, grad_shift_two = jax.vjp(layer_norm, mid, params[2], params[3])[1](
        back_two
    )
    grad_mid = grad_out + back_mid
    grad_att_low = grad_mid.astype(low_type)
    grad_wout = rows_product(att_low, grad_att_low)
    back_att = back_product(grad_att_low, full_out)
    grad_heads = back_att.astype(low_type).reshape(seqs, span, heads, head)
    delta = jnp.einsum("sqhd,sqhd->shq", grad_heads.astype(wide), attended)
    query_all, grad_all = (
        lax.all_gather(queries.reshape(seqs, pair, half, width), "ctx", axis=1, tiled=True),
        lax.all_gather(grad_heads.reshape(seqs, pair, half, width), "ctx", axis=1, tiled=True),
    )
    top_all, total_all, delta_all = (
        lax.all_gather(top.reshape(seqs, heads, pair, half), "ctx", axis=2, tiled=True),
        lax.all_gather(total.reshape(seqs, heads, pair, half), "ctx", axis=2, tiled=True),
        lax.all_gather(delta.reshape(seqs, heads, pair, half), "ctx", axis=2, tiled=True),
    )

    def query_step(piece, grad_query):
        key_part = piece_of(key_all, piece)
        value_part = piece_of(value_all, piece)
        weights_low, grad_score = pair_grads(
            query_heads,
            grad_heads,
            key_part,
            value_part,
            top,
            total,
            delta,
            scale,
            allowed_for(piece),
        )
        return grad_query + jnp.einsum(
            "shqk,skhd->sqhd", grad_score, key_part, preferred_element_type=wide
        )

    grad_query = lax.fori_loop(0, count, query_step, jnp.zeros((seqs, span, heads, head), wide))
    key_heads = keys.reshape(seqs, span, heads, head)
    value_heads = values.reshape(seqs, span, heads, head)

    def stat_piece(source, piece):
        return lax.dynamic_slice_in_dim(source, 2 * piece, 2, 2).reshape(seqs, heads, span)

    def key_step(piece, carry):
        grad_key, grad_value = carry
        query_part = piece_of(query_all, piece)
        grad_part = piece_of(grad_all, piece)
        allowed = block_places(piece, count, half)[:, None] >= own_places[None, :]
        weights_low, grad_score = pair_grads(
            query_part,
            grad_part,
            key_heads,
            value_heads,
            stat_piece(top_all, piece),
            stat_piece(total_all, piece),
            stat_piece(delta_all, piece),
            scale,
            allowed,
        )
        grad_key = grad_key + jnp.einsum(
            "shqk,sqhd->skhd", grad_score, query_part, preferred_element_type=wide
        )
        grad_value = grad_value + jnp.einsum(
            "shqk,sqhd->skhd", weights_low, grad_part, preferred_element_type=wide
        )
        return (grad_key, grad_value)

    start_keys = (
        jnp.zeros((seqs, span, heads, head), wide),
        jnp.zeros((seqs, span, heads, head), wide),
    )
    grad_key, grad_value = lax.fori_loop(0, count, key_step, start_keys)
    grad_keys = (grad_key * scale).reshape(seqs, pair, half, width)
    grad_values = grad_value.reshape(seqs, pair, half, width)
    grad_q_low = (grad_query * scale).reshape(rows, width).astype(low_type)
    grad_k_low = grad_keys.reshape(rows, width).astype(low_type)
    grad_v_low = grad_values.reshape(rows, width).astype(low_type)
    grad_mixed = jnp.concatenate([grad_q_low, grad_k_low, grad_v_low], axis=1)
    grad_wqkv = rows_product(normed_one, grad_mixed)
    back_one = back_product(grad_mixed, full_qkv)
    back_in, grad_gain_one, grad_shift_one = jax.vjp(layer_norm, inputs, params[0], params[1])[1](
        back_one
    )
    grad_input = (grad_mid + back_in).reshape(block_in.shape)
    grad_bias_q = jnp.sum(grad_q_low.astype(wide), axis=0)
    grad_bias_v = jnp.sum(grad_v_low.astype(wide), axis=0)
    grad_bias_out = jnp.sum(grad_att_low.astype(wide), axis=0)
    grad_bias_proj = jnp.sum(grad_out, axis=0)
    grad_bias_fc = jnp.sum(grad_pre.astype(wide), axis=0).reshape(4, width)
    small_rows = jnp.stack(
        [
            grad_gain_one,
            grad_shift_one,
            grad_gain_two,
            grad_shift_two,
            grad_bias_q,
            grad_bias_v,
            grad_bias_out,
            grad_bias_proj,
        ]
    )
    grad_vectors = jnp.concatenate([small_rows, grad_bias_fc], axis=0)
    col_sums = (
        lax.psum_scatter(grad_wqkv, "ctx", scatter_dimension=1, tiled=True),
        lax.psum_scatter(grad_wout, "ctx", scatter_dimension=1, tiled=True),
        lax.psum_scatter(grad_wfc, "ctx", scatter_dimension=1, tiled=True),
        lax.psum_scatter(grad_wproj, "ctx", scatter_dimension=1, tiled=True),
        lax.psum_scatter(grad_vectors, "ctx", scatter_dimension=1, tiled=True),
    )
    qkv_grad, out_grad, fc_grad, proj_grad = (
        lax.psum_scatter(col_sums[0], "batch", scatter_dimension=0, tiled=True),
        lax.psum_scatter(col_sums[1], "batch", scatter_dimension=0, tiled=True),
        lax.psum_scatter(col_sums[2], "batch", scatter_dimension=0, tiled=True),
        lax.psum_scatter(col_sums[3], "batch", scatter_dimension=0, tiled=True),
    )
    vec_grad = lax.psum(col_sums[4], "batch")
    qkv_m, qkv_s, qkv_w = adamw(w_qkv, qkv_grad, qkv_first, qkv_second, 0.06, 0.1)
    out_m, out_s, out_w = adamw(w_out, out_grad, out_first, out_second, 0.06, 0.1)
    fc_m, fc_s, fc_w = adamw(w_fc, fc_grad, fc_first, fc_second, 0.06, 0.1)
    proj_m, proj_s, proj_w = adamw(w_proj, proj_grad, proj_first, proj_second, 0.06, 0.1)
    vec_m, vec_s, vec_w = adamw(vectors, vec_grad, vec_first, vec_second, 0.2, 0.0)
    return (
        out_block,
        grad_input,
        qkv_m,
        qkv_s,
        qkv_w,
        out_m,
        out_s,
        out_w,
        fc_m,
        fc_s,
        fc_w,
        proj_m,
        proj_s,
        proj_w,
        vec_m,
        vec_s,
        vec_w,
    )


BATCH = 8
CTX = 4
WIDTH = 768
HEAD = 64
GROUP = WIDTH // CTX
TOKENS = 256
HALF = 128
FF_SIDE = 384
ROWS = WIDTH // BATCH
MLP = WIDTH + 2 * FF_SIDE + 256
SPAN = TOKENS * CTX
TILE = 256
LOW = jnp.bfloat16
WIDE = jnp.float32
CORE, XBIT, YBIT = 1, 2, 4
PLACES = (0, 1, 2, 3)
DIFFERENCES = (0, 2, 1, 3)
SOURCES = (
    (0, PLACES),
    (XBIT, PLACES),
    (YBIT, PLACES),
    (XBIT + YBIT, PLACES[:2]),
    (XBIT + YBIT, PLACES[2:]),
    (CORE, PLACES),
    (CORE + XBIT, PLACES),
    (CORE + YBIT, PLACES),
    (CORE + XBIT + YBIT, PLACES[:2]),
    (CORE + XBIT + YBIT, PLACES[2:]),
)
PARTS = len(SOURCES)
VMEM_LIMIT = 56 * 1024 * 1024


def swap(value, axis, bit):
    size = BATCH if axis == "batch" else CTX
    return lax.ppermute(value, axis, [(i, i ^ bit) for i in range(size)])


def mm(left, right):
    return lax.dot_general(left, right, (((1,), (0,)), ((), ())), preferred_element_type=WIDE)


def mt(left, right):
    return lax.dot_general(left, right, (((1,), (1,)), ((), ())), preferred_element_type=WIDE)


def tm(left, right):
    return lax.dot_general(left, right, (((0,), (0,)), ((), ())), preferred_element_type=WIDE)


def turned(value):
    return value.astype(WIDE).T.astype(LOW)


def moments(value):
    mean = jnp.mean(value, axis=-1, keepdims=True)
    centred = value - mean
    spread = jnp.mean(centred * centred, axis=-1, keepdims=True)
    return centred, lax.rsqrt(spread + 1e-05)


def norm_back(grad, normed, inverse, gain):
    part = grad * gain
    mean = jnp.mean(part, axis=-1, keepdims=True)
    cross = jnp.mean(part * normed, axis=-1, keepdims=True)
    return inverse * (part - mean - normed * cross)


def exchange(value):
    return swap(value, "ctx", 1), swap(value, "ctx", 2), swap(value, "ctx", 3)


def gather_first(own):
    return swap(own, "batch", XBIT), swap(own, "batch", YBIT)


def gather_second(from_x, from_y):
    return swap(from_x[:2], "batch", YBIT), swap(from_y[2:], "batch", XBIT)


def to_core(parts):
    return [swap(part, "batch", CORE) for part in parts]


def swap_pair(pair, first, second):
    return swap(pair[0], "batch", first), swap(pair[1], "batch", second)


def scatter_second(kept, back):
    one = kept[0].astype(WIDE) + back[0].astype(WIDE)
    two = kept[1].astype(WIDE) + back[1].astype(WIDE)
    return (one[0], two[0]), (one[1].astype(LOW), two[1].astype(LOW))


def scatter_near(kept, back):
    one = kept[0].astype(WIDE) + back[0].astype(WIDE)
    two = (kept[1].astype(WIDE) + back[1].astype(WIDE)).astype(LOW)
    return one, swap(two, "ctx", 1)


def scatter_far(one, two):
    one = one + two.astype(WIDE)
    return one[0] + swap(one[1].astype(LOW), "ctx", 2).astype(WIDE)


def rows_of(index, size):
    return pl.ds(pl.multiple_of(index * size, 16), size)


def qkv_place(held, batch, ctx):
    return [(pl.ds(0, 3 * GROUP), held.at[ctx, rows_of(batch, ROWS), :])]


def mlp_place(held_out, held_fc, held_proj, batch, ctx):
    return [
        (pl.ds(WIDTH + 2 * FF_SIDE, TILE), held_out.at[ctx, rows_of(batch, ROWS), :]),
        (pl.ds(0, WIDTH), held_fc.at[ctx, rows_of(batch, ROWS), :]),
        (pl.ds(WIDTH, FF_SIDE), held_proj.at[batch, rows_of(2 * ctx, ROWS), :]),
        (pl.ds(WIDTH + FF_SIDE, FF_SIDE), held_proj.at[batch, rows_of(2 * ctx + 1, ROWS), :]),
    ]


def load_weight(meta, parts, place, sems, shift):
    copies = []
    for part, (source, places) in zip(parts, SOURCES):
        for index, ctx in enumerate(places):
            ranges = place(meta[0] ^ source, shift ^ ctx)
            copies.append([(part.at[index, :, lanes], target) for lanes, target in ranges])
    started = []
    for kind in range(len(copies[0])):
        group = []
        for number, copy in enumerate(copies):
            group.append(pltpu.make_async_copy(*copy[kind], sems.at[kind, number]))
            group[-1].start()
        started.append(group)
    return started


def store_grad(held, targets, sems):
    one_kept, one_sent, two_kept, two_sent = targets
    copies = []
    for y in range(2):
        for x in range(2):
            for index, ctx in enumerate(DIFFERENCES):
                if index < 2:
                    target = (one_sent if y else one_kept).at[x, index]
                else:
                    target = (two_sent if x else two_kept).at[y, index - 2]
                for kind, (lanes, source) in enumerate(held(2 * y + x, ctx)):
                    number = (2 * y + x) * CTX + ctx
                    copies.append(
                        pltpu.make_async_copy(source, target.at[:, lanes], sems.at[kind, number])
                    )
                    copies[-1].start()
    wait_all(copies)


def half_rows(meta, pair, held):
    for index, value in enumerate(pair):
        held[index] = turned(value)
    parts = []
    for index in range(2):
        rows = [held[index, rows_of(meta[0] ^ (2 * part), ROWS), :] for part in range(BATCH // 2)]
        parts.append(jnp.concatenate(rows, axis=0))
    return parts


def over_both(left, right):
    return mm(left[0], right[0]) + mm(left[1], right[1])


def wait_all(copies):
    for copy in copies:
        copy.wait()


LANES = 128


def write_packed(target, value):
    full = value.shape[1] // LANES
    for index in range(full):
        target[index * TOKENS : (index + 1) * TOKENS, :] = value[
            :, index * LANES : (index + 1) * LANES
        ]
    rest = value[:, full * LANES :]
    target[full * TOKENS :, :] = jnp.concatenate([rest[:HALF], rest[HALF:]], axis=1)


def read_packed(source):
    full = source.shape[0] // TOKENS
    parts = [source[index * TOKENS : (index + 1) * TOKENS, :] for index in range(full)]
    rest = source[full * TOKENS :, :]
    parts.append(jnp.concatenate([rest[:, : LANES // 2], rest[:, LANES // 2 :]], axis=0))
    return jnp.concatenate(parts, axis=1)


def in_place(ctx, block):
    first = ctx if block == 0 else 2 * CTX - 1 - ctx
    return pl.ds(pl.multiple_of(first * HALF, HALF), HALF)


def read_vectors(meta, parts, chunks):
    for ctx, part in enumerate(parts):
        rows = [part[16 * index : 16 * (index + 1), :] for index in range(GROUP // HEAD)]
        chunks[meta[1] ^ ctx] = jnp.concatenate(rows, axis=1).astype(WIDE)
    return jnp.concatenate([chunks[index] for index in range(CTX)], axis=1)


def qkv_kernel(meta, x_ref, *refs):
    vectors, parts, refs = refs[:4], refs[4 : 4 + PARTS], refs[4 + PARTS :]
    h_ref, own, near, far, last, held, units, chunks, sems = refs
    (copies,) = load_weight(meta, parts, functools.partial(qkv_place, held), sems, meta[1])
    params = read_vectors(meta, vectors, chunks)
    bias = jnp.concatenate([params[4:5], jnp.zeros((1, WIDTH), WIDE), params[5:6]], axis=1)
    centred, inverse = moments(x_ref[...].astype(WIDE))
    normed = (centred * inverse * params[0:1] + params[1:2]).astype(LOW)
    h_ref[...] = normed
    wait_all(copies)
    for chunk in range(CTX):
        mixed = mm(normed, held[chunk]) + bias[:, 3 * GROUP * chunk : 3 * GROUP * (chunk + 1)]
        mixed = mixed.astype(LOW)
        for part in range(3):
            unit = 3 * chunk + part
            units[unit % CTX, :, (unit // CTX) * GROUP : (unit // CTX + 1) * GROUP] = mixed[
                :, part * GROUP : (part + 1) * GROUP
            ]
    for ctx, target in enumerate((own, near, far, last)):
        write_packed(target, units[meta[1] ^ ctx])


def read_sequence(meta, pieces, targets):
    for ctx, piece in enumerate(pieces):
        value = read_packed(piece)
        for block in range(2):
            place = in_place(meta[1] ^ ctx, block)
            rows = value[block * HALF : (block + 1) * HALF, :]
            for index, target in enumerate(targets):
                target[place, :] = rows[:, index * GROUP : (index + 1) * GROUP]


def write_sequence(meta, pieces, sources):
    for ctx, piece in enumerate(pieces):
        parts = []
        for source in sources:
            blocks = [source[in_place(meta[1] ^ ctx, block), :] for block in range(2)]
            parts.append(jnp.concatenate(blocks, axis=0).astype(LOW))
        write_packed(piece, jnp.concatenate(parts, axis=1))


def head_mask(head, scale=1.0):
    lane = lax.broadcasted_iota(jnp.int32, (1, GROUP), 1)
    inside = (lane >= head * HEAD) & (lane < (head + 1) * HEAD)
    return jnp.where(inside, scale, 0.0).astype(LOW)


def tile_of(index):
    return slice(index * TILE, (index + 1) * TILE)


def weights_of(queries, k_seq, tile, causal):
    scores = [mt(queries, k_seq[tile_of(other), :]) for other in range(tile + 1)]
    scores[tile] = jnp.where(causal, scores[tile], -1e30)
    top = jnp.max(functools.reduce(jnp.maximum, scores), axis=-1, keepdims=True)
    expo = [jnp.exp(score - top) for score in scores]
    total = jnp.sum(functools.reduce(jnp.add, expo), axis=-1, keepdims=True)
    inverse = 1.0 / total
    return [value * inverse for value in expo]


def causal_tile():
    row = lax.broadcasted_iota(jnp.int32, (TILE, TILE), 0)
    column = lax.broadcasted_iota(jnp.int32, (TILE, TILE), 1)
    return row >= column


def attend_kernel(meta, *refs):
    pieces, results, (q_seq, k_seq, v_seq, out) = refs[:4], refs[4:8], refs[8:]
    read_sequence(meta, pieces, (q_seq, k_seq, v_seq))
    causal = causal_tile()
    scale = 1.0 / math.sqrt(HEAD)
    for tile in range(SPAN // TILE):

        def one_head(head, total, tile=tile):
            mask = head_mask(head)
            queries = q_seq[tile_of(tile), :] * head_mask(head, scale)
            weights = weights_of(queries, k_seq, tile, causal)
            for other, weight in enumerate(weights):
                total = total + mm(weight.astype(LOW), v_seq[tile_of(other), :] * mask)
            return total

        out[tile_of(tile), :] = lax.fori_loop(
            0, GROUP // HEAD, one_head, jnp.zeros((TILE, GROUP), WIDE), unroll=True
        )
    write_sequence(meta, results, (out,))


def attend_back_kernel(meta, *refs):
    pieces, grads, results = refs[:4], refs[4:8], refs[8:12]
    q_seq, k_seq, v_seq, g_seq, dq, dk, dv = refs[12:]
    read_sequence(meta, pieces, (q_seq, k_seq, v_seq))
    read_sequence(meta, grads, (g_seq,))
    causal = causal_tile()
    scale = 1.0 / math.sqrt(HEAD)
    dk[...] = jnp.zeros_like(dk)
    dv[...] = jnp.zeros_like(dv)
    for tile in range(SPAN // TILE):

        def one_head(head, total, tile=tile):
            mask = head_mask(head)
            scaled = head_mask(head, scale)
            queries = q_seq[tile_of(tile), :] * scaled
            grad = g_seq[tile_of(tile), :] * mask
            weights = weights_of(queries, k_seq, tile, causal)
            backs = [mt(grad, v_seq[tile_of(other), :]) for other in range(tile + 1)]
            products = [weight * back for weight, back in zip(weights, backs)]
            delta = jnp.sum(functools.reduce(jnp.add, products), axis=-1, keepdims=True)
            for other, (weight, back) in enumerate(zip(weights, backs)):
                step = (weight * (back - delta)).astype(LOW)
                total = total + mm(step, k_seq[tile_of(other), :] * scaled)
                dk[tile_of(other), :] += tm(step, queries)
                dv[tile_of(other), :] += tm(weight.astype(LOW), grad)
            return total

        dq[tile_of(tile), :] = lax.fori_loop(
            0, GROUP // HEAD, one_head, jnp.zeros((TILE, GROUP), WIDE), unroll=True
        )
    write_sequence(meta, results, (dq, dk, dv))


def middle_kernel(meta, x_ref, dy_ref, h_one_ref, *refs):
    vectors, pieces, parts, refs = refs[:4], refs[4:8], refs[8 : 8 + PARTS], refs[8 + PARTS :]
    (out_ref, pack_ref, mine, theirs, dmid_ref), refs = refs[:5], refs[5:]
    results, (rows_ref, dbias_ref), refs = refs[:4], refs[4:6], refs[6:]
    out_parts, held_out, held_fc, held_proj, units, total, back, chunks, bias, acts, sems = refs
    place = functools.partial(mlp_place, out_parts, held_fc, held_proj)
    copies = load_weight(meta, parts, place, sems, 0)
    vec = read_vectors(meta, vectors, chunks)
    for chunk in range(CTX):
        bias[chunk] = vec[8 + chunk : 9 + chunk]
    for ctx, piece in enumerate(pieces):
        units[meta[1] ^ ctx] = read_packed(piece)
    att = jnp.concatenate([units[index] for index in range(CTX)], axis=1)
    pack_ref[CTX + 1] = att
    pack_ref[CTX + 3] = dy_ref[...]
    pack_ref[CTX + 4] = h_one_ref[...]
    wait_all(copies[0])
    for chunk in range(CTX):
        held_out[:, chunk * GROUP : (chunk + 1) * GROUP] = out_parts[chunk, :, :GROUP]
    mid = x_ref[...].astype(WIDE) + mm(att, held_out[...]) + vec[6:7]
    centred, inverse = moments(mid)
    normed = centred * inverse
    pack_ref[CTX] = (normed * vec[2:3] + vec[3:4]).astype(LOW)
    total[...] = mid + vec[7:8]
    back[...] = jnp.zeros_like(back)
    for group in copies[1:]:
        wait_all(group)
    side = FF_SIDE

    def chunk_step(chunk, carry):
        pre = mm(pack_ref[CTX], held_fc[chunk]) + bias[chunk]
        square = pre * pre
        tanh = jnp.tanh(0.7978845608028654 * (pre + 0.044715 * square * pre))
        act = (0.5 * pre * (1.0 + tanh)).astype(LOW)
        slope = 0.5 * (1.0 + tanh) + 0.5 * pre * (1.0 - tanh * tanh) * (
            0.7978845608028654 * (1.0 + 3.0 * 0.044715 * square)
        )
        grads = []
        for half in range(2):
            weight = held_proj[2 * chunk + half]
            part = act[:, half * side : (half + 1) * side]
            acts[2 * chunk + half] = part
            total[...] += mt(part, weight)
            grads.append(mm(dy_ref[...], weight))
        dpre = (jnp.concatenate(grads, axis=1) * slope).astype(LOW)
        pack_ref[chunk] = dpre
        dbias_ref[chunk] = jnp.sum(dpre.astype(WIDE), axis=0, keepdims=True)
        back[...] += mt(dpre, held_fc[chunk])
        return carry

    lax.fori_loop(0, CTX, chunk_step, 0)
    out_ref[...] = total[...].astype(LOW)
    core = meta[0] & 1
    for chunk in range(CTX):
        mine[chunk] = acts[2 * chunk + core]
        theirs[chunk] = acts[2 * chunk + 1 - core]
    grad = back[...]
    dy = dy_ref[...].astype(WIDE)
    dmid = dy + norm_back(grad, normed, inverse, vec[2:3])
    dmid_ref[...] = dmid
    datt = dmid.astype(LOW)
    pack_ref[CTX + 2] = datt
    rows_ref[0:1] = jnp.sum(grad * normed, axis=0, keepdims=True)
    rows_ref[1:2] = jnp.sum(grad, axis=0, keepdims=True)
    rows_ref[2:3] = jnp.sum(datt.astype(WIDE), axis=0, keepdims=True)
    rows_ref[3:4] = jnp.sum(dy, axis=0, keepdims=True)
    rows_ref[4:8] = jnp.zeros((4, WIDTH), WIDE)
    dout = mt(datt, held_out[...]).astype(LOW)
    for index in range(CTX):
        units[index] = dout[:, index * GROUP : (index + 1) * GROUP]
    for ctx, target in enumerate(results):
        write_packed(target, units[meta[1] ^ ctx])


def mlp_grad_kernel(meta, *refs):
    acts, packs, targets = refs[:2], refs[2:4], refs[4:8]
    held_out, held_fc, held_proj, turn, sems = refs[8:]
    dy = [turned(pack[CTX + 3]) for pack in packs]
    for chunk in range(CTX):
        held_proj[chunk] = over_both(dy, [act[chunk] for act in acts]).astype(LOW)
    left = half_rows(meta, [pack[CTX] for pack in packs], turn)
    for chunk in range(CTX):
        held_fc[chunk] = over_both(left, [pack[chunk] for pack in packs]).astype(LOW)
    left = half_rows(meta, [pack[CTX + 1] for pack in packs], turn)
    grad = over_both(left, [pack[CTX + 2] for pack in packs]).astype(LOW)
    for chunk in range(CTX):
        held_out[chunk, :, :GROUP] = grad[:, chunk * GROUP : (chunk + 1) * GROUP]
        held_out[chunk, :, GROUP:] = jnp.zeros((WIDTH // 2, TILE - GROUP), LOW)

    def place(part, ctx):
        ctx = meta[1] ^ ctx
        chunk = (meta[0] ^ (2 * part)) // 2
        rows = pl.ds(part * ROWS, ROWS)
        return [
            (pl.ds(WIDTH + 2 * FF_SIDE, TILE), held_out.at[ctx, rows, :]),
            (pl.ds(0, WIDTH), held_fc.at[ctx, rows, :]),
            (pl.ds(WIDTH, FF_SIDE), held_proj.at[chunk, rows_of(2 * ctx, ROWS), :]),
            (pl.ds(WIDTH + FF_SIDE, FF_SIDE), held_proj.at[chunk, rows_of(2 * ctx + 1, ROWS), :]),
        ]

    store_grad(place, targets, sems)


def qkv_grad_kernel(meta, *refs):
    pack, own, came, targets = refs[:2], refs[2:4], refs[4:6], refs[6:10]
    mixed_ref, dbias_ref, held, units, turn, sems = refs[10:]
    for core in range(2):
        for ctx in range(CTX):
            value = read_packed(own[core] if ctx == 0 else came[core].at[ctx - 1])
            for part in range(3):
                units[core, CTX * part + (meta[1] ^ ctx)] = value[
                    :, part * GROUP : (part + 1) * GROUP
                ]
    left = half_rows(meta, [pack[0][...], pack[1][...]], turn)
    for chunk in range(CTX):
        mixed = [
            jnp.concatenate([units[core, 3 * chunk + part] for part in range(3)], axis=1)
            for core in range(2)
        ]
        mixed_ref[chunk] = mixed[0]
        bias = jnp.sum(mixed[0].astype(WIDE), axis=0, keepdims=True)
        for part in range(3):
            dbias_ref[3 * chunk + part] = bias[:, part * GROUP : (part + 1) * GROUP]
        held[chunk] = over_both(left, mixed).astype(LOW)

    def place(part, ctx):
        return [(pl.ds(0, 3 * GROUP), held.at[meta[1] ^ ctx, pl.ds(part * ROWS, ROWS), :])]

    store_grad(place, targets, sems)


def input_grad_kernel(meta, x_ref, dmid_ref, mixed_ref, rows_ref, dfc_ref, dqkv_ref, *refs):
    vectors, parts, refs = refs[:4], refs[4 : 4 + PARTS], refs[4 + PARTS :]
    grad_ref, results, (held, chunks, rows, sums, sems) = refs[0], refs[1:5], refs[5:]
    (copies,) = load_weight(meta, parts, functools.partial(qkv_place, held), sems, meta[1])
    params = read_vectors(meta, vectors, chunks)
    centred, inverse = moments(x_ref[...].astype(WIDE))
    normed = centred * inverse
    wait_all(copies)
    grad = jnp.zeros((TOKENS, WIDTH), WIDE)
    for chunk in range(CTX):
        grad = grad + mt(mixed_ref[chunk], held[chunk])
    grad_ref[...] = dmid_ref[...] + norm_back(grad, normed, inverse, params[0:1])
    rows[0:1] = jnp.sum(grad * normed, axis=0, keepdims=True)
    rows[1:2] = jnp.sum(grad, axis=0, keepdims=True)
    rows[2:4] = rows_ref[0:2]
    for chunk in range(CTX):
        lanes = slice(chunk * GROUP, (chunk + 1) * GROUP)
        rows[4:5, lanes] = dqkv_ref[chunk]
        rows[5:6, lanes] = dqkv_ref[2 * CTX + chunk]
        rows[8 + chunk : 9 + chunk] = dfc_ref[chunk]
    rows[6:8] = rows_ref[2:4]
    rows[12:16] = jnp.zeros((4, WIDTH), WIDE)
    for chunk in range(CTX):
        sums[chunk] = rows[:, chunk * GROUP : (chunk + 1) * GROUP]
    for ctx, target in enumerate(results):
        target[...] = sums[meta[1] ^ ctx]


def sum_kernel(one_kept, one_back, two_kept, two_back, one_keep, one_send, two_keep, two_send):
    pairs = ((one_kept, one_back, one_keep, one_send), (two_kept, two_back, two_keep, two_send))
    for kept, back, keep, send in pairs:
        keep[...] = kept[0].astype(WIDE) + back[0].astype(WIDE)
        send[...] = (kept[1].astype(WIDE) + back[1].astype(WIDE)).astype(LOW)


def shape_of(dtype, *dims):
    return jax.ShapeDtypeStruct(dims, dtype)


def call(kernel, arguments, kinds, outputs, out_kinds, scratch):
    spec = {
        "v": pl.BlockSpec(memory_space=pltpu.VMEM),
        "s": pl.BlockSpec(memory_space=pltpu.SMEM),
        "a": pl.BlockSpec(memory_space=pl.ANY),
        "h": pl.BlockSpec((None, TOKENS, WIDTH), lambda step: (CTX + 4, 0, 0)),
    }
    return pl.pallas_call(
        kernel,
        grid=(1,),
        out_shape=tuple(outputs),
        in_specs=[spec[kind] for kind in kinds],
        out_specs=tuple(spec[kind] for kind in out_kinds),
        scratch_shapes=scratch,
        cost_estimate=pl.CostEstimate(flops=1, bytes_accessed=1, transcendentals=0),
        compiler_params=pltpu.CompilerParams(vmem_limit_bytes=VMEM_LIMIT),
    )(*arguments)


def local_fast(
    block_in,
    cotangent,
    w_qkv,
    w_out,
    w_fc,
    w_proj,
    vectors,
    qkv_first,
    qkv_second,
    out_first,
    out_second,
    fc_first,
    fc_second,
    proj_first,
    proj_second,
    vec_first,
    vec_second,
):
    batch, ctx = lax.axis_index("batch"), lax.axis_index("ctx")
    meta = jnp.stack([batch, ctx]).astype(jnp.int32)
    inputs = block_in.reshape(TOKENS, WIDTH)
    grad_low = cotangent.reshape(TOKENS, WIDTH)
    tie = lax.optimization_barrier

    qkv_sems = pltpu.SemaphoreType.DMA((1, BATCH * CTX))
    mlp_sems = pltpu.SemaphoreType.DMA((4, BATCH * CTX))
    qkv_held = pltpu.VMEM((CTX, WIDTH, 3 * GROUP), LOW)
    vec_held = pltpu.VMEM((CTX, 16, GROUP), WIDE)

    low_vec = jnp.pad(vectors.astype(LOW), ((0, 4), (0, 0)))
    low_vec = [low_vec[:, start : start + HEAD] for start in range(0, GROUP, HEAD)]
    low_vec = jnp.concatenate(low_vec + [jnp.zeros((ROWS - 48, HEAD), LOW)], axis=0)
    piece_one = jnp.concatenate([w_qkv.astype(LOW), low_vec], axis=1)
    low_proj = w_proj.astype(LOW).T
    piece_two = jnp.concatenate(
        [
            w_fc.astype(LOW),
            low_proj[:ROWS],
            low_proj[ROWS:],
            w_out.astype(LOW),
            jnp.zeros((ROWS, TILE - GROUP), LOW),
        ],
        axis=1,
    )
    parts_one = (piece_one,) + exchange(piece_one)
    vec_parts = [part[:48, 3 * GROUP :] for part in parts_one]
    own_one = jnp.stack([part[:, : 3 * GROUP] for part in parts_one])
    piece_two, late_vec = tie((piece_two, vec_parts))
    own_two = lax.all_gather(piece_two, "ctx", axis=0)
    x_one, y_one = gather_first(own_one)
    parts_one = [own_one, x_one, y_one, *gather_second(x_one, y_one)]
    parts_one = parts_one + to_core(parts_one)

    packed = shape_of(LOW, TOKENS * 3 * GROUP // LANES, LANES)
    single = shape_of(LOW, TOKENS * GROUP // LANES, LANES)
    tokens_low = shape_of(LOW, TOKENS, WIDTH)
    hidden_low = shape_of(LOW, CTX, TOKENS, WIDTH)
    h_one, own, *sent = call(
        qkv_kernel,
        (meta, inputs, *vec_parts, *parts_one),
        "s" + "v" * 5 + "a" * PARTS,
        [tokens_low] + [packed] * 4,
        "v" * 5,
        [qkv_held, pltpu.VMEM((CTX, TOKENS, 3 * GROUP), LOW), vec_held, qkv_sems],
    )
    qkv_pieces = [own] + [swap(part, "ctx", bit) for bit, part in zip((1, 2, 3), sent)]

    own_two, late_h = tie((own_two, h_one))
    x_two, y_two = gather_first(own_two)
    qkv_pieces, x_two, y_two = tie((qkv_pieces, x_two, y_two))
    across_two = gather_second(x_two, y_two)
    parts_two = [own_two, x_two, y_two]
    swapped_two = to_core(parts_two)

    sequence_low = pltpu.VMEM((SPAN, GROUP), LOW)
    sequence_wide = pltpu.VMEM((SPAN, GROUP), WIDE)
    own, *sent = call(
        attend_kernel,
        (meta, *qkv_pieces),
        "s" + "v" * 4,
        [single] * 4,
        "v" * 4,
        [sequence_low] * 3 + [sequence_wide],
    )
    sent, swapped_two = tie((sent, swapped_two))
    att_pieces = [own] + [swap(part, "ctx", bit) for bit, part in zip((1, 2, 3), sent)]
    across_two, att_pieces = tie((across_two, att_pieces))
    parts_two = parts_two + list(across_two) + swapped_two + to_core(across_two)

    pack_shape = shape_of(LOW, CTX + 5, TOKENS, WIDTH)
    act_shape = shape_of(LOW, BATCH // 2, TOKENS, FF_SIDE)
    out, pack, act_mine, act_theirs, dmid, own, *sent = call(
        middle_kernel,
        (meta, inputs, grad_low, late_h, *vec_parts, *att_pieces, *parts_two),
        "s" + "v" * 11 + "a" * PARTS,
        [tokens_low, pack_shape, act_shape, act_shape, shape_of(WIDE, TOKENS, WIDTH)]
        + [single] * 4
        + [shape_of(WIDE, 8, WIDTH), shape_of(WIDE, CTX, 1, WIDTH)],
        "v" * 11,
        [
            pltpu.VMEM((CTX, WIDTH, TILE), LOW),
            pltpu.VMEM((WIDTH, WIDTH), LOW),
            pltpu.VMEM((CTX, WIDTH, WIDTH), LOW),
            pltpu.VMEM((BATCH, WIDTH, FF_SIDE), LOW),
            pltpu.VMEM((CTX, TOKENS, GROUP), LOW),
            pltpu.VMEM((TOKENS, WIDTH), WIDE),
            pltpu.VMEM((TOKENS, WIDTH), WIDE),
            vec_held,
            pltpu.VMEM((CTX, 1, WIDTH), WIDE),
            pltpu.VMEM((BATCH, TOKENS, FF_SIDE), LOW),
            mlp_sems,
        ],
    )
    sent, (rows_two, dbias_fc) = sent[:3], sent[3:]
    grad_pieces = [own] + [swap(part, "ctx", bit) for bit, part in zip((1, 2, 3), sent)]
    act_came, pack_came = swap(act_theirs, "batch", CORE), swap(pack, "batch", CORE)

    half_sems = BATCH * CTX // 2
    turn_held = pltpu.VMEM((2, WIDTH, TOKENS), LOW)
    mlp_parts = call(
        mlp_grad_kernel,
        (meta, act_mine, act_came, pack, pack_came),
        "s" + "v" * 4,
        [shape_of(LOW, 2, 2, ROWS, MLP)] * 4,
        "aaaa",
        [
            pltpu.VMEM((CTX, WIDTH // 2, TILE), LOW),
            pltpu.VMEM((CTX, WIDTH // 2, WIDTH), LOW),
            pltpu.VMEM((BATCH // 2, WIDTH, FF_SIDE), LOW),
            turn_held,
            pltpu.SemaphoreType.DMA((4, half_sems)),
        ],
    )
    mlp_parts, grad_pieces = tie((mlp_parts, grad_pieces))
    mlp_kept = mlp_parts[0], mlp_parts[2]
    mlp_back = swap_pair((mlp_parts[1], mlp_parts[3]), YBIT, XBIT)
    own, *sent = call(
        attend_back_kernel,
        (meta, *qkv_pieces, *grad_pieces),
        "s" + "v" * 8,
        [packed] * 4,
        "v" * 4,
        [sequence_low] * 4 + [sequence_wide] * 3,
    )
    own_came = swap(own, "batch", CORE)
    received = [swap(part, "ctx", bit) for bit, part in zip((1, 2, 3), sent)]
    mlp_back, received[0] = tie((mlp_back, received[0]))
    pair = [shape_of(WIDE, 2, ROWS, MLP), shape_of(LOW, 2, ROWS, MLP)]
    one_keep, one_send, two_keep, two_send = call(
        sum_kernel,
        (mlp_kept[0], mlp_back[0], mlp_kept[1], mlp_back[1]),
        "vvvv",
        pair + pair,
        "vvvv",
        [],
    )
    one_keep, received[1], received[2] = tie((one_keep, received[1], received[2]))
    mlp_back = swap_pair((one_send, two_send), XBIT, YBIT)
    received = jnp.stack(received)
    received_came = swap(received, "batch", CORE)

    *qkv_parts, mixed, dbias_qkv = call(
        qkv_grad_kernel,
        (meta, pack, pack_came, own, own_came, received, received_came),
        "shhvvvv",
        [shape_of(LOW, 2, 2, ROWS, 3 * GROUP)] * 4
        + [shape_of(LOW, CTX, TOKENS, 3 * GROUP), shape_of(WIDE, 3 * CTX, 1, GROUP)],
        "aaaavv",
        [
            pltpu.VMEM((CTX, WIDTH // 2, 3 * GROUP), LOW),
            pltpu.VMEM((2, 3 * CTX, TOKENS, GROUP), LOW),
            turn_held,
            pltpu.SemaphoreType.DMA((1, half_sems)),
        ],
    )
    qkv_kept = qkv_parts[0], qkv_parts[2]
    mlp_back, qkv_parts = tie((mlp_back, qkv_parts))
    mlp_one, mlp_two = scatter_near((one_keep, two_keep), mlp_back)
    qkv_kept = qkv_parts[0], qkv_parts[2]
    qkv_back = swap_pair((qkv_parts[1], qkv_parts[3]), YBIT, XBIT)
    grad_input, own, *sent = call(
        input_grad_kernel,
        (meta, inputs, dmid, mixed, rows_two, dbias_fc, dbias_qkv, *late_vec, *parts_one),
        "s" + "v" * 10 + "a" * PARTS,
        [shape_of(WIDE, TOKENS, WIDTH)] + [shape_of(WIDE, 16, GROUP)] * 4,
        "v" * 5,
        [qkv_held, vec_held, pltpu.VMEM((16, WIDTH), WIDE), vec_held, qkv_sems],
    )
    qkv_kept, qkv_sent = scatter_second(qkv_kept, qkv_back)
    qkv_back = swap_pair(qkv_sent, XBIT, YBIT)
    qkv_back, own, sent = tie((qkv_back, own, sent))
    mlp_grad = scatter_far(mlp_one, mlp_two)
    qkv_grad = scatter_far(*scatter_near(qkv_kept, qkv_back))

    vec_grad = own + sum(swap(part, "ctx", bit) for bit, part in zip((1, 2, 3), sent))
    for bit in (CORE, XBIT, YBIT):
        vec_grad = vec_grad + swap(vec_grad, "batch", bit)
    vec_grad = vec_grad[:12]
    fc_grad = mlp_grad[:, :WIDTH]
    proj_grad = jnp.concatenate(
        [mlp_grad[:, WIDTH : WIDTH + FF_SIDE], mlp_grad[:, WIDTH + FF_SIDE : WIDTH + 2 * FF_SIDE]],
        axis=0,
    )
    out_grad = mlp_grad[:, WIDTH + 2 * FF_SIDE : WIDTH + 2 * FF_SIDE + GROUP]

    qkv_m, qkv_s, qkv_w = adamw(w_qkv, qkv_grad, qkv_first, qkv_second, 0.06, 0.1)
    out_m, out_s, out_w = adamw(w_out, out_grad, out_first, out_second, 0.06, 0.1)
    fc_m, fc_s, fc_w = adamw(w_fc, fc_grad, fc_first, fc_second, 0.06, 0.1)
    proj_m, proj_s, proj_w = adamw(w_proj, proj_grad.T, proj_first, proj_second, 0.06, 0.1)
    vec_m, vec_s, vec_w = adamw(vectors, vec_grad, vec_first, vec_second, 0.2, 0.0)
    return (
        out.reshape(block_in.shape),
        grad_input.reshape(block_in.shape),
        qkv_m,
        qkv_s,
        qkv_w,
        out_m,
        out_s,
        out_w,
        fc_m,
        fc_s,
        fc_w,
        proj_m,
        proj_s,
        proj_w,
        vec_m,
        vec_s,
        vec_w,
    )


def solution(mesh):
    in_specs = (
        P("batch", "ctx", None, None),
        P("batch", "ctx", None, None),
        P("batch", "ctx"),
        P("batch", "ctx"),
        P("batch", "ctx"),
        P("batch", "ctx"),
        P(None, "ctx"),
        P("batch", "ctx"),
        P("batch", "ctx"),
        P("batch", "ctx"),
        P("batch", "ctx"),
        P("batch", "ctx"),
        P("batch", "ctx"),
        P("batch", "ctx"),
        P("batch", "ctx"),
        P(None, "ctx"),
        P(None, "ctx"),
    )
    out_specs = (
        P("batch", "ctx", None, None),
        P("batch", "ctx", None, None),
        P("batch", "ctx"),
        P("batch", "ctx"),
        P("batch", "ctx"),
        P("batch", "ctx"),
        P("batch", "ctx"),
        P("batch", "ctx"),
        P("batch", "ctx"),
        P("batch", "ctx"),
        P("batch", "ctx"),
        P("batch", "ctx"),
        P("batch", "ctx"),
        P("batch", "ctx"),
        P(None, "ctx"),
        P(None, "ctx"),
        P(None, "ctx"),
    )
    sizes = (mesh.shape["batch"], mesh.shape["ctx"])
    local = local_fast if sizes == (BATCH, CTX) else local_any
    return jax.shard_map(local, mesh=mesh, in_specs=in_specs, out_specs=out_specs, check_vma=False)
```

```python
import functools
import math

import jax
import jax.numpy as jnp
from jax import lax
from jax.experimental import pallas as pl
from jax.experimental.pallas import tpu as pltpu
from jax.sharding import PartitionSpec as P

HEADS = 12
STEP = 10


def layer_norm(value, gain, shift):
    mean = jnp.mean(value, axis=-1, keepdims=True)
    centred = value - mean
    spread = jnp.mean(centred * centred, axis=-1, keepdims=True)
    return centred * lax.rsqrt(spread + 1e-05) * gain + shift


def gelu_tanh(value):
    return (
        0.5
        * value
        * (1.0 + jnp.tanh(0.7978845608028654 * (value + 0.044715 * value * value * value)))
    )


def block_places(index, count, half):
    offsets = jnp.arange(half, dtype=jnp.int32)
    first = index * half + offsets
    second = (2 * count - 1 - index) * half + offsets
    return jnp.concatenate([first, second])


def scores_of(queries, keys, scale, allowed):
    raw = jnp.einsum("sqhd,skhd->shqk", queries, keys, preferred_element_type=jnp.float32) * scale
    return jnp.where(allowed[None, None], raw, -1e30)


def pair_grads(queries, grads, keys, values, top, total, delta, scale, allowed):
    score = scores_of(queries, keys, scale, allowed)
    weights = jnp.exp(score - top[..., None]) / total[..., None]
    back_weights = jnp.einsum("sqhd,skhd->shqk", grads, values, preferred_element_type=jnp.float32)
    grad_score = (weights * (back_weights - delta[..., None])).astype(jnp.bfloat16)
    return (weights.astype(jnp.bfloat16), grad_score)


def rows_product(left, right):
    return jnp.einsum("ra,rb->ab", left, right, preferred_element_type=jnp.float32)


def back_product(grad, weight):
    return jnp.einsum("rb,ab->ra", grad, weight, preferred_element_type=jnp.float32)


def adamw(weight, grad, first, second, rate, decay):
    first = 0.9 * first + 0.1 * grad
    second = 0.999 * second + 0.001 * grad * grad
    first_hat = first / (1.0 - 0.9**STEP)
    second_hat = second / (1.0 - 0.999**STEP)
    weight = weight - rate * (first_hat / (jnp.sqrt(second_hat) + 1e-08) + decay * weight)
    return (first, second, weight)


def local_any(
    block_in,
    cotangent,
    w_qkv,
    w_out,
    w_fc,
    w_proj,
    vectors,
    qkv_first,
    qkv_second,
    out_first,
    out_second,
    fc_first,
    fc_second,
    proj_first,
    proj_second,
    vec_first,
    vec_second,
):
    low_type = jnp.bfloat16
    wide = jnp.float32
    row_parts = (
        lax.all_gather(w_qkv.astype(low_type), "batch", axis=0, tiled=True),
        lax.all_gather(w_out.astype(low_type), "batch", axis=0, tiled=True),
        lax.all_gather(w_fc.astype(low_type), "batch", axis=0, tiled=True),
        lax.all_gather(w_proj.astype(low_type), "batch", axis=0, tiled=True),
    )
    full_qkv, full_out, full_fc, full_proj, full_vec = (
        lax.all_gather(row_parts[0], "ctx", axis=1, tiled=True),
        lax.all_gather(row_parts[1], "ctx", axis=1, tiled=True),
        lax.all_gather(row_parts[2], "ctx", axis=1, tiled=True),
        lax.all_gather(row_parts[3], "ctx", axis=1, tiled=True),
        lax.all_gather(vectors.astype(low_type), "ctx", axis=1, tiled=True),
    )
    params = full_vec.astype(wide)
    seqs, pair, half, width = block_in.shape
    heads = HEADS
    head = width // heads
    rows = seqs * pair * half
    span = pair * half
    count = lax.axis_size("ctx")
    index = lax.axis_index("ctx")
    scale = 1.0 / math.sqrt(head)
    inputs = block_in.astype(wide).reshape(rows, width)
    normed_one = layer_norm(inputs, params[0], params[1]).astype(low_type)
    mixed = jnp.dot(normed_one, full_qkv, preferred_element_type=wide)
    queries = (mixed[:, :width] + params[4]).astype(low_type)
    keys = mixed[:, width : 2 * width].astype(low_type)
    values = (mixed[:, 2 * width :] + params[5]).astype(low_type)
    key_all, value_all = (
        lax.all_gather(keys.reshape(seqs, pair, half, width), "ctx", axis=1, tiled=True),
        lax.all_gather(values.reshape(seqs, pair, half, width), "ctx", axis=1, tiled=True),
    )
    query_heads = queries.reshape(seqs, span, heads, head)
    own_places = block_places(index, count, half)

    def piece_of(source, piece):
        return lax.dynamic_slice_in_dim(source, 2 * piece, 2, 1).reshape(seqs, span, heads, head)

    def allowed_for(piece):
        return own_places[:, None] >= block_places(piece, count, half)[None, :]

    def stats_step(piece, carry):
        top, total = carry
        score = scores_of(query_heads, piece_of(key_all, piece), scale, allowed_for(piece))
        new_top = jnp.maximum(top, jnp.max(score, axis=-1))
        total = total * jnp.exp(top - new_top) + jnp.sum(
            jnp.exp(score - new_top[..., None]), axis=-1
        )
        return (new_top, total)

    start_stats = (jnp.full((seqs, heads, span), -1e30, wide), jnp.zeros((seqs, heads, span), wide))
    top, total = lax.fori_loop(0, count, stats_step, start_stats)

    def output_step(piece, acc):
        score = scores_of(query_heads, piece_of(key_all, piece), scale, allowed_for(piece))
        weights = (jnp.exp(score - top[..., None]) / total[..., None]).astype(low_type)
        return acc + jnp.einsum(
            "shqk,skhd->sqhd", weights, piece_of(value_all, piece), preferred_element_type=wide
        )

    attended = lax.fori_loop(0, count, output_step, jnp.zeros((seqs, span, heads, head), wide))
    att_low = attended.reshape(rows, width).astype(low_type)
    mid = inputs + jnp.dot(att_low, full_out, preferred_element_type=wide) + params[6]
    normed_two = layer_norm(mid, params[2], params[3]).astype(low_type)
    pre = jnp.dot(normed_two, full_fc, preferred_element_type=wide) + params[8:12].reshape(-1)
    act_low = gelu_tanh(pre).astype(low_type)
    result = mid + jnp.dot(act_low, full_proj, preferred_element_type=wide) + params[7]
    out_block = result.astype(low_type).reshape(block_in.shape)
    grad_low = cotangent.reshape(rows, width)
    grad_out = grad_low.astype(wide)
    grad_wproj = rows_product(act_low, grad_low)
    back_act = back_product(grad_low, full_proj)
    grad_pre = jax.vjp(gelu_tanh, pre)[1](back_act)[0].astype(low_type)
    grad_wfc = rows_product(normed_two, grad_pre)
    back_two = back_product(grad_pre, full_fc)
    back_mid, grad_gain_two, grad_shift_two = jax.vjp(layer_norm, mid, params[2], params[3])[1](
        back_two
    )
    grad_mid = grad_out + back_mid
    grad_att_low = grad_mid.astype(low_type)
    grad_wout = rows_product(att_low, grad_att_low)
    back_att = back_product(grad_att_low, full_out)
    grad_heads = back_att.astype(low_type).reshape(seqs, span, heads, head)
    delta = jnp.einsum("sqhd,sqhd->shq", grad_heads.astype(wide), attended)
    query_all, grad_all = (
        lax.all_gather(queries.reshape(seqs, pair, half, width), "ctx", axis=1, tiled=True),
        lax.all_gather(grad_heads.reshape(seqs, pair, half, width), "ctx", axis=1, tiled=True),
    )
    top_all, total_all, delta_all = (
        lax.all_gather(top.reshape(seqs, heads, pair, half), "ctx", axis=2, tiled=True),
        lax.all_gather(total.reshape(seqs, heads, pair, half), "ctx", axis=2, tiled=True),
        lax.all_gather(delta.reshape(seqs, heads, pair, half), "ctx", axis=2, tiled=True),
    )

    def query_step(piece, grad_query):
        key_part = piece_of(key_all, piece)
        value_part = piece_of(value_all, piece)
        weights_low, grad_score = pair_grads(
            query_heads,
            grad_heads,
            key_part,
            value_part,
            top,
            total,
            delta,
            scale,
            allowed_for(piece),
        )
        return grad_query + jnp.einsum(
            "shqk,skhd->sqhd", grad_score, key_part, preferred_element_type=wide
        )

    grad_query = lax.fori_loop(0, count, query_step, jnp.zeros((seqs, span, heads, head), wide))
    key_heads = keys.reshape(seqs, span, heads, head)
    value_heads = values.reshape(seqs, span, heads, head)

    def stat_piece(source, piece):
        return lax.dynamic_slice_in_dim(source, 2 * piece, 2, 2).reshape(seqs, heads, span)

    def key_step(piece, carry):
        grad_key, grad_value = carry
        query_part = piece_of(query_all, piece)
        grad_part = piece_of(grad_all, piece)
        allowed = block_places(piece, count, half)[:, None] >= own_places[None, :]
        weights_low, grad_score = pair_grads(
            query_part,
            grad_part,
            key_heads,
            value_heads,
            stat_piece(top_all, piece),
            stat_piece(total_all, piece),
            stat_piece(delta_all, piece),
            scale,
            allowed,
        )
        grad_key = grad_key + jnp.einsum(
            "shqk,sqhd->skhd", grad_score, query_part, preferred_element_type=wide
        )
        grad_value = grad_value + jnp.einsum(
            "shqk,sqhd->skhd", weights_low, grad_part, preferred_element_type=wide
        )
        return (grad_key, grad_value)

    start_keys = (
        jnp.zeros((seqs, span, heads, head), wide),
        jnp.zeros((seqs, span, heads, head), wide),
    )
    grad_key, grad_value = lax.fori_loop(0, count, key_step, start_keys)
    grad_keys = (grad_key * scale).reshape(seqs, pair, half, width)
    grad_values = grad_value.reshape(seqs, pair, half, width)
    grad_q_low = (grad_query * scale).reshape(rows, width).astype(low_type)
    grad_k_low = grad_keys.reshape(rows, width).astype(low_type)
    grad_v_low = grad_values.reshape(rows, width).astype(low_type)
    grad_mixed = jnp.concatenate([grad_q_low, grad_k_low, grad_v_low], axis=1)
    grad_wqkv = rows_product(normed_one, grad_mixed)
    back_one = back_product(grad_mixed, full_qkv)
    back_in, grad_gain_one, grad_shift_one = jax.vjp(layer_norm, inputs, params[0], params[1])[1](
        back_one
    )
    grad_input = (grad_mid + back_in).reshape(block_in.shape)
    grad_bias_q = jnp.sum(grad_q_low.astype(wide), axis=0)
    grad_bias_v = jnp.sum(grad_v_low.astype(wide), axis=0)
    grad_bias_out = jnp.sum(grad_att_low.astype(wide), axis=0)
    grad_bias_proj = jnp.sum(grad_out, axis=0)
    grad_bias_fc = jnp.sum(grad_pre.astype(wide), axis=0).reshape(4, width)
    small_rows = jnp.stack(
        [
            grad_gain_one,
            grad_shift_one,
            grad_gain_two,
            grad_shift_two,
            grad_bias_q,
            grad_bias_v,
            grad_bias_out,
            grad_bias_proj,
        ]
    )
    grad_vectors = jnp.concatenate([small_rows, grad_bias_fc], axis=0)
    col_sums = (
        lax.psum_scatter(grad_wqkv, "ctx", scatter_dimension=1, tiled=True),
        lax.psum_scatter(grad_wout, "ctx", scatter_dimension=1, tiled=True),
        lax.psum_scatter(grad_wfc, "ctx", scatter_dimension=1, tiled=True),
        lax.psum_scatter(grad_wproj, "ctx", scatter_dimension=1, tiled=True),
        lax.psum_scatter(grad_vectors, "ctx", scatter_dimension=1, tiled=True),
    )
    qkv_grad, out_grad, fc_grad, proj_grad = (
        lax.psum_scatter(col_sums[0], "batch", scatter_dimension=0, tiled=True),
        lax.psum_scatter(col_sums[1], "batch", scatter_dimension=0, tiled=True),
        lax.psum_scatter(col_sums[2], "batch", scatter_dimension=0, tiled=True),
        lax.psum_scatter(col_sums[3], "batch", scatter_dimension=0, tiled=True),
    )
    vec_grad = lax.psum(col_sums[4], "batch")
    qkv_m, qkv_s, qkv_w = adamw(w_qkv, qkv_grad, qkv_first, qkv_second, 0.06, 0.1)
    out_m, out_s, out_w = adamw(w_out, out_grad, out_first, out_second, 0.06, 0.1)
    fc_m, fc_s, fc_w = adamw(w_fc, fc_grad, fc_first, fc_second, 0.06, 0.1)
    proj_m, proj_s, proj_w = adamw(w_proj, proj_grad, proj_first, proj_second, 0.06, 0.1)
    vec_m, vec_s, vec_w = adamw(vectors, vec_grad, vec_first, vec_second, 0.2, 0.0)
    return (
        out_block,
        grad_input,
        qkv_m,
        qkv_s,
        qkv_w,
        out_m,
        out_s,
        out_w,
        fc_m,
        fc_s,
        fc_w,
        proj_m,
        proj_s,
        proj_w,
        vec_m,
        vec_s,
        vec_w,
    )


BATCH = 8
CTX = 4
WIDTH = 768
HEAD = 64
GROUP = WIDTH // CTX
TOKENS = 256
HALF = 128
FF_SIDE = 384
ROWS = WIDTH // BATCH
MLP = WIDTH + 2 * FF_SIDE + 256
SPAN = TOKENS * CTX
TILE = 256
LOW = jnp.bfloat16
WIDE = jnp.float32
CORE, XBIT, YBIT = 1, 2, 4
PLACES = (0, 2, 1, 3)
SOURCES = (
    (0, PLACES),
    (XBIT, PLACES),
    (YBIT, PLACES),
    (XBIT + YBIT, PLACES[:2]),
    (XBIT + YBIT, PLACES[2:]),
    (CORE, PLACES),
    (CORE + XBIT, PLACES),
    (CORE + YBIT, PLACES),
    (CORE + XBIT + YBIT, PLACES[:2]),
    (CORE + XBIT + YBIT, PLACES[2:]),
)
PARTS = len(SOURCES)
VMEM_LIMIT = 56 * 1024 * 1024


def swap(value, axis, bit):
    size = BATCH if axis == "batch" else CTX
    return lax.ppermute(value, axis, [(i, i ^ bit) for i in range(size)])


def mm(left, right):
    return lax.dot_general(left, right, (((1,), (0,)), ((), ())), preferred_element_type=WIDE)


def mt(left, right):
    return lax.dot_general(left, right, (((1,), (1,)), ((), ())), preferred_element_type=WIDE)


def tm(left, right):
    return lax.dot_general(left, right, (((0,), (0,)), ((), ())), preferred_element_type=WIDE)


def turned(value):
    return value.astype(WIDE).T.astype(LOW)


def moments(value):
    mean = jnp.mean(value, axis=-1, keepdims=True)
    centred = value - mean
    spread = jnp.mean(centred * centred, axis=-1, keepdims=True)
    return centred, lax.rsqrt(spread + 1e-05)


def norm_back(grad, normed, inverse, gain):
    part = grad * gain
    mean = jnp.mean(part, axis=-1, keepdims=True)
    cross = jnp.mean(part * normed, axis=-1, keepdims=True)
    return inverse * (part - mean - normed * cross)


def gather_first(own):
    return swap(own, "batch", XBIT), swap(own, "batch", YBIT)


def gather_second(from_x, from_y):
    return swap(from_x[:2], "batch", YBIT), swap(from_y[2:], "batch", XBIT)


def to_core(parts):
    return [swap(part, "batch", CORE) for part in parts]


def swap_pair(pair, first, second):
    return swap(pair[0], "batch", first), swap(pair[1], "batch", second)


def scatter_second(kept, back):
    one = kept[0].astype(WIDE) + back[0].astype(WIDE)
    two = kept[1].astype(WIDE) + back[1].astype(WIDE)
    return (one[0], two[0]), (one[1].astype(LOW), two[1].astype(LOW))


def scatter_near(kept, back):
    one = kept[0].astype(WIDE) + back[0].astype(WIDE)
    two = (kept[1].astype(WIDE) + back[1].astype(WIDE)).astype(LOW)
    return one, swap(two, "ctx", 1)


def scatter_far(one, two):
    one = one + two.astype(WIDE)
    return one[0] + swap(one[1].astype(LOW), "ctx", 2).astype(WIDE)


def rows_of(index, size):
    return pl.ds(pl.multiple_of(index * size, 16), size)


def qkv_place(held, batch, ctx):
    return [(pl.ds(0, 3 * GROUP), held.at[ctx, rows_of(batch, ROWS), :])]


def mlp_place(held_out, held_fc, held_proj, batch, ctx):
    return [
        (pl.ds(WIDTH + 2 * FF_SIDE, TILE), held_out.at[ctx, rows_of(batch, ROWS), :]),
        (pl.ds(0, WIDTH), held_fc.at[ctx, rows_of(batch, ROWS), :]),
        (pl.ds(WIDTH, FF_SIDE), held_proj.at[batch, rows_of(2 * ctx, ROWS), :]),
        (pl.ds(WIDTH + FF_SIDE, FF_SIDE), held_proj.at[batch, rows_of(2 * ctx + 1, ROWS), :]),
    ]


def load_weight(meta, parts, place, sems):
    copies = []
    for part, (source, places) in zip(parts, SOURCES):
        for index, ctx in enumerate(places):
            ranges = place(meta[0] ^ source, meta[1] ^ ctx)
            copies.append([(part.at[index, :, lanes], target) for lanes, target in ranges])
    started = []
    for kind in range(len(copies[0])):
        group = []
        for number, copy in enumerate(copies):
            group.append(pltpu.make_async_copy(*copy[kind], sems.at[kind, number]))
            group[-1].start()
        started.append(group)
    return started


def store_grad(held, targets, sems):
    one_kept, one_sent, two_kept, two_sent = targets
    copies = []
    for y in range(2):
        for x in range(2):
            for index, ctx in enumerate(PLACES):
                if index < 2:
                    target = (one_sent if y else one_kept).at[x, index]
                else:
                    target = (two_sent if x else two_kept).at[y, index - 2]
                for kind, (lanes, source) in enumerate(held(2 * y + x, ctx)):
                    number = (2 * y + x) * CTX + ctx
                    copies.append(
                        pltpu.make_async_copy(source, target.at[:, lanes], sems.at[kind, number])
                    )
                    copies[-1].start()
    wait_all(copies)


def half_rows(meta, pair, held):
    for index, value in enumerate(pair):
        held[index] = turned(value)
    parts = []
    for index in range(2):
        rows = [held[index, rows_of(meta[0] ^ (2 * part), ROWS), :] for part in range(BATCH // 2)]
        parts.append(jnp.concatenate(rows, axis=0))
    return parts


def over_both(left, right):
    return mm(left[0], right[0]) + mm(left[1], right[1])


def wait_all(copies):
    for copy in copies:
        copy.wait()


LANES = 128


def write_packed(target, value):
    full = value.shape[1] // LANES
    for index in range(full):
        target[index * TOKENS : (index + 1) * TOKENS, :] = value[
            :, index * LANES : (index + 1) * LANES
        ]
    rest = value[:, full * LANES :]
    target[full * TOKENS :, :] = jnp.concatenate([rest[:HALF], rest[HALF:]], axis=1)


def read_packed(source):
    full = source.shape[0] // TOKENS
    parts = [source[index * TOKENS : (index + 1) * TOKENS, :] for index in range(full)]
    rest = source[full * TOKENS :, :]
    parts.append(jnp.concatenate([rest[:, : LANES // 2], rest[:, LANES // 2 :]], axis=0))
    return jnp.concatenate(parts, axis=1)


def in_place(ctx, block):
    first = ctx if block == 0 else 2 * CTX - 1 - ctx
    return pl.ds(pl.multiple_of(first * HALF, HALF), HALF)


def read_vectors(meta, parts, chunks):
    for ctx, part in enumerate(parts):
        rows = [part[16 * index : 16 * (index + 1), :] for index in range(GROUP // HEAD)]
        chunks[meta[1] ^ ctx] = jnp.concatenate(rows, axis=1).astype(WIDE)
    return jnp.concatenate([chunks[index] for index in range(CTX)], axis=1)


def qkv_kernel(meta, x_ref, *refs):
    vectors, parts, refs = refs[:4], refs[4 : 4 + PARTS], refs[4 + PARTS :]
    h_ref, own, near, far, last, held, units, chunks, sems = refs
    (copies,) = load_weight(meta, parts, functools.partial(qkv_place, held), sems)
    params = read_vectors(meta, vectors, chunks)
    bias = jnp.concatenate([params[4:5], jnp.zeros((1, WIDTH), WIDE), params[5:6]], axis=1)
    centred, inverse = moments(x_ref[...].astype(WIDE))
    normed = (centred * inverse * params[0:1] + params[1:2]).astype(LOW)
    h_ref[...] = normed
    wait_all(copies)
    for chunk in range(CTX):
        mixed = mm(normed, held[chunk]) + bias[:, 3 * GROUP * chunk : 3 * GROUP * (chunk + 1)]
        mixed = mixed.astype(LOW)
        for part in range(3):
            unit = 3 * chunk + part
            units[unit % CTX, :, (unit // CTX) * GROUP : (unit // CTX + 1) * GROUP] = mixed[
                :, part * GROUP : (part + 1) * GROUP
            ]
    for ctx, target in enumerate((own, near, far, last)):
        write_packed(target, units[meta[1] ^ ctx])


def read_sequence(meta, pieces, targets):
    for ctx, piece in enumerate(pieces):
        value = read_packed(piece)
        for block in range(2):
            place = in_place(meta[1] ^ ctx, block)
            rows = value[block * HALF : (block + 1) * HALF, :]
            for index, target in enumerate(targets):
                target[place, :] = rows[:, index * GROUP : (index + 1) * GROUP]


def write_sequence(meta, pieces, sources):
    for ctx, piece in enumerate(pieces):
        parts = []
        for source in sources:
            blocks = [source[in_place(meta[1] ^ ctx, block), :] for block in range(2)]
            parts.append(jnp.concatenate(blocks, axis=0).astype(LOW))
        write_packed(piece, jnp.concatenate(parts, axis=1))


def head_mask(head, scale=1.0):
    lane = lax.broadcasted_iota(jnp.int32, (1, GROUP), 1)
    inside = (lane >= head * HEAD) & (lane < (head + 1) * HEAD)
    return jnp.where(inside, scale, 0.0).astype(LOW)


def tile_of(index):
    return slice(index * TILE, (index + 1) * TILE)


def weights_of(queries, k_seq, tile, causal):
    scores = [mt(queries, k_seq[tile_of(other), :]) for other in range(tile + 1)]
    scores[tile] = jnp.where(causal, scores[tile], -1e30)
    top = jnp.max(functools.reduce(jnp.maximum, scores), axis=-1, keepdims=True)
    expo = [jnp.exp(score - top) for score in scores]
    total = jnp.sum(functools.reduce(jnp.add, expo), axis=-1, keepdims=True)
    inverse = 1.0 / total
    return [value * inverse for value in expo]


def causal_tile():
    row = lax.broadcasted_iota(jnp.int32, (TILE, TILE), 0)
    column = lax.broadcasted_iota(jnp.int32, (TILE, TILE), 1)
    return row >= column


def attend_kernel(meta, *refs):
    pieces, results, (q_seq, k_seq, v_seq, out) = refs[:4], refs[4:8], refs[8:]
    read_sequence(meta, pieces, (q_seq, k_seq, v_seq))
    causal = causal_tile()
    scale = 1.0 / math.sqrt(HEAD)
    for tile in range(SPAN // TILE):

        def one_head(head, total, tile=tile):
            mask = head_mask(head)
            queries = q_seq[tile_of(tile), :] * head_mask(head, scale)
            weights = weights_of(queries, k_seq, tile, causal)
            for other, weight in enumerate(weights):
                total = total + mm(weight.astype(LOW), v_seq[tile_of(other), :] * mask)
            return total

        out[tile_of(tile), :] = lax.fori_loop(
            0, GROUP // HEAD, one_head, jnp.zeros((TILE, GROUP), WIDE), unroll=True
        )
    write_sequence(meta, results, (out,))


def attend_back_kernel(meta, *refs):
    pieces, grads, results = refs[:4], refs[4:8], refs[8:12]
    q_seq, k_seq, v_seq, g_seq, dq, dk, dv = refs[12:]
    read_sequence(meta, pieces, (q_seq, k_seq, v_seq))
    read_sequence(meta, grads, (g_seq,))
    causal = causal_tile()
    scale = 1.0 / math.sqrt(HEAD)
    dk[...] = jnp.zeros_like(dk)
    dv[...] = jnp.zeros_like(dv)
    for tile in range(SPAN // TILE):

        def one_head(head, total, tile=tile):
            mask = head_mask(head)
            scaled = head_mask(head, scale)
            queries = q_seq[tile_of(tile), :] * scaled
            grad = g_seq[tile_of(tile), :] * mask
            weights = weights_of(queries, k_seq, tile, causal)
            backs = [mt(grad, v_seq[tile_of(other), :]) for other in range(tile + 1)]
            products = [weight * back for weight, back in zip(weights, backs)]
            delta = jnp.sum(functools.reduce(jnp.add, products), axis=-1, keepdims=True)
            for other, (weight, back) in enumerate(zip(weights, backs)):
                step = (weight * (back - delta)).astype(LOW)
                total = total + mm(step, k_seq[tile_of(other), :] * scaled)
                dk[tile_of(other), :] += tm(step, queries)
                dv[tile_of(other), :] += tm(weight.astype(LOW), grad)
            return total

        dq[tile_of(tile), :] = lax.fori_loop(
            0, GROUP // HEAD, one_head, jnp.zeros((TILE, GROUP), WIDE), unroll=True
        )
    write_sequence(meta, results, (dq, dk, dv))


def middle_kernel(meta, x_ref, dy_ref, h_one_ref, *refs):
    vectors, pieces, parts, refs = refs[:4], refs[4:8], refs[8 : 8 + PARTS], refs[8 + PARTS :]
    (out_ref, pack_ref, mine, theirs, dmid_ref), refs = refs[:5], refs[5:]
    results, (rows_ref, dbias_ref), refs = refs[:4], refs[4:6], refs[6:]
    out_parts, held_out, held_fc, held_proj, units, total, back, chunks, bias, acts, sems = refs
    place = functools.partial(mlp_place, out_parts, held_fc, held_proj)
    copies = load_weight(meta, parts, place, sems)
    vec = read_vectors(meta, vectors, chunks)
    for chunk in range(CTX):
        bias[chunk] = vec[8 + chunk : 9 + chunk]
    for ctx, piece in enumerate(pieces):
        units[meta[1] ^ ctx] = read_packed(piece)
    att = jnp.concatenate([units[index] for index in range(CTX)], axis=1)
    pack_ref[CTX + 1] = att
    pack_ref[CTX + 3] = dy_ref[...]
    pack_ref[CTX + 4] = h_one_ref[...]
    wait_all(copies[0])
    for chunk in range(CTX):
        held_out[:, chunk * GROUP : (chunk + 1) * GROUP] = out_parts[chunk, :, :GROUP]
    mid = x_ref[...].astype(WIDE) + mm(att, held_out[...]) + vec[6:7]
    centred, inverse = moments(mid)
    normed = centred * inverse
    pack_ref[CTX] = (normed * vec[2:3] + vec[3:4]).astype(LOW)
    total[...] = mid + vec[7:8]
    back[...] = jnp.zeros_like(back)
    for group in copies[1:]:
        wait_all(group)
    side = FF_SIDE

    def chunk_step(chunk, carry):
        pre = mm(pack_ref[CTX], held_fc[chunk]) + bias[chunk]
        square = pre * pre
        tanh = jnp.tanh(0.7978845608028654 * (pre + 0.044715 * square * pre))
        act = (0.5 * pre * (1.0 + tanh)).astype(LOW)
        slope = 0.5 * (1.0 + tanh) + 0.5 * pre * (1.0 - tanh * tanh) * (
            0.7978845608028654 * (1.0 + 3.0 * 0.044715 * square)
        )
        grads = []
        for half in range(2):
            weight = held_proj[2 * chunk + half]
            part = act[:, half * side : (half + 1) * side]
            acts[2 * chunk + half] = part
            total[...] += mt(part, weight)
            grads.append(mm(dy_ref[...], weight))
        dpre = (jnp.concatenate(grads, axis=1) * slope).astype(LOW)
        pack_ref[chunk] = dpre
        dbias_ref[chunk] = jnp.sum(dpre.astype(WIDE), axis=0, keepdims=True)
        back[...] += mt(dpre, held_fc[chunk])
        return carry

    lax.fori_loop(0, CTX, chunk_step, 0)
    out_ref[...] = total[...].astype(LOW)
    core = meta[0] & 1
    for chunk in range(CTX):
        mine[chunk] = acts[2 * chunk + core]
        theirs[chunk] = acts[2 * chunk + 1 - core]
    grad = back[...]
    dy = dy_ref[...].astype(WIDE)
    dmid = dy + norm_back(grad, normed, inverse, vec[2:3])
    dmid_ref[...] = dmid
    datt = dmid.astype(LOW)
    pack_ref[CTX + 2] = datt
    rows_ref[0:1] = jnp.sum(grad * normed, axis=0, keepdims=True)
    rows_ref[1:2] = jnp.sum(grad, axis=0, keepdims=True)
    rows_ref[2:3] = jnp.sum(datt.astype(WIDE), axis=0, keepdims=True)
    rows_ref[3:4] = jnp.sum(dy, axis=0, keepdims=True)
    rows_ref[4:8] = jnp.zeros((4, WIDTH), WIDE)
    dout = mt(datt, held_out[...]).astype(LOW)
    for index in range(CTX):
        units[index] = dout[:, index * GROUP : (index + 1) * GROUP]
    for ctx, target in enumerate(results):
        write_packed(target, units[meta[1] ^ ctx])


def mlp_grad_kernel(meta, *refs):
    acts, packs, targets = refs[:2], refs[2:4], refs[4:8]
    held_out, held_fc, held_proj, turn, sems = refs[8:]
    dy = [turned(pack[CTX + 3]) for pack in packs]
    for chunk in range(CTX):
        held_proj[chunk] = over_both(dy, [act[chunk] for act in acts]).astype(LOW)
    left = half_rows(meta, [pack[CTX] for pack in packs], turn)
    for chunk in range(CTX):
        held_fc[chunk] = over_both(left, [pack[chunk] for pack in packs]).astype(LOW)
    left = half_rows(meta, [pack[CTX + 1] for pack in packs], turn)
    grad = over_both(left, [pack[CTX + 2] for pack in packs]).astype(LOW)
    for chunk in range(CTX):
        held_out[chunk, :, :GROUP] = grad[:, chunk * GROUP : (chunk + 1) * GROUP]
        held_out[chunk, :, GROUP:] = jnp.zeros((WIDTH // 2, TILE - GROUP), LOW)

    def place(part, ctx):
        ctx = meta[1] ^ ctx
        chunk = (meta[0] ^ (2 * part)) // 2
        rows = pl.ds(part * ROWS, ROWS)
        return [
            (pl.ds(WIDTH + 2 * FF_SIDE, TILE), held_out.at[ctx, rows, :]),
            (pl.ds(0, WIDTH), held_fc.at[ctx, rows, :]),
            (pl.ds(WIDTH, FF_SIDE), held_proj.at[chunk, rows_of(2 * ctx, ROWS), :]),
            (pl.ds(WIDTH + FF_SIDE, FF_SIDE), held_proj.at[chunk, rows_of(2 * ctx + 1, ROWS), :]),
        ]

    store_grad(place, targets, sems)


def qkv_grad_kernel(meta, *refs):
    pack, own, came, targets = refs[:2], refs[2:4], refs[4:6], refs[6:10]
    mixed_ref, dbias_ref, held, units, turn, sems = refs[10:]
    for core in range(2):
        for ctx in range(CTX):
            value = read_packed(own[core] if ctx == 0 else came[core].at[ctx - 1])
            for part in range(3):
                units[core, CTX * part + (meta[1] ^ ctx)] = value[
                    :, part * GROUP : (part + 1) * GROUP
                ]
    left = half_rows(meta, [pack[0][...], pack[1][...]], turn)
    for chunk in range(CTX):
        mixed = [
            jnp.concatenate([units[core, 3 * chunk + part] for part in range(3)], axis=1)
            for core in range(2)
        ]
        mixed_ref[chunk] = mixed[0]
        bias = jnp.sum(mixed[0].astype(WIDE), axis=0, keepdims=True)
        for part in range(3):
            dbias_ref[3 * chunk + part] = bias[:, part * GROUP : (part + 1) * GROUP]
        held[chunk] = over_both(left, mixed).astype(LOW)

    def place(part, ctx):
        return [(pl.ds(0, 3 * GROUP), held.at[meta[1] ^ ctx, pl.ds(part * ROWS, ROWS), :])]

    store_grad(place, targets, sems)


def input_grad_kernel(meta, x_ref, dmid_ref, mixed_ref, rows_ref, dfc_ref, dqkv_ref, *refs):
    vectors, parts, refs = refs[:4], refs[4 : 4 + PARTS], refs[4 + PARTS :]
    grad_ref, results, (held, chunks, rows, sums, sems) = refs[0], refs[1:5], refs[5:]
    (copies,) = load_weight(meta, parts, functools.partial(qkv_place, held), sems)
    params = read_vectors(meta, vectors, chunks)
    centred, inverse = moments(x_ref[...].astype(WIDE))
    normed = centred * inverse
    wait_all(copies)
    grad = jnp.zeros((TOKENS, WIDTH), WIDE)
    for chunk in range(CTX):
        grad = grad + mt(mixed_ref[chunk], held[chunk])
    grad_ref[...] = dmid_ref[...] + norm_back(grad, normed, inverse, params[0:1])
    rows[0:1] = jnp.sum(grad * normed, axis=0, keepdims=True)
    rows[1:2] = jnp.sum(grad, axis=0, keepdims=True)
    rows[2:4] = rows_ref[0:2]
    for chunk in range(CTX):
        lanes = slice(chunk * GROUP, (chunk + 1) * GROUP)
        rows[4:5, lanes] = dqkv_ref[chunk]
        rows[5:6, lanes] = dqkv_ref[2 * CTX + chunk]
        rows[8 + chunk : 9 + chunk] = dfc_ref[chunk]
    rows[6:8] = rows_ref[2:4]
    rows[12:16] = jnp.zeros((4, WIDTH), WIDE)
    for chunk in range(CTX):
        sums[chunk] = rows[:, chunk * GROUP : (chunk + 1) * GROUP]
    for ctx, target in enumerate(results):
        target[...] = sums[meta[1] ^ ctx]


def sum_kernel(one_kept, one_back, two_kept, two_back, one_keep, one_send, two_keep, two_send):
    pairs = ((one_kept, one_back, one_keep, one_send), (two_kept, two_back, two_keep, two_send))
    for kept, back, keep, send in pairs:
        keep[...] = kept[0].astype(WIDE) + back[0].astype(WIDE)
        send[...] = (kept[1].astype(WIDE) + back[1].astype(WIDE)).astype(LOW)


def near_kernel(one_kept, one_back, two_kept, two_back, one_keep, two_send):
    one_keep[...] = one_kept[...] + one_back[...].astype(WIDE)
    two_send[...] = (two_kept[...] + two_back[...].astype(WIDE)).astype(LOW)


def shape_of(dtype, *dims):
    return jax.ShapeDtypeStruct(dims, dtype)


def call(kernel, arguments, kinds, outputs, out_kinds, scratch, moved=1):
    spec = {
        "v": pl.BlockSpec(memory_space=pltpu.VMEM),
        "s": pl.BlockSpec(memory_space=pltpu.SMEM),
        "a": pl.BlockSpec(memory_space=pl.ANY),
        "h": pl.BlockSpec((None, TOKENS, WIDTH), lambda step: (CTX + 4, 0, 0)),
    }
    return pl.pallas_call(
        kernel,
        grid=(1,),
        out_shape=tuple(outputs),
        in_specs=[spec[kind] for kind in kinds],
        out_specs=tuple(spec[kind] for kind in out_kinds),
        scratch_shapes=scratch,
        cost_estimate=pl.CostEstimate(flops=1, bytes_accessed=moved, transcendentals=0),
        compiler_params=pltpu.CompilerParams(vmem_limit_bytes=VMEM_LIMIT),
    )(*arguments)


def local_fast(
    block_in,
    cotangent,
    w_qkv,
    w_out,
    w_fc,
    w_proj,
    vectors,
    qkv_first,
    qkv_second,
    out_first,
    out_second,
    fc_first,
    fc_second,
    proj_first,
    proj_second,
    vec_first,
    vec_second,
):
    batch, ctx = lax.axis_index("batch"), lax.axis_index("ctx")
    meta = jnp.stack([batch, ctx]).astype(jnp.int32)
    inputs = block_in.reshape(TOKENS, WIDTH)
    grad_low = cotangent.reshape(TOKENS, WIDTH)
    tie = lax.optimization_barrier

    qkv_sems = pltpu.SemaphoreType.DMA((1, BATCH * CTX))
    mlp_sems = pltpu.SemaphoreType.DMA((4, BATCH * CTX))
    qkv_held = pltpu.VMEM((CTX, WIDTH, 3 * GROUP), LOW)
    vec_held = pltpu.VMEM((CTX, 16, GROUP), WIDE)

    low_vec = jnp.pad(vectors.astype(LOW), ((0, 4), (0, 0)))
    low_vec = [low_vec[:, start : start + HEAD] for start in range(0, GROUP, HEAD)]
    low_vec = jnp.concatenate(low_vec + [jnp.zeros((ROWS - 48, HEAD), LOW)], axis=0)
    piece_one = jnp.concatenate([w_qkv.astype(LOW), low_vec], axis=1)
    low_proj = w_proj.astype(LOW).T
    piece_two = jnp.concatenate(
        [
            w_fc.astype(LOW),
            low_proj[:ROWS],
            low_proj[ROWS:],
            w_out.astype(LOW),
            jnp.zeros((ROWS, TILE - GROUP), LOW),
        ],
        axis=1,
    )
    near = jnp.stack([piece_one, swap(piece_one, "ctx", 2)])
    far = swap(near, "ctx", 1)
    vec_parts = [part[:48, 3 * GROUP :] for part in (near[0], far[0], near[1], far[1])]
    own_one = jnp.concatenate([near, far], axis=0)[:, :, : 3 * GROUP]
    piece_two, late_vec = tie((piece_two, vec_parts))
    far = swap(piece_two, "ctx", 2)
    x_one, y_one = gather_first(own_one)
    across_one = gather_second(x_one, y_one)
    far, across_one = tie((far, across_one))
    near = jnp.stack([piece_two, far])
    far = swap(near, "ctx", 1)
    parts_one = [own_one, x_one, y_one, *across_one]
    parts_one = parts_one + to_core(parts_one)

    packed = shape_of(LOW, TOKENS * 3 * GROUP // LANES, LANES)
    single = shape_of(LOW, TOKENS * GROUP // LANES, LANES)
    tokens_low = shape_of(LOW, TOKENS, WIDTH)
    hidden_low = shape_of(LOW, CTX, TOKENS, WIDTH)
    h_one, own, *sent = call(
        qkv_kernel,
        (meta, inputs, *vec_parts, *parts_one),
        "s" + "v" * 5 + "a" * PARTS,
        [tokens_low] + [packed] * 4,
        "v" * 5,
        [qkv_held, pltpu.VMEM((CTX, TOKENS, 3 * GROUP), LOW), vec_held, qkv_sems],
    )
    qkv_pieces = [own] + [swap(part, "ctx", bit) for bit, part in zip((1, 2, 3), sent)]

    far, late_h = tie((far, h_one))
    own_two = jnp.concatenate([near, far], axis=0)
    x_two, y_two = gather_first(own_two)
    qkv_pieces, x_two, y_two = tie((qkv_pieces, x_two, y_two))
    across_two = gather_second(x_two, y_two)
    parts_two = [own_two, x_two, y_two]
    swapped_two = to_core(parts_two)

    sequence_low = pltpu.VMEM((SPAN, GROUP), LOW)
    sequence_wide = pltpu.VMEM((SPAN, GROUP), WIDE)
    own, *sent = call(
        attend_kernel,
        (meta, *qkv_pieces),
        "s" + "v" * 4,
        [single] * 4,
        "v" * 4,
        [sequence_low] * 3 + [sequence_wide],
    )
    sent, swapped_two = tie((sent, swapped_two))
    att_pieces = [own] + [swap(part, "ctx", bit) for bit, part in zip((1, 2, 3), sent)]
    across_two, att_pieces = tie((across_two, att_pieces))
    parts_two = parts_two + list(across_two) + swapped_two + to_core(across_two)

    pack_shape = shape_of(LOW, CTX + 5, TOKENS, WIDTH)
    act_shape = shape_of(LOW, BATCH // 2, TOKENS, FF_SIDE)
    out, pack, act_mine, act_theirs, dmid, own, *sent = call(
        middle_kernel,
        (meta, inputs, grad_low, late_h, *vec_parts, *att_pieces, *parts_two),
        "s" + "v" * 11 + "a" * PARTS,
        [tokens_low, pack_shape, act_shape, act_shape, shape_of(WIDE, TOKENS, WIDTH)]
        + [single] * 4
        + [shape_of(WIDE, 8, WIDTH), shape_of(WIDE, CTX, 1, WIDTH)],
        "v" * 11,
        [
            pltpu.VMEM((CTX, WIDTH, TILE), LOW),
            pltpu.VMEM((WIDTH, WIDTH), LOW),
            pltpu.VMEM((CTX, WIDTH, WIDTH), LOW),
            pltpu.VMEM((BATCH, WIDTH, FF_SIDE), LOW),
            pltpu.VMEM((CTX, TOKENS, GROUP), LOW),
            pltpu.VMEM((TOKENS, WIDTH), WIDE),
            pltpu.VMEM((TOKENS, WIDTH), WIDE),
            vec_held,
            pltpu.VMEM((CTX, 1, WIDTH), WIDE),
            pltpu.VMEM((BATCH, TOKENS, FF_SIDE), LOW),
            mlp_sems,
        ],
    )
    sent, (rows_two, dbias_fc) = sent[:3], sent[3:]
    grad_pieces = [own] + [swap(part, "ctx", bit) for bit, part in zip((1, 2, 3), sent)]
    act_came, pack_came = swap(act_theirs, "batch", CORE), swap(pack, "batch", CORE)

    half_sems = BATCH * CTX // 2
    turn_held = pltpu.VMEM((2, WIDTH, TOKENS), LOW)
    mlp_parts = call(
        mlp_grad_kernel,
        (meta, act_mine, act_came, pack, pack_came),
        "s" + "v" * 4,
        [shape_of(LOW, 2, 2, ROWS, MLP)] * 4,
        "aaaa",
        [
            pltpu.VMEM((CTX, WIDTH // 2, TILE), LOW),
            pltpu.VMEM((CTX, WIDTH // 2, WIDTH), LOW),
            pltpu.VMEM((BATCH // 2, WIDTH, FF_SIDE), LOW),
            turn_held,
            pltpu.SemaphoreType.DMA((4, half_sems)),
        ],
    )
    mlp_parts, grad_pieces = tie((mlp_parts, grad_pieces))
    mlp_kept = mlp_parts[0], mlp_parts[2]
    mlp_back = swap_pair((mlp_parts[1], mlp_parts[3]), YBIT, XBIT)
    own, *sent = call(
        attend_back_kernel,
        (meta, *qkv_pieces, *grad_pieces),
        "s" + "v" * 8,
        [packed] * 4,
        "v" * 4,
        [sequence_low] * 4 + [sequence_wide] * 3,
    )
    own_came = swap(own, "batch", CORE)
    received = [swap(part, "ctx", bit) for bit, part in zip((1, 2, 3), sent)]
    mlp_back, received[0] = tie((mlp_back, received[0]))
    pair = [shape_of(WIDE, 2, ROWS, MLP), shape_of(LOW, 2, ROWS, MLP)]
    one_keep, one_send, two_keep, two_send = call(
        sum_kernel,
        (mlp_kept[0], mlp_back[0], mlp_kept[1], mlp_back[1]),
        "vvvv",
        pair + pair,
        "vvvv",
        [],
    )
    one_keep, received[1], received[2] = tie((one_keep, received[1], received[2]))
    mlp_back = swap_pair((one_send, two_send), XBIT, YBIT)
    received = jnp.stack(received)
    received_came = swap(received, "batch", CORE)

    *qkv_parts, mixed, dbias_qkv = call(
        qkv_grad_kernel,
        (meta, pack, pack_came, own, own_came, received, received_came),
        "shhvvvv",
        [shape_of(LOW, 2, 2, ROWS, 3 * GROUP)] * 4
        + [shape_of(LOW, CTX, TOKENS, 3 * GROUP), shape_of(WIDE, 3 * CTX, 1, GROUP)],
        "aaaavv",
        [
            pltpu.VMEM((CTX, WIDTH // 2, 3 * GROUP), LOW),
            pltpu.VMEM((2, 3 * CTX, TOKENS, GROUP), LOW),
            turn_held,
            pltpu.SemaphoreType.DMA((1, half_sems)),
        ],
    )
    qkv_kept = qkv_parts[0], qkv_parts[2]
    qkv_kept = qkv_parts[0], qkv_parts[2]
    qkv_back = swap_pair((qkv_parts[1], qkv_parts[3]), YBIT, XBIT)
    grad_input, own, *sent = call(
        input_grad_kernel,
        (meta, inputs, dmid, mixed, rows_two, dbias_fc, dbias_qkv, *late_vec, *parts_one),
        "s" + "v" * 10 + "a" * PARTS,
        [shape_of(WIDE, TOKENS, WIDTH)] + [shape_of(WIDE, 16, GROUP)] * 4,
        "v" * 5,
        [qkv_held, vec_held, pltpu.VMEM((16, WIDTH), WIDE), vec_held, qkv_sems],
        moved=40_000_000,
    )
    mlp_back, own, sent = tie((mlp_back, own, sent))
    mlp_one, mlp_two = call(
        near_kernel, (one_keep, mlp_back[0], two_keep, mlp_back[1]), "vvvv", pair, "vv", []
    )
    mlp_two = swap(mlp_two, "ctx", 1)
    qkv_kept, qkv_sent = scatter_second(qkv_kept, qkv_back)
    qkv_sent, own, sent = tie((qkv_sent, own, sent))
    qkv_back = swap_pair(qkv_sent, XBIT, YBIT)
    vec_grad = own + sum(swap(part, "ctx", bit) for bit, part in zip((1, 2, 3), sent))
    qkv_back, mlp_two, vec_grad = tie((qkv_back, mlp_two, vec_grad))
    qkv_one, qkv_two = scatter_near(qkv_kept, qkv_back)
    mlp_grad = scatter_far(mlp_one, mlp_two)
    vec_grad = vec_grad + swap(vec_grad, "batch", CORE)
    qkv_two, vec_grad = tie((qkv_two, vec_grad))
    qkv_grad = scatter_far(qkv_one, qkv_two)
    for bit in (XBIT, YBIT):
        vec_grad = vec_grad + swap(vec_grad, "batch", bit)
    vec_grad = vec_grad[:12]
    fc_grad = mlp_grad[:, :WIDTH]
    proj_grad = jnp.concatenate(
        [mlp_grad[:, WIDTH : WIDTH + FF_SIDE], mlp_grad[:, WIDTH + FF_SIDE : WIDTH + 2 * FF_SIDE]],
        axis=0,
    )
    out_grad = mlp_grad[:, WIDTH + 2 * FF_SIDE : WIDTH + 2 * FF_SIDE + GROUP]

    qkv_m, qkv_s, qkv_w = adamw(w_qkv, qkv_grad, qkv_first, qkv_second, 0.06, 0.1)
    out_m, out_s, out_w = adamw(w_out, out_grad, out_first, out_second, 0.06, 0.1)
    fc_m, fc_s, fc_w = adamw(w_fc, fc_grad, fc_first, fc_second, 0.06, 0.1)
    proj_m, proj_s, proj_w = adamw(w_proj, proj_grad.T, proj_first, proj_second, 0.06, 0.1)
    vec_m, vec_s, vec_w = adamw(vectors, vec_grad, vec_first, vec_second, 0.2, 0.0)
    return (
        out.reshape(block_in.shape),
        grad_input.reshape(block_in.shape),
        qkv_m,
        qkv_s,
        qkv_w,
        out_m,
        out_s,
        out_w,
        fc_m,
        fc_s,
        fc_w,
        proj_m,
        proj_s,
        proj_w,
        vec_m,
        vec_s,
        vec_w,
    )


def solution(mesh):
    in_specs = (
        P("batch", "ctx", None, None),
        P("batch", "ctx", None, None),
        P("batch", "ctx"),
        P("batch", "ctx"),
        P("batch", "ctx"),
        P("batch", "ctx"),
        P(None, "ctx"),
        P("batch", "ctx"),
        P("batch", "ctx"),
        P("batch", "ctx"),
        P("batch", "ctx"),
        P("batch", "ctx"),
        P("batch", "ctx"),
        P("batch", "ctx"),
        P("batch", "ctx"),
        P(None, "ctx"),
        P(None, "ctx"),
    )
    out_specs = (
        P("batch", "ctx", None, None),
        P("batch", "ctx", None, None),
        P("batch", "ctx"),
        P("batch", "ctx"),
        P("batch", "ctx"),
        P("batch", "ctx"),
        P("batch", "ctx"),
        P("batch", "ctx"),
        P("batch", "ctx"),
        P("batch", "ctx"),
        P("batch", "ctx"),
        P("batch", "ctx"),
        P("batch", "ctx"),
        P("batch", "ctx"),
        P(None, "ctx"),
        P(None, "ctx"),
        P(None, "ctx"),
    )
    sizes = (mesh.shape["batch"], mesh.shape["ctx"])
    local = local_fast if sizes == (BATCH, CTX) else local_any
    return jax.shard_map(local, mesh=mesh, in_specs=in_specs, out_specs=out_specs, check_vma=False)
```

```python
import functools
import math

import jax
import jax.numpy as jnp
from jax import lax
from jax.experimental import pallas as pl
from jax.experimental.pallas import tpu as pltpu
from jax.sharding import PartitionSpec as P

HEADS = 12
STEP = 10


def layer_norm(value, gain, shift):
    mean = jnp.mean(value, axis=-1, keepdims=True)
    centred = value - mean
    spread = jnp.mean(centred * centred, axis=-1, keepdims=True)
    return centred * lax.rsqrt(spread + 1e-05) * gain + shift


def gelu_tanh(value):
    return (
        0.5
        * value
        * (1.0 + jnp.tanh(0.7978845608028654 * (value + 0.044715 * value * value * value)))
    )


def block_places(index, count, half):
    offsets = jnp.arange(half, dtype=jnp.int32)
    first = index * half + offsets
    second = (2 * count - 1 - index) * half + offsets
    return jnp.concatenate([first, second])


def scores_of(queries, keys, scale, allowed):
    raw = jnp.einsum("sqhd,skhd->shqk", queries, keys, preferred_element_type=jnp.float32) * scale
    return jnp.where(allowed[None, None], raw, -1e30)


def pair_grads(queries, grads, keys, values, top, total, delta, scale, allowed):
    score = scores_of(queries, keys, scale, allowed)
    weights = jnp.exp(score - top[..., None]) / total[..., None]
    back_weights = jnp.einsum("sqhd,skhd->shqk", grads, values, preferred_element_type=jnp.float32)
    grad_score = (weights * (back_weights - delta[..., None])).astype(jnp.bfloat16)
    return (weights.astype(jnp.bfloat16), grad_score)


def rows_product(left, right):
    return jnp.einsum("ra,rb->ab", left, right, preferred_element_type=jnp.float32)


def back_product(grad, weight):
    return jnp.einsum("rb,ab->ra", grad, weight, preferred_element_type=jnp.float32)


def adamw(weight, grad, first, second, rate, decay):
    first = 0.9 * first + 0.1 * grad
    second = 0.999 * second + 0.001 * grad * grad
    first_hat = first / (1.0 - 0.9**STEP)
    second_hat = second / (1.0 - 0.999**STEP)
    weight = weight - rate * (first_hat / (jnp.sqrt(second_hat) + 1e-08) + decay * weight)
    return (first, second, weight)


def local_any(
    block_in,
    cotangent,
    w_qkv,
    w_out,
    w_fc,
    w_proj,
    vectors,
    qkv_first,
    qkv_second,
    out_first,
    out_second,
    fc_first,
    fc_second,
    proj_first,
    proj_second,
    vec_first,
    vec_second,
):
    low_type = jnp.bfloat16
    wide = jnp.float32
    row_parts = (
        lax.all_gather(w_qkv.astype(low_type), "batch", axis=0, tiled=True),
        lax.all_gather(w_out.astype(low_type), "batch", axis=0, tiled=True),
        lax.all_gather(w_fc.astype(low_type), "batch", axis=0, tiled=True),
        lax.all_gather(w_proj.astype(low_type), "batch", axis=0, tiled=True),
    )
    full_qkv, full_out, full_fc, full_proj, full_vec = (
        lax.all_gather(row_parts[0], "ctx", axis=1, tiled=True),
        lax.all_gather(row_parts[1], "ctx", axis=1, tiled=True),
        lax.all_gather(row_parts[2], "ctx", axis=1, tiled=True),
        lax.all_gather(row_parts[3], "ctx", axis=1, tiled=True),
        lax.all_gather(vectors.astype(low_type), "ctx", axis=1, tiled=True),
    )
    params = full_vec.astype(wide)
    seqs, pair, half, width = block_in.shape
    heads = HEADS
    head = width // heads
    rows = seqs * pair * half
    span = pair * half
    count = lax.axis_size("ctx")
    index = lax.axis_index("ctx")
    scale = 1.0 / math.sqrt(head)
    inputs = block_in.astype(wide).reshape(rows, width)
    normed_one = layer_norm(inputs, params[0], params[1]).astype(low_type)
    mixed = jnp.dot(normed_one, full_qkv, preferred_element_type=wide)
    queries = (mixed[:, :width] + params[4]).astype(low_type)
    keys = mixed[:, width : 2 * width].astype(low_type)
    values = (mixed[:, 2 * width :] + params[5]).astype(low_type)
    key_all, value_all = (
        lax.all_gather(keys.reshape(seqs, pair, half, width), "ctx", axis=1, tiled=True),
        lax.all_gather(values.reshape(seqs, pair, half, width), "ctx", axis=1, tiled=True),
    )
    query_heads = queries.reshape(seqs, span, heads, head)
    own_places = block_places(index, count, half)

    def piece_of(source, piece):
        return lax.dynamic_slice_in_dim(source, 2 * piece, 2, 1).reshape(seqs, span, heads, head)

    def allowed_for(piece):
        return own_places[:, None] >= block_places(piece, count, half)[None, :]

    def stats_step(piece, carry):
        top, total = carry
        score = scores_of(query_heads, piece_of(key_all, piece), scale, allowed_for(piece))
        new_top = jnp.maximum(top, jnp.max(score, axis=-1))
        total = total * jnp.exp(top - new_top) + jnp.sum(
            jnp.exp(score - new_top[..., None]), axis=-1
        )
        return (new_top, total)

    start_stats = (jnp.full((seqs, heads, span), -1e30, wide), jnp.zeros((seqs, heads, span), wide))
    top, total = lax.fori_loop(0, count, stats_step, start_stats)

    def output_step(piece, acc):
        score = scores_of(query_heads, piece_of(key_all, piece), scale, allowed_for(piece))
        weights = (jnp.exp(score - top[..., None]) / total[..., None]).astype(low_type)
        return acc + jnp.einsum(
            "shqk,skhd->sqhd", weights, piece_of(value_all, piece), preferred_element_type=wide
        )

    attended = lax.fori_loop(0, count, output_step, jnp.zeros((seqs, span, heads, head), wide))
    att_low = attended.reshape(rows, width).astype(low_type)
    mid = inputs + jnp.dot(att_low, full_out, preferred_element_type=wide) + params[6]
    normed_two = layer_norm(mid, params[2], params[3]).astype(low_type)
    pre = jnp.dot(normed_two, full_fc, preferred_element_type=wide) + params[8:12].reshape(-1)
    act_low = gelu_tanh(pre).astype(low_type)
    result = mid + jnp.dot(act_low, full_proj, preferred_element_type=wide) + params[7]
    out_block = result.astype(low_type).reshape(block_in.shape)
    grad_low = cotangent.reshape(rows, width)
    grad_out = grad_low.astype(wide)
    grad_wproj = rows_product(act_low, grad_low)
    back_act = back_product(grad_low, full_proj)
    grad_pre = jax.vjp(gelu_tanh, pre)[1](back_act)[0].astype(low_type)
    grad_wfc = rows_product(normed_two, grad_pre)
    back_two = back_product(grad_pre, full_fc)
    back_mid, grad_gain_two, grad_shift_two = jax.vjp(layer_norm, mid, params[2], params[3])[1](
        back_two
    )
    grad_mid = grad_out + back_mid
    grad_att_low = grad_mid.astype(low_type)
    grad_wout = rows_product(att_low, grad_att_low)
    back_att = back_product(grad_att_low, full_out)
    grad_heads = back_att.astype(low_type).reshape(seqs, span, heads, head)
    delta = jnp.einsum("sqhd,sqhd->shq", grad_heads.astype(wide), attended)
    query_all, grad_all = (
        lax.all_gather(queries.reshape(seqs, pair, half, width), "ctx", axis=1, tiled=True),
        lax.all_gather(grad_heads.reshape(seqs, pair, half, width), "ctx", axis=1, tiled=True),
    )
    top_all, total_all, delta_all = (
        lax.all_gather(top.reshape(seqs, heads, pair, half), "ctx", axis=2, tiled=True),
        lax.all_gather(total.reshape(seqs, heads, pair, half), "ctx", axis=2, tiled=True),
        lax.all_gather(delta.reshape(seqs, heads, pair, half), "ctx", axis=2, tiled=True),
    )

    def query_step(piece, grad_query):
        key_part = piece_of(key_all, piece)
        value_part = piece_of(value_all, piece)
        weights_low, grad_score = pair_grads(
            query_heads,
            grad_heads,
            key_part,
            value_part,
            top,
            total,
            delta,
            scale,
            allowed_for(piece),
        )
        return grad_query + jnp.einsum(
            "shqk,skhd->sqhd", grad_score, key_part, preferred_element_type=wide
        )

    grad_query = lax.fori_loop(0, count, query_step, jnp.zeros((seqs, span, heads, head), wide))
    key_heads = keys.reshape(seqs, span, heads, head)
    value_heads = values.reshape(seqs, span, heads, head)

    def stat_piece(source, piece):
        return lax.dynamic_slice_in_dim(source, 2 * piece, 2, 2).reshape(seqs, heads, span)

    def key_step(piece, carry):
        grad_key, grad_value = carry
        query_part = piece_of(query_all, piece)
        grad_part = piece_of(grad_all, piece)
        allowed = block_places(piece, count, half)[:, None] >= own_places[None, :]
        weights_low, grad_score = pair_grads(
            query_part,
            grad_part,
            key_heads,
            value_heads,
            stat_piece(top_all, piece),
            stat_piece(total_all, piece),
            stat_piece(delta_all, piece),
            scale,
            allowed,
        )
        grad_key = grad_key + jnp.einsum(
            "shqk,sqhd->skhd", grad_score, query_part, preferred_element_type=wide
        )
        grad_value = grad_value + jnp.einsum(
            "shqk,sqhd->skhd", weights_low, grad_part, preferred_element_type=wide
        )
        return (grad_key, grad_value)

    start_keys = (
        jnp.zeros((seqs, span, heads, head), wide),
        jnp.zeros((seqs, span, heads, head), wide),
    )
    grad_key, grad_value = lax.fori_loop(0, count, key_step, start_keys)
    grad_keys = (grad_key * scale).reshape(seqs, pair, half, width)
    grad_values = grad_value.reshape(seqs, pair, half, width)
    grad_q_low = (grad_query * scale).reshape(rows, width).astype(low_type)
    grad_k_low = grad_keys.reshape(rows, width).astype(low_type)
    grad_v_low = grad_values.reshape(rows, width).astype(low_type)
    grad_mixed = jnp.concatenate([grad_q_low, grad_k_low, grad_v_low], axis=1)
    grad_wqkv = rows_product(normed_one, grad_mixed)
    back_one = back_product(grad_mixed, full_qkv)
    back_in, grad_gain_one, grad_shift_one = jax.vjp(layer_norm, inputs, params[0], params[1])[1](
        back_one
    )
    grad_input = (grad_mid + back_in).reshape(block_in.shape)
    grad_bias_q = jnp.sum(grad_q_low.astype(wide), axis=0)
    grad_bias_v = jnp.sum(grad_v_low.astype(wide), axis=0)
    grad_bias_out = jnp.sum(grad_att_low.astype(wide), axis=0)
    grad_bias_proj = jnp.sum(grad_out, axis=0)
    grad_bias_fc = jnp.sum(grad_pre.astype(wide), axis=0).reshape(4, width)
    small_rows = jnp.stack(
        [
            grad_gain_one,
            grad_shift_one,
            grad_gain_two,
            grad_shift_two,
            grad_bias_q,
            grad_bias_v,
            grad_bias_out,
            grad_bias_proj,
        ]
    )
    grad_vectors = jnp.concatenate([small_rows, grad_bias_fc], axis=0)
    col_sums = (
        lax.psum_scatter(grad_wqkv, "ctx", scatter_dimension=1, tiled=True),
        lax.psum_scatter(grad_wout, "ctx", scatter_dimension=1, tiled=True),
        lax.psum_scatter(grad_wfc, "ctx", scatter_dimension=1, tiled=True),
        lax.psum_scatter(grad_wproj, "ctx", scatter_dimension=1, tiled=True),
        lax.psum_scatter(grad_vectors, "ctx", scatter_dimension=1, tiled=True),
    )
    qkv_grad, out_grad, fc_grad, proj_grad = (
        lax.psum_scatter(col_sums[0], "batch", scatter_dimension=0, tiled=True),
        lax.psum_scatter(col_sums[1], "batch", scatter_dimension=0, tiled=True),
        lax.psum_scatter(col_sums[2], "batch", scatter_dimension=0, tiled=True),
        lax.psum_scatter(col_sums[3], "batch", scatter_dimension=0, tiled=True),
    )
    vec_grad = lax.psum(col_sums[4], "batch")
    qkv_m, qkv_s, qkv_w = adamw(w_qkv, qkv_grad, qkv_first, qkv_second, 0.06, 0.1)
    out_m, out_s, out_w = adamw(w_out, out_grad, out_first, out_second, 0.06, 0.1)
    fc_m, fc_s, fc_w = adamw(w_fc, fc_grad, fc_first, fc_second, 0.06, 0.1)
    proj_m, proj_s, proj_w = adamw(w_proj, proj_grad, proj_first, proj_second, 0.06, 0.1)
    vec_m, vec_s, vec_w = adamw(vectors, vec_grad, vec_first, vec_second, 0.2, 0.0)
    return (
        out_block,
        grad_input,
        qkv_m,
        qkv_s,
        qkv_w,
        out_m,
        out_s,
        out_w,
        fc_m,
        fc_s,
        fc_w,
        proj_m,
        proj_s,
        proj_w,
        vec_m,
        vec_s,
        vec_w,
    )


BATCH = 8
CTX = 4
WIDTH = 768
HEAD = 64
GROUP = WIDTH // CTX
TOKENS = 256
HALF = 128
FF_SIDE = 384
ROWS = WIDTH // BATCH
MLP = WIDTH + 2 * FF_SIDE + 256
SPAN = TOKENS * CTX
TILE = 256
LOW = jnp.bfloat16
WIDE = jnp.float32
CORE, XBIT, YBIT = 1, 2, 4
PLACES = (0, 2, 1, 3)
SOURCES = (
    (0, PLACES),
    (XBIT, PLACES),
    (YBIT, PLACES),
    (XBIT + YBIT, PLACES[:2]),
    (XBIT + YBIT, PLACES[2:]),
    (CORE, PLACES),
    (CORE + XBIT, PLACES),
    (CORE + YBIT, PLACES),
    (CORE + XBIT + YBIT, PLACES[:2]),
    (CORE + XBIT + YBIT, PLACES[2:]),
)
PARTS = len(SOURCES)
VMEM_LIMIT = 56 * 1024 * 1024


def swap(value, axis, bit):
    size = BATCH if axis == "batch" else CTX
    return lax.ppermute(value, axis, [(i, i ^ bit) for i in range(size)])


def mm(left, right):
    return lax.dot_general(left, right, (((1,), (0,)), ((), ())), preferred_element_type=WIDE)


def mt(left, right):
    return lax.dot_general(left, right, (((1,), (1,)), ((), ())), preferred_element_type=WIDE)


def tm(left, right):
    return lax.dot_general(left, right, (((0,), (0,)), ((), ())), preferred_element_type=WIDE)


def turned(value):
    return value.astype(WIDE).T.astype(LOW)


def moments(value):
    mean = jnp.mean(value, axis=-1, keepdims=True)
    centred = value - mean
    spread = jnp.mean(centred * centred, axis=-1, keepdims=True)
    return centred, lax.rsqrt(spread + 1e-05)


def norm_back(grad, normed, inverse, gain):
    part = grad * gain
    mean = jnp.mean(part, axis=-1, keepdims=True)
    cross = jnp.mean(part * normed, axis=-1, keepdims=True)
    return inverse * (part - mean - normed * cross)


def gather_first(own):
    return swap(own, "batch", XBIT), swap(own, "batch", YBIT)


def gather_second(from_x, from_y):
    return swap(from_x[:2], "batch", YBIT), swap(from_y[2:], "batch", XBIT)


def to_core(parts):
    return [swap(part, "batch", CORE) for part in parts]


def swap_pair(pair, first, second):
    return swap(pair[0], "batch", first), swap(pair[1], "batch", second)


def scatter_second(kept, back):
    one = kept[0].astype(WIDE) + back[0].astype(WIDE)
    two = kept[1].astype(WIDE) + back[1].astype(WIDE)
    return (one[0], two[0]), (one[1].astype(LOW), two[1].astype(LOW))


def scatter_near(kept, back):
    one = kept[0].astype(WIDE) + back[0].astype(WIDE)
    two = (kept[1].astype(WIDE) + back[1].astype(WIDE)).astype(LOW)
    return one, swap(two, "ctx", 1)


def scatter_far(one, two):
    one = one + two.astype(WIDE)
    return one[0] + swap(one[1].astype(LOW), "ctx", 2).astype(WIDE)


def rows_of(index, size):
    return pl.ds(pl.multiple_of(index * size, 16), size)


def qkv_place(held, batch, ctx):
    return [(pl.ds(0, 3 * GROUP), held.at[ctx, rows_of(batch, ROWS), :])]


def mlp_place(held_out, held_fc, held_proj, batch, ctx):
    return [
        (pl.ds(WIDTH + 2 * FF_SIDE, TILE), held_out.at[ctx, rows_of(batch, ROWS), :]),
        (pl.ds(0, WIDTH), held_fc.at[ctx, rows_of(batch, ROWS), :]),
        (pl.ds(WIDTH, FF_SIDE), held_proj.at[batch, rows_of(2 * ctx, ROWS), :]),
        (pl.ds(WIDTH + FF_SIDE, FF_SIDE), held_proj.at[batch, rows_of(2 * ctx + 1, ROWS), :]),
    ]


def load_weight(meta, parts, place, sems):
    copies = []
    for part, (source, places) in zip(parts, SOURCES):
        for index, ctx in enumerate(places):
            ranges = place(meta[0] ^ source, meta[1] ^ ctx)
            copies.append([(part.at[index, :, lanes], target) for lanes, target in ranges])
    started = []
    for kind in range(len(copies[0])):
        group = []
        for number, copy in enumerate(copies):
            group.append(pltpu.make_async_copy(*copy[kind], sems.at[kind, number]))
            group[-1].start()
        started.append(group)
    return started


def store_grad(held, targets, sems, kinds):
    one_kept, one_sent, two_kept, two_sent = targets
    copies = []
    for y in range(2):
        for x in range(2):
            for index, ctx in enumerate(PLACES):
                if index < 2:
                    target = (one_sent if y else one_kept).at[x, index]
                else:
                    target = (two_sent if x else two_kept).at[y, index - 2]
                ranges = held(2 * y + x, ctx)
                for kind in kinds:
                    lanes, source = ranges[kind]
                    number = (2 * y + x) * CTX + ctx
                    copies.append(
                        pltpu.make_async_copy(source, target.at[:, lanes], sems.at[kind, number])
                    )
                    copies[-1].start()
    return copies


def half_rows(meta, pair, held):
    for index, value in enumerate(pair):
        held[index] = turned(value)
    parts = []
    for index in range(2):
        rows = [held[index, rows_of(meta[0] ^ (2 * part), ROWS), :] for part in range(BATCH // 2)]
        parts.append(jnp.concatenate(rows, axis=0))
    return parts


def over_both(left, right):
    return mm(left[0], right[0]) + mm(left[1], right[1])


def wait_all(copies):
    for copy in copies:
        copy.wait()


LANES = 128


def write_packed(target, value):
    full = value.shape[1] // LANES
    for index in range(full):
        target[index * TOKENS : (index + 1) * TOKENS, :] = value[
            :, index * LANES : (index + 1) * LANES
        ]
    rest = value[:, full * LANES :]
    target[full * TOKENS :, :] = jnp.concatenate([rest[:HALF], rest[HALF:]], axis=1)


def read_packed(source):
    full = source.shape[0] // TOKENS
    parts = [source[index * TOKENS : (index + 1) * TOKENS, :] for index in range(full)]
    rest = source[full * TOKENS :, :]
    parts.append(jnp.concatenate([rest[:, : LANES // 2], rest[:, LANES // 2 :]], axis=0))
    return jnp.concatenate(parts, axis=1)


def in_place(ctx, block):
    first = ctx if block == 0 else 2 * CTX - 1 - ctx
    return pl.ds(pl.multiple_of(first * HALF, HALF), HALF)


def read_vectors(meta, parts, chunks):
    for ctx, part in enumerate(parts):
        rows = [part[16 * index : 16 * (index + 1), :] for index in range(GROUP // HEAD)]
        chunks[meta[1] ^ ctx] = jnp.concatenate(rows, axis=1).astype(WIDE)
    return jnp.concatenate([chunks[index] for index in range(CTX)], axis=1)


def qkv_kernel(meta, x_ref, *refs):
    vectors, parts, refs = refs[:4], refs[4 : 4 + PARTS], refs[4 + PARTS :]
    h_ref, own, near, far, last, held, units, chunks, sems = refs
    (copies,) = load_weight(meta, parts, functools.partial(qkv_place, held), sems)
    params = read_vectors(meta, vectors, chunks)
    bias = jnp.concatenate([params[4:5], jnp.zeros((1, WIDTH), WIDE), params[5:6]], axis=1)
    centred, inverse = moments(x_ref[...].astype(WIDE))
    normed = (centred * inverse * params[0:1] + params[1:2]).astype(LOW)
    h_ref[...] = normed
    wait_all(copies)
    for chunk in range(CTX):
        mixed = mm(normed, held[chunk]) + bias[:, 3 * GROUP * chunk : 3 * GROUP * (chunk + 1)]
        mixed = mixed.astype(LOW)
        for part in range(3):
            unit = 3 * chunk + part
            units[unit % CTX, :, (unit // CTX) * GROUP : (unit // CTX + 1) * GROUP] = mixed[
                :, part * GROUP : (part + 1) * GROUP
            ]
    for ctx, target in enumerate((own, near, far, last)):
        write_packed(target, units[meta[1] ^ ctx])


def read_sequence(meta, pieces, targets):
    for ctx, piece in enumerate(pieces):
        value = read_packed(piece)
        for block in range(2):
            place = in_place(meta[1] ^ ctx, block)
            rows = value[block * HALF : (block + 1) * HALF, :]
            for index, target in enumerate(targets):
                target[place, :] = rows[:, index * GROUP : (index + 1) * GROUP]


def write_sequence(meta, pieces, sources):
    for ctx, piece in enumerate(pieces):
        parts = []
        for source in sources:
            blocks = [source[in_place(meta[1] ^ ctx, block), :] for block in range(2)]
            parts.append(jnp.concatenate(blocks, axis=0).astype(LOW))
        write_packed(piece, jnp.concatenate(parts, axis=1))


def head_mask(head, scale=1.0):
    lane = lax.broadcasted_iota(jnp.int32, (1, GROUP), 1)
    inside = (lane >= head * HEAD) & (lane < (head + 1) * HEAD)
    return jnp.where(inside, scale, 0.0).astype(LOW)


def tile_of(index):
    return slice(index * TILE, (index + 1) * TILE)


def weights_of(queries, k_seq, tile, causal):
    scores = [mt(queries, k_seq[tile_of(other), :]) for other in range(tile + 1)]
    scores[tile] = jnp.where(causal, scores[tile], -1e30)
    top = jnp.max(functools.reduce(jnp.maximum, scores), axis=-1, keepdims=True)
    expo = [jnp.exp(score - top) for score in scores]
    total = jnp.sum(functools.reduce(jnp.add, expo), axis=-1, keepdims=True)
    inverse = 1.0 / total
    return [value * inverse for value in expo]


def causal_tile():
    row = lax.broadcasted_iota(jnp.int32, (TILE, TILE), 0)
    column = lax.broadcasted_iota(jnp.int32, (TILE, TILE), 1)
    return row >= column


def attend_kernel(meta, *refs):
    pieces, results, (q_seq, k_seq, v_seq, out) = refs[:4], refs[4:8], refs[8:]
    read_sequence(meta, pieces, (q_seq, k_seq, v_seq))
    causal = causal_tile()
    scale = 1.0 / math.sqrt(HEAD)
    for tile in range(SPAN // TILE):

        def one_head(head, total, tile=tile):
            mask = head_mask(head)
            queries = q_seq[tile_of(tile), :] * head_mask(head, scale)
            weights = weights_of(queries, k_seq, tile, causal)
            for other, weight in enumerate(weights):
                total = total + mm(weight.astype(LOW), v_seq[tile_of(other), :] * mask)
            return total

        out[tile_of(tile), :] = lax.fori_loop(
            0, GROUP // HEAD, one_head, jnp.zeros((TILE, GROUP), WIDE), unroll=True
        )
    write_sequence(meta, results, (out,))


def attend_back_kernel(meta, *refs):
    pieces, grads, results = refs[:4], refs[4:8], refs[8:12]
    q_seq, k_seq, v_seq, g_seq, dq, dk, dv = refs[12:]
    read_sequence(meta, pieces, (q_seq, k_seq, v_seq))
    read_sequence(meta, grads, (g_seq,))
    causal = causal_tile()
    scale = 1.0 / math.sqrt(HEAD)
    dk[...] = jnp.zeros_like(dk)
    dv[...] = jnp.zeros_like(dv)
    for tile in range(SPAN // TILE):

        def one_head(head, total, tile=tile):
            mask = head_mask(head)
            scaled = head_mask(head, scale)
            queries = q_seq[tile_of(tile), :] * scaled
            grad = g_seq[tile_of(tile), :] * mask
            weights = weights_of(queries, k_seq, tile, causal)
            backs = [mt(grad, v_seq[tile_of(other), :]) for other in range(tile + 1)]
            products = [weight * back for weight, back in zip(weights, backs)]
            delta = jnp.sum(functools.reduce(jnp.add, products), axis=-1, keepdims=True)
            for other, (weight, back) in enumerate(zip(weights, backs)):
                step = (weight * (back - delta)).astype(LOW)
                total = total + mm(step, k_seq[tile_of(other), :] * scaled)
                dk[tile_of(other), :] += tm(step, queries)
                dv[tile_of(other), :] += tm(weight.astype(LOW), grad)
            return total

        dq[tile_of(tile), :] = lax.fori_loop(
            0, GROUP // HEAD, one_head, jnp.zeros((TILE, GROUP), WIDE), unroll=True
        )
    write_sequence(meta, results, (dq, dk, dv))


def middle_kernel(meta, x_ref, dy_ref, h_one_ref, *refs):
    vectors, pieces, parts, refs = refs[:4], refs[4:8], refs[8 : 8 + PARTS], refs[8 + PARTS :]
    (out_ref, pack_ref, mine, theirs, dmid_ref), refs = refs[:5], refs[5:]
    results, (rows_ref, dbias_ref), refs = refs[:4], refs[4:6], refs[6:]
    out_parts, held_out, held_fc, held_proj, units, total, back, chunks, bias, acts, sems = refs
    place = functools.partial(mlp_place, out_parts, held_fc, held_proj)
    copies = load_weight(meta, parts, place, sems)
    vec = read_vectors(meta, vectors, chunks)
    for chunk in range(CTX):
        bias[chunk] = vec[8 + chunk : 9 + chunk]
    for ctx, piece in enumerate(pieces):
        units[meta[1] ^ ctx] = read_packed(piece)
    att = jnp.concatenate([units[index] for index in range(CTX)], axis=1)
    pack_ref[CTX + 1] = att
    pack_ref[CTX + 3] = dy_ref[...]
    pack_ref[CTX + 4] = h_one_ref[...]
    wait_all(copies[0])
    for chunk in range(CTX):
        held_out[:, chunk * GROUP : (chunk + 1) * GROUP] = out_parts[chunk, :, :GROUP]
    mid = x_ref[...].astype(WIDE) + mm(att, held_out[...]) + vec[6:7]
    centred, inverse = moments(mid)
    normed = centred * inverse
    pack_ref[CTX] = (normed * vec[2:3] + vec[3:4]).astype(LOW)
    total[...] = mid + vec[7:8]
    back[...] = jnp.zeros_like(back)
    for group in copies[1:]:
        wait_all(group)
    side = FF_SIDE

    def chunk_step(chunk, carry):
        pre = mm(pack_ref[CTX], held_fc[chunk]) + bias[chunk]
        square = pre * pre
        tanh = jnp.tanh(0.7978845608028654 * (pre + 0.044715 * square * pre))
        act = (0.5 * pre * (1.0 + tanh)).astype(LOW)
        slope = 0.5 * (1.0 + tanh) + 0.5 * pre * (1.0 - tanh * tanh) * (
            0.7978845608028654 * (1.0 + 3.0 * 0.044715 * square)
        )
        grads = []
        for half in range(2):
            weight = held_proj[2 * chunk + half]
            part = act[:, half * side : (half + 1) * side]
            acts[2 * chunk + half] = part
            total[...] += mt(part, weight)
            grads.append(mm(dy_ref[...], weight))
        dpre = (jnp.concatenate(grads, axis=1) * slope).astype(LOW)
        pack_ref[chunk] = dpre
        dbias_ref[chunk] = jnp.sum(dpre.astype(WIDE), axis=0, keepdims=True)
        back[...] += mt(dpre, held_fc[chunk])
        return carry

    lax.fori_loop(0, CTX, chunk_step, 0)
    out_ref[...] = total[...].astype(LOW)
    core = meta[0] & 1
    for chunk in range(CTX):
        mine[chunk] = acts[2 * chunk + core]
        theirs[chunk] = acts[2 * chunk + 1 - core]
    grad = back[...]
    dy = dy_ref[...].astype(WIDE)
    dmid = dy + norm_back(grad, normed, inverse, vec[2:3])
    dmid_ref[...] = dmid
    datt = dmid.astype(LOW)
    pack_ref[CTX + 2] = datt
    rows_ref[0:1] = jnp.sum(grad * normed, axis=0, keepdims=True)
    rows_ref[1:2] = jnp.sum(grad, axis=0, keepdims=True)
    rows_ref[2:3] = jnp.sum(datt.astype(WIDE), axis=0, keepdims=True)
    rows_ref[3:4] = jnp.sum(dy, axis=0, keepdims=True)
    rows_ref[4:8] = jnp.zeros((4, WIDTH), WIDE)
    dout = mt(datt, held_out[...]).astype(LOW)
    for index in range(CTX):
        units[index] = dout[:, index * GROUP : (index + 1) * GROUP]
    for ctx, target in enumerate(results):
        write_packed(target, units[meta[1] ^ ctx])


def mlp_grad_kernel(meta, *refs):
    acts, packs, targets = refs[:2], refs[2:4], refs[4:8]
    held_out, held_fc, held_proj, turn, sems = refs[8:]

    def place(part, ctx):
        ctx = meta[1] ^ ctx
        chunk = (meta[0] ^ (2 * part)) // 2
        rows = pl.ds(part * ROWS, ROWS)
        return [
            (pl.ds(WIDTH + 2 * FF_SIDE, TILE), held_out.at[ctx, rows, :]),
            (pl.ds(0, WIDTH), held_fc.at[ctx, rows, :]),
            (pl.ds(WIDTH, FF_SIDE), held_proj.at[chunk, rows_of(2 * ctx, ROWS), :]),
            (pl.ds(WIDTH + FF_SIDE, FF_SIDE), held_proj.at[chunk, rows_of(2 * ctx + 1, ROWS), :]),
        ]

    dy = [turned(pack[CTX + 3]) for pack in packs]
    for chunk in range(CTX):
        held_proj[chunk] = over_both(dy, [act[chunk] for act in acts]).astype(LOW)
    copies = store_grad(place, targets, sems, (2, 3))
    left = half_rows(meta, [pack[CTX] for pack in packs], turn)
    for chunk in range(CTX):
        held_fc[chunk] = over_both(left, [pack[chunk] for pack in packs]).astype(LOW)
    copies += store_grad(place, targets, sems, (1,))
    left = half_rows(meta, [pack[CTX + 1] for pack in packs], turn)
    grad = over_both(left, [pack[CTX + 2] for pack in packs]).astype(LOW)
    for chunk in range(CTX):
        held_out[chunk, :, :GROUP] = grad[:, chunk * GROUP : (chunk + 1) * GROUP]
        held_out[chunk, :, GROUP:] = jnp.zeros((WIDTH // 2, TILE - GROUP), LOW)

    wait_all(copies + store_grad(place, targets, sems, (0,)))


def qkv_grad_kernel(meta, *refs):
    pack, own, came, targets = refs[:2], refs[2:4], refs[4:6], refs[6:10]
    mixed_ref, dbias_ref, held, units, turn, sems = refs[10:]
    for core in range(2):
        for ctx in range(CTX):
            value = read_packed(own[core] if ctx == 0 else came[core].at[ctx - 1])
            for part in range(3):
                units[core, CTX * part + (meta[1] ^ ctx)] = value[
                    :, part * GROUP : (part + 1) * GROUP
                ]
    left = half_rows(meta, [pack[0][...], pack[1][...]], turn)
    for chunk in range(CTX):
        mixed = [
            jnp.concatenate([units[core, 3 * chunk + part] for part in range(3)], axis=1)
            for core in range(2)
        ]
        mixed_ref[chunk] = mixed[0]
        bias = jnp.sum(mixed[0].astype(WIDE), axis=0, keepdims=True)
        for part in range(3):
            dbias_ref[3 * chunk + part] = bias[:, part * GROUP : (part + 1) * GROUP]
        held[chunk] = over_both(left, mixed).astype(LOW)

    def place(part, ctx):
        return [(pl.ds(0, 3 * GROUP), held.at[meta[1] ^ ctx, pl.ds(part * ROWS, ROWS), :])]

    wait_all(store_grad(place, targets, sems, (0,)))


def input_grad_kernel(meta, x_ref, dmid_ref, mixed_ref, rows_ref, dfc_ref, dqkv_ref, *refs):
    vectors, parts, refs = refs[:4], refs[4 : 4 + PARTS], refs[4 + PARTS :]
    grad_ref, keep, send, held, chunks, rows, sums, sems = refs
    (copies,) = load_weight(meta, parts, functools.partial(qkv_place, held), sems)
    params = read_vectors(meta, vectors, chunks)
    centred, inverse = moments(x_ref[...].astype(WIDE))
    normed = centred * inverse
    wait_all(copies)
    grad = jnp.zeros((TOKENS, WIDTH), WIDE)
    for chunk in range(CTX):
        grad = grad + mt(mixed_ref[chunk], held[chunk])
    grad_ref[...] = dmid_ref[...] + norm_back(grad, normed, inverse, params[0:1])
    rows[0:1] = jnp.sum(grad * normed, axis=0, keepdims=True)
    rows[1:2] = jnp.sum(grad, axis=0, keepdims=True)
    rows[2:4] = rows_ref[0:2]
    for chunk in range(CTX):
        lanes = slice(chunk * GROUP, (chunk + 1) * GROUP)
        rows[4:5, lanes] = dqkv_ref[chunk]
        rows[5:6, lanes] = dqkv_ref[2 * CTX + chunk]
        rows[8 + chunk : 9 + chunk] = dfc_ref[chunk]
    rows[6:8] = rows_ref[2:4]
    rows[12:16] = jnp.zeros((4, WIDTH), WIDE)
    for chunk in range(CTX):
        sums[chunk] = rows[:, chunk * GROUP : (chunk + 1) * GROUP]
    for index in range(2):
        keep[index] = sums[meta[1] ^ PLACES[index]]
        send[index] = sums[meta[1] ^ PLACES[2 + index]]


def sum_kernel(one_kept, one_back, two_kept, two_back, one_keep, one_send, two_keep, two_send):
    pairs = ((one_kept, one_back, one_keep, one_send), (two_kept, two_back, two_keep, two_send))
    for kept, back, keep, send in pairs:
        keep[...] = kept[0].astype(WIDE) + back[0].astype(WIDE)
        send[...] = (kept[1].astype(WIDE) + back[1].astype(WIDE)).astype(LOW)


def near_kernel(one_kept, one_back, two_kept, two_back, one_keep, two_send):
    one_keep[...] = one_kept[...] + one_back[...].astype(WIDE)
    two_send[...] = (two_kept[...] + two_back[...].astype(WIDE)).astype(LOW)


def shape_of(dtype, *dims):
    return jax.ShapeDtypeStruct(dims, dtype)


def call(kernel, arguments, kinds, outputs, out_kinds, scratch, moved=1):
    spec = {
        "v": pl.BlockSpec(memory_space=pltpu.VMEM),
        "s": pl.BlockSpec(memory_space=pltpu.SMEM),
        "a": pl.BlockSpec(memory_space=pl.ANY),
        "h": pl.BlockSpec((None, TOKENS, WIDTH), lambda step: (CTX + 4, 0, 0)),
    }
    return pl.pallas_call(
        kernel,
        grid=(1,),
        out_shape=tuple(outputs),
        in_specs=[spec[kind] for kind in kinds],
        out_specs=tuple(spec[kind] for kind in out_kinds),
        scratch_shapes=scratch,
        cost_estimate=pl.CostEstimate(flops=1, bytes_accessed=moved, transcendentals=0),
        compiler_params=pltpu.CompilerParams(vmem_limit_bytes=VMEM_LIMIT),
    )(*arguments)


def local_fast(
    block_in,
    cotangent,
    w_qkv,
    w_out,
    w_fc,
    w_proj,
    vectors,
    qkv_first,
    qkv_second,
    out_first,
    out_second,
    fc_first,
    fc_second,
    proj_first,
    proj_second,
    vec_first,
    vec_second,
):
    batch, ctx = lax.axis_index("batch"), lax.axis_index("ctx")
    meta = jnp.stack([batch, ctx]).astype(jnp.int32)
    inputs = block_in.reshape(TOKENS, WIDTH)
    grad_low = cotangent.reshape(TOKENS, WIDTH)
    tie = lax.optimization_barrier

    qkv_sems = pltpu.SemaphoreType.DMA((1, BATCH * CTX))
    mlp_sems = pltpu.SemaphoreType.DMA((4, BATCH * CTX))
    qkv_held = pltpu.VMEM((CTX, WIDTH, 3 * GROUP), LOW)
    vec_held = pltpu.VMEM((CTX, 16, GROUP), WIDE)

    low_vec = jnp.pad(vectors.astype(LOW), ((0, 4), (0, 0)))
    low_vec = [low_vec[:, start : start + HEAD] for start in range(0, GROUP, HEAD)]
    low_vec = jnp.concatenate(low_vec + [jnp.zeros((ROWS - 48, HEAD), LOW)], axis=0)
    piece_one = jnp.concatenate([w_qkv.astype(LOW), low_vec], axis=1)
    low_proj = w_proj.astype(LOW).T
    piece_two = jnp.concatenate(
        [
            w_fc.astype(LOW),
            low_proj[:ROWS],
            low_proj[ROWS:],
            w_out.astype(LOW),
            jnp.zeros((ROWS, TILE - GROUP), LOW),
        ],
        axis=1,
    )
    near = jnp.stack([piece_one, swap(piece_one, "ctx", 2)])
    far = swap(near, "ctx", 1)
    own_one = jnp.concatenate([near, far], axis=0)[:, :, : 3 * GROUP]
    piece_two, late = tie((piece_two, far))
    vec_parts = [part[:48, 3 * GROUP :] for part in (near[0], late[0], near[1], late[1])]
    x_one, y_one = gather_first(own_one)
    across_one = gather_second(x_one, y_one)
    far = swap(piece_two, "ctx", 2)
    far, across_one = tie((far, across_one))
    near = jnp.stack([piece_two, far])
    far = swap(near, "ctx", 1)
    parts_one = [own_one, x_one, y_one, *across_one]
    parts_one = parts_one + to_core(parts_one)

    packed = shape_of(LOW, TOKENS * 3 * GROUP // LANES, LANES)
    single = shape_of(LOW, TOKENS * GROUP // LANES, LANES)
    tokens_low = shape_of(LOW, TOKENS, WIDTH)
    hidden_low = shape_of(LOW, CTX, TOKENS, WIDTH)
    h_one, own, *sent = call(
        qkv_kernel,
        (meta, inputs, *vec_parts, *parts_one),
        "s" + "v" * 5 + "a" * PARTS,
        [tokens_low] + [packed] * 4,
        "v" * 5,
        [qkv_held, pltpu.VMEM((CTX, TOKENS, 3 * GROUP), LOW), vec_held, qkv_sems],
    )
    qkv_pieces = [own] + [swap(part, "ctx", bit) for bit, part in zip((1, 2, 3), sent)]

    far, late_h = tie((far, h_one))
    own_two = jnp.concatenate([near, far], axis=0)
    x_two, y_two = gather_first(own_two)
    qkv_pieces, x_two, y_two = tie((qkv_pieces, x_two, y_two))
    across_two = gather_second(x_two, y_two)
    parts_two = [own_two, x_two, y_two]
    swapped_two = to_core(parts_two)

    sequence_low = pltpu.VMEM((SPAN, GROUP), LOW)
    sequence_wide = pltpu.VMEM((SPAN, GROUP), WIDE)
    own, *sent = call(
        attend_kernel,
        (meta, *qkv_pieces),
        "s" + "v" * 4,
        [single] * 4,
        "v" * 4,
        [sequence_low] * 3 + [sequence_wide],
    )
    sent, swapped_two = tie((sent, swapped_two))
    att_pieces = [own] + [swap(part, "ctx", bit) for bit, part in zip((1, 2, 3), sent)]
    across_two, att_pieces = tie((across_two, att_pieces))
    parts_two = parts_two + list(across_two) + swapped_two + to_core(across_two)

    pack_shape = shape_of(LOW, CTX + 5, TOKENS, WIDTH)
    act_shape = shape_of(LOW, BATCH // 2, TOKENS, FF_SIDE)
    out, pack, act_mine, act_theirs, dmid, own, *sent = call(
        middle_kernel,
        (meta, inputs, grad_low, late_h, *vec_parts, *att_pieces, *parts_two),
        "s" + "v" * 11 + "a" * PARTS,
        [tokens_low, pack_shape, act_shape, act_shape, shape_of(WIDE, TOKENS, WIDTH)]
        + [single] * 4
        + [shape_of(WIDE, 8, WIDTH), shape_of(WIDE, CTX, 1, WIDTH)],
        "v" * 11,
        [
            pltpu.VMEM((CTX, WIDTH, TILE), LOW),
            pltpu.VMEM((WIDTH, WIDTH), LOW),
            pltpu.VMEM((CTX, WIDTH, WIDTH), LOW),
            pltpu.VMEM((BATCH, WIDTH, FF_SIDE), LOW),
            pltpu.VMEM((CTX, TOKENS, GROUP), LOW),
            pltpu.VMEM((TOKENS, WIDTH), WIDE),
            pltpu.VMEM((TOKENS, WIDTH), WIDE),
            vec_held,
            pltpu.VMEM((CTX, 1, WIDTH), WIDE),
            pltpu.VMEM((BATCH, TOKENS, FF_SIDE), LOW),
            mlp_sems,
        ],
    )
    sent, (rows_two, dbias_fc) = sent[:3], sent[3:]
    grad_pieces = [own] + [swap(part, "ctx", bit) for bit, part in zip((1, 2, 3), sent)]
    act_came, pack_came = swap(act_theirs, "batch", CORE), swap(pack, "batch", CORE)

    half_sems = BATCH * CTX // 2
    turn_held = pltpu.VMEM((2, WIDTH, TOKENS), LOW)
    mlp_parts = call(
        mlp_grad_kernel,
        (meta, act_mine, act_came, pack, pack_came),
        "s" + "v" * 4,
        [shape_of(LOW, 2, 2, ROWS, MLP)] * 4,
        "aaaa",
        [
            pltpu.VMEM((CTX, WIDTH // 2, TILE), LOW),
            pltpu.VMEM((CTX, WIDTH // 2, WIDTH), LOW),
            pltpu.VMEM((BATCH // 2, WIDTH, FF_SIDE), LOW),
            turn_held,
            pltpu.SemaphoreType.DMA((4, half_sems)),
        ],
    )
    mlp_parts, grad_pieces = tie((mlp_parts, grad_pieces))
    mlp_kept = mlp_parts[0], mlp_parts[2]
    mlp_back = swap_pair((mlp_parts[1], mlp_parts[3]), YBIT, XBIT)
    own, *sent = call(
        attend_back_kernel,
        (meta, *qkv_pieces, *grad_pieces),
        "s" + "v" * 8,
        [packed] * 4,
        "v" * 4,
        [sequence_low] * 4 + [sequence_wide] * 3,
    )
    own_came = swap(own, "batch", CORE)
    received = [swap(part, "ctx", bit) for bit, part in zip((1, 2, 3), sent)]
    mlp_back, received[0] = tie((mlp_back, received[0]))
    pair = [shape_of(WIDE, 2, ROWS, MLP), shape_of(LOW, 2, ROWS, MLP)]
    one_keep, one_send, two_keep, two_send = call(
        sum_kernel,
        (mlp_kept[0], mlp_back[0], mlp_kept[1], mlp_back[1]),
        "vvvv",
        pair + pair,
        "vvvv",
        [],
    )
    one_keep, received[1], received[2] = tie((one_keep, received[1], received[2]))
    mlp_back = swap_pair((one_send, two_send), XBIT, YBIT)
    received = jnp.stack(received)
    received_came = swap(received, "batch", CORE)

    *qkv_parts, mixed, dbias_qkv = call(
        qkv_grad_kernel,
        (meta, pack, pack_came, own, own_came, received, received_came),
        "shhvvvv",
        [shape_of(LOW, 2, 2, ROWS, 3 * GROUP)] * 4
        + [shape_of(LOW, CTX, TOKENS, 3 * GROUP), shape_of(WIDE, 3 * CTX, 1, GROUP)],
        "aaaavv",
        [
            pltpu.VMEM((CTX, WIDTH // 2, 3 * GROUP), LOW),
            pltpu.VMEM((2, 3 * CTX, TOKENS, GROUP), LOW),
            turn_held,
            pltpu.SemaphoreType.DMA((1, half_sems)),
        ],
    )
    qkv_kept = qkv_parts[0], qkv_parts[2]
    qkv_kept = qkv_parts[0], qkv_parts[2]
    qkv_back = swap_pair((qkv_parts[1], qkv_parts[3]), YBIT, XBIT)
    grad_input, vec_one, vec_two = call(
        input_grad_kernel,
        (meta, inputs, dmid, mixed, rows_two, dbias_fc, dbias_qkv, *vec_parts, *parts_one),
        "s" + "v" * 10 + "a" * PARTS,
        [shape_of(WIDE, TOKENS, WIDTH)] + [shape_of(WIDE, 2, 16, GROUP)] * 2,
        "vvv",
        [qkv_held, vec_held, pltpu.VMEM((16, WIDTH), WIDE), vec_held, qkv_sems],
        moved=40_000_000,
    )
    mlp_back, vec_one, vec_two = tie((mlp_back, vec_one, vec_two))
    mlp_one, mlp_two = call(
        near_kernel, (one_keep, mlp_back[0], two_keep, mlp_back[1]), "vvvv", pair, "vv", []
    )
    mlp_two = swap(mlp_two, "ctx", 1)
    vec_grad = vec_one + swap(vec_two, "ctx", 1)
    mlp_one, qkv_back, vec_grad = tie((mlp_one, qkv_back, vec_grad))
    qkv_kept, qkv_sent = scatter_second(qkv_kept, qkv_back)
    qkv_back = swap_pair(qkv_sent, XBIT, YBIT)
    vec_grad = vec_grad[0] + swap(vec_grad[1], "ctx", 2)
    vec_grad = vec_grad + swap(vec_grad, "batch", CORE)
    mlp_two, qkv_back, vec_grad = tie((mlp_two, qkv_back, vec_grad))
    mlp_grad = scatter_far(mlp_one, mlp_two)
    qkv_grad = scatter_far(*scatter_near(qkv_kept, qkv_back))
    for bit in (XBIT, YBIT):
        vec_grad = vec_grad + swap(vec_grad, "batch", bit)
    vec_grad = vec_grad[:12]
    fc_grad = mlp_grad[:, :WIDTH]
    proj_grad = jnp.concatenate(
        [mlp_grad[:, WIDTH : WIDTH + FF_SIDE], mlp_grad[:, WIDTH + FF_SIDE : WIDTH + 2 * FF_SIDE]],
        axis=0,
    )
    out_grad = mlp_grad[:, WIDTH + 2 * FF_SIDE : WIDTH + 2 * FF_SIDE + GROUP]

    qkv_m, qkv_s, qkv_w = adamw(w_qkv, qkv_grad, qkv_first, qkv_second, 0.06, 0.1)
    out_m, out_s, out_w = adamw(w_out, out_grad, out_first, out_second, 0.06, 0.1)
    fc_m, fc_s, fc_w = adamw(w_fc, fc_grad, fc_first, fc_second, 0.06, 0.1)
    proj_m, proj_s, proj_w = adamw(w_proj, proj_grad.T, proj_first, proj_second, 0.06, 0.1)
    vec_m, vec_s, vec_w = adamw(vectors, vec_grad, vec_first, vec_second, 0.2, 0.0)
    return (
        out.reshape(block_in.shape),
        grad_input.reshape(block_in.shape),
        qkv_m,
        qkv_s,
        qkv_w,
        out_m,
        out_s,
        out_w,
        fc_m,
        fc_s,
        fc_w,
        proj_m,
        proj_s,
        proj_w,
        vec_m,
        vec_s,
        vec_w,
    )


def solution(mesh):
    in_specs = (
        P("batch", "ctx", None, None),
        P("batch", "ctx", None, None),
        P("batch", "ctx"),
        P("batch", "ctx"),
        P("batch", "ctx"),
        P("batch", "ctx"),
        P(None, "ctx"),
        P("batch", "ctx"),
        P("batch", "ctx"),
        P("batch", "ctx"),
        P("batch", "ctx"),
        P("batch", "ctx"),
        P("batch", "ctx"),
        P("batch", "ctx"),
        P("batch", "ctx"),
        P(None, "ctx"),
        P(None, "ctx"),
    )
    out_specs = (
        P("batch", "ctx", None, None),
        P("batch", "ctx", None, None),
        P("batch", "ctx"),
        P("batch", "ctx"),
        P("batch", "ctx"),
        P("batch", "ctx"),
        P("batch", "ctx"),
        P("batch", "ctx"),
        P("batch", "ctx"),
        P("batch", "ctx"),
        P("batch", "ctx"),
        P("batch", "ctx"),
        P("batch", "ctx"),
        P("batch", "ctx"),
        P(None, "ctx"),
        P(None, "ctx"),
        P(None, "ctx"),
    )
    sizes = (mesh.shape["batch"], mesh.shape["ctx"])
    local = local_fast if sizes == (BATCH, CTX) else local_any
    return jax.shard_map(local, mesh=mesh, in_specs=in_specs, out_specs=out_specs, check_vma=False)
```

```python
import functools
import math

import jax
import jax.numpy as jnp
from jax import lax
from jax.experimental import pallas as pl
from jax.experimental.pallas import tpu as pltpu
from jax.sharding import PartitionSpec as P

HEADS = 12
STEP = 10


def layer_norm(value, gain, shift):
    mean = jnp.mean(value, axis=-1, keepdims=True)
    centred = value - mean
    spread = jnp.mean(centred * centred, axis=-1, keepdims=True)
    return centred * lax.rsqrt(spread + 1e-05) * gain + shift


def gelu_tanh(value):
    return (
        0.5
        * value
        * (1.0 + jnp.tanh(0.7978845608028654 * (value + 0.044715 * value * value * value)))
    )


def block_places(index, count, half):
    offsets = jnp.arange(half, dtype=jnp.int32)
    first = index * half + offsets
    second = (2 * count - 1 - index) * half + offsets
    return jnp.concatenate([first, second])


def scores_of(queries, keys, scale, allowed):
    raw = jnp.einsum("sqhd,skhd->shqk", queries, keys, preferred_element_type=jnp.float32) * scale
    return jnp.where(allowed[None, None], raw, -1e30)


def pair_grads(queries, grads, keys, values, top, total, delta, scale, allowed):
    score = scores_of(queries, keys, scale, allowed)
    weights = jnp.exp(score - top[..., None]) / total[..., None]
    back_weights = jnp.einsum("sqhd,skhd->shqk", grads, values, preferred_element_type=jnp.float32)
    grad_score = (weights * (back_weights - delta[..., None])).astype(jnp.bfloat16)
    return (weights.astype(jnp.bfloat16), grad_score)


def rows_product(left, right):
    return jnp.einsum("ra,rb->ab", left, right, preferred_element_type=jnp.float32)


def back_product(grad, weight):
    return jnp.einsum("rb,ab->ra", grad, weight, preferred_element_type=jnp.float32)


def adamw(weight, grad, first, second, rate, decay):
    first = 0.9 * first + 0.1 * grad
    second = 0.999 * second + 0.001 * grad * grad
    first_hat = first / (1.0 - 0.9**STEP)
    second_hat = second / (1.0 - 0.999**STEP)
    weight = weight - rate * (first_hat / (jnp.sqrt(second_hat) + 1e-08) + decay * weight)
    return (first, second, weight)


def local_any(
    block_in,
    cotangent,
    w_qkv,
    w_out,
    w_fc,
    w_proj,
    vectors,
    qkv_first,
    qkv_second,
    out_first,
    out_second,
    fc_first,
    fc_second,
    proj_first,
    proj_second,
    vec_first,
    vec_second,
):
    low_type = jnp.bfloat16
    wide = jnp.float32
    row_parts = (
        lax.all_gather(w_qkv.astype(low_type), "batch", axis=0, tiled=True),
        lax.all_gather(w_out.astype(low_type), "batch", axis=0, tiled=True),
        lax.all_gather(w_fc.astype(low_type), "batch", axis=0, tiled=True),
        lax.all_gather(w_proj.astype(low_type), "batch", axis=0, tiled=True),
    )
    full_qkv, full_out, full_fc, full_proj, full_vec = (
        lax.all_gather(row_parts[0], "ctx", axis=1, tiled=True),
        lax.all_gather(row_parts[1], "ctx", axis=1, tiled=True),
        lax.all_gather(row_parts[2], "ctx", axis=1, tiled=True),
        lax.all_gather(row_parts[3], "ctx", axis=1, tiled=True),
        lax.all_gather(vectors.astype(low_type), "ctx", axis=1, tiled=True),
    )
    params = full_vec.astype(wide)
    seqs, pair, half, width = block_in.shape
    heads = HEADS
    head = width // heads
    rows = seqs * pair * half
    span = pair * half
    count = lax.axis_size("ctx")
    index = lax.axis_index("ctx")
    scale = 1.0 / math.sqrt(head)
    inputs = block_in.astype(wide).reshape(rows, width)
    normed_one = layer_norm(inputs, params[0], params[1]).astype(low_type)
    mixed = jnp.dot(normed_one, full_qkv, preferred_element_type=wide)
    queries = (mixed[:, :width] + params[4]).astype(low_type)
    keys = mixed[:, width : 2 * width].astype(low_type)
    values = (mixed[:, 2 * width :] + params[5]).astype(low_type)
    key_all, value_all = (
        lax.all_gather(keys.reshape(seqs, pair, half, width), "ctx", axis=1, tiled=True),
        lax.all_gather(values.reshape(seqs, pair, half, width), "ctx", axis=1, tiled=True),
    )
    query_heads = queries.reshape(seqs, span, heads, head)
    own_places = block_places(index, count, half)

    def piece_of(source, piece):
        return lax.dynamic_slice_in_dim(source, 2 * piece, 2, 1).reshape(seqs, span, heads, head)

    def allowed_for(piece):
        return own_places[:, None] >= block_places(piece, count, half)[None, :]

    def stats_step(piece, carry):
        top, total = carry
        score = scores_of(query_heads, piece_of(key_all, piece), scale, allowed_for(piece))
        new_top = jnp.maximum(top, jnp.max(score, axis=-1))
        total = total * jnp.exp(top - new_top) + jnp.sum(
            jnp.exp(score - new_top[..., None]), axis=-1
        )
        return (new_top, total)

    start_stats = (jnp.full((seqs, heads, span), -1e30, wide), jnp.zeros((seqs, heads, span), wide))
    top, total = lax.fori_loop(0, count, stats_step, start_stats)

    def output_step(piece, acc):
        score = scores_of(query_heads, piece_of(key_all, piece), scale, allowed_for(piece))
        weights = (jnp.exp(score - top[..., None]) / total[..., None]).astype(low_type)
        return acc + jnp.einsum(
            "shqk,skhd->sqhd", weights, piece_of(value_all, piece), preferred_element_type=wide
        )

    attended = lax.fori_loop(0, count, output_step, jnp.zeros((seqs, span, heads, head), wide))
    att_low = attended.reshape(rows, width).astype(low_type)
    mid = inputs + jnp.dot(att_low, full_out, preferred_element_type=wide) + params[6]
    normed_two = layer_norm(mid, params[2], params[3]).astype(low_type)
    pre = jnp.dot(normed_two, full_fc, preferred_element_type=wide) + params[8:12].reshape(-1)
    act_low = gelu_tanh(pre).astype(low_type)
    result = mid + jnp.dot(act_low, full_proj, preferred_element_type=wide) + params[7]
    out_block = result.astype(low_type).reshape(block_in.shape)
    grad_low = cotangent.reshape(rows, width)
    grad_out = grad_low.astype(wide)
    grad_wproj = rows_product(act_low, grad_low)
    back_act = back_product(grad_low, full_proj)
    grad_pre = jax.vjp(gelu_tanh, pre)[1](back_act)[0].astype(low_type)
    grad_wfc = rows_product(normed_two, grad_pre)
    back_two = back_product(grad_pre, full_fc)
    back_mid, grad_gain_two, grad_shift_two = jax.vjp(layer_norm, mid, params[2], params[3])[1](
        back_two
    )
    grad_mid = grad_out + back_mid
    grad_att_low = grad_mid.astype(low_type)
    grad_wout = rows_product(att_low, grad_att_low)
    back_att = back_product(grad_att_low, full_out)
    grad_heads = back_att.astype(low_type).reshape(seqs, span, heads, head)
    delta = jnp.einsum("sqhd,sqhd->shq", grad_heads.astype(wide), attended)
    query_all, grad_all = (
        lax.all_gather(queries.reshape(seqs, pair, half, width), "ctx", axis=1, tiled=True),
        lax.all_gather(grad_heads.reshape(seqs, pair, half, width), "ctx", axis=1, tiled=True),
    )
    top_all, total_all, delta_all = (
        lax.all_gather(top.reshape(seqs, heads, pair, half), "ctx", axis=2, tiled=True),
        lax.all_gather(total.reshape(seqs, heads, pair, half), "ctx", axis=2, tiled=True),
        lax.all_gather(delta.reshape(seqs, heads, pair, half), "ctx", axis=2, tiled=True),
    )

    def query_step(piece, grad_query):
        key_part = piece_of(key_all, piece)
        value_part = piece_of(value_all, piece)
        weights_low, grad_score = pair_grads(
            query_heads,
            grad_heads,
            key_part,
            value_part,
            top,
            total,
            delta,
            scale,
            allowed_for(piece),
        )
        return grad_query + jnp.einsum(
            "shqk,skhd->sqhd", grad_score, key_part, preferred_element_type=wide
        )

    grad_query = lax.fori_loop(0, count, query_step, jnp.zeros((seqs, span, heads, head), wide))
    key_heads = keys.reshape(seqs, span, heads, head)
    value_heads = values.reshape(seqs, span, heads, head)

    def stat_piece(source, piece):
        return lax.dynamic_slice_in_dim(source, 2 * piece, 2, 2).reshape(seqs, heads, span)

    def key_step(piece, carry):
        grad_key, grad_value = carry
        query_part = piece_of(query_all, piece)
        grad_part = piece_of(grad_all, piece)
        allowed = block_places(piece, count, half)[:, None] >= own_places[None, :]
        weights_low, grad_score = pair_grads(
            query_part,
            grad_part,
            key_heads,
            value_heads,
            stat_piece(top_all, piece),
            stat_piece(total_all, piece),
            stat_piece(delta_all, piece),
            scale,
            allowed,
        )
        grad_key = grad_key + jnp.einsum(
            "shqk,sqhd->skhd", grad_score, query_part, preferred_element_type=wide
        )
        grad_value = grad_value + jnp.einsum(
            "shqk,sqhd->skhd", weights_low, grad_part, preferred_element_type=wide
        )
        return (grad_key, grad_value)

    start_keys = (
        jnp.zeros((seqs, span, heads, head), wide),
        jnp.zeros((seqs, span, heads, head), wide),
    )
    grad_key, grad_value = lax.fori_loop(0, count, key_step, start_keys)
    grad_keys = (grad_key * scale).reshape(seqs, pair, half, width)
    grad_values = grad_value.reshape(seqs, pair, half, width)
    grad_q_low = (grad_query * scale).reshape(rows, width).astype(low_type)
    grad_k_low = grad_keys.reshape(rows, width).astype(low_type)
    grad_v_low = grad_values.reshape(rows, width).astype(low_type)
    grad_mixed = jnp.concatenate([grad_q_low, grad_k_low, grad_v_low], axis=1)
    grad_wqkv = rows_product(normed_one, grad_mixed)
    back_one = back_product(grad_mixed, full_qkv)
    back_in, grad_gain_one, grad_shift_one = jax.vjp(layer_norm, inputs, params[0], params[1])[1](
        back_one
    )
    grad_input = (grad_mid + back_in).reshape(block_in.shape)
    grad_bias_q = jnp.sum(grad_q_low.astype(wide), axis=0)
    grad_bias_v = jnp.sum(grad_v_low.astype(wide), axis=0)
    grad_bias_out = jnp.sum(grad_att_low.astype(wide), axis=0)
    grad_bias_proj = jnp.sum(grad_out, axis=0)
    grad_bias_fc = jnp.sum(grad_pre.astype(wide), axis=0).reshape(4, width)
    small_rows = jnp.stack(
        [
            grad_gain_one,
            grad_shift_one,
            grad_gain_two,
            grad_shift_two,
            grad_bias_q,
            grad_bias_v,
            grad_bias_out,
            grad_bias_proj,
        ]
    )
    grad_vectors = jnp.concatenate([small_rows, grad_bias_fc], axis=0)
    col_sums = (
        lax.psum_scatter(grad_wqkv, "ctx", scatter_dimension=1, tiled=True),
        lax.psum_scatter(grad_wout, "ctx", scatter_dimension=1, tiled=True),
        lax.psum_scatter(grad_wfc, "ctx", scatter_dimension=1, tiled=True),
        lax.psum_scatter(grad_wproj, "ctx", scatter_dimension=1, tiled=True),
        lax.psum_scatter(grad_vectors, "ctx", scatter_dimension=1, tiled=True),
    )
    qkv_grad, out_grad, fc_grad, proj_grad = (
        lax.psum_scatter(col_sums[0], "batch", scatter_dimension=0, tiled=True),
        lax.psum_scatter(col_sums[1], "batch", scatter_dimension=0, tiled=True),
        lax.psum_scatter(col_sums[2], "batch", scatter_dimension=0, tiled=True),
        lax.psum_scatter(col_sums[3], "batch", scatter_dimension=0, tiled=True),
    )
    vec_grad = lax.psum(col_sums[4], "batch")
    qkv_m, qkv_s, qkv_w = adamw(w_qkv, qkv_grad, qkv_first, qkv_second, 0.06, 0.1)
    out_m, out_s, out_w = adamw(w_out, out_grad, out_first, out_second, 0.06, 0.1)
    fc_m, fc_s, fc_w = adamw(w_fc, fc_grad, fc_first, fc_second, 0.06, 0.1)
    proj_m, proj_s, proj_w = adamw(w_proj, proj_grad, proj_first, proj_second, 0.06, 0.1)
    vec_m, vec_s, vec_w = adamw(vectors, vec_grad, vec_first, vec_second, 0.2, 0.0)
    return (
        out_block,
        grad_input,
        qkv_m,
        qkv_s,
        qkv_w,
        out_m,
        out_s,
        out_w,
        fc_m,
        fc_s,
        fc_w,
        proj_m,
        proj_s,
        proj_w,
        vec_m,
        vec_s,
        vec_w,
    )


BATCH = 8
CTX = 4
WIDTH = 768
HEAD = 64
GROUP = WIDTH // CTX
TOKENS = 256
HALF = 128
FF_SIDE = 384
ROWS = WIDTH // BATCH
MLP = WIDTH + 2 * FF_SIDE + 256
SPAN = TOKENS * CTX
TILE = 256
LOW = jnp.bfloat16
WIDE = jnp.float32
CORE, XBIT, YBIT = 1, 2, 4
PLACES = (0, 2, 1, 3)
SOURCES = (
    (0, PLACES),
    (XBIT, PLACES),
    (YBIT, PLACES),
    (XBIT + YBIT, PLACES[:2]),
    (XBIT + YBIT, PLACES[2:]),
    (CORE, PLACES),
    (CORE + XBIT, PLACES),
    (CORE + YBIT, PLACES),
    (CORE + XBIT + YBIT, PLACES[:2]),
    (CORE + XBIT + YBIT, PLACES[2:]),
)
PARTS = len(SOURCES)
VMEM_LIMIT = 56 * 1024 * 1024


def swap(value, axis, bit):
    size = BATCH if axis == "batch" else CTX
    return lax.ppermute(value, axis, [(i, i ^ bit) for i in range(size)])


def mm(left, right):
    return lax.dot_general(left, right, (((1,), (0,)), ((), ())), preferred_element_type=WIDE)


def mt(left, right):
    return lax.dot_general(left, right, (((1,), (1,)), ((), ())), preferred_element_type=WIDE)


def tm(left, right):
    return lax.dot_general(left, right, (((0,), (0,)), ((), ())), preferred_element_type=WIDE)


def turned(value):
    return value.astype(WIDE).T.astype(LOW)


def moments(value):
    mean = jnp.mean(value, axis=-1, keepdims=True)
    centred = value - mean
    spread = jnp.mean(centred * centred, axis=-1, keepdims=True)
    return centred, lax.rsqrt(spread + 1e-05)


def norm_back(grad, normed, inverse, gain):
    part = grad * gain
    mean = jnp.mean(part, axis=-1, keepdims=True)
    cross = jnp.mean(part * normed, axis=-1, keepdims=True)
    return inverse * (part - mean - normed * cross)


def gather_first(own):
    return swap(own, "batch", XBIT), swap(own, "batch", YBIT)


def gather_second(from_x, from_y):
    return swap(from_x[:2], "batch", YBIT), swap(from_y[2:], "batch", XBIT)


def to_core(parts):
    return [swap(part, "batch", CORE) for part in parts]


def swap_pair(pair, first, second):
    return swap(pair[0], "batch", first), swap(pair[1], "batch", second)


def scatter_second(kept, back):
    one = kept[0].astype(WIDE) + back[0].astype(WIDE)
    two = kept[1].astype(WIDE) + back[1].astype(WIDE)
    return (one[0], two[0]), (one[1].astype(LOW), two[1].astype(LOW))


def scatter_near(kept, back):
    one = kept[0].astype(WIDE) + back[0].astype(WIDE)
    two = (kept[1].astype(WIDE) + back[1].astype(WIDE)).astype(LOW)
    return one, swap(two, "ctx", 1)


def scatter_far(one, two):
    one = one + two.astype(WIDE)
    return one[0] + swap(one[1].astype(LOW), "ctx", 2).astype(WIDE)


def rows_of(index, size):
    return pl.ds(pl.multiple_of(index * size, 16), size)


def qkv_place(held, batch, ctx):
    return [(pl.ds(0, 3 * GROUP), held.at[ctx, rows_of(batch, ROWS), :])]


def mlp_place(held_out, held_fc, held_proj, batch, ctx):
    return [
        (pl.ds(WIDTH + 2 * FF_SIDE, TILE), held_out.at[ctx, rows_of(batch, ROWS), :]),
        (pl.ds(0, WIDTH), held_fc.at[ctx, rows_of(batch, ROWS), :]),
        (pl.ds(WIDTH, FF_SIDE), held_proj.at[batch, rows_of(2 * ctx, ROWS), :]),
        (pl.ds(WIDTH + FF_SIDE, FF_SIDE), held_proj.at[batch, rows_of(2 * ctx + 1, ROWS), :]),
    ]


def load_weight(meta, parts, place, sems):
    copies = []
    for part, (source, places) in zip(parts, SOURCES):
        for index, ctx in enumerate(places):
            ranges = place(meta[0] ^ source, meta[1] ^ ctx)
            copies.append([(part.at[index, :, lanes], target) for lanes, target in ranges])
    started = []
    for kind in range(len(copies[0])):
        group = []
        for number, copy in enumerate(copies):
            group.append(pltpu.make_async_copy(*copy[kind], sems.at[kind, number]))
            group[-1].start()
        started.append(group)
    return started


def store_grad(held, targets, sems, kinds):
    one_kept, one_sent, two_kept, two_sent = targets
    copies = []
    for y in range(2):
        for x in range(2):
            for index, ctx in enumerate(PLACES):
                if index < 2:
                    target = (one_sent if y else one_kept).at[x, index]
                else:
                    target = (two_sent if x else two_kept).at[y, index - 2]
                ranges = held(2 * y + x, ctx)
                for kind in kinds:
                    lanes, source = ranges[kind]
                    number = (2 * y + x) * CTX + ctx
                    copies.append(
                        pltpu.make_async_copy(source, target.at[:, lanes], sems.at[kind, number])
                    )
                    copies[-1].start()
    return copies


def half_rows(meta, pair, held):
    for index, value in enumerate(pair):
        held[index] = turned(value)
    parts = []
    for index in range(2):
        rows = [held[index, rows_of(meta[0] ^ (2 * part), ROWS), :] for part in range(BATCH // 2)]
        parts.append(jnp.concatenate(rows, axis=0))
    return parts


def over_both(left, right):
    return mm(left[0], right[0]) + mm(left[1], right[1])


def wait_all(copies):
    for copy in copies:
        copy.wait()


LANES = 128


def write_packed(target, value):
    full = value.shape[1] // LANES
    for index in range(full):
        target[index * TOKENS : (index + 1) * TOKENS, :] = value[
            :, index * LANES : (index + 1) * LANES
        ]
    rest = value[:, full * LANES :]
    target[full * TOKENS :, :] = jnp.concatenate([rest[:HALF], rest[HALF:]], axis=1)


def read_packed(source):
    full = source.shape[0] // TOKENS
    parts = [source[index * TOKENS : (index + 1) * TOKENS, :] for index in range(full)]
    rest = source[full * TOKENS :, :]
    parts.append(jnp.concatenate([rest[:, : LANES // 2], rest[:, LANES // 2 :]], axis=0))
    return jnp.concatenate(parts, axis=1)


def in_place(ctx, block):
    first = ctx if block == 0 else 2 * CTX - 1 - ctx
    return pl.ds(pl.multiple_of(first * HALF, HALF), HALF)


def read_vectors(meta, parts, chunks):
    for ctx, part in enumerate(parts):
        rows = [part[16 * index : 16 * (index + 1), :] for index in range(GROUP // HEAD)]
        chunks[meta[1] ^ ctx] = jnp.concatenate(rows, axis=1).astype(WIDE)
    return jnp.concatenate([chunks[index] for index in range(CTX)], axis=1)


def qkv_kernel(meta, x_ref, *refs):
    vectors, parts, refs = refs[:4], refs[4 : 4 + PARTS], refs[4 + PARTS :]
    h_ref, own, near, far, last, held, units, chunks, sems = refs
    (copies,) = load_weight(meta, parts, functools.partial(qkv_place, held), sems)
    params = read_vectors(meta, vectors, chunks)
    bias = jnp.concatenate([params[4:5], jnp.zeros((1, WIDTH), WIDE), params[5:6]], axis=1)
    centred, inverse = moments(x_ref[...].astype(WIDE))
    normed = (centred * inverse * params[0:1] + params[1:2]).astype(LOW)
    h_ref[...] = normed
    wait_all(copies)
    for chunk in range(CTX):
        mixed = mm(normed, held[chunk]) + bias[:, 3 * GROUP * chunk : 3 * GROUP * (chunk + 1)]
        mixed = mixed.astype(LOW)
        for part in range(3):
            unit = 3 * chunk + part
            units[unit % CTX, :, (unit // CTX) * GROUP : (unit // CTX + 1) * GROUP] = mixed[
                :, part * GROUP : (part + 1) * GROUP
            ]
    for ctx, target in enumerate((own, near, far, last)):
        write_packed(target, units[meta[1] ^ ctx])


def read_sequence(meta, pieces, targets):
    for ctx, piece in enumerate(pieces):
        value = read_packed(piece)
        for block in range(2):
            place = in_place(meta[1] ^ ctx, block)
            rows = value[block * HALF : (block + 1) * HALF, :]
            for index, target in enumerate(targets):
                target[place, :] = rows[:, index * GROUP : (index + 1) * GROUP]


def write_sequence(meta, pieces, sources):
    for ctx, piece in enumerate(pieces):
        parts = []
        for source in sources:
            blocks = [source[in_place(meta[1] ^ ctx, block), :] for block in range(2)]
            parts.append(jnp.concatenate(blocks, axis=0).astype(LOW))
        write_packed(piece, jnp.concatenate(parts, axis=1))


def head_mask(head, scale=1.0):
    lane = lax.broadcasted_iota(jnp.int32, (1, GROUP), 1)
    inside = (lane >= head * HEAD) & (lane < (head + 1) * HEAD)
    return jnp.where(inside, scale, 0.0).astype(LOW)


def tile_of(index):
    return slice(index * TILE, (index + 1) * TILE)


def weights_of(queries, k_seq, tile, causal):
    scores = [mt(queries, k_seq[tile_of(other), :]) for other in range(tile + 1)]
    scores[tile] = jnp.where(causal, scores[tile], -1e30)
    top = jnp.max(functools.reduce(jnp.maximum, scores), axis=-1, keepdims=True)
    expo = [jnp.exp(score - top) for score in scores]
    total = jnp.sum(functools.reduce(jnp.add, expo), axis=-1, keepdims=True)
    inverse = 1.0 / total
    return [value * inverse for value in expo]


def causal_tile():
    row = lax.broadcasted_iota(jnp.int32, (TILE, TILE), 0)
    column = lax.broadcasted_iota(jnp.int32, (TILE, TILE), 1)
    return row >= column


def attend_kernel(meta, *refs):
    pieces, results, (q_seq, k_seq, v_seq, out) = refs[:4], refs[4:8], refs[8:]
    read_sequence(meta, pieces, (q_seq, k_seq, v_seq))
    causal = causal_tile()
    scale = 1.0 / math.sqrt(HEAD)
    for tile in range(SPAN // TILE):

        def one_head(head, total, tile=tile):
            mask = head_mask(head)
            queries = q_seq[tile_of(tile), :] * head_mask(head, scale)
            weights = weights_of(queries, k_seq, tile, causal)
            for other, weight in enumerate(weights):
                total = total + mm(weight.astype(LOW), v_seq[tile_of(other), :] * mask)
            return total

        out[tile_of(tile), :] = lax.fori_loop(
            0, GROUP // HEAD, one_head, jnp.zeros((TILE, GROUP), WIDE), unroll=True
        )
    write_sequence(meta, results, (out,))


def attend_back_kernel(meta, *refs):
    pieces, grads, results = refs[:4], refs[4:8], refs[8:12]
    q_seq, k_seq, v_seq, g_seq, dq, dk, dv = refs[12:]
    read_sequence(meta, pieces, (q_seq, k_seq, v_seq))
    read_sequence(meta, grads, (g_seq,))
    causal = causal_tile()
    scale = 1.0 / math.sqrt(HEAD)
    dk[...] = jnp.zeros_like(dk)
    dv[...] = jnp.zeros_like(dv)
    for tile in range(SPAN // TILE):

        def one_head(head, total, tile=tile):
            mask = head_mask(head)
            scaled = head_mask(head, scale)
            queries = q_seq[tile_of(tile), :] * scaled
            grad = g_seq[tile_of(tile), :] * mask
            weights = weights_of(queries, k_seq, tile, causal)
            backs = [mt(grad, v_seq[tile_of(other), :]) for other in range(tile + 1)]
            products = [weight * back for weight, back in zip(weights, backs)]
            delta = jnp.sum(functools.reduce(jnp.add, products), axis=-1, keepdims=True)
            for other, (weight, back) in enumerate(zip(weights, backs)):
                step = (weight * (back - delta)).astype(LOW)
                total = total + mm(step, k_seq[tile_of(other), :] * scaled)
                dk[tile_of(other), :] += tm(step, queries)
                dv[tile_of(other), :] += tm(weight.astype(LOW), grad)
            return total

        dq[tile_of(tile), :] = lax.fori_loop(
            0, GROUP // HEAD, one_head, jnp.zeros((TILE, GROUP), WIDE), unroll=True
        )
    write_sequence(meta, results, (dq, dk, dv))


def middle_kernel(meta, x_ref, dy_ref, h_one_ref, *refs):
    vectors, pieces, parts, refs = refs[:4], refs[4:8], refs[8 : 8 + PARTS], refs[8 + PARTS :]
    (out_ref, pack_ref, mine, theirs, dmid_ref), refs = refs[:5], refs[5:]
    results, (rows_ref, dbias_ref), refs = refs[:4], refs[4:6], refs[6:]
    out_parts, held_out, held_fc, held_proj, units, total, back, chunks, bias, acts, sems = refs
    place = functools.partial(mlp_place, out_parts, held_fc, held_proj)
    copies = load_weight(meta, parts, place, sems)
    vec = read_vectors(meta, vectors, chunks)
    for chunk in range(CTX):
        bias[chunk] = vec[8 + chunk : 9 + chunk]
    for ctx, piece in enumerate(pieces):
        units[meta[1] ^ ctx] = read_packed(piece)
    att = jnp.concatenate([units[index] for index in range(CTX)], axis=1)
    pack_ref[CTX + 1] = att
    pack_ref[CTX + 3] = dy_ref[...]
    pack_ref[CTX + 4] = h_one_ref[...]
    wait_all(copies[0])
    for chunk in range(CTX):
        held_out[:, chunk * GROUP : (chunk + 1) * GROUP] = out_parts[chunk, :, :GROUP]
    mid = x_ref[...].astype(WIDE) + mm(att, held_out[...]) + vec[6:7]
    centred, inverse = moments(mid)
    normed = centred * inverse
    pack_ref[CTX] = (normed * vec[2:3] + vec[3:4]).astype(LOW)
    total[...] = mid + vec[7:8]
    back[...] = jnp.zeros_like(back)
    for group in copies[1:]:
        wait_all(group)
    side = FF_SIDE

    def chunk_step(chunk, carry):
        pre = mm(pack_ref[CTX], held_fc[chunk]) + bias[chunk]
        square = pre * pre
        tanh = jnp.tanh(0.7978845608028654 * (pre + 0.044715 * square * pre))
        act = (0.5 * pre * (1.0 + tanh)).astype(LOW)
        slope = 0.5 * (1.0 + tanh) + 0.5 * pre * (1.0 - tanh * tanh) * (
            0.7978845608028654 * (1.0 + 3.0 * 0.044715 * square)
        )
        grads = []
        for half in range(2):
            weight = held_proj[2 * chunk + half]
            part = act[:, half * side : (half + 1) * side]
            acts[2 * chunk + half] = part
            total[...] += mt(part, weight)
            grads.append(mm(dy_ref[...], weight))
        dpre = (jnp.concatenate(grads, axis=1) * slope).astype(LOW)
        pack_ref[chunk] = dpre
        dbias_ref[chunk] = jnp.sum(dpre.astype(WIDE), axis=0, keepdims=True)
        back[...] += mt(dpre, held_fc[chunk])
        return carry

    lax.fori_loop(0, CTX, chunk_step, 0, unroll=True)
    out_ref[...] = total[...].astype(LOW)
    core = meta[0] & 1
    for chunk in range(CTX):
        mine[chunk] = acts[2 * chunk + core]
        theirs[chunk] = acts[2 * chunk + 1 - core]
    grad = back[...]
    dy = dy_ref[...].astype(WIDE)
    dmid = dy + norm_back(grad, normed, inverse, vec[2:3])
    dmid_ref[...] = dmid
    datt = dmid.astype(LOW)
    pack_ref[CTX + 2] = datt
    rows_ref[0:1] = jnp.sum(grad * normed, axis=0, keepdims=True)
    rows_ref[1:2] = jnp.sum(grad, axis=0, keepdims=True)
    rows_ref[2:3] = jnp.sum(datt.astype(WIDE), axis=0, keepdims=True)
    rows_ref[3:4] = jnp.sum(dy, axis=0, keepdims=True)
    rows_ref[4:8] = jnp.zeros((4, WIDTH), WIDE)
    dout = mt(datt, held_out[...]).astype(LOW)
    for index in range(CTX):
        units[index] = dout[:, index * GROUP : (index + 1) * GROUP]
    for ctx, target in enumerate(results):
        write_packed(target, units[meta[1] ^ ctx])


def mlp_grad_kernel(meta, *refs):
    acts, packs, targets = refs[:2], refs[2:4], refs[4:8]
    held_out, held_fc, held_proj, turn, sems = refs[8:]

    def place(part, ctx):
        ctx = meta[1] ^ ctx
        chunk = (meta[0] ^ (2 * part)) // 2
        rows = pl.ds(part * ROWS, ROWS)
        return [
            (pl.ds(WIDTH + 2 * FF_SIDE, TILE), held_out.at[ctx, rows, :]),
            (pl.ds(0, WIDTH), held_fc.at[ctx, rows, :]),
            (pl.ds(WIDTH, FF_SIDE), held_proj.at[chunk, rows_of(2 * ctx, ROWS), :]),
            (pl.ds(WIDTH + FF_SIDE, FF_SIDE), held_proj.at[chunk, rows_of(2 * ctx + 1, ROWS), :]),
        ]

    dy = [turned(pack[CTX + 3]) for pack in packs]
    for chunk in range(CTX):
        held_proj[chunk] = over_both(dy, [act[chunk] for act in acts]).astype(LOW)
    copies = store_grad(place, targets, sems, (2, 3))
    left = half_rows(meta, [pack[CTX] for pack in packs], turn)
    for chunk in range(CTX):
        held_fc[chunk] = over_both(left, [pack[chunk] for pack in packs]).astype(LOW)
    copies += store_grad(place, targets, sems, (1,))
    left = half_rows(meta, [pack[CTX + 1] for pack in packs], turn)
    grad = over_both(left, [pack[CTX + 2] for pack in packs]).astype(LOW)
    for chunk in range(CTX):
        held_out[chunk, :, :GROUP] = grad[:, chunk * GROUP : (chunk + 1) * GROUP]
        held_out[chunk, :, GROUP:] = jnp.zeros((WIDTH // 2, TILE - GROUP), LOW)

    wait_all(copies + store_grad(place, targets, sems, (0,)))


def qkv_grad_kernel(meta, *refs):
    pack, own, came, targets = refs[:2], refs[2:4], refs[4:6], refs[6:10]
    mixed_ref, dbias_ref, held, units, turn, sems = refs[10:]
    for core in range(2):
        for ctx in range(CTX):
            value = read_packed(own[core] if ctx == 0 else came[core].at[ctx - 1])
            for part in range(3):
                units[core, CTX * part + (meta[1] ^ ctx)] = value[
                    :, part * GROUP : (part + 1) * GROUP
                ]
    left = half_rows(meta, [pack[0][...], pack[1][...]], turn)
    for chunk in range(CTX):
        mixed = [
            jnp.concatenate([units[core, 3 * chunk + part] for part in range(3)], axis=1)
            for core in range(2)
        ]
        mixed_ref[chunk] = mixed[0]
        bias = jnp.sum(mixed[0].astype(WIDE), axis=0, keepdims=True)
        for part in range(3):
            dbias_ref[3 * chunk + part] = bias[:, part * GROUP : (part + 1) * GROUP]
        held[chunk] = over_both(left, mixed).astype(LOW)

    def place(part, ctx):
        return [(pl.ds(0, 3 * GROUP), held.at[meta[1] ^ ctx, pl.ds(part * ROWS, ROWS), :])]

    wait_all(store_grad(place, targets, sems, (0,)))


def input_grad_kernel(meta, x_ref, dmid_ref, mixed_ref, rows_ref, dfc_ref, dqkv_ref, *refs):
    vectors, parts, refs = refs[:4], refs[4 : 4 + PARTS], refs[4 + PARTS :]
    grad_ref, keep, send, held, chunks, rows, sums, sems = refs
    (copies,) = load_weight(meta, parts, functools.partial(qkv_place, held), sems)
    params = read_vectors(meta, vectors, chunks)
    centred, inverse = moments(x_ref[...].astype(WIDE))
    normed = centred * inverse
    wait_all(copies)
    grad = jnp.zeros((TOKENS, WIDTH), WIDE)
    for chunk in range(CTX):
        grad = grad + mt(mixed_ref[chunk], held[chunk])
    grad_ref[...] = dmid_ref[...] + norm_back(grad, normed, inverse, params[0:1])
    rows[0:1] = jnp.sum(grad * normed, axis=0, keepdims=True)
    rows[1:2] = jnp.sum(grad, axis=0, keepdims=True)
    rows[2:4] = rows_ref[0:2]
    for chunk in range(CTX):
        lanes = slice(chunk * GROUP, (chunk + 1) * GROUP)
        rows[4:5, lanes] = dqkv_ref[chunk]
        rows[5:6, lanes] = dqkv_ref[2 * CTX + chunk]
        rows[8 + chunk : 9 + chunk] = dfc_ref[chunk]
    rows[6:8] = rows_ref[2:4]
    rows[12:16] = jnp.zeros((4, WIDTH), WIDE)
    for chunk in range(CTX):
        sums[chunk] = rows[:, chunk * GROUP : (chunk + 1) * GROUP]
    for index in range(2):
        keep[index] = sums[meta[1] ^ PLACES[index]]
        send[index] = sums[meta[1] ^ PLACES[2 + index]]


def sum_kernel(one_kept, one_back, two_kept, two_back, one_keep, one_send, two_keep, two_send):
    pairs = ((one_kept, one_back, one_keep, one_send), (two_kept, two_back, two_keep, two_send))
    for kept, back, keep, send in pairs:
        keep[...] = kept[0].astype(WIDE) + back[0].astype(WIDE)
        send[...] = (kept[1].astype(WIDE) + back[1].astype(WIDE)).astype(LOW)


def near_kernel(one_kept, one_back, two_kept, two_back, one_keep, two_send):
    one_keep[...] = one_kept[...] + one_back[...].astype(WIDE)
    two_send[...] = (two_kept[...] + two_back[...].astype(WIDE)).astype(LOW)


def shape_of(dtype, *dims):
    return jax.ShapeDtypeStruct(dims, dtype)


def call(kernel, arguments, kinds, outputs, out_kinds, scratch, moved=1):
    spec = {
        "v": pl.BlockSpec(memory_space=pltpu.VMEM),
        "s": pl.BlockSpec(memory_space=pltpu.SMEM),
        "a": pl.BlockSpec(memory_space=pl.ANY),
        "h": pl.BlockSpec((None, TOKENS, WIDTH), lambda step: (CTX + 4, 0, 0)),
    }
    return pl.pallas_call(
        kernel,
        grid=(1,),
        out_shape=tuple(outputs),
        in_specs=[spec[kind] for kind in kinds],
        out_specs=tuple(spec[kind] for kind in out_kinds),
        scratch_shapes=scratch,
        cost_estimate=pl.CostEstimate(flops=1, bytes_accessed=moved, transcendentals=0),
        compiler_params=pltpu.CompilerParams(vmem_limit_bytes=VMEM_LIMIT),
    )(*arguments)


def local_fast(
    block_in,
    cotangent,
    w_qkv,
    w_out,
    w_fc,
    w_proj,
    vectors,
    qkv_first,
    qkv_second,
    out_first,
    out_second,
    fc_first,
    fc_second,
    proj_first,
    proj_second,
    vec_first,
    vec_second,
):
    batch, ctx = lax.axis_index("batch"), lax.axis_index("ctx")
    meta = jnp.stack([batch, ctx]).astype(jnp.int32)
    inputs = block_in.reshape(TOKENS, WIDTH)
    grad_low = cotangent.reshape(TOKENS, WIDTH)
    tie = lax.optimization_barrier

    qkv_sems = pltpu.SemaphoreType.DMA((1, BATCH * CTX))
    mlp_sems = pltpu.SemaphoreType.DMA((4, BATCH * CTX))
    qkv_held = pltpu.VMEM((CTX, WIDTH, 3 * GROUP), LOW)
    vec_held = pltpu.VMEM((CTX, 16, GROUP), WIDE)

    low_vec = jnp.pad(vectors.astype(LOW), ((0, 4), (0, 0)))
    low_vec = [low_vec[:, start : start + HEAD] for start in range(0, GROUP, HEAD)]
    low_vec = jnp.concatenate(low_vec + [jnp.zeros((ROWS - 48, HEAD), LOW)], axis=0)
    piece_one = jnp.concatenate([w_qkv.astype(LOW), low_vec], axis=1)
    low_proj = w_proj.astype(LOW).T
    piece_two = jnp.concatenate(
        [
            w_fc.astype(LOW),
            low_proj[:ROWS],
            low_proj[ROWS:],
            w_out.astype(LOW),
            jnp.zeros((ROWS, TILE - GROUP), LOW),
        ],
        axis=1,
    )
    near = jnp.stack([piece_one, swap(piece_one, "ctx", 2)])
    far = swap(near, "ctx", 1)
    own_one = jnp.concatenate([near, far], axis=0)[:, :, : 3 * GROUP]
    piece_two, late = tie((piece_two, far))
    vec_parts = [part[:48, 3 * GROUP :] for part in (near[0], late[0], near[1], late[1])]
    x_one, y_one = gather_first(own_one)
    across_one = gather_second(x_one, y_one)
    near, far = swap(piece_two, "ctx", 1), swap(piece_two, "ctx", 2)
    near, far, across_one = tie((near, far, across_one))
    last = swap(far, "ctx", 1)
    parts_one = [own_one, x_one, y_one, *across_one]
    parts_one = parts_one + to_core(parts_one)

    packed = shape_of(LOW, TOKENS * 3 * GROUP // LANES, LANES)
    single = shape_of(LOW, TOKENS * GROUP // LANES, LANES)
    tokens_low = shape_of(LOW, TOKENS, WIDTH)
    hidden_low = shape_of(LOW, CTX, TOKENS, WIDTH)
    h_one, own, *sent = call(
        qkv_kernel,
        (meta, inputs, *vec_parts, *parts_one),
        "s" + "v" * 5 + "a" * PARTS,
        [tokens_low] + [packed] * 4,
        "v" * 5,
        [qkv_held, pltpu.VMEM((CTX, TOKENS, 3 * GROUP), LOW), vec_held, qkv_sems],
    )
    qkv_pieces = [own] + [swap(part, "ctx", bit) for bit, part in zip((1, 2, 3), sent)]

    last, late_h = tie((last, h_one))
    own_two = jnp.stack([piece_two, far, near, last])
    x_two, y_two = gather_first(own_two)
    qkv_pieces, x_two, y_two = tie((qkv_pieces, x_two, y_two))
    across_two = gather_second(x_two, y_two)
    parts_two = [own_two, x_two, y_two]
    swapped_two = to_core(parts_two)

    sequence_low = pltpu.VMEM((SPAN, GROUP), LOW)
    sequence_wide = pltpu.VMEM((SPAN, GROUP), WIDE)
    own, *sent = call(
        attend_kernel,
        (meta, *qkv_pieces),
        "s" + "v" * 4,
        [single] * 4,
        "v" * 4,
        [sequence_low] * 3 + [sequence_wide],
    )
    sent, swapped_two = tie((sent, swapped_two))
    att_pieces = [own] + [swap(part, "ctx", bit) for bit, part in zip((1, 2, 3), sent)]
    across_two, att_pieces = tie((across_two, att_pieces))
    parts_two = parts_two + list(across_two) + swapped_two + to_core(across_two)

    pack_shape = shape_of(LOW, CTX + 5, TOKENS, WIDTH)
    act_shape = shape_of(LOW, BATCH // 2, TOKENS, FF_SIDE)
    out, pack, act_mine, act_theirs, dmid, own, *sent = call(
        middle_kernel,
        (meta, inputs, grad_low, late_h, *vec_parts, *att_pieces, *parts_two),
        "s" + "v" * 11 + "a" * PARTS,
        [tokens_low, pack_shape, act_shape, act_shape, shape_of(WIDE, TOKENS, WIDTH)]
        + [single] * 4
        + [shape_of(WIDE, 8, WIDTH), shape_of(WIDE, CTX, 1, WIDTH)],
        "v" * 11,
        [
            pltpu.VMEM((CTX, WIDTH, TILE), LOW),
            pltpu.VMEM((WIDTH, WIDTH), LOW),
            pltpu.VMEM((CTX, WIDTH, WIDTH), LOW),
            pltpu.VMEM((BATCH, WIDTH, FF_SIDE), LOW),
            pltpu.VMEM((CTX, TOKENS, GROUP), LOW),
            pltpu.VMEM((TOKENS, WIDTH), WIDE),
            pltpu.VMEM((TOKENS, WIDTH), WIDE),
            vec_held,
            pltpu.VMEM((CTX, 1, WIDTH), WIDE),
            pltpu.VMEM((BATCH, TOKENS, FF_SIDE), LOW),
            mlp_sems,
        ],
    )
    sent, (rows_two, dbias_fc) = sent[:3], sent[3:]
    grad_pieces = [own] + [swap(part, "ctx", bit) for bit, part in zip((1, 2, 3), sent)]
    act_came, pack_came = swap(act_theirs, "batch", CORE), swap(pack, "batch", CORE)

    half_sems = BATCH * CTX // 2
    turn_held = pltpu.VMEM((2, WIDTH, TOKENS), LOW)
    mlp_parts = call(
        mlp_grad_kernel,
        (meta, act_mine, act_came, pack, pack_came),
        "s" + "v" * 4,
        [shape_of(LOW, 2, 2, ROWS, MLP)] * 4,
        "aaaa",
        [
            pltpu.VMEM((CTX, WIDTH // 2, TILE), LOW),
            pltpu.VMEM((CTX, WIDTH // 2, WIDTH), LOW),
            pltpu.VMEM((BATCH // 2, WIDTH, FF_SIDE), LOW),
            turn_held,
            pltpu.SemaphoreType.DMA((4, half_sems)),
        ],
    )
    mlp_parts, grad_pieces = tie((mlp_parts, grad_pieces))
    mlp_kept = mlp_parts[0], mlp_parts[2]
    mlp_back = swap_pair((mlp_parts[1], mlp_parts[3]), YBIT, XBIT)
    own, *sent = call(
        attend_back_kernel,
        (meta, *qkv_pieces, *grad_pieces),
        "s" + "v" * 8,
        [packed] * 4,
        "v" * 4,
        [sequence_low] * 4 + [sequence_wide] * 3,
    )
    own_came = swap(own, "batch", CORE)
    received = [swap(part, "ctx", bit) for bit, part in zip((1, 2, 3), sent)]
    mlp_back, received[0] = tie((mlp_back, received[0]))
    pair = [shape_of(WIDE, 2, ROWS, MLP), shape_of(LOW, 2, ROWS, MLP)]
    one_keep, one_send, two_keep, two_send = call(
        sum_kernel,
        (mlp_kept[0], mlp_back[0], mlp_kept[1], mlp_back[1]),
        "vvvv",
        pair + pair,
        "vvvv",
        [],
    )
    one_keep, received[1], received[2] = tie((one_keep, received[1], received[2]))
    mlp_back = swap_pair((one_send, two_send), XBIT, YBIT)
    received = jnp.stack(received)
    received_came = swap(received, "batch", CORE)

    *qkv_parts, mixed, dbias_qkv = call(
        qkv_grad_kernel,
        (meta, pack, pack_came, own, own_came, received, received_came),
        "shhvvvv",
        [shape_of(LOW, 2, 2, ROWS, 3 * GROUP)] * 4
        + [shape_of(LOW, CTX, TOKENS, 3 * GROUP), shape_of(WIDE, 3 * CTX, 1, GROUP)],
        "aaaavv",
        [
            pltpu.VMEM((CTX, WIDTH // 2, 3 * GROUP), LOW),
            pltpu.VMEM((2, 3 * CTX, TOKENS, GROUP), LOW),
            turn_held,
            pltpu.SemaphoreType.DMA((1, half_sems)),
        ],
    )
    qkv_kept = qkv_parts[0], qkv_parts[2]
    qkv_kept = qkv_parts[0], qkv_parts[2]
    qkv_back = swap_pair((qkv_parts[1], qkv_parts[3]), YBIT, XBIT)
    grad_input, vec_one, vec_two = call(
        input_grad_kernel,
        (meta, inputs, dmid, mixed, rows_two, dbias_fc, dbias_qkv, *vec_parts, *parts_one),
        "s" + "v" * 10 + "a" * PARTS,
        [shape_of(WIDE, TOKENS, WIDTH)] + [shape_of(WIDE, 2, 16, GROUP)] * 2,
        "vvv",
        [qkv_held, vec_held, pltpu.VMEM((16, WIDTH), WIDE), vec_held, qkv_sems],
        moved=40_000_000,
    )
    mlp_back, vec_one, vec_two = tie((mlp_back, vec_one, vec_two))
    mlp_one, mlp_two = call(
        near_kernel, (one_keep, mlp_back[0], two_keep, mlp_back[1]), "vvvv", pair, "vv", []
    )
    mlp_one, vec_two = tie((mlp_one, vec_two))
    mlp_two = swap(mlp_two, "ctx", 1)
    vec_grad = vec_one + swap(vec_two, "ctx", 1)
    mlp_one, qkv_back, vec_grad = tie((mlp_one, qkv_back, vec_grad))
    qkv_kept, qkv_sent = scatter_second(qkv_kept, qkv_back)
    qkv_back = swap_pair(qkv_sent, XBIT, YBIT)
    mlp_two, qkv_back, vec_grad = tie((mlp_two, qkv_back, vec_grad))
    mlp_grad = scatter_far(mlp_one, mlp_two)
    qkv_grad = scatter_far(*scatter_near(qkv_kept, qkv_back))
    vec_grad = vec_grad[0] + swap(vec_grad[1], "ctx", 2)
    for bit in (CORE, XBIT, YBIT):
        vec_grad = vec_grad + swap(vec_grad, "batch", bit)
    vec_grad = vec_grad[:12]
    fc_grad = mlp_grad[:, :WIDTH]
    proj_grad = jnp.concatenate(
        [mlp_grad[:, WIDTH : WIDTH + FF_SIDE], mlp_grad[:, WIDTH + FF_SIDE : WIDTH + 2 * FF_SIDE]],
        axis=0,
    )
    out_grad = mlp_grad[:, WIDTH + 2 * FF_SIDE : WIDTH + 2 * FF_SIDE + GROUP]

    qkv_m, qkv_s, qkv_w = adamw(w_qkv, qkv_grad, qkv_first, qkv_second, 0.06, 0.1)
    out_m, out_s, out_w = adamw(w_out, out_grad, out_first, out_second, 0.06, 0.1)
    fc_m, fc_s, fc_w = adamw(w_fc, fc_grad, fc_first, fc_second, 0.06, 0.1)
    proj_m, proj_s, proj_w = adamw(w_proj, proj_grad.T, proj_first, proj_second, 0.06, 0.1)
    vec_m, vec_s, vec_w = adamw(vectors, vec_grad, vec_first, vec_second, 0.2, 0.0)
    return (
        out.reshape(block_in.shape),
        grad_input.reshape(block_in.shape),
        qkv_m,
        qkv_s,
        qkv_w,
        out_m,
        out_s,
        out_w,
        fc_m,
        fc_s,
        fc_w,
        proj_m,
        proj_s,
        proj_w,
        vec_m,
        vec_s,
        vec_w,
    )


def solution(mesh):
    in_specs = (
        P("batch", "ctx", None, None),
        P("batch", "ctx", None, None),
        P("batch", "ctx"),
        P("batch", "ctx"),
        P("batch", "ctx"),
        P("batch", "ctx"),
        P(None, "ctx"),
        P("batch", "ctx"),
        P("batch", "ctx"),
        P("batch", "ctx"),
        P("batch", "ctx"),
        P("batch", "ctx"),
        P("batch", "ctx"),
        P("batch", "ctx"),
        P("batch", "ctx"),
        P(None, "ctx"),
        P(None, "ctx"),
    )
    out_specs = (
        P("batch", "ctx", None, None),
        P("batch", "ctx", None, None),
        P("batch", "ctx"),
        P("batch", "ctx"),
        P("batch", "ctx"),
        P("batch", "ctx"),
        P("batch", "ctx"),
        P("batch", "ctx"),
        P("batch", "ctx"),
        P("batch", "ctx"),
        P("batch", "ctx"),
        P("batch", "ctx"),
        P("batch", "ctx"),
        P("batch", "ctx"),
        P(None, "ctx"),
        P(None, "ctx"),
        P(None, "ctx"),
    )
    sizes = (mesh.shape["batch"], mesh.shape["ctx"])
    local = local_fast if sizes == (BATCH, CTX) else local_any
    return jax.shard_map(local, mesh=mesh, in_specs=in_specs, out_specs=out_specs, check_vma=False)
```

```python
import functools
import math

import jax
import jax.numpy as jnp
from jax import lax
from jax.experimental import pallas as pl
from jax.experimental.pallas import tpu as pltpu
from jax.sharding import PartitionSpec as P

HEADS = 12
STEP = 10


def layer_norm(value, gain, shift):
    mean = jnp.mean(value, axis=-1, keepdims=True)
    centred = value - mean
    spread = jnp.mean(centred * centred, axis=-1, keepdims=True)
    return centred * lax.rsqrt(spread + 1e-05) * gain + shift


def gelu_tanh(value):
    return (
        0.5
        * value
        * (1.0 + jnp.tanh(0.7978845608028654 * (value + 0.044715 * value * value * value)))
    )


def block_places(index, count, half):
    offsets = jnp.arange(half, dtype=jnp.int32)
    first = index * half + offsets
    second = (2 * count - 1 - index) * half + offsets
    return jnp.concatenate([first, second])


def scores_of(queries, keys, scale, allowed):
    raw = jnp.einsum("sqhd,skhd->shqk", queries, keys, preferred_element_type=jnp.float32) * scale
    return jnp.where(allowed[None, None], raw, -1e30)


def pair_grads(queries, grads, keys, values, top, total, delta, scale, allowed):
    score = scores_of(queries, keys, scale, allowed)
    weights = jnp.exp(score - top[..., None]) / total[..., None]
    back_weights = jnp.einsum("sqhd,skhd->shqk", grads, values, preferred_element_type=jnp.float32)
    grad_score = (weights * (back_weights - delta[..., None])).astype(jnp.bfloat16)
    return (weights.astype(jnp.bfloat16), grad_score)


def rows_product(left, right):
    return jnp.einsum("ra,rb->ab", left, right, preferred_element_type=jnp.float32)


def back_product(grad, weight):
    return jnp.einsum("rb,ab->ra", grad, weight, preferred_element_type=jnp.float32)


def adamw(weight, grad, first, second, rate, decay):
    first = 0.9 * first + 0.1 * grad
    second = 0.999 * second + 0.001 * grad * grad
    first_hat = first / (1.0 - 0.9**STEP)
    second_hat = second / (1.0 - 0.999**STEP)
    weight = weight - rate * (first_hat / (jnp.sqrt(second_hat) + 1e-08) + decay * weight)
    return (first, second, weight)


def local_any(
    block_in,
    cotangent,
    w_qkv,
    w_out,
    w_fc,
    w_proj,
    vectors,
    qkv_first,
    qkv_second,
    out_first,
    out_second,
    fc_first,
    fc_second,
    proj_first,
    proj_second,
    vec_first,
    vec_second,
):
    low_type = jnp.bfloat16
    wide = jnp.float32
    row_parts = (
        lax.all_gather(w_qkv.astype(low_type), "batch", axis=0, tiled=True),
        lax.all_gather(w_out.astype(low_type), "batch", axis=0, tiled=True),
        lax.all_gather(w_fc.astype(low_type), "batch", axis=0, tiled=True),
        lax.all_gather(w_proj.astype(low_type), "batch", axis=0, tiled=True),
    )
    full_qkv, full_out, full_fc, full_proj, full_vec = (
        lax.all_gather(row_parts[0], "ctx", axis=1, tiled=True),
        lax.all_gather(row_parts[1], "ctx", axis=1, tiled=True),
        lax.all_gather(row_parts[2], "ctx", axis=1, tiled=True),
        lax.all_gather(row_parts[3], "ctx", axis=1, tiled=True),
        lax.all_gather(vectors.astype(low_type), "ctx", axis=1, tiled=True),
    )
    params = full_vec.astype(wide)
    seqs, pair, half, width = block_in.shape
    heads = HEADS
    head = width // heads
    rows = seqs * pair * half
    span = pair * half
    count = lax.axis_size("ctx")
    index = lax.axis_index("ctx")
    scale = 1.0 / math.sqrt(head)
    inputs = block_in.astype(wide).reshape(rows, width)
    normed_one = layer_norm(inputs, params[0], params[1]).astype(low_type)
    mixed = jnp.dot(normed_one, full_qkv, preferred_element_type=wide)
    queries = (mixed[:, :width] + params[4]).astype(low_type)
    keys = mixed[:, width : 2 * width].astype(low_type)
    values = (mixed[:, 2 * width :] + params[5]).astype(low_type)
    key_all, value_all = (
        lax.all_gather(keys.reshape(seqs, pair, half, width), "ctx", axis=1, tiled=True),
        lax.all_gather(values.reshape(seqs, pair, half, width), "ctx", axis=1, tiled=True),
    )
    query_heads = queries.reshape(seqs, span, heads, head)
    own_places = block_places(index, count, half)

    def piece_of(source, piece):
        return lax.dynamic_slice_in_dim(source, 2 * piece, 2, 1).reshape(seqs, span, heads, head)

    def allowed_for(piece):
        return own_places[:, None] >= block_places(piece, count, half)[None, :]

    def stats_step(piece, carry):
        top, total = carry
        score = scores_of(query_heads, piece_of(key_all, piece), scale, allowed_for(piece))
        new_top = jnp.maximum(top, jnp.max(score, axis=-1))
        total = total * jnp.exp(top - new_top) + jnp.sum(
            jnp.exp(score - new_top[..., None]), axis=-1
        )
        return (new_top, total)

    start_stats = (jnp.full((seqs, heads, span), -1e30, wide), jnp.zeros((seqs, heads, span), wide))
    top, total = lax.fori_loop(0, count, stats_step, start_stats)

    def output_step(piece, acc):
        score = scores_of(query_heads, piece_of(key_all, piece), scale, allowed_for(piece))
        weights = (jnp.exp(score - top[..., None]) / total[..., None]).astype(low_type)
        return acc + jnp.einsum(
            "shqk,skhd->sqhd", weights, piece_of(value_all, piece), preferred_element_type=wide
        )

    attended = lax.fori_loop(0, count, output_step, jnp.zeros((seqs, span, heads, head), wide))
    att_low = attended.reshape(rows, width).astype(low_type)
    mid = inputs + jnp.dot(att_low, full_out, preferred_element_type=wide) + params[6]
    normed_two = layer_norm(mid, params[2], params[3]).astype(low_type)
    pre = jnp.dot(normed_two, full_fc, preferred_element_type=wide) + params[8:12].reshape(-1)
    act_low = gelu_tanh(pre).astype(low_type)
    result = mid + jnp.dot(act_low, full_proj, preferred_element_type=wide) + params[7]
    out_block = result.astype(low_type).reshape(block_in.shape)
    grad_low = cotangent.reshape(rows, width)
    grad_out = grad_low.astype(wide)
    grad_wproj = rows_product(act_low, grad_low)
    back_act = back_product(grad_low, full_proj)
    grad_pre = jax.vjp(gelu_tanh, pre)[1](back_act)[0].astype(low_type)
    grad_wfc = rows_product(normed_two, grad_pre)
    back_two = back_product(grad_pre, full_fc)
    back_mid, grad_gain_two, grad_shift_two = jax.vjp(layer_norm, mid, params[2], params[3])[1](
        back_two
    )
    grad_mid = grad_out + back_mid
    grad_att_low = grad_mid.astype(low_type)
    grad_wout = rows_product(att_low, grad_att_low)
    back_att = back_product(grad_att_low, full_out)
    grad_heads = back_att.astype(low_type).reshape(seqs, span, heads, head)
    delta = jnp.einsum("sqhd,sqhd->shq", grad_heads.astype(wide), attended)
    query_all, grad_all = (
        lax.all_gather(queries.reshape(seqs, pair, half, width), "ctx", axis=1, tiled=True),
        lax.all_gather(grad_heads.reshape(seqs, pair, half, width), "ctx", axis=1, tiled=True),
    )
    top_all, total_all, delta_all = (
        lax.all_gather(top.reshape(seqs, heads, pair, half), "ctx", axis=2, tiled=True),
        lax.all_gather(total.reshape(seqs, heads, pair, half), "ctx", axis=2, tiled=True),
        lax.all_gather(delta.reshape(seqs, heads, pair, half), "ctx", axis=2, tiled=True),
    )

    def query_step(piece, grad_query):
        key_part = piece_of(key_all, piece)
        value_part = piece_of(value_all, piece)
        weights_low, grad_score = pair_grads(
            query_heads,
            grad_heads,
            key_part,
            value_part,
            top,
            total,
            delta,
            scale,
            allowed_for(piece),
        )
        return grad_query + jnp.einsum(
            "shqk,skhd->sqhd", grad_score, key_part, preferred_element_type=wide
        )

    grad_query = lax.fori_loop(0, count, query_step, jnp.zeros((seqs, span, heads, head), wide))
    key_heads = keys.reshape(seqs, span, heads, head)
    value_heads = values.reshape(seqs, span, heads, head)

    def stat_piece(source, piece):
        return lax.dynamic_slice_in_dim(source, 2 * piece, 2, 2).reshape(seqs, heads, span)

    def key_step(piece, carry):
        grad_key, grad_value = carry
        query_part = piece_of(query_all, piece)
        grad_part = piece_of(grad_all, piece)
        allowed = block_places(piece, count, half)[:, None] >= own_places[None, :]
        weights_low, grad_score = pair_grads(
            query_part,
            grad_part,
            key_heads,
            value_heads,
            stat_piece(top_all, piece),
            stat_piece(total_all, piece),
            stat_piece(delta_all, piece),
            scale,
            allowed,
        )
        grad_key = grad_key + jnp.einsum(
            "shqk,sqhd->skhd", grad_score, query_part, preferred_element_type=wide
        )
        grad_value = grad_value + jnp.einsum(
            "shqk,sqhd->skhd", weights_low, grad_part, preferred_element_type=wide
        )
        return (grad_key, grad_value)

    start_keys = (
        jnp.zeros((seqs, span, heads, head), wide),
        jnp.zeros((seqs, span, heads, head), wide),
    )
    grad_key, grad_value = lax.fori_loop(0, count, key_step, start_keys)
    grad_keys = (grad_key * scale).reshape(seqs, pair, half, width)
    grad_values = grad_value.reshape(seqs, pair, half, width)
    grad_q_low = (grad_query * scale).reshape(rows, width).astype(low_type)
    grad_k_low = grad_keys.reshape(rows, width).astype(low_type)
    grad_v_low = grad_values.reshape(rows, width).astype(low_type)
    grad_mixed = jnp.concatenate([grad_q_low, grad_k_low, grad_v_low], axis=1)
    grad_wqkv = rows_product(normed_one, grad_mixed)
    back_one = back_product(grad_mixed, full_qkv)
    back_in, grad_gain_one, grad_shift_one = jax.vjp(layer_norm, inputs, params[0], params[1])[1](
        back_one
    )
    grad_input = (grad_mid + back_in).reshape(block_in.shape)
    grad_bias_q = jnp.sum(grad_q_low.astype(wide), axis=0)
    grad_bias_v = jnp.sum(grad_v_low.astype(wide), axis=0)
    grad_bias_out = jnp.sum(grad_att_low.astype(wide), axis=0)
    grad_bias_proj = jnp.sum(grad_out, axis=0)
    grad_bias_fc = jnp.sum(grad_pre.astype(wide), axis=0).reshape(4, width)
    small_rows = jnp.stack(
        [
            grad_gain_one,
            grad_shift_one,
            grad_gain_two,
            grad_shift_two,
            grad_bias_q,
            grad_bias_v,
            grad_bias_out,
            grad_bias_proj,
        ]
    )
    grad_vectors = jnp.concatenate([small_rows, grad_bias_fc], axis=0)
    col_sums = (
        lax.psum_scatter(grad_wqkv, "ctx", scatter_dimension=1, tiled=True),
        lax.psum_scatter(grad_wout, "ctx", scatter_dimension=1, tiled=True),
        lax.psum_scatter(grad_wfc, "ctx", scatter_dimension=1, tiled=True),
        lax.psum_scatter(grad_wproj, "ctx", scatter_dimension=1, tiled=True),
        lax.psum_scatter(grad_vectors, "ctx", scatter_dimension=1, tiled=True),
    )
    qkv_grad, out_grad, fc_grad, proj_grad = (
        lax.psum_scatter(col_sums[0], "batch", scatter_dimension=0, tiled=True),
        lax.psum_scatter(col_sums[1], "batch", scatter_dimension=0, tiled=True),
        lax.psum_scatter(col_sums[2], "batch", scatter_dimension=0, tiled=True),
        lax.psum_scatter(col_sums[3], "batch", scatter_dimension=0, tiled=True),
    )
    vec_grad = lax.psum(col_sums[4], "batch")
    qkv_m, qkv_s, qkv_w = adamw(w_qkv, qkv_grad, qkv_first, qkv_second, 0.06, 0.1)
    out_m, out_s, out_w = adamw(w_out, out_grad, out_first, out_second, 0.06, 0.1)
    fc_m, fc_s, fc_w = adamw(w_fc, fc_grad, fc_first, fc_second, 0.06, 0.1)
    proj_m, proj_s, proj_w = adamw(w_proj, proj_grad, proj_first, proj_second, 0.06, 0.1)
    vec_m, vec_s, vec_w = adamw(vectors, vec_grad, vec_first, vec_second, 0.2, 0.0)
    return (
        out_block,
        grad_input,
        qkv_m,
        qkv_s,
        qkv_w,
        out_m,
        out_s,
        out_w,
        fc_m,
        fc_s,
        fc_w,
        proj_m,
        proj_s,
        proj_w,
        vec_m,
        vec_s,
        vec_w,
    )


BATCH = 8
CTX = 4
WIDTH = 768
HEAD = 64
GROUP = WIDTH // CTX
TOKENS = 256
HALF = 128
FF_SIDE = 384
ROWS = WIDTH // BATCH
MLP = WIDTH + 2 * FF_SIDE + 256
SPAN = TOKENS * CTX
TILE = 256
LOW = jnp.bfloat16
WIDE = jnp.float32
CORE, XBIT, YBIT = 1, 2, 4
PLACES = (0, 2, 1, 3)
SOURCES = (
    (0, PLACES),
    (XBIT, PLACES),
    (YBIT, PLACES),
    (XBIT + YBIT, PLACES[:2]),
    (XBIT + YBIT, PLACES[2:]),
    (CORE, PLACES),
    (CORE + XBIT, PLACES),
    (CORE + YBIT, PLACES),
    (CORE + XBIT + YBIT, PLACES[:2]),
    (CORE + XBIT + YBIT, PLACES[2:]),
)
PARTS = len(SOURCES)
VMEM_LIMIT = 56 * 1024 * 1024


def swap(value, axis, bit):
    size = BATCH if axis == "batch" else CTX
    return lax.ppermute(value, axis, [(i, i ^ bit) for i in range(size)])


def mm(left, right):
    return lax.dot_general(left, right, (((1,), (0,)), ((), ())), preferred_element_type=WIDE)


def mt(left, right):
    return lax.dot_general(left, right, (((1,), (1,)), ((), ())), preferred_element_type=WIDE)


def tm(left, right):
    return lax.dot_general(left, right, (((0,), (0,)), ((), ())), preferred_element_type=WIDE)


def turned(value):
    return value.T


def moments(value):
    mean = jnp.mean(value, axis=-1, keepdims=True)
    centred = value - mean
    spread = jnp.mean(centred * centred, axis=-1, keepdims=True)
    return centred, lax.rsqrt(spread + 1e-05)


def norm_back(grad, normed, inverse, gain):
    part = grad * gain
    mean = jnp.mean(part, axis=-1, keepdims=True)
    cross = jnp.mean(part * normed, axis=-1, keepdims=True)
    return inverse * (part - mean - normed * cross)


def gather_first(own):
    return swap(own, "batch", XBIT), swap(own, "batch", YBIT)


def gather_second(from_x, from_y):
    return swap(from_x[:2], "batch", YBIT), swap(from_y[2:], "batch", XBIT)


def to_core(parts):
    return [swap(part, "batch", CORE) for part in parts]


def swap_pair(pair, first, second):
    return swap(pair[0], "batch", first), swap(pair[1], "batch", second)


def scatter_second(kept, back):
    one = kept[0].astype(WIDE) + back[0].astype(WIDE)
    two = kept[1].astype(WIDE) + back[1].astype(WIDE)
    return (one[0], two[0]), (one[1].astype(LOW), two[1].astype(LOW))


def scatter_near(kept, back):
    one = kept[0].astype(WIDE) + back[0].astype(WIDE)
    two = (kept[1].astype(WIDE) + back[1].astype(WIDE)).astype(LOW)
    return one, swap(two, "ctx", 1)


def scatter_far(one, two):
    one = one + two.astype(WIDE)
    return one[0] + swap(one[1].astype(LOW), "ctx", 2).astype(WIDE)


def rows_of(index, size):
    return pl.ds(pl.multiple_of(index * size, 16), size)


def qkv_place(held, batch, ctx):
    return [(pl.ds(0, 3 * GROUP), held.at[ctx, rows_of(batch, ROWS), :])]


def mlp_place(held_out, held_fc, held_proj, batch, ctx):
    return [
        (pl.ds(WIDTH + 2 * FF_SIDE, TILE), held_out.at[ctx, rows_of(batch, ROWS), :]),
        (pl.ds(0, WIDTH), held_fc.at[ctx, rows_of(batch, ROWS), :]),
        (pl.ds(WIDTH, FF_SIDE), held_proj.at[batch, rows_of(2 * ctx, ROWS), :]),
        (pl.ds(WIDTH + FF_SIDE, FF_SIDE), held_proj.at[batch, rows_of(2 * ctx + 1, ROWS), :]),
    ]


def load_weight(meta, parts, place, sems):
    copies = []
    for part, (source, places) in zip(parts, SOURCES):
        for index, ctx in enumerate(places):
            ranges = place(meta[0] ^ source, meta[1] ^ ctx)
            copies.append([(part.at[index, :, lanes], target) for lanes, target in ranges])
    started = []
    for kind in range(len(copies[0])):
        group = []
        for number, copy in enumerate(copies):
            group.append(pltpu.make_async_copy(*copy[kind], sems.at[kind, number]))
            group[-1].start()
        started.append(group)
    return started


def store_grad(held, targets, sems, kinds):
    one_kept, one_sent, two_kept, two_sent = targets
    copies = []
    for y in range(2):
        for x in range(2):
            for index, ctx in enumerate(PLACES):
                if index < 2:
                    target = (one_sent if y else one_kept).at[x, index]
                else:
                    target = (two_sent if x else two_kept).at[y, index - 2]
                ranges = held(2 * y + x, ctx)
                for kind in kinds:
                    lanes, source = ranges[kind]
                    number = (2 * y + x) * CTX + ctx
                    copies.append(
                        pltpu.make_async_copy(source, target.at[:, lanes], sems.at[kind, number])
                    )
                    copies[-1].start()
    return copies


def half_rows(meta, pair, held):
    for index, value in enumerate(pair):
        held[index] = turned(value)
    parts = []
    for index in range(2):
        rows = [held[index, rows_of(meta[0] ^ (2 * part), ROWS), :] for part in range(BATCH // 2)]
        parts.append(jnp.concatenate(rows, axis=0))
    return parts


def over_both(left, right):
    return mm(left[0], right[0]) + mm(left[1], right[1])


def wait_all(copies):
    for copy in copies:
        copy.wait()


LANES = 128


def write_packed(target, value):
    full = value.shape[1] // LANES
    for index in range(full):
        target[index * TOKENS : (index + 1) * TOKENS, :] = value[
            :, index * LANES : (index + 1) * LANES
        ]
    rest = value[:, full * LANES :]
    target[full * TOKENS :, :] = jnp.concatenate([rest[:HALF], rest[HALF:]], axis=1)


def read_packed(source):
    full = source.shape[0] // TOKENS
    parts = [source[index * TOKENS : (index + 1) * TOKENS, :] for index in range(full)]
    rest = source[full * TOKENS :, :]
    parts.append(jnp.concatenate([rest[:, : LANES // 2], rest[:, LANES // 2 :]], axis=0))
    return jnp.concatenate(parts, axis=1)


def in_place(ctx, block):
    first = ctx if block == 0 else 2 * CTX - 1 - ctx
    return pl.ds(pl.multiple_of(first * HALF, HALF), HALF)


def read_vectors(meta, parts, chunks):
    for ctx, part in enumerate(parts):
        rows = [part[16 * index : 16 * (index + 1), :] for index in range(GROUP // HEAD)]
        chunks[meta[1] ^ ctx] = jnp.concatenate(rows, axis=1).astype(WIDE)
    return jnp.concatenate([chunks[index] for index in range(CTX)], axis=1)


def qkv_kernel(meta, x_ref, *refs):
    vectors, parts, refs = refs[:4], refs[4 : 4 + PARTS], refs[4 + PARTS :]
    h_ref, own, near, far, last, held, units, chunks, sems = refs
    (copies,) = load_weight(meta, parts, functools.partial(qkv_place, held), sems)
    params = read_vectors(meta, vectors, chunks)
    bias = jnp.concatenate([params[4:5], jnp.zeros((1, WIDTH), WIDE), params[5:6]], axis=1)
    centred, inverse = moments(x_ref[...].astype(WIDE))
    normed = (centred * inverse * params[0:1] + params[1:2]).astype(LOW)
    h_ref[...] = normed
    wait_all(copies)
    for chunk in range(CTX):
        mixed = mm(normed, held[chunk]) + bias[:, 3 * GROUP * chunk : 3 * GROUP * (chunk + 1)]
        mixed = mixed.astype(LOW)
        for part in range(3):
            unit = 3 * chunk + part
            units[unit % CTX, :, (unit // CTX) * GROUP : (unit // CTX + 1) * GROUP] = mixed[
                :, part * GROUP : (part + 1) * GROUP
            ]
    for ctx, target in enumerate((own, near, far, last)):
        write_packed(target, units[meta[1] ^ ctx])


def read_sequence(meta, pieces, targets):
    for ctx, piece in enumerate(pieces):
        value = read_packed(piece)
        for block in range(2):
            place = in_place(meta[1] ^ ctx, block)
            rows = value[block * HALF : (block + 1) * HALF, :]
            for index, target in enumerate(targets):
                target[place, :] = rows[:, index * GROUP : (index + 1) * GROUP]


def write_sequence(meta, pieces, sources):
    for ctx, piece in enumerate(pieces):
        parts = []
        for source in sources:
            blocks = [source[in_place(meta[1] ^ ctx, block), :] for block in range(2)]
            parts.append(jnp.concatenate(blocks, axis=0).astype(LOW))
        write_packed(piece, jnp.concatenate(parts, axis=1))


def head_mask(head, scale=1.0):
    lane = lax.broadcasted_iota(jnp.int32, (1, GROUP), 1)
    inside = (lane >= head * HEAD) & (lane < (head + 1) * HEAD)
    return jnp.where(inside, scale, 0.0).astype(LOW)


def tile_of(index):
    return slice(index * TILE, (index + 1) * TILE)


def weights_of(queries, k_seq, tile, causal):
    scores = [mt(queries, k_seq[tile_of(other), :]) for other in range(tile + 1)]
    scores[tile] = jnp.where(causal, scores[tile], -1e30)
    top = jnp.max(functools.reduce(jnp.maximum, scores), axis=-1, keepdims=True)
    expo = [jnp.exp(score - top) for score in scores]
    total = jnp.sum(functools.reduce(jnp.add, expo), axis=-1, keepdims=True)
    inverse = 1.0 / total
    return [value * inverse for value in expo]


def causal_tile():
    row = lax.broadcasted_iota(jnp.int32, (TILE, TILE), 0)
    column = lax.broadcasted_iota(jnp.int32, (TILE, TILE), 1)
    return row >= column


def attend_kernel(meta, *refs):
    pieces, results, (q_seq, k_seq, v_seq, out) = refs[:4], refs[4:8], refs[8:]
    read_sequence(meta, pieces, (q_seq, k_seq, v_seq))
    causal = causal_tile()
    scale = 1.0 / math.sqrt(HEAD)
    for tile in range(SPAN // TILE):

        def one_head(head, total, tile=tile):
            mask = head_mask(head)
            queries = q_seq[tile_of(tile), :] * head_mask(head, scale)
            weights = weights_of(queries, k_seq, tile, causal)
            for other, weight in enumerate(weights):
                total = total + mm(weight.astype(LOW), v_seq[tile_of(other), :] * mask)
            return total

        out[tile_of(tile), :] = lax.fori_loop(
            0, GROUP // HEAD, one_head, jnp.zeros((TILE, GROUP), WIDE), unroll=True
        )
    write_sequence(meta, results, (out,))


def attend_back_kernel(meta, *refs):
    pieces, grads, results = refs[:4], refs[4:8], refs[8:12]
    q_seq, k_seq, v_seq, g_seq, dq, dk, dv = refs[12:]
    read_sequence(meta, pieces, (q_seq, k_seq, v_seq))
    read_sequence(meta, grads, (g_seq,))
    causal = causal_tile()
    scale = 1.0 / math.sqrt(HEAD)
    dk[...] = jnp.zeros_like(dk)
    dv[...] = jnp.zeros_like(dv)
    for tile in range(SPAN // TILE):

        def one_head(head, total, tile=tile):
            mask = head_mask(head)
            scaled = head_mask(head, scale)
            queries = q_seq[tile_of(tile), :] * scaled
            grad = g_seq[tile_of(tile), :] * mask
            weights = weights_of(queries, k_seq, tile, causal)
            backs = [mt(grad, v_seq[tile_of(other), :]) for other in range(tile + 1)]
            products = [weight * back for weight, back in zip(weights, backs)]
            delta = jnp.sum(functools.reduce(jnp.add, products), axis=-1, keepdims=True)
            for other, (weight, back) in enumerate(zip(weights, backs)):
                step = (weight * (back - delta)).astype(LOW)
                total = total + mm(step, k_seq[tile_of(other), :] * scaled)
                dk[tile_of(other), :] += tm(step, queries)
                dv[tile_of(other), :] += tm(weight.astype(LOW), grad)
            return total

        dq[tile_of(tile), :] = lax.fori_loop(
            0, GROUP // HEAD, one_head, jnp.zeros((TILE, GROUP), WIDE), unroll=True
        )
    write_sequence(meta, results, (dq, dk, dv))


def middle_kernel(meta, x_ref, dy_ref, h_one_ref, *refs):
    vectors, pieces, parts, refs = refs[:4], refs[4:8], refs[8 : 8 + PARTS], refs[8 + PARTS :]
    (out_ref, pack_ref, mine, theirs, dmid_ref), refs = refs[:5], refs[5:]
    results, (rows_ref, dbias_ref), refs = refs[:4], refs[4:6], refs[6:]
    out_parts, held_out, held_fc, held_proj, units, total, back, chunks, bias, acts, sems = refs
    place = functools.partial(mlp_place, out_parts, held_fc, held_proj)
    copies = load_weight(meta, parts, place, sems)
    vec = read_vectors(meta, vectors, chunks)
    for chunk in range(CTX):
        bias[chunk] = vec[8 + chunk : 9 + chunk]
    for ctx, piece in enumerate(pieces):
        units[meta[1] ^ ctx] = read_packed(piece)
    att = jnp.concatenate([units[index] for index in range(CTX)], axis=1)
    pack_ref[CTX + 1] = att
    pack_ref[CTX + 3] = dy_ref[...]
    pack_ref[CTX + 4] = h_one_ref[...]
    wait_all(copies[0])
    for chunk in range(CTX):
        held_out[:, chunk * GROUP : (chunk + 1) * GROUP] = out_parts[chunk, :, :GROUP]
    mid = x_ref[...].astype(WIDE) + mm(att, held_out[...]) + vec[6:7]
    centred, inverse = moments(mid)
    normed = centred * inverse
    pack_ref[CTX] = (normed * vec[2:3] + vec[3:4]).astype(LOW)
    total[...] = mid + vec[7:8]
    back[...] = jnp.zeros_like(back)
    for group in copies[1:]:
        wait_all(group)
    side = FF_SIDE

    def chunk_step(chunk, carry):
        pre = mm(pack_ref[CTX], held_fc[chunk]) + bias[chunk]
        square = pre * pre
        tanh = jnp.tanh(0.7978845608028654 * (pre + 0.044715 * square * pre))
        act = (0.5 * pre * (1.0 + tanh)).astype(LOW)
        slope = 0.5 * (1.0 + tanh) + 0.5 * pre * (1.0 - tanh * tanh) * (
            0.7978845608028654 * (1.0 + 3.0 * 0.044715 * square)
        )
        grads = []
        for half in range(2):
            weight = held_proj[2 * chunk + half]
            part = act[:, half * side : (half + 1) * side]
            acts[2 * chunk + half] = part
            total[...] += mt(part, weight)
            grads.append(mm(dy_ref[...], weight))
        dpre = (jnp.concatenate(grads, axis=1) * slope).astype(LOW)
        pack_ref[chunk] = dpre
        dbias_ref[chunk] = jnp.sum(dpre.astype(WIDE), axis=0, keepdims=True)
        back[...] += mt(dpre, held_fc[chunk])
        return carry

    lax.fori_loop(0, CTX, chunk_step, 0, unroll=True)
    out_ref[...] = total[...].astype(LOW)
    core = meta[0] & 1
    for chunk in range(CTX):
        mine[chunk] = acts[2 * chunk + core]
        theirs[chunk] = acts[2 * chunk + 1 - core]
    grad = back[...]
    dy = dy_ref[...].astype(WIDE)
    dmid = dy + norm_back(grad, normed, inverse, vec[2:3])
    dmid_ref[...] = dmid
    datt = dmid.astype(LOW)
    pack_ref[CTX + 2] = datt
    rows_ref[0:1] = jnp.sum(grad * normed, axis=0, keepdims=True)
    rows_ref[1:2] = jnp.sum(grad, axis=0, keepdims=True)
    rows_ref[2:3] = jnp.sum(datt.astype(WIDE), axis=0, keepdims=True)
    rows_ref[3:4] = jnp.sum(dy, axis=0, keepdims=True)
    rows_ref[4:8] = jnp.zeros((4, WIDTH), WIDE)
    dout = mt(datt, held_out[...]).astype(LOW)
    for index in range(CTX):
        units[index] = dout[:, index * GROUP : (index + 1) * GROUP]
    for ctx, target in enumerate(results):
        write_packed(target, units[meta[1] ^ ctx])


def mlp_grad_kernel(meta, *refs):
    acts, packs, targets = refs[:2], refs[2:4], refs[4:8]
    held_out, held_fc, held_proj, turn, sems = refs[8:]

    def place(part, ctx):
        ctx = meta[1] ^ ctx
        chunk = (meta[0] ^ (2 * part)) // 2
        rows = pl.ds(part * ROWS, ROWS)
        return [
            (pl.ds(WIDTH + 2 * FF_SIDE, TILE), held_out.at[ctx, rows, :]),
            (pl.ds(0, WIDTH), held_fc.at[ctx, rows, :]),
            (pl.ds(WIDTH, FF_SIDE), held_proj.at[chunk, rows_of(2 * ctx, ROWS), :]),
            (pl.ds(WIDTH + FF_SIDE, FF_SIDE), held_proj.at[chunk, rows_of(2 * ctx + 1, ROWS), :]),
        ]

    dy = [turned(pack[CTX + 3]) for pack in packs]
    for chunk in range(CTX):
        held_proj[chunk] = over_both(dy, [act[chunk] for act in acts]).astype(LOW)
    copies = store_grad(place, targets, sems, (2, 3))
    left = half_rows(meta, [pack[CTX] for pack in packs], turn)
    for chunk in range(CTX):
        held_fc[chunk] = over_both(left, [pack[chunk] for pack in packs]).astype(LOW)
    copies += store_grad(place, targets, sems, (1,))
    left = half_rows(meta, [pack[CTX + 1] for pack in packs], turn)
    grad = over_both(left, [pack[CTX + 2] for pack in packs]).astype(LOW)
    for chunk in range(CTX):
        held_out[chunk, :, :GROUP] = grad[:, chunk * GROUP : (chunk + 1) * GROUP]
        held_out[chunk, :, GROUP:] = jnp.zeros((WIDTH // 2, TILE - GROUP), LOW)

    wait_all(copies + store_grad(place, targets, sems, (0,)))


def qkv_grad_kernel(meta, *refs):
    pack, own, came, targets = refs[:2], refs[2:4], refs[4:6], refs[6:10]
    mixed_ref, dbias_ref, held, units, turn, sems = refs[10:]
    for core in range(2):
        for ctx in range(CTX):
            value = read_packed(own[core] if ctx == 0 else came[core].at[ctx - 1])
            for part in range(3):
                units[core, CTX * part + (meta[1] ^ ctx)] = value[
                    :, part * GROUP : (part + 1) * GROUP
                ]
    left = half_rows(meta, [pack[0][...], pack[1][...]], turn)
    for chunk in range(CTX):
        mixed = [
            jnp.concatenate([units[core, 3 * chunk + part] for part in range(3)], axis=1)
            for core in range(2)
        ]
        mixed_ref[chunk] = mixed[0]
        bias = jnp.sum(mixed[0].astype(WIDE), axis=0, keepdims=True)
        for part in range(3):
            dbias_ref[3 * chunk + part] = bias[:, part * GROUP : (part + 1) * GROUP]
        held[chunk] = over_both(left, mixed).astype(LOW)

    def place(part, ctx):
        return [(pl.ds(0, 3 * GROUP), held.at[meta[1] ^ ctx, pl.ds(part * ROWS, ROWS), :])]

    wait_all(store_grad(place, targets, sems, (0,)))


def input_grad_kernel(meta, x_ref, dmid_ref, mixed_ref, rows_ref, dfc_ref, dqkv_ref, *refs):
    vectors, parts, refs = refs[:4], refs[4 : 4 + PARTS], refs[4 + PARTS :]
    grad_ref, keep, send, held, chunks, rows, sums, sems = refs
    (copies,) = load_weight(meta, parts, functools.partial(qkv_place, held), sems)
    params = read_vectors(meta, vectors, chunks)
    centred, inverse = moments(x_ref[...].astype(WIDE))
    normed = centred * inverse
    wait_all(copies)
    grad = jnp.zeros((TOKENS, WIDTH), WIDE)
    for chunk in range(CTX):
        grad = grad + mt(mixed_ref[chunk], held[chunk])
    grad_ref[...] = dmid_ref[...] + norm_back(grad, normed, inverse, params[0:1])
    rows[0:1] = jnp.sum(grad * normed, axis=0, keepdims=True)
    rows[1:2] = jnp.sum(grad, axis=0, keepdims=True)
    rows[2:4] = rows_ref[0:2]
    for chunk in range(CTX):
        lanes = slice(chunk * GROUP, (chunk + 1) * GROUP)
        rows[4:5, lanes] = dqkv_ref[chunk]
        rows[5:6, lanes] = dqkv_ref[2 * CTX + chunk]
        rows[8 + chunk : 9 + chunk] = dfc_ref[chunk]
    rows[6:8] = rows_ref[2:4]
    rows[12:16] = jnp.zeros((4, WIDTH), WIDE)
    for chunk in range(CTX):
        sums[chunk] = rows[:, chunk * GROUP : (chunk + 1) * GROUP]
    for index in range(2):
        keep[index] = sums[meta[1] ^ PLACES[index]]
        send[index] = sums[meta[1] ^ PLACES[2 + index]]


def sum_kernel(one_kept, one_back, two_kept, two_back, one_keep, one_send, two_keep, two_send):
    pairs = ((one_kept, one_back, one_keep, one_send), (two_kept, two_back, two_keep, two_send))
    for kept, back, keep, send in pairs:
        keep[...] = kept[0].astype(WIDE) + back[0].astype(WIDE)
        send[...] = (kept[1].astype(WIDE) + back[1].astype(WIDE)).astype(LOW)


def near_kernel(one_kept, one_back, two_kept, two_back, one_keep, two_send):
    one_keep[...] = one_kept[...] + one_back[...].astype(WIDE)
    two_send[...] = (two_kept[...] + two_back[...].astype(WIDE)).astype(LOW)


def shape_of(dtype, *dims):
    return jax.ShapeDtypeStruct(dims, dtype)


def call(kernel, arguments, kinds, outputs, out_kinds, scratch, moved=1):
    spec = {
        "v": pl.BlockSpec(memory_space=pltpu.VMEM),
        "s": pl.BlockSpec(memory_space=pltpu.SMEM),
        "a": pl.BlockSpec(memory_space=pl.ANY),
        "h": pl.BlockSpec((None, TOKENS, WIDTH), lambda step: (CTX + 4, 0, 0)),
    }
    return pl.pallas_call(
        kernel,
        grid=(1,),
        out_shape=tuple(outputs),
        in_specs=[spec[kind] for kind in kinds],
        out_specs=tuple(spec[kind] for kind in out_kinds),
        scratch_shapes=scratch,
        cost_estimate=pl.CostEstimate(flops=1, bytes_accessed=moved, transcendentals=0),
        compiler_params=pltpu.CompilerParams(vmem_limit_bytes=VMEM_LIMIT),
    )(*arguments)


def local_fast(
    block_in,
    cotangent,
    w_qkv,
    w_out,
    w_fc,
    w_proj,
    vectors,
    qkv_first,
    qkv_second,
    out_first,
    out_second,
    fc_first,
    fc_second,
    proj_first,
    proj_second,
    vec_first,
    vec_second,
):
    batch, ctx = lax.axis_index("batch"), lax.axis_index("ctx")
    meta = jnp.stack([batch, ctx]).astype(jnp.int32)
    inputs = block_in.reshape(TOKENS, WIDTH)
    grad_low = cotangent.reshape(TOKENS, WIDTH)
    tie = lax.optimization_barrier

    qkv_sems = pltpu.SemaphoreType.DMA((1, BATCH * CTX))
    mlp_sems = pltpu.SemaphoreType.DMA((4, BATCH * CTX))
    qkv_held = pltpu.VMEM((CTX, WIDTH, 3 * GROUP), LOW)
    vec_held = pltpu.VMEM((CTX, 16, GROUP), WIDE)

    low_vec = jnp.pad(vectors.astype(LOW), ((0, 4), (0, 0)))
    low_vec = [low_vec[:, start : start + HEAD] for start in range(0, GROUP, HEAD)]
    low_vec = jnp.concatenate(low_vec + [jnp.zeros((ROWS - 48, HEAD), LOW)], axis=0)
    piece_one = jnp.concatenate([w_qkv.astype(LOW), low_vec], axis=1)
    low_proj = w_proj.astype(LOW).T
    piece_two = jnp.concatenate(
        [
            w_fc.astype(LOW),
            low_proj[:ROWS],
            low_proj[ROWS:],
            w_out.astype(LOW),
            jnp.zeros((ROWS, TILE - GROUP), LOW),
        ],
        axis=1,
    )
    near = jnp.stack([piece_one, swap(piece_one, "ctx", 2)])
    far = swap(near, "ctx", 1)
    own_one = jnp.concatenate([near, far], axis=0)[:, :, : 3 * GROUP]
    piece_two, late = tie((piece_two, far))
    vec_parts = [part[:48, 3 * GROUP :] for part in (near[0], late[0], near[1], late[1])]
    x_one, y_one = gather_first(own_one)
    across_one = gather_second(x_one, y_one)
    near, far = swap(piece_two, "ctx", 1), swap(piece_two, "ctx", 2)
    near, far, across_one = tie((near, far, across_one))
    last = swap(far, "ctx", 1)
    parts_one = [own_one, x_one, y_one, *across_one]
    parts_one = parts_one + to_core(parts_one)
    last, parts_one = tie((last, parts_one))
    own_two = jnp.stack([piece_two, far, near, last])
    x_two, y_two = gather_first(own_two)

    packed = shape_of(LOW, TOKENS * 3 * GROUP // LANES, LANES)
    single = shape_of(LOW, TOKENS * GROUP // LANES, LANES)
    tokens_low = shape_of(LOW, TOKENS, WIDTH)
    hidden_low = shape_of(LOW, CTX, TOKENS, WIDTH)
    h_one, own, *sent = call(
        qkv_kernel,
        (meta, inputs, *vec_parts, *parts_one),
        "s" + "v" * 5 + "a" * PARTS,
        [tokens_low] + [packed] * 4,
        "v" * 5,
        [qkv_held, pltpu.VMEM((CTX, TOKENS, 3 * GROUP), LOW), vec_held, qkv_sems],
    )
    qkv_pieces = [own] + [swap(part, "ctx", bit) for bit, part in zip((1, 2, 3), sent)]

    qkv_pieces, x_two, y_two = tie((qkv_pieces, x_two, y_two))
    across_two = gather_second(x_two, y_two)
    parts_two = [own_two, x_two, y_two]
    swapped_two = to_core(parts_two)

    sequence_low = pltpu.VMEM((SPAN, GROUP), LOW)
    sequence_wide = pltpu.VMEM((SPAN, GROUP), WIDE)
    own, *sent = call(
        attend_kernel,
        (meta, *qkv_pieces),
        "s" + "v" * 4,
        [single] * 4,
        "v" * 4,
        [sequence_low] * 3 + [sequence_wide],
    )
    sent, swapped_two = tie((sent, swapped_two))
    att_pieces = [own] + [swap(part, "ctx", bit) for bit, part in zip((1, 2, 3), sent)]
    across_two, att_pieces = tie((across_two, att_pieces))
    parts_two = parts_two + list(across_two) + swapped_two + to_core(across_two)

    pack_shape = shape_of(LOW, CTX + 5, TOKENS, WIDTH)
    act_shape = shape_of(LOW, BATCH // 2, TOKENS, FF_SIDE)
    out, pack, act_mine, act_theirs, dmid, own, *sent = call(
        middle_kernel,
        (meta, inputs, grad_low, h_one, *vec_parts, *att_pieces, *parts_two),
        "s" + "v" * 11 + "a" * PARTS,
        [tokens_low, pack_shape, act_shape, act_shape, shape_of(WIDE, TOKENS, WIDTH)]
        + [single] * 4
        + [shape_of(WIDE, 8, WIDTH), shape_of(WIDE, CTX, 1, WIDTH)],
        "v" * 11,
        [
            pltpu.VMEM((CTX, WIDTH, TILE), LOW),
            pltpu.VMEM((WIDTH, WIDTH), LOW),
            pltpu.VMEM((CTX, WIDTH, WIDTH), LOW),
            pltpu.VMEM((BATCH, WIDTH, FF_SIDE), LOW),
            pltpu.VMEM((CTX, TOKENS, GROUP), LOW),
            pltpu.VMEM((TOKENS, WIDTH), WIDE),
            pltpu.VMEM((TOKENS, WIDTH), WIDE),
            vec_held,
            pltpu.VMEM((CTX, 1, WIDTH), WIDE),
            pltpu.VMEM((BATCH, TOKENS, FF_SIDE), LOW),
            mlp_sems,
        ],
    )
    sent, (rows_two, dbias_fc) = sent[:3], sent[3:]
    grad_pieces = [own] + [swap(part, "ctx", bit) for bit, part in zip((1, 2, 3), sent)]
    act_came, pack_came = swap(act_theirs, "batch", CORE), swap(pack, "batch", CORE)

    half_sems = BATCH * CTX // 2
    turn_held = pltpu.VMEM((2, WIDTH, TOKENS), LOW)
    mlp_parts = call(
        mlp_grad_kernel,
        (meta, act_mine, act_came, pack, pack_came),
        "s" + "v" * 4,
        [shape_of(LOW, 2, 2, ROWS, MLP)] * 4,
        "aaaa",
        [
            pltpu.VMEM((CTX, WIDTH // 2, TILE), LOW),
            pltpu.VMEM((CTX, WIDTH // 2, WIDTH), LOW),
            pltpu.VMEM((BATCH // 2, WIDTH, FF_SIDE), LOW),
            turn_held,
            pltpu.SemaphoreType.DMA((4, half_sems)),
        ],
    )
    mlp_parts, grad_pieces = tie((mlp_parts, grad_pieces))
    mlp_kept = mlp_parts[0], mlp_parts[2]
    mlp_back = swap_pair((mlp_parts[1], mlp_parts[3]), YBIT, XBIT)
    own, *sent = call(
        attend_back_kernel,
        (meta, *qkv_pieces, *grad_pieces),
        "s" + "v" * 8,
        [packed] * 4,
        "v" * 4,
        [sequence_low] * 4 + [sequence_wide] * 3,
    )
    own_came = swap(own, "batch", CORE)
    received = [swap(part, "ctx", bit) for bit, part in zip((1, 2, 3), sent)]
    mlp_back, received[0] = tie((mlp_back, received[0]))
    pair = [shape_of(WIDE, 2, ROWS, MLP), shape_of(LOW, 2, ROWS, MLP)]
    one_keep, one_send, two_keep, two_send = call(
        sum_kernel,
        (mlp_kept[0], mlp_back[0], mlp_kept[1], mlp_back[1]),
        "vvvv",
        pair + pair,
        "vvvv",
        [],
    )
    one_keep, received[1], received[2] = tie((one_keep, received[1], received[2]))
    mlp_back = swap_pair((one_send, two_send), XBIT, YBIT)
    received = jnp.stack(received)
    received_came = swap(received, "batch", CORE)

    *qkv_parts, mixed, dbias_qkv = call(
        qkv_grad_kernel,
        (meta, pack, pack_came, own, own_came, received, received_came),
        "shhvvvv",
        [shape_of(LOW, 2, 2, ROWS, 3 * GROUP)] * 4
        + [shape_of(LOW, CTX, TOKENS, 3 * GROUP), shape_of(WIDE, 3 * CTX, 1, GROUP)],
        "aaaavv",
        [
            pltpu.VMEM((CTX, WIDTH // 2, 3 * GROUP), LOW),
            pltpu.VMEM((2, 3 * CTX, TOKENS, GROUP), LOW),
            turn_held,
            pltpu.SemaphoreType.DMA((1, half_sems)),
        ],
    )
    qkv_kept = qkv_parts[0], qkv_parts[2]
    qkv_kept = qkv_parts[0], qkv_parts[2]
    qkv_back = swap_pair((qkv_parts[1], qkv_parts[3]), YBIT, XBIT)
    grad_input, vec_one, vec_two = call(
        input_grad_kernel,
        (meta, inputs, dmid, mixed, rows_two, dbias_fc, dbias_qkv, *vec_parts, *parts_one),
        "s" + "v" * 10 + "a" * PARTS,
        [shape_of(WIDE, TOKENS, WIDTH)] + [shape_of(WIDE, 2, 16, GROUP)] * 2,
        "vvv",
        [qkv_held, vec_held, pltpu.VMEM((16, WIDTH), WIDE), vec_held, qkv_sems],
        moved=40_000_000,
    )
    mlp_back, vec_one, vec_two = tie((mlp_back, vec_one, vec_two))
    mlp_one, mlp_two = call(
        near_kernel, (one_keep, mlp_back[0], two_keep, mlp_back[1]), "vvvv", pair, "vv", []
    )
    mlp_one, vec_two = tie((mlp_one, vec_two))
    mlp_two = swap(mlp_two, "ctx", 1)
    vec_grad = vec_one + swap(vec_two, "ctx", 1)
    mlp_one, qkv_back, vec_grad = tie((mlp_one, qkv_back, vec_grad))
    qkv_kept, qkv_sent = scatter_second(qkv_kept, qkv_back)
    qkv_back = swap_pair(qkv_sent, XBIT, YBIT)
    qkv_one, qkv_two = scatter_near(qkv_kept, tie(qkv_back))
    mlp_one = mlp_one + mlp_two.astype(WIDE)
    mlp_far = mlp_one[1].astype(LOW)
    mlp_far, qkv_two, vec_grad = tie((mlp_far, qkv_two, vec_grad))
    mlp_far = swap(mlp_far, "ctx", 2)
    qkv_grad = scatter_far(qkv_one, qkv_two)
    vec_grad = vec_grad[0] + swap(vec_grad[1], "ctx", 2)
    vec_grad = vec_grad + swap(vec_grad, "batch", CORE)
    mlp_far, vec_grad = tie((mlp_far, vec_grad))
    mlp_grad = mlp_one[0] + mlp_far.astype(WIDE)
    for bit in (XBIT, YBIT):
        vec_grad = vec_grad + swap(vec_grad, "batch", bit)
    vec_grad = vec_grad[:12]
    fc_grad = mlp_grad[:, :WIDTH]
    proj_grad = jnp.concatenate(
        [mlp_grad[:, WIDTH : WIDTH + FF_SIDE], mlp_grad[:, WIDTH + FF_SIDE : WIDTH + 2 * FF_SIDE]],
        axis=0,
    )
    out_grad = mlp_grad[:, WIDTH + 2 * FF_SIDE : WIDTH + 2 * FF_SIDE + GROUP]

    qkv_m, qkv_s, qkv_w = adamw(w_qkv, qkv_grad, qkv_first, qkv_second, 0.06, 0.1)
    out_m, out_s, out_w = adamw(w_out, out_grad, out_first, out_second, 0.06, 0.1)
    fc_m, fc_s, fc_w = adamw(w_fc, fc_grad, fc_first, fc_second, 0.06, 0.1)
    proj_m, proj_s, proj_w = adamw(w_proj, proj_grad.T, proj_first, proj_second, 0.06, 0.1)
    vec_m, vec_s, vec_w = adamw(vectors, vec_grad, vec_first, vec_second, 0.2, 0.0)
    return (
        out.reshape(block_in.shape),
        grad_input.reshape(block_in.shape),
        qkv_m,
        qkv_s,
        qkv_w,
        out_m,
        out_s,
        out_w,
        fc_m,
        fc_s,
        fc_w,
        proj_m,
        proj_s,
        proj_w,
        vec_m,
        vec_s,
        vec_w,
    )


def solution(mesh):
    in_specs = (
        P("batch", "ctx", None, None),
        P("batch", "ctx", None, None),
        P("batch", "ctx"),
        P("batch", "ctx"),
        P("batch", "ctx"),
        P("batch", "ctx"),
        P(None, "ctx"),
        P("batch", "ctx"),
        P("batch", "ctx"),
        P("batch", "ctx"),
        P("batch", "ctx"),
        P("batch", "ctx"),
        P("batch", "ctx"),
        P("batch", "ctx"),
        P("batch", "ctx"),
        P(None, "ctx"),
        P(None, "ctx"),
    )
    out_specs = (
        P("batch", "ctx", None, None),
        P("batch", "ctx", None, None),
        P("batch", "ctx"),
        P("batch", "ctx"),
        P("batch", "ctx"),
        P("batch", "ctx"),
        P("batch", "ctx"),
        P("batch", "ctx"),
        P("batch", "ctx"),
        P("batch", "ctx"),
        P("batch", "ctx"),
        P("batch", "ctx"),
        P("batch", "ctx"),
        P("batch", "ctx"),
        P(None, "ctx"),
        P(None, "ctx"),
        P(None, "ctx"),
    )
    sizes = (mesh.shape["batch"], mesh.shape["ctx"])
    local = local_fast if sizes == (BATCH, CTX) else local_any
    return jax.shard_map(local, mesh=mesh, in_specs=in_specs, out_specs=out_specs, check_vma=False)
```

```python
import functools
import math

import jax
import jax.numpy as jnp
from jax import lax
from jax.experimental import pallas as pl
from jax.experimental.pallas import tpu as pltpu
from jax.sharding import PartitionSpec as P

HEADS = 12
STEP = 10


def layer_norm(value, gain, shift):
    mean = jnp.mean(value, axis=-1, keepdims=True)
    centred = value - mean
    spread = jnp.mean(centred * centred, axis=-1, keepdims=True)
    return centred * lax.rsqrt(spread + 1e-05) * gain + shift


def gelu_tanh(value):
    return (
        0.5
        * value
        * (1.0 + jnp.tanh(0.7978845608028654 * (value + 0.044715 * value * value * value)))
    )


def block_places(index, count, half):
    offsets = jnp.arange(half, dtype=jnp.int32)
    first = index * half + offsets
    second = (2 * count - 1 - index) * half + offsets
    return jnp.concatenate([first, second])


def scores_of(queries, keys, scale, allowed):
    raw = jnp.einsum("sqhd,skhd->shqk", queries, keys, preferred_element_type=jnp.float32) * scale
    return jnp.where(allowed[None, None], raw, -1e30)


def pair_grads(queries, grads, keys, values, top, total, delta, scale, allowed):
    score = scores_of(queries, keys, scale, allowed)
    weights = jnp.exp(score - top[..., None]) / total[..., None]
    back_weights = jnp.einsum("sqhd,skhd->shqk", grads, values, preferred_element_type=jnp.float32)
    grad_score = (weights * (back_weights - delta[..., None])).astype(jnp.bfloat16)
    return (weights.astype(jnp.bfloat16), grad_score)


def rows_product(left, right):
    return jnp.einsum("ra,rb->ab", left, right, preferred_element_type=jnp.float32)


def back_product(grad, weight):
    return jnp.einsum("rb,ab->ra", grad, weight, preferred_element_type=jnp.float32)


def adamw(weight, grad, first, second, rate, decay):
    first = 0.9 * first + 0.1 * grad
    second = 0.999 * second + 0.001 * grad * grad
    first_hat = first / (1.0 - 0.9**STEP)
    second_hat = second / (1.0 - 0.999**STEP)
    weight = weight - rate * (first_hat / (jnp.sqrt(second_hat) + 1e-08) + decay * weight)
    return (first, second, weight)


def local_any(
    block_in,
    cotangent,
    w_qkv,
    w_out,
    w_fc,
    w_proj,
    vectors,
    qkv_first,
    qkv_second,
    out_first,
    out_second,
    fc_first,
    fc_second,
    proj_first,
    proj_second,
    vec_first,
    vec_second,
):
    low_type = jnp.bfloat16
    wide = jnp.float32
    row_parts = (
        lax.all_gather(w_qkv.astype(low_type), "batch", axis=0, tiled=True),
        lax.all_gather(w_out.astype(low_type), "batch", axis=0, tiled=True),
        lax.all_gather(w_fc.astype(low_type), "batch", axis=0, tiled=True),
        lax.all_gather(w_proj.astype(low_type), "batch", axis=0, tiled=True),
    )
    full_qkv, full_out, full_fc, full_proj, full_vec = (
        lax.all_gather(row_parts[0], "ctx", axis=1, tiled=True),
        lax.all_gather(row_parts[1], "ctx", axis=1, tiled=True),
        lax.all_gather(row_parts[2], "ctx", axis=1, tiled=True),
        lax.all_gather(row_parts[3], "ctx", axis=1, tiled=True),
        lax.all_gather(vectors.astype(low_type), "ctx", axis=1, tiled=True),
    )
    params = full_vec.astype(wide)
    seqs, pair, half, width = block_in.shape
    heads = HEADS
    head = width // heads
    rows = seqs * pair * half
    span = pair * half
    count = lax.axis_size("ctx")
    index = lax.axis_index("ctx")
    scale = 1.0 / math.sqrt(head)
    inputs = block_in.astype(wide).reshape(rows, width)
    normed_one = layer_norm(inputs, params[0], params[1]).astype(low_type)
    mixed = jnp.dot(normed_one, full_qkv, preferred_element_type=wide)
    queries = (mixed[:, :width] + params[4]).astype(low_type)
    keys = mixed[:, width : 2 * width].astype(low_type)
    values = (mixed[:, 2 * width :] + params[5]).astype(low_type)
    key_all, value_all = (
        lax.all_gather(keys.reshape(seqs, pair, half, width), "ctx", axis=1, tiled=True),
        lax.all_gather(values.reshape(seqs, pair, half, width), "ctx", axis=1, tiled=True),
    )
    query_heads = queries.reshape(seqs, span, heads, head)
    own_places = block_places(index, count, half)

    def piece_of(source, piece):
        return lax.dynamic_slice_in_dim(source, 2 * piece, 2, 1).reshape(seqs, span, heads, head)

    def allowed_for(piece):
        return own_places[:, None] >= block_places(piece, count, half)[None, :]

    def stats_step(piece, carry):
        top, total = carry
        score = scores_of(query_heads, piece_of(key_all, piece), scale, allowed_for(piece))
        new_top = jnp.maximum(top, jnp.max(score, axis=-1))
        total = total * jnp.exp(top - new_top) + jnp.sum(
            jnp.exp(score - new_top[..., None]), axis=-1
        )
        return (new_top, total)

    start_stats = (jnp.full((seqs, heads, span), -1e30, wide), jnp.zeros((seqs, heads, span), wide))
    top, total = lax.fori_loop(0, count, stats_step, start_stats)

    def output_step(piece, acc):
        score = scores_of(query_heads, piece_of(key_all, piece), scale, allowed_for(piece))
        weights = (jnp.exp(score - top[..., None]) / total[..., None]).astype(low_type)
        return acc + jnp.einsum(
            "shqk,skhd->sqhd", weights, piece_of(value_all, piece), preferred_element_type=wide
        )

    attended = lax.fori_loop(0, count, output_step, jnp.zeros((seqs, span, heads, head), wide))
    att_low = attended.reshape(rows, width).astype(low_type)
    mid = inputs + jnp.dot(att_low, full_out, preferred_element_type=wide) + params[6]
    normed_two = layer_norm(mid, params[2], params[3]).astype(low_type)
    pre = jnp.dot(normed_two, full_fc, preferred_element_type=wide) + params[8:12].reshape(-1)
    act_low = gelu_tanh(pre).astype(low_type)
    result = mid + jnp.dot(act_low, full_proj, preferred_element_type=wide) + params[7]
    out_block = result.astype(low_type).reshape(block_in.shape)
    grad_low = cotangent.reshape(rows, width)
    grad_out = grad_low.astype(wide)
    grad_wproj = rows_product(act_low, grad_low)
    back_act = back_product(grad_low, full_proj)
    grad_pre = jax.vjp(gelu_tanh, pre)[1](back_act)[0].astype(low_type)
    grad_wfc = rows_product(normed_two, grad_pre)
    back_two = back_product(grad_pre, full_fc)
    back_mid, grad_gain_two, grad_shift_two = jax.vjp(layer_norm, mid, params[2], params[3])[1](
        back_two
    )
    grad_mid = grad_out + back_mid
    grad_att_low = grad_mid.astype(low_type)
    grad_wout = rows_product(att_low, grad_att_low)
    back_att = back_product(grad_att_low, full_out)
    grad_heads = back_att.astype(low_type).reshape(seqs, span, heads, head)
    delta = jnp.einsum("sqhd,sqhd->shq", grad_heads.astype(wide), attended)
    query_all, grad_all = (
        lax.all_gather(queries.reshape(seqs, pair, half, width), "ctx", axis=1, tiled=True),
        lax.all_gather(grad_heads.reshape(seqs, pair, half, width), "ctx", axis=1, tiled=True),
    )
    top_all, total_all, delta_all = (
        lax.all_gather(top.reshape(seqs, heads, pair, half), "ctx", axis=2, tiled=True),
        lax.all_gather(total.reshape(seqs, heads, pair, half), "ctx", axis=2, tiled=True),
        lax.all_gather(delta.reshape(seqs, heads, pair, half), "ctx", axis=2, tiled=True),
    )

    def query_step(piece, grad_query):
        key_part = piece_of(key_all, piece)
        value_part = piece_of(value_all, piece)
        weights_low, grad_score = pair_grads(
            query_heads,
            grad_heads,
            key_part,
            value_part,
            top,
            total,
            delta,
            scale,
            allowed_for(piece),
        )
        return grad_query + jnp.einsum(
            "shqk,skhd->sqhd", grad_score, key_part, preferred_element_type=wide
        )

    grad_query = lax.fori_loop(0, count, query_step, jnp.zeros((seqs, span, heads, head), wide))
    key_heads = keys.reshape(seqs, span, heads, head)
    value_heads = values.reshape(seqs, span, heads, head)

    def stat_piece(source, piece):
        return lax.dynamic_slice_in_dim(source, 2 * piece, 2, 2).reshape(seqs, heads, span)

    def key_step(piece, carry):
        grad_key, grad_value = carry
        query_part = piece_of(query_all, piece)
        grad_part = piece_of(grad_all, piece)
        allowed = block_places(piece, count, half)[:, None] >= own_places[None, :]
        weights_low, grad_score = pair_grads(
            query_part,
            grad_part,
            key_heads,
            value_heads,
            stat_piece(top_all, piece),
            stat_piece(total_all, piece),
            stat_piece(delta_all, piece),
            scale,
            allowed,
        )
        grad_key = grad_key + jnp.einsum(
            "shqk,sqhd->skhd", grad_score, query_part, preferred_element_type=wide
        )
        grad_value = grad_value + jnp.einsum(
            "shqk,sqhd->skhd", weights_low, grad_part, preferred_element_type=wide
        )
        return (grad_key, grad_value)

    start_keys = (
        jnp.zeros((seqs, span, heads, head), wide),
        jnp.zeros((seqs, span, heads, head), wide),
    )
    grad_key, grad_value = lax.fori_loop(0, count, key_step, start_keys)
    grad_keys = (grad_key * scale).reshape(seqs, pair, half, width)
    grad_values = grad_value.reshape(seqs, pair, half, width)
    grad_q_low = (grad_query * scale).reshape(rows, width).astype(low_type)
    grad_k_low = grad_keys.reshape(rows, width).astype(low_type)
    grad_v_low = grad_values.reshape(rows, width).astype(low_type)
    grad_mixed = jnp.concatenate([grad_q_low, grad_k_low, grad_v_low], axis=1)
    grad_wqkv = rows_product(normed_one, grad_mixed)
    back_one = back_product(grad_mixed, full_qkv)
    back_in, grad_gain_one, grad_shift_one = jax.vjp(layer_norm, inputs, params[0], params[1])[1](
        back_one
    )
    grad_input = (grad_mid + back_in).reshape(block_in.shape)
    grad_bias_q = jnp.sum(grad_q_low.astype(wide), axis=0)
    grad_bias_v = jnp.sum(grad_v_low.astype(wide), axis=0)
    grad_bias_out = jnp.sum(grad_att_low.astype(wide), axis=0)
    grad_bias_proj = jnp.sum(grad_out, axis=0)
    grad_bias_fc = jnp.sum(grad_pre.astype(wide), axis=0).reshape(4, width)
    small_rows = jnp.stack(
        [
            grad_gain_one,
            grad_shift_one,
            grad_gain_two,
            grad_shift_two,
            grad_bias_q,
            grad_bias_v,
            grad_bias_out,
            grad_bias_proj,
        ]
    )
    grad_vectors = jnp.concatenate([small_rows, grad_bias_fc], axis=0)
    col_sums = (
        lax.psum_scatter(grad_wqkv, "ctx", scatter_dimension=1, tiled=True),
        lax.psum_scatter(grad_wout, "ctx", scatter_dimension=1, tiled=True),
        lax.psum_scatter(grad_wfc, "ctx", scatter_dimension=1, tiled=True),
        lax.psum_scatter(grad_wproj, "ctx", scatter_dimension=1, tiled=True),
        lax.psum_scatter(grad_vectors, "ctx", scatter_dimension=1, tiled=True),
    )
    qkv_grad, out_grad, fc_grad, proj_grad = (
        lax.psum_scatter(col_sums[0], "batch", scatter_dimension=0, tiled=True),
        lax.psum_scatter(col_sums[1], "batch", scatter_dimension=0, tiled=True),
        lax.psum_scatter(col_sums[2], "batch", scatter_dimension=0, tiled=True),
        lax.psum_scatter(col_sums[3], "batch", scatter_dimension=0, tiled=True),
    )
    vec_grad = lax.psum(col_sums[4], "batch")
    qkv_m, qkv_s, qkv_w = adamw(w_qkv, qkv_grad, qkv_first, qkv_second, 0.06, 0.1)
    out_m, out_s, out_w = adamw(w_out, out_grad, out_first, out_second, 0.06, 0.1)
    fc_m, fc_s, fc_w = adamw(w_fc, fc_grad, fc_first, fc_second, 0.06, 0.1)
    proj_m, proj_s, proj_w = adamw(w_proj, proj_grad, proj_first, proj_second, 0.06, 0.1)
    vec_m, vec_s, vec_w = adamw(vectors, vec_grad, vec_first, vec_second, 0.2, 0.0)
    return (
        out_block,
        grad_input,
        qkv_m,
        qkv_s,
        qkv_w,
        out_m,
        out_s,
        out_w,
        fc_m,
        fc_s,
        fc_w,
        proj_m,
        proj_s,
        proj_w,
        vec_m,
        vec_s,
        vec_w,
    )


BATCH = 8
CTX = 4
WIDTH = 768
HEAD = 64
GROUP = WIDTH // CTX
TOKENS = 256
HALF = 128
FF_SIDE = 384
ROWS = WIDTH // BATCH
MLP = WIDTH + 2 * FF_SIDE + 256
SPAN = TOKENS * CTX
TILE = 256
LOW = jnp.bfloat16
WIDE = jnp.float32
CORE, XBIT, YBIT = 1, 2, 4
PLACES = (0, 2, 1, 3)
SOURCES = (
    (0, PLACES),
    (XBIT, PLACES),
    (YBIT, PLACES),
    (XBIT + YBIT, PLACES[:2]),
    (XBIT + YBIT, PLACES[2:]),
    (CORE, PLACES),
    (CORE + XBIT, PLACES),
    (CORE + YBIT, PLACES),
    (CORE + XBIT + YBIT, PLACES[:2]),
    (CORE + XBIT + YBIT, PLACES[2:]),
)
PARTS = len(SOURCES)
VMEM_LIMIT = 56 * 1024 * 1024


def swap(value, axis, bit):
    size = BATCH if axis == "batch" else CTX
    return lax.ppermute(value, axis, [(i, i ^ bit) for i in range(size)])


def mm(left, right):
    return lax.dot_general(left, right, (((1,), (0,)), ((), ())), preferred_element_type=WIDE)


def mt(left, right):
    return lax.dot_general(left, right, (((1,), (1,)), ((), ())), preferred_element_type=WIDE)


def tm(left, right):
    return lax.dot_general(left, right, (((0,), (0,)), ((), ())), preferred_element_type=WIDE)


def turned(value):
    return value.T


def moments(value):
    mean = jnp.mean(value, axis=-1, keepdims=True)
    centred = value - mean
    spread = jnp.mean(centred * centred, axis=-1, keepdims=True)
    return centred, lax.rsqrt(spread + 1e-05)


def norm_back(grad, normed, inverse, gain):
    part = grad * gain
    mean = jnp.mean(part, axis=-1, keepdims=True)
    cross = jnp.mean(part * normed, axis=-1, keepdims=True)
    return inverse * (part - mean - normed * cross)


def gather_first(own):
    return swap(own, "batch", XBIT), swap(own, "batch", YBIT)


def gather_second(from_x, from_y):
    return swap(from_x[:2], "batch", YBIT), swap(from_y[2:], "batch", XBIT)


def to_core(parts):
    return [swap(part, "batch", CORE) for part in parts]


def swap_pair(pair, first, second):
    return swap(pair[0], "batch", first), swap(pair[1], "batch", second)


def scatter_second(kept, back):
    one = kept[0].astype(WIDE) + back[0].astype(WIDE)
    two = kept[1].astype(WIDE) + back[1].astype(WIDE)
    return (one[0], two[0]), (one[1].astype(LOW), two[1].astype(LOW))


def scatter_near(kept, back):
    one = kept[0].astype(WIDE) + back[0].astype(WIDE)
    two = (kept[1].astype(WIDE) + back[1].astype(WIDE)).astype(LOW)
    return one, swap(two, "ctx", 1)


def scatter_far(one, two):
    one = one + two.astype(WIDE)
    return one[0] + swap(one[1].astype(LOW), "ctx", 2).astype(WIDE)


def rows_of(index, size):
    return pl.ds(pl.multiple_of(index * size, 16), size)


def qkv_place(held, batch, ctx):
    return [(pl.ds(0, 3 * GROUP), held.at[ctx, rows_of(batch, ROWS), :])]


def mlp_place(held_out, held_fc, held_proj, batch, ctx):
    return [
        (pl.ds(WIDTH + 2 * FF_SIDE, TILE), held_out.at[ctx, rows_of(batch, ROWS), :]),
        (pl.ds(0, WIDTH), held_fc.at[ctx, rows_of(batch, ROWS), :]),
        (pl.ds(WIDTH, FF_SIDE), held_proj.at[batch, rows_of(2 * ctx, ROWS), :]),
        (pl.ds(WIDTH + FF_SIDE, FF_SIDE), held_proj.at[batch, rows_of(2 * ctx + 1, ROWS), :]),
    ]


def load_weight(meta, parts, place, sems):
    copies = []
    for part, (source, places) in zip(parts, SOURCES):
        for index, ctx in enumerate(places):
            ranges = place(meta[0] ^ source, meta[1] ^ ctx)
            copies.append([(part.at[index, :, lanes], target) for lanes, target in ranges])
    started = []
    for kind in range(len(copies[0])):
        group = []
        for number, copy in enumerate(copies):
            group.append(pltpu.make_async_copy(*copy[kind], sems.at[kind, number]))
            group[-1].start()
        started.append(group)
    return started


def store_grad(held, targets, sems, kinds):
    one_kept, one_sent, two_kept, two_sent = targets
    copies = []
    for y in range(2):
        for x in range(2):
            for index, ctx in enumerate(PLACES):
                if index < 2:
                    target = (one_sent if y else one_kept).at[x, index]
                else:
                    target = (two_sent if x else two_kept).at[y, index - 2]
                ranges = held(2 * y + x, ctx)
                for kind in kinds:
                    lanes, source = ranges[kind]
                    number = (2 * y + x) * CTX + ctx
                    copies.append(
                        pltpu.make_async_copy(source, target.at[:, lanes], sems.at[kind, number])
                    )
                    copies[-1].start()
    return copies


def half_rows(meta, pair, held):
    for index, value in enumerate(pair):
        held[index] = turned(value)
    parts = []
    for index in range(2):
        rows = [held[index, rows_of(meta[0] ^ (2 * part), ROWS), :] for part in range(BATCH // 2)]
        parts.append(jnp.concatenate(rows, axis=0))
    return parts


def over_both(left, right):
    return mm(left[0], right[0]) + mm(left[1], right[1])


def wait_all(copies):
    for copy in copies:
        copy.wait()


LANES = 128


def write_packed(target, value):
    full = value.shape[1] // LANES
    for index in range(full):
        target[index * TOKENS : (index + 1) * TOKENS, :] = value[
            :, index * LANES : (index + 1) * LANES
        ]
    rest = value[:, full * LANES :]
    target[full * TOKENS :, :] = jnp.concatenate([rest[:HALF], rest[HALF:]], axis=1)


def read_packed(source):
    full = source.shape[0] // TOKENS
    parts = [source[index * TOKENS : (index + 1) * TOKENS, :] for index in range(full)]
    rest = source[full * TOKENS :, :]
    parts.append(jnp.concatenate([rest[:, : LANES // 2], rest[:, LANES // 2 :]], axis=0))
    return jnp.concatenate(parts, axis=1)


def in_place(ctx, block):
    first = ctx if block == 0 else 2 * CTX - 1 - ctx
    return pl.ds(pl.multiple_of(first * HALF, HALF), HALF)


def read_vectors(meta, parts, chunks):
    for ctx, part in enumerate(parts):
        rows = [part[16 * index : 16 * (index + 1), :] for index in range(GROUP // HEAD)]
        chunks[meta[1] ^ ctx] = jnp.concatenate(rows, axis=1).astype(WIDE)
    return jnp.concatenate([chunks[index] for index in range(CTX)], axis=1)


def qkv_kernel(meta, x_ref, *refs):
    vectors, parts, refs = refs[:4], refs[4 : 4 + PARTS], refs[4 + PARTS :]
    h_ref, own, near, far, last, held, units, chunks, sems = refs
    (copies,) = load_weight(meta, parts, functools.partial(qkv_place, held), sems)
    params = read_vectors(meta, vectors, chunks)
    bias = jnp.concatenate([params[4:5], jnp.zeros((1, WIDTH), WIDE), params[5:6]], axis=1)
    centred, inverse = moments(x_ref[...].astype(WIDE))
    normed = (centred * inverse * params[0:1] + params[1:2]).astype(LOW)
    h_ref[...] = normed
    wait_all(copies)
    for chunk in range(CTX):
        mixed = mm(normed, held[chunk]) + bias[:, 3 * GROUP * chunk : 3 * GROUP * (chunk + 1)]
        mixed = mixed.astype(LOW)
        for part in range(3):
            unit = 3 * chunk + part
            units[unit % CTX, :, (unit // CTX) * GROUP : (unit // CTX + 1) * GROUP] = mixed[
                :, part * GROUP : (part + 1) * GROUP
            ]
    for ctx, target in enumerate((own, near, far, last)):
        write_packed(target, units[meta[1] ^ ctx])


def read_sequence(meta, pieces, targets):
    for ctx, piece in enumerate(pieces):
        value = read_packed(piece)
        for block in range(2):
            place = in_place(meta[1] ^ ctx, block)
            rows = value[block * HALF : (block + 1) * HALF, :]
            for index, target in enumerate(targets):
                target[place, :] = rows[:, index * GROUP : (index + 1) * GROUP]


def write_sequence(meta, pieces, sources):
    for ctx, piece in enumerate(pieces):
        parts = []
        for source in sources:
            blocks = [source[in_place(meta[1] ^ ctx, block), :] for block in range(2)]
            parts.append(jnp.concatenate(blocks, axis=0).astype(LOW))
        write_packed(piece, jnp.concatenate(parts, axis=1))


def head_mask(head, scale=1.0):
    lane = lax.broadcasted_iota(jnp.int32, (1, GROUP), 1)
    inside = (lane >= head * HEAD) & (lane < (head + 1) * HEAD)
    return jnp.where(inside, scale, 0.0).astype(LOW)


def tile_of(index):
    return slice(index * TILE, (index + 1) * TILE)


def weights_of(queries, k_seq, tile, causal):
    scores = [mt(queries, k_seq[tile_of(other), :]) for other in range(tile + 1)]
    scores[tile] = jnp.where(causal, scores[tile], -1e30)
    top = jnp.max(functools.reduce(jnp.maximum, scores), axis=-1, keepdims=True)
    expo = [jnp.exp(score - top) for score in scores]
    total = jnp.sum(functools.reduce(jnp.add, expo), axis=-1, keepdims=True)
    inverse = 1.0 / total
    return [value * inverse for value in expo]


def causal_tile():
    row = lax.broadcasted_iota(jnp.int32, (TILE, TILE), 0)
    column = lax.broadcasted_iota(jnp.int32, (TILE, TILE), 1)
    return row >= column


def attend_kernel(meta, *refs):
    pieces, results, (q_seq, k_seq, v_seq, out) = refs[:4], refs[4:8], refs[8:]
    read_sequence(meta, pieces, (q_seq, k_seq, v_seq))
    causal = causal_tile()
    scale = 1.0 / math.sqrt(HEAD)
    for tile in range(SPAN // TILE):

        def one_head(head, total, tile=tile):
            mask = head_mask(head)
            queries = q_seq[tile_of(tile), :] * head_mask(head, scale)
            weights = weights_of(queries, k_seq, tile, causal)
            for other, weight in enumerate(weights):
                total = total + mm(weight.astype(LOW), v_seq[tile_of(other), :] * mask)
            return total

        out[tile_of(tile), :] = lax.fori_loop(
            0, GROUP // HEAD, one_head, jnp.zeros((TILE, GROUP), WIDE), unroll=True
        )
    write_sequence(meta, results, (out,))


def attend_back_kernel(meta, *refs):
    pieces, grads, results = refs[:4], refs[4:8], refs[8:12]
    q_seq, k_seq, v_seq, g_seq, dq, dk, dv = refs[12:]
    read_sequence(meta, pieces, (q_seq, k_seq, v_seq))
    read_sequence(meta, grads, (g_seq,))
    causal = causal_tile()
    scale = 1.0 / math.sqrt(HEAD)
    dk[...] = jnp.zeros_like(dk)
    dv[...] = jnp.zeros_like(dv)
    for tile in range(SPAN // TILE):

        def one_head(head, total, tile=tile):
            mask = head_mask(head)
            scaled = head_mask(head, scale)
            queries = q_seq[tile_of(tile), :] * scaled
            grad = g_seq[tile_of(tile), :] * mask
            weights = weights_of(queries, k_seq, tile, causal)
            backs = [mt(grad, v_seq[tile_of(other), :]) for other in range(tile + 1)]
            products = [weight * back for weight, back in zip(weights, backs)]
            delta = jnp.sum(functools.reduce(jnp.add, products), axis=-1, keepdims=True)
            for other, (weight, back) in enumerate(zip(weights, backs)):
                step = (weight * (back - delta)).astype(LOW)
                total = total + mm(step, k_seq[tile_of(other), :] * scaled)
                dk[tile_of(other), :] += tm(step, queries)
                dv[tile_of(other), :] += tm(weight.astype(LOW), grad)
            return total

        dq[tile_of(tile), :] = lax.fori_loop(
            0, GROUP // HEAD, one_head, jnp.zeros((TILE, GROUP), WIDE), unroll=True
        )
    write_sequence(meta, results, (dq, dk, dv))


def middle_kernel(meta, x_ref, dy_ref, h_one_ref, *refs):
    vectors, pieces, parts, refs = refs[:4], refs[4:8], refs[8 : 8 + PARTS], refs[8 + PARTS :]
    (out_ref, pack_ref, mine, theirs, dmid_ref), refs = refs[:5], refs[5:]
    results, (rows_ref, dbias_ref), refs = refs[:4], refs[4:6], refs[6:]
    out_parts, held_out, held_fc, held_proj, units, total, back, chunks, bias, acts, sems = refs
    place = functools.partial(mlp_place, out_parts, held_fc, held_proj)
    copies = load_weight(meta, parts, place, sems)
    vec = read_vectors(meta, vectors, chunks)
    for chunk in range(CTX):
        bias[chunk] = vec[8 + chunk : 9 + chunk]
    for ctx, piece in enumerate(pieces):
        units[meta[1] ^ ctx] = read_packed(piece)
    att = jnp.concatenate([units[index] for index in range(CTX)], axis=1)
    pack_ref[CTX + 1] = att
    pack_ref[CTX + 3] = dy_ref[...]
    pack_ref[CTX + 4] = h_one_ref[...]
    wait_all(copies[0])
    for chunk in range(CTX):
        held_out[:, chunk * GROUP : (chunk + 1) * GROUP] = out_parts[chunk, :, :GROUP]
    mid = x_ref[...].astype(WIDE) + mm(att, held_out[...]) + vec[6:7]
    centred, inverse = moments(mid)
    normed = centred * inverse
    pack_ref[CTX] = (normed * vec[2:3] + vec[3:4]).astype(LOW)
    total[...] = mid + vec[7:8]
    back[...] = jnp.zeros_like(back)
    for group in copies[1:]:
        wait_all(group)
    side = FF_SIDE

    def chunk_step(chunk, carry):
        pre = mm(pack_ref[CTX], held_fc[chunk]) + bias[chunk]
        square = pre * pre
        tanh = jnp.tanh(0.7978845608028654 * (pre + 0.044715 * square * pre))
        act = (0.5 * pre * (1.0 + tanh)).astype(LOW)
        slope = 0.5 * (1.0 + tanh) + 0.5 * pre * (1.0 - tanh * tanh) * (
            0.7978845608028654 * (1.0 + 3.0 * 0.044715 * square)
        )
        grads = []
        for half in range(2):
            weight = held_proj[2 * chunk + half]
            part = act[:, half * side : (half + 1) * side]
            acts[2 * chunk + half] = part
            total[...] += mt(part, weight)
            grads.append(mm(dy_ref[...], weight))
        dpre = (jnp.concatenate(grads, axis=1) * slope).astype(LOW)
        pack_ref[chunk] = dpre
        dbias_ref[chunk] = jnp.sum(dpre.astype(WIDE), axis=0, keepdims=True)
        back[...] += mt(dpre, held_fc[chunk])
        return carry

    lax.fori_loop(0, CTX, chunk_step, 0, unroll=True)
    out_ref[...] = total[...].astype(LOW)
    core = meta[0] & 1
    for chunk in range(CTX):
        mine[chunk] = acts[2 * chunk + core]
        theirs[chunk] = acts[2 * chunk + 1 - core]
    grad = back[...]
    dy = dy_ref[...].astype(WIDE)
    dmid = dy + norm_back(grad, normed, inverse, vec[2:3])
    dmid_ref[...] = dmid
    datt = dmid.astype(LOW)
    pack_ref[CTX + 2] = datt
    rows_ref[0:1] = jnp.sum(grad * normed, axis=0, keepdims=True)
    rows_ref[1:2] = jnp.sum(grad, axis=0, keepdims=True)
    rows_ref[2:3] = jnp.sum(datt.astype(WIDE), axis=0, keepdims=True)
    rows_ref[3:4] = jnp.sum(dy, axis=0, keepdims=True)
    rows_ref[4:8] = jnp.zeros((4, WIDTH), WIDE)
    dout = mt(datt, held_out[...]).astype(LOW)
    for index in range(CTX):
        units[index] = dout[:, index * GROUP : (index + 1) * GROUP]
    for ctx, target in enumerate(results):
        write_packed(target, units[meta[1] ^ ctx])


def mlp_grad_kernel(meta, *refs):
    acts, packs, targets = refs[:2], refs[2:4], refs[4:8]
    held_out, held_fc, held_proj, turn, sems = refs[8:]

    def place(part, ctx):
        ctx = meta[1] ^ ctx
        chunk = (meta[0] ^ (2 * part)) // 2
        rows = pl.ds(part * ROWS, ROWS)
        return [
            (pl.ds(WIDTH + 2 * FF_SIDE, TILE), held_out.at[ctx, rows, :]),
            (pl.ds(0, WIDTH), held_fc.at[ctx, rows, :]),
            (pl.ds(WIDTH, FF_SIDE), held_proj.at[chunk, rows_of(2 * ctx, ROWS), :]),
            (pl.ds(WIDTH + FF_SIDE, FF_SIDE), held_proj.at[chunk, rows_of(2 * ctx + 1, ROWS), :]),
        ]

    dy = [turned(pack[CTX + 3]) for pack in packs]
    for chunk in range(CTX):
        held_proj[chunk] = over_both(dy, [act[chunk] for act in acts]).astype(LOW)
    copies = store_grad(place, targets, sems, (2, 3))
    left = half_rows(meta, [pack[CTX] for pack in packs], turn)
    for chunk in range(CTX):
        held_fc[chunk] = over_both(left, [pack[chunk] for pack in packs]).astype(LOW)
    copies += store_grad(place, targets, sems, (1,))
    left = half_rows(meta, [pack[CTX + 1] for pack in packs], turn)
    grad = over_both(left, [pack[CTX + 2] for pack in packs]).astype(LOW)
    for chunk in range(CTX):
        held_out[chunk, :, :GROUP] = grad[:, chunk * GROUP : (chunk + 1) * GROUP]
        held_out[chunk, :, GROUP:] = jnp.zeros((WIDTH // 2, TILE - GROUP), LOW)

    wait_all(copies + store_grad(place, targets, sems, (0,)))


def qkv_grad_kernel(meta, *refs):
    pack, own, came, targets = refs[:2], refs[2:4], refs[4:6], refs[6:10]
    mixed_ref, dbias_ref, held, units, turn, sems = refs[10:]
    for core in range(2):
        for ctx in range(CTX):
            value = read_packed(own[core] if ctx == 0 else came[core].at[ctx - 1])
            for part in range(3):
                units[core, CTX * part + (meta[1] ^ ctx)] = value[
                    :, part * GROUP : (part + 1) * GROUP
                ]
    left = half_rows(meta, [pack[0][...], pack[1][...]], turn)
    for chunk in range(CTX):
        mixed = [
            jnp.concatenate([units[core, 3 * chunk + part] for part in range(3)], axis=1)
            for core in range(2)
        ]
        mixed_ref[chunk] = mixed[0]
        bias = jnp.sum(mixed[0].astype(WIDE), axis=0, keepdims=True)
        for part in range(3):
            dbias_ref[3 * chunk + part] = bias[:, part * GROUP : (part + 1) * GROUP]
        held[chunk] = over_both(left, mixed).astype(LOW)

    def place(part, ctx):
        return [(pl.ds(0, 3 * GROUP), held.at[meta[1] ^ ctx, pl.ds(part * ROWS, ROWS), :])]

    wait_all(store_grad(place, targets, sems, (0,)))


def input_grad_kernel(meta, x_ref, dmid_ref, mixed_ref, rows_ref, dfc_ref, dqkv_ref, *refs):
    vectors, parts, refs = refs[:4], refs[4 : 4 + PARTS], refs[4 + PARTS :]
    grad_ref, results, (held, chunks, rows, sums, sems) = refs[0], refs[1:5], refs[5:]
    (copies,) = load_weight(meta, parts, functools.partial(qkv_place, held), sems)
    params = read_vectors(meta, vectors, chunks)
    centred, inverse = moments(x_ref[...].astype(WIDE))
    normed = centred * inverse
    wait_all(copies)
    grad = jnp.zeros((TOKENS, WIDTH), WIDE)
    for chunk in range(CTX):
        grad = grad + mt(mixed_ref[chunk], held[chunk])
    grad_ref[...] = dmid_ref[...] + norm_back(grad, normed, inverse, params[0:1])
    rows[0:1] = jnp.sum(grad * normed, axis=0, keepdims=True)
    rows[1:2] = jnp.sum(grad, axis=0, keepdims=True)
    rows[2:4] = rows_ref[0:2]
    for chunk in range(CTX):
        lanes = slice(chunk * GROUP, (chunk + 1) * GROUP)
        rows[4:5, lanes] = dqkv_ref[chunk]
        rows[5:6, lanes] = dqkv_ref[2 * CTX + chunk]
        rows[8 + chunk : 9 + chunk] = dfc_ref[chunk]
    rows[6:8] = rows_ref[2:4]
    rows[12:16] = jnp.zeros((4, WIDTH), WIDE)
    for chunk in range(CTX):
        sums[chunk] = rows[:, chunk * GROUP : (chunk + 1) * GROUP]
    for ctx, target in enumerate(results):
        target[...] = sums[meta[1] ^ ctx]


def sum_kernel(one_kept, one_back, two_kept, two_back, one_keep, one_send, two_keep, two_send):
    pairs = ((one_kept, one_back, one_keep, one_send), (two_kept, two_back, two_keep, two_send))
    for kept, back, keep, send in pairs:
        keep[...] = kept[0].astype(WIDE) + back[0].astype(WIDE)
        send[...] = (kept[1].astype(WIDE) + back[1].astype(WIDE)).astype(LOW)


def near_kernel(one_kept, one_back, two_kept, two_back, one_keep, two_send):
    one_keep[...] = one_kept[...] + one_back[...].astype(WIDE)
    two_send[...] = (two_kept[...] + two_back[...].astype(WIDE)).astype(LOW)


def shape_of(dtype, *dims):
    return jax.ShapeDtypeStruct(dims, dtype)


def call(kernel, arguments, kinds, outputs, out_kinds, scratch, moved=1):
    spec = {
        "v": pl.BlockSpec(memory_space=pltpu.VMEM),
        "s": pl.BlockSpec(memory_space=pltpu.SMEM),
        "a": pl.BlockSpec(memory_space=pl.ANY),
        "h": pl.BlockSpec((None, TOKENS, WIDTH), lambda step: (CTX + 4, 0, 0)),
    }
    return pl.pallas_call(
        kernel,
        grid=(1,),
        out_shape=tuple(outputs),
        in_specs=[spec[kind] for kind in kinds],
        out_specs=tuple(spec[kind] for kind in out_kinds),
        scratch_shapes=scratch,
        cost_estimate=pl.CostEstimate(flops=1, bytes_accessed=moved, transcendentals=0),
        compiler_params=pltpu.CompilerParams(vmem_limit_bytes=VMEM_LIMIT),
    )(*arguments)


def local_fast(
    block_in,
    cotangent,
    w_qkv,
    w_out,
    w_fc,
    w_proj,
    vectors,
    qkv_first,
    qkv_second,
    out_first,
    out_second,
    fc_first,
    fc_second,
    proj_first,
    proj_second,
    vec_first,
    vec_second,
):
    batch, ctx = lax.axis_index("batch"), lax.axis_index("ctx")
    meta = jnp.stack([batch, ctx]).astype(jnp.int32)
    inputs = block_in.reshape(TOKENS, WIDTH)
    grad_low = cotangent.reshape(TOKENS, WIDTH)
    tie = lax.optimization_barrier

    qkv_sems = pltpu.SemaphoreType.DMA((1, BATCH * CTX))
    mlp_sems = pltpu.SemaphoreType.DMA((4, BATCH * CTX))
    qkv_held = pltpu.VMEM((CTX, WIDTH, 3 * GROUP), LOW)
    vec_held = pltpu.VMEM((CTX, 16, GROUP), WIDE)

    low_vec = jnp.pad(vectors.astype(LOW), ((0, 4), (0, 0)))
    low_vec = [low_vec[:, start : start + HEAD] for start in range(0, GROUP, HEAD)]
    low_vec = jnp.concatenate(low_vec + [jnp.zeros((ROWS - 48, HEAD), LOW)], axis=0)
    piece_one = jnp.concatenate([w_qkv.astype(LOW), low_vec], axis=1)
    low_proj = w_proj.astype(LOW).T
    piece_two = jnp.concatenate(
        [
            w_fc.astype(LOW),
            low_proj[:ROWS],
            low_proj[ROWS:],
            w_out.astype(LOW),
            jnp.zeros((ROWS, TILE - GROUP), LOW),
        ],
        axis=1,
    )
    near = jnp.stack([piece_one, swap(piece_one, "ctx", 2)])
    far = swap(near, "ctx", 1)
    own_one = jnp.concatenate([near, far], axis=0)[:, :, : 3 * GROUP]
    piece_two, late = tie((piece_two, far))
    vec_parts = [part[:48, 3 * GROUP :] for part in (near[0], late[0], near[1], late[1])]
    x_one, y_one = gather_first(own_one)
    across_one = gather_second(x_one, y_one)
    near, far = swap(piece_two, "ctx", 1), swap(piece_two, "ctx", 2)
    near, far, across_one = tie((near, far, across_one))
    last = swap(far, "ctx", 1)
    parts_one = [own_one, x_one, y_one, *across_one]
    parts_one = parts_one + to_core(parts_one)

    packed = shape_of(LOW, TOKENS * 3 * GROUP // LANES, LANES)
    single = shape_of(LOW, TOKENS * GROUP // LANES, LANES)
    tokens_low = shape_of(LOW, TOKENS, WIDTH)
    hidden_low = shape_of(LOW, CTX, TOKENS, WIDTH)
    h_one, own, *sent = call(
        qkv_kernel,
        (meta, inputs, *vec_parts, *parts_one),
        "s" + "v" * 5 + "a" * PARTS,
        [tokens_low] + [packed] * 4,
        "v" * 5,
        [qkv_held, pltpu.VMEM((CTX, TOKENS, 3 * GROUP), LOW), vec_held, qkv_sems],
    )
    qkv_pieces = [own] + [swap(part, "ctx", bit) for bit, part in zip((1, 2, 3), sent)]

    last, late_h = tie((last, h_one))
    own_two = jnp.stack([piece_two, far, near, last])
    x_two, y_two = gather_first(own_two)
    qkv_pieces, x_two, y_two = tie((qkv_pieces, x_two, y_two))
    across_two = gather_second(x_two, y_two)
    parts_two = [own_two, x_two, y_two]
    swapped_two = to_core(parts_two)

    sequence_low = pltpu.VMEM((SPAN, GROUP), LOW)
    sequence_wide = pltpu.VMEM((SPAN, GROUP), WIDE)
    own, *sent = call(
        attend_kernel,
        (meta, *qkv_pieces),
        "s" + "v" * 4,
        [single] * 4,
        "v" * 4,
        [sequence_low] * 3 + [sequence_wide],
    )
    sent, swapped_two = tie((sent, swapped_two))
    att_pieces = [own] + [swap(part, "ctx", bit) for bit, part in zip((1, 2, 3), sent)]
    across_two, att_pieces = tie((across_two, att_pieces))
    parts_two = parts_two + list(across_two) + swapped_two + to_core(across_two)

    pack_shape = shape_of(LOW, CTX + 5, TOKENS, WIDTH)
    act_shape = shape_of(LOW, BATCH // 2, TOKENS, FF_SIDE)
    out, pack, act_mine, act_theirs, dmid, own, *sent = call(
        middle_kernel,
        (meta, inputs, grad_low, late_h, *vec_parts, *att_pieces, *parts_two),
        "s" + "v" * 11 + "a" * PARTS,
        [tokens_low, pack_shape, act_shape, act_shape, shape_of(WIDE, TOKENS, WIDTH)]
        + [single] * 4
        + [shape_of(WIDE, 8, WIDTH), shape_of(WIDE, CTX, 1, WIDTH)],
        "v" * 11,
        [
            pltpu.VMEM((CTX, WIDTH, TILE), LOW),
            pltpu.VMEM((WIDTH, WIDTH), LOW),
            pltpu.VMEM((CTX, WIDTH, WIDTH), LOW),
            pltpu.VMEM((BATCH, WIDTH, FF_SIDE), LOW),
            pltpu.VMEM((CTX, TOKENS, GROUP), LOW),
            pltpu.VMEM((TOKENS, WIDTH), WIDE),
            pltpu.VMEM((TOKENS, WIDTH), WIDE),
            vec_held,
            pltpu.VMEM((CTX, 1, WIDTH), WIDE),
            pltpu.VMEM((BATCH, TOKENS, FF_SIDE), LOW),
            mlp_sems,
        ],
    )
    sent, (rows_two, dbias_fc) = sent[:3], sent[3:]
    grad_pieces = [own] + [swap(part, "ctx", bit) for bit, part in zip((1, 2, 3), sent)]
    act_came, pack_came = swap(act_theirs, "batch", CORE), swap(pack, "batch", CORE)

    half_sems = BATCH * CTX // 2
    turn_held = pltpu.VMEM((2, WIDTH, TOKENS), LOW)
    mlp_parts = call(
        mlp_grad_kernel,
        (meta, act_mine, act_came, pack, pack_came),
        "s" + "v" * 4,
        [shape_of(LOW, 2, 2, ROWS, MLP)] * 4,
        "aaaa",
        [
            pltpu.VMEM((CTX, WIDTH // 2, TILE), LOW),
            pltpu.VMEM((CTX, WIDTH // 2, WIDTH), LOW),
            pltpu.VMEM((BATCH // 2, WIDTH, FF_SIDE), LOW),
            turn_held,
            pltpu.SemaphoreType.DMA((4, half_sems)),
        ],
    )
    mlp_parts, grad_pieces = tie((mlp_parts, grad_pieces))
    mlp_kept = mlp_parts[0], mlp_parts[2]
    mlp_back = swap_pair((mlp_parts[1], mlp_parts[3]), YBIT, XBIT)
    own, *sent = call(
        attend_back_kernel,
        (meta, *qkv_pieces, *grad_pieces),
        "s" + "v" * 8,
        [packed] * 4,
        "v" * 4,
        [sequence_low] * 4 + [sequence_wide] * 3,
    )
    own_came = swap(own, "batch", CORE)
    received = [swap(part, "ctx", bit) for bit, part in zip((1, 2, 3), sent)]
    mlp_back, received[0] = tie((mlp_back, received[0]))
    pair = [shape_of(WIDE, 2, ROWS, MLP), shape_of(LOW, 2, ROWS, MLP)]
    one_keep, one_send, two_keep, two_send = call(
        sum_kernel,
        (mlp_kept[0], mlp_back[0], mlp_kept[1], mlp_back[1]),
        "vvvv",
        pair + pair,
        "vvvv",
        [],
    )
    one_keep, received[1], received[2] = tie((one_keep, received[1], received[2]))
    mlp_back = swap_pair((one_send, two_send), XBIT, YBIT)
    received = jnp.stack(received)
    received_came = swap(received, "batch", CORE)

    *qkv_parts, mixed, dbias_qkv = call(
        qkv_grad_kernel,
        (meta, pack, pack_came, own, own_came, received, received_came),
        "shhvvvv",
        [shape_of(LOW, 2, 2, ROWS, 3 * GROUP)] * 4
        + [shape_of(LOW, CTX, TOKENS, 3 * GROUP), shape_of(WIDE, 3 * CTX, 1, GROUP)],
        "aaaavv",
        [
            pltpu.VMEM((CTX, WIDTH // 2, 3 * GROUP), LOW),
            pltpu.VMEM((2, 3 * CTX, TOKENS, GROUP), LOW),
            turn_held,
            pltpu.SemaphoreType.DMA((1, half_sems)),
        ],
    )
    qkv_kept = qkv_parts[0], qkv_parts[2]
    qkv_kept = qkv_parts[0], qkv_parts[2]
    qkv_back = swap_pair((qkv_parts[1], qkv_parts[3]), YBIT, XBIT)
    grad_input, own, *sent = call(
        input_grad_kernel,
        (meta, inputs, dmid, mixed, rows_two, dbias_fc, dbias_qkv, *vec_parts, *parts_one),
        "s" + "v" * 10 + "a" * PARTS,
        [shape_of(WIDE, TOKENS, WIDTH)] + [shape_of(WIDE, 16, GROUP)] * 4,
        "v" * 5,
        [qkv_held, vec_held, pltpu.VMEM((16, WIDTH), WIDE), vec_held, qkv_sems],
        moved=40_000_000,
    )
    mlp_back, own, sent = tie((mlp_back, own, sent))
    vec_grad = own + sum(swap(part, "ctx", bit) for bit, part in zip((1, 2, 3), sent))
    mlp_one, mlp_two = call(
        near_kernel, (one_keep, mlp_back[0], two_keep, mlp_back[1]), "vvvv", pair, "vv", []
    )
    mlp_two, vec_grad = tie((mlp_two, vec_grad))
    mlp_two = swap(mlp_two, "ctx", 1)
    mlp_one, qkv_back = tie((mlp_one, qkv_back))
    qkv_kept, qkv_sent = scatter_second(qkv_kept, qkv_back)
    qkv_back = swap_pair(qkv_sent, XBIT, YBIT)
    qkv_back, vec_grad = tie((qkv_back, vec_grad))
    qkv_one, qkv_two = scatter_near(qkv_kept, qkv_back)
    for bit in (CORE, XBIT, YBIT):
        vec_grad = vec_grad + swap(vec_grad, "batch", bit)
    mlp_two, vec_grad = tie((mlp_two, vec_grad))
    mlp_grad = scatter_far(mlp_one, mlp_two)
    qkv_grad = scatter_far(qkv_one, qkv_two)
    vec_grad = vec_grad[:12]
    fc_grad = mlp_grad[:, :WIDTH]
    proj_grad = jnp.concatenate(
        [mlp_grad[:, WIDTH : WIDTH + FF_SIDE], mlp_grad[:, WIDTH + FF_SIDE : WIDTH + 2 * FF_SIDE]],
        axis=0,
    )
    out_grad = mlp_grad[:, WIDTH + 2 * FF_SIDE : WIDTH + 2 * FF_SIDE + GROUP]

    qkv_m, qkv_s, qkv_w = adamw(w_qkv, qkv_grad, qkv_first, qkv_second, 0.06, 0.1)
    out_m, out_s, out_w = adamw(w_out, out_grad, out_first, out_second, 0.06, 0.1)
    fc_m, fc_s, fc_w = adamw(w_fc, fc_grad, fc_first, fc_second, 0.06, 0.1)
    proj_m, proj_s, proj_w = adamw(w_proj, proj_grad.T, proj_first, proj_second, 0.06, 0.1)
    vec_m, vec_s, vec_w = adamw(vectors, vec_grad, vec_first, vec_second, 0.2, 0.0)
    return (
        out.reshape(block_in.shape),
        grad_input.reshape(block_in.shape),
        qkv_m,
        qkv_s,
        qkv_w,
        out_m,
        out_s,
        out_w,
        fc_m,
        fc_s,
        fc_w,
        proj_m,
        proj_s,
        proj_w,
        vec_m,
        vec_s,
        vec_w,
    )


def solution(mesh):
    in_specs = (
        P("batch", "ctx", None, None),
        P("batch", "ctx", None, None),
        P("batch", "ctx"),
        P("batch", "ctx"),
        P("batch", "ctx"),
        P("batch", "ctx"),
        P(None, "ctx"),
        P("batch", "ctx"),
        P("batch", "ctx"),
        P("batch", "ctx"),
        P("batch", "ctx"),
        P("batch", "ctx"),
        P("batch", "ctx"),
        P("batch", "ctx"),
        P("batch", "ctx"),
        P(None, "ctx"),
        P(None, "ctx"),
    )
    out_specs = (
        P("batch", "ctx", None, None),
        P("batch", "ctx", None, None),
        P("batch", "ctx"),
        P("batch", "ctx"),
        P("batch", "ctx"),
        P("batch", "ctx"),
        P("batch", "ctx"),
        P("batch", "ctx"),
        P("batch", "ctx"),
        P("batch", "ctx"),
        P("batch", "ctx"),
        P("batch", "ctx"),
        P("batch", "ctx"),
        P("batch", "ctx"),
        P(None, "ctx"),
        P(None, "ctx"),
        P(None, "ctx"),
    )
    sizes = (mesh.shape["batch"], mesh.shape["ctx"])
    local = local_fast if sizes == (BATCH, CTX) else local_any
    return jax.shard_map(local, mesh=mesh, in_specs=in_specs, out_specs=out_specs, check_vma=False)
```

```python
import functools
import math

import jax
import jax.numpy as jnp
from jax import lax
from jax.experimental import pallas as pl
from jax.experimental.pallas import tpu as pltpu
from jax.sharding import PartitionSpec as P

HEADS = 12
STEP = 10


def layer_norm(value, gain, shift):
    mean = jnp.mean(value, axis=-1, keepdims=True)
    centred = value - mean
    spread = jnp.mean(centred * centred, axis=-1, keepdims=True)
    return centred * lax.rsqrt(spread + 1e-05) * gain + shift


def gelu_tanh(value):
    return (
        0.5
        * value
        * (1.0 + jnp.tanh(0.7978845608028654 * (value + 0.044715 * value * value * value)))
    )


def block_places(index, count, half):
    offsets = jnp.arange(half, dtype=jnp.int32)
    first = index * half + offsets
    second = (2 * count - 1 - index) * half + offsets
    return jnp.concatenate([first, second])


def scores_of(queries, keys, scale, allowed):
    raw = jnp.einsum("sqhd,skhd->shqk", queries, keys, preferred_element_type=jnp.float32) * scale
    return jnp.where(allowed[None, None], raw, -1e30)


def pair_grads(queries, grads, keys, values, top, total, delta, scale, allowed):
    score = scores_of(queries, keys, scale, allowed)
    weights = jnp.exp(score - top[..., None]) / total[..., None]
    back_weights = jnp.einsum("sqhd,skhd->shqk", grads, values, preferred_element_type=jnp.float32)
    grad_score = (weights * (back_weights - delta[..., None])).astype(jnp.bfloat16)
    return (weights.astype(jnp.bfloat16), grad_score)


def rows_product(left, right):
    return jnp.einsum("ra,rb->ab", left, right, preferred_element_type=jnp.float32)


def back_product(grad, weight):
    return jnp.einsum("rb,ab->ra", grad, weight, preferred_element_type=jnp.float32)


def adamw(weight, grad, first, second, rate, decay):
    first = 0.9 * first + 0.1 * grad
    second = 0.999 * second + 0.001 * grad * grad
    first_hat = first / (1.0 - 0.9**STEP)
    second_hat = second / (1.0 - 0.999**STEP)
    weight = weight - rate * (first_hat / (jnp.sqrt(second_hat) + 1e-08) + decay * weight)
    return (first, second, weight)


def local_any(
    block_in,
    cotangent,
    w_qkv,
    w_out,
    w_fc,
    w_proj,
    vectors,
    qkv_first,
    qkv_second,
    out_first,
    out_second,
    fc_first,
    fc_second,
    proj_first,
    proj_second,
    vec_first,
    vec_second,
):
    low_type = jnp.bfloat16
    wide = jnp.float32
    row_parts = (
        lax.all_gather(w_qkv.astype(low_type), "batch", axis=0, tiled=True),
        lax.all_gather(w_out.astype(low_type), "batch", axis=0, tiled=True),
        lax.all_gather(w_fc.astype(low_type), "batch", axis=0, tiled=True),
        lax.all_gather(w_proj.astype(low_type), "batch", axis=0, tiled=True),
    )
    full_qkv, full_out, full_fc, full_proj, full_vec = (
        lax.all_gather(row_parts[0], "ctx", axis=1, tiled=True),
        lax.all_gather(row_parts[1], "ctx", axis=1, tiled=True),
        lax.all_gather(row_parts[2], "ctx", axis=1, tiled=True),
        lax.all_gather(row_parts[3], "ctx", axis=1, tiled=True),
        lax.all_gather(vectors.astype(low_type), "ctx", axis=1, tiled=True),
    )
    params = full_vec.astype(wide)
    seqs, pair, half, width = block_in.shape
    heads = HEADS
    head = width // heads
    rows = seqs * pair * half
    span = pair * half
    count = lax.axis_size("ctx")
    index = lax.axis_index("ctx")
    scale = 1.0 / math.sqrt(head)
    inputs = block_in.astype(wide).reshape(rows, width)
    normed_one = layer_norm(inputs, params[0], params[1]).astype(low_type)
    mixed = jnp.dot(normed_one, full_qkv, preferred_element_type=wide)
    queries = (mixed[:, :width] + params[4]).astype(low_type)
    keys = mixed[:, width : 2 * width].astype(low_type)
    values = (mixed[:, 2 * width :] + params[5]).astype(low_type)
    key_all, value_all = (
        lax.all_gather(keys.reshape(seqs, pair, half, width), "ctx", axis=1, tiled=True),
        lax.all_gather(values.reshape(seqs, pair, half, width), "ctx", axis=1, tiled=True),
    )
    query_heads = queries.reshape(seqs, span, heads, head)
    own_places = block_places(index, count, half)

    def piece_of(source, piece):
        return lax.dynamic_slice_in_dim(source, 2 * piece, 2, 1).reshape(seqs, span, heads, head)

    def allowed_for(piece):
        return own_places[:, None] >= block_places(piece, count, half)[None, :]

    def stats_step(piece, carry):
        top, total = carry
        score = scores_of(query_heads, piece_of(key_all, piece), scale, allowed_for(piece))
        new_top = jnp.maximum(top, jnp.max(score, axis=-1))
        total = total * jnp.exp(top - new_top) + jnp.sum(
            jnp.exp(score - new_top[..., None]), axis=-1
        )
        return (new_top, total)

    start_stats = (jnp.full((seqs, heads, span), -1e30, wide), jnp.zeros((seqs, heads, span), wide))
    top, total = lax.fori_loop(0, count, stats_step, start_stats)

    def output_step(piece, acc):
        score = scores_of(query_heads, piece_of(key_all, piece), scale, allowed_for(piece))
        weights = (jnp.exp(score - top[..., None]) / total[..., None]).astype(low_type)
        return acc + jnp.einsum(
            "shqk,skhd->sqhd", weights, piece_of(value_all, piece), preferred_element_type=wide
        )

    attended = lax.fori_loop(0, count, output_step, jnp.zeros((seqs, span, heads, head), wide))
    att_low = attended.reshape(rows, width).astype(low_type)
    mid = inputs + jnp.dot(att_low, full_out, preferred_element_type=wide) + params[6]
    normed_two = layer_norm(mid, params[2], params[3]).astype(low_type)
    pre = jnp.dot(normed_two, full_fc, preferred_element_type=wide) + params[8:12].reshape(-1)
    act_low = gelu_tanh(pre).astype(low_type)
    result = mid + jnp.dot(act_low, full_proj, preferred_element_type=wide) + params[7]
    out_block = result.astype(low_type).reshape(block_in.shape)
    grad_low = cotangent.reshape(rows, width)
    grad_out = grad_low.astype(wide)
    grad_wproj = rows_product(act_low, grad_low)
    back_act = back_product(grad_low, full_proj)
    grad_pre = jax.vjp(gelu_tanh, pre)[1](back_act)[0].astype(low_type)
    grad_wfc = rows_product(normed_two, grad_pre)
    back_two = back_product(grad_pre, full_fc)
    back_mid, grad_gain_two, grad_shift_two = jax.vjp(layer_norm, mid, params[2], params[3])[1](
        back_two
    )
    grad_mid = grad_out + back_mid
    grad_att_low = grad_mid.astype(low_type)
    grad_wout = rows_product(att_low, grad_att_low)
    back_att = back_product(grad_att_low, full_out)
    grad_heads = back_att.astype(low_type).reshape(seqs, span, heads, head)
    delta = jnp.einsum("sqhd,sqhd->shq", grad_heads.astype(wide), attended)
    query_all, grad_all = (
        lax.all_gather(queries.reshape(seqs, pair, half, width), "ctx", axis=1, tiled=True),
        lax.all_gather(grad_heads.reshape(seqs, pair, half, width), "ctx", axis=1, tiled=True),
    )
    top_all, total_all, delta_all = (
        lax.all_gather(top.reshape(seqs, heads, pair, half), "ctx", axis=2, tiled=True),
        lax.all_gather(total.reshape(seqs, heads, pair, half), "ctx", axis=2, tiled=True),
        lax.all_gather(delta.reshape(seqs, heads, pair, half), "ctx", axis=2, tiled=True),
    )

    def query_step(piece, grad_query):
        key_part = piece_of(key_all, piece)
        value_part = piece_of(value_all, piece)
        weights_low, grad_score = pair_grads(
            query_heads,
            grad_heads,
            key_part,
            value_part,
            top,
            total,
            delta,
            scale,
            allowed_for(piece),
        )
        return grad_query + jnp.einsum(
            "shqk,skhd->sqhd", grad_score, key_part, preferred_element_type=wide
        )

    grad_query = lax.fori_loop(0, count, query_step, jnp.zeros((seqs, span, heads, head), wide))
    key_heads = keys.reshape(seqs, span, heads, head)
    value_heads = values.reshape(seqs, span, heads, head)

    def stat_piece(source, piece):
        return lax.dynamic_slice_in_dim(source, 2 * piece, 2, 2).reshape(seqs, heads, span)

    def key_step(piece, carry):
        grad_key, grad_value = carry
        query_part = piece_of(query_all, piece)
        grad_part = piece_of(grad_all, piece)
        allowed = block_places(piece, count, half)[:, None] >= own_places[None, :]
        weights_low, grad_score = pair_grads(
            query_part,
            grad_part,
            key_heads,
            value_heads,
            stat_piece(top_all, piece),
            stat_piece(total_all, piece),
            stat_piece(delta_all, piece),
            scale,
            allowed,
        )
        grad_key = grad_key + jnp.einsum(
            "shqk,sqhd->skhd", grad_score, query_part, preferred_element_type=wide
        )
        grad_value = grad_value + jnp.einsum(
            "shqk,sqhd->skhd", weights_low, grad_part, preferred_element_type=wide
        )
        return (grad_key, grad_value)

    start_keys = (
        jnp.zeros((seqs, span, heads, head), wide),
        jnp.zeros((seqs, span, heads, head), wide),
    )
    grad_key, grad_value = lax.fori_loop(0, count, key_step, start_keys)
    grad_keys = (grad_key * scale).reshape(seqs, pair, half, width)
    grad_values = grad_value.reshape(seqs, pair, half, width)
    grad_q_low = (grad_query * scale).reshape(rows, width).astype(low_type)
    grad_k_low = grad_keys.reshape(rows, width).astype(low_type)
    grad_v_low = grad_values.reshape(rows, width).astype(low_type)
    grad_mixed = jnp.concatenate([grad_q_low, grad_k_low, grad_v_low], axis=1)
    grad_wqkv = rows_product(normed_one, grad_mixed)
    back_one = back_product(grad_mixed, full_qkv)
    back_in, grad_gain_one, grad_shift_one = jax.vjp(layer_norm, inputs, params[0], params[1])[1](
        back_one
    )
    grad_input = (grad_mid + back_in).reshape(block_in.shape)
    grad_bias_q = jnp.sum(grad_q_low.astype(wide), axis=0)
    grad_bias_v = jnp.sum(grad_v_low.astype(wide), axis=0)
    grad_bias_out = jnp.sum(grad_att_low.astype(wide), axis=0)
    grad_bias_proj = jnp.sum(grad_out, axis=0)
    grad_bias_fc = jnp.sum(grad_pre.astype(wide), axis=0).reshape(4, width)
    small_rows = jnp.stack(
        [
            grad_gain_one,
            grad_shift_one,
            grad_gain_two,
            grad_shift_two,
            grad_bias_q,
            grad_bias_v,
            grad_bias_out,
            grad_bias_proj,
        ]
    )
    grad_vectors = jnp.concatenate([small_rows, grad_bias_fc], axis=0)
    col_sums = (
        lax.psum_scatter(grad_wqkv, "ctx", scatter_dimension=1, tiled=True),
        lax.psum_scatter(grad_wout, "ctx", scatter_dimension=1, tiled=True),
        lax.psum_scatter(grad_wfc, "ctx", scatter_dimension=1, tiled=True),
        lax.psum_scatter(grad_wproj, "ctx", scatter_dimension=1, tiled=True),
        lax.psum_scatter(grad_vectors, "ctx", scatter_dimension=1, tiled=True),
    )
    qkv_grad, out_grad, fc_grad, proj_grad = (
        lax.psum_scatter(col_sums[0], "batch", scatter_dimension=0, tiled=True),
        lax.psum_scatter(col_sums[1], "batch", scatter_dimension=0, tiled=True),
        lax.psum_scatter(col_sums[2], "batch", scatter_dimension=0, tiled=True),
        lax.psum_scatter(col_sums[3], "batch", scatter_dimension=0, tiled=True),
    )
    vec_grad = lax.psum(col_sums[4], "batch")
    qkv_m, qkv_s, qkv_w = adamw(w_qkv, qkv_grad, qkv_first, qkv_second, 0.06, 0.1)
    out_m, out_s, out_w = adamw(w_out, out_grad, out_first, out_second, 0.06, 0.1)
    fc_m, fc_s, fc_w = adamw(w_fc, fc_grad, fc_first, fc_second, 0.06, 0.1)
    proj_m, proj_s, proj_w = adamw(w_proj, proj_grad, proj_first, proj_second, 0.06, 0.1)
    vec_m, vec_s, vec_w = adamw(vectors, vec_grad, vec_first, vec_second, 0.2, 0.0)
    return (
        out_block,
        grad_input,
        qkv_m,
        qkv_s,
        qkv_w,
        out_m,
        out_s,
        out_w,
        fc_m,
        fc_s,
        fc_w,
        proj_m,
        proj_s,
        proj_w,
        vec_m,
        vec_s,
        vec_w,
    )


BATCH = 8
CTX = 4
WIDTH = 768
HEAD = 64
GROUP = WIDTH // CTX
TOKENS = 256
HALF = 128
FF_SIDE = 384
ROWS = WIDTH // BATCH
MLP = WIDTH + 2 * FF_SIDE + 256
SPAN = TOKENS * CTX
TILE = 256
LOW = jnp.bfloat16
WIDE = jnp.float32
CORE, XBIT, YBIT = 1, 2, 4
PLACES = (0, 2, 1, 3)
SOURCES = (
    (0, PLACES),
    (XBIT, PLACES),
    (YBIT, PLACES),
    (XBIT + YBIT, PLACES[:2]),
    (XBIT + YBIT, PLACES[2:]),
    (CORE, PLACES),
    (CORE + XBIT, PLACES),
    (CORE + YBIT, PLACES),
    (CORE + XBIT + YBIT, PLACES[:2]),
    (CORE + XBIT + YBIT, PLACES[2:]),
)
PARTS = len(SOURCES)
VMEM_LIMIT = 56 * 1024 * 1024


def swap(value, axis, bit):
    size = BATCH if axis == "batch" else CTX
    return lax.ppermute(value, axis, [(i, i ^ bit) for i in range(size)])


def mm(left, right):
    return lax.dot_general(left, right, (((1,), (0,)), ((), ())), preferred_element_type=WIDE)


def mt(left, right):
    return lax.dot_general(left, right, (((1,), (1,)), ((), ())), preferred_element_type=WIDE)


def tm(left, right):
    return lax.dot_general(left, right, (((0,), (0,)), ((), ())), preferred_element_type=WIDE)


def turned(value):
    return value.T


def moments(value):
    mean = jnp.mean(value, axis=-1, keepdims=True)
    centred = value - mean
    spread = jnp.mean(centred * centred, axis=-1, keepdims=True)
    return centred, lax.rsqrt(spread + 1e-05)


def norm_back(grad, normed, inverse, gain):
    part = grad * gain
    mean = jnp.mean(part, axis=-1, keepdims=True)
    cross = jnp.mean(part * normed, axis=-1, keepdims=True)
    return inverse * (part - mean - normed * cross)


def gather_first(own):
    return swap(own, "batch", XBIT), swap(own, "batch", YBIT)


def gather_second(from_x, from_y):
    return swap(from_x[:2], "batch", YBIT), swap(from_y[2:], "batch", XBIT)


def to_core(parts):
    return [swap(part, "batch", CORE) for part in parts]


def swap_pair(pair, first, second):
    return swap(pair[0], "batch", first), swap(pair[1], "batch", second)


def scatter_second(kept, back):
    one = kept[0].astype(WIDE) + back[0].astype(WIDE)
    two = kept[1].astype(WIDE) + back[1].astype(WIDE)
    return (one[0], two[0]), (one[1].astype(LOW), two[1].astype(LOW))


def scatter_near(kept, back):
    one = kept[0].astype(WIDE) + back[0].astype(WIDE)
    two = (kept[1].astype(WIDE) + back[1].astype(WIDE)).astype(LOW)
    return one, swap(two, "ctx", 1)


def scatter_far(one, two):
    one = one + two.astype(WIDE)
    return one[0] + swap(one[1].astype(LOW), "ctx", 2).astype(WIDE)


def rows_of(index, size):
    return pl.ds(pl.multiple_of(index * size, 16), size)


def qkv_place(held, batch, ctx):
    return [(pl.ds(0, 3 * GROUP), held.at[ctx, rows_of(batch, ROWS), :])]


def mlp_place(held_out, held_fc, held_proj, batch, ctx):
    return [
        (pl.ds(WIDTH + 2 * FF_SIDE, TILE), held_out.at[ctx, rows_of(batch, ROWS), :]),
        (pl.ds(0, WIDTH), held_fc.at[ctx, rows_of(batch, ROWS), :]),
        (pl.ds(WIDTH, FF_SIDE), held_proj.at[batch, rows_of(2 * ctx, ROWS), :]),
        (pl.ds(WIDTH + FF_SIDE, FF_SIDE), held_proj.at[batch, rows_of(2 * ctx + 1, ROWS), :]),
    ]


def load_weight(meta, parts, place, sems):
    copies = []
    for part, (source, places) in zip(parts, SOURCES):
        for index, ctx in enumerate(places):
            ranges = place(meta[0] ^ source, meta[1] ^ ctx)
            copies.append([(part.at[index, :, lanes], target) for lanes, target in ranges])
    started = []
    for kind in range(len(copies[0])):
        group = []
        for number, copy in enumerate(copies):
            group.append(pltpu.make_async_copy(*copy[kind], sems.at[kind, number]))
            group[-1].start()
        started.append(group)
    return started


def store_grad(held, targets, sems, kinds):
    one_kept, one_sent, two_kept, two_sent = targets
    copies = []
    for y in range(2):
        for x in range(2):
            for index, ctx in enumerate(PLACES):
                if index < 2:
                    target = (one_sent if y else one_kept).at[x, index]
                else:
                    target = (two_sent if x else two_kept).at[y, index - 2]
                ranges = held(2 * y + x, ctx)
                for kind in kinds:
                    lanes, source = ranges[kind]
                    number = (2 * y + x) * CTX + ctx
                    copies.append(
                        pltpu.make_async_copy(source, target.at[:, lanes], sems.at[kind, number])
                    )
                    copies[-1].start()
    return copies


def half_rows(meta, pair, held):
    for index, value in enumerate(pair):
        held[index] = turned(value)
    parts = []
    for index in range(2):
        rows = [held[index, rows_of(meta[0] ^ (2 * part), ROWS), :] for part in range(BATCH // 2)]
        parts.append(jnp.concatenate(rows, axis=0))
    return parts


def over_both(left, right):
    return mm(left[0], right[0]) + mm(left[1], right[1])


def wait_all(copies):
    for copy in copies:
        copy.wait()


LANES = 128


def write_packed(target, value):
    full = value.shape[1] // LANES
    for index in range(full):
        target[index * TOKENS : (index + 1) * TOKENS, :] = value[
            :, index * LANES : (index + 1) * LANES
        ]
    rest = value[:, full * LANES :]
    target[full * TOKENS :, :] = jnp.concatenate([rest[:HALF], rest[HALF:]], axis=1)


def read_packed(source):
    full = source.shape[0] // TOKENS
    parts = [source[index * TOKENS : (index + 1) * TOKENS, :] for index in range(full)]
    rest = source[full * TOKENS :, :]
    parts.append(jnp.concatenate([rest[:, : LANES // 2], rest[:, LANES // 2 :]], axis=0))
    return jnp.concatenate(parts, axis=1)


def in_place(ctx, block):
    first = ctx if block == 0 else 2 * CTX - 1 - ctx
    return pl.ds(pl.multiple_of(first * HALF, HALF), HALF)


def read_vectors(meta, parts, chunks):
    for ctx, part in enumerate(parts):
        rows = [part[16 * index : 16 * (index + 1), :] for index in range(GROUP // HEAD)]
        chunks[meta[1] ^ ctx] = jnp.concatenate(rows, axis=1).astype(WIDE)
    return jnp.concatenate([chunks[index] for index in range(CTX)], axis=1)


def qkv_kernel(meta, x_ref, *refs):
    vectors, parts, refs = refs[:4], refs[4 : 4 + PARTS], refs[4 + PARTS :]
    h_ref, own, near, far, last, held, units, chunks, sems = refs
    (copies,) = load_weight(meta, parts, functools.partial(qkv_place, held), sems)
    params = read_vectors(meta, vectors, chunks)
    bias = jnp.concatenate([params[4:5], jnp.zeros((1, WIDTH), WIDE), params[5:6]], axis=1)
    centred, inverse = moments(x_ref[...].astype(WIDE))
    normed = (centred * inverse * params[0:1] + params[1:2]).astype(LOW)
    h_ref[...] = normed
    wait_all(copies)
    for chunk in range(CTX):
        mixed = mm(normed, held[chunk]) + bias[:, 3 * GROUP * chunk : 3 * GROUP * (chunk + 1)]
        mixed = mixed.astype(LOW)
        for part in range(3):
            unit = 3 * chunk + part
            units[unit % CTX, :, (unit // CTX) * GROUP : (unit // CTX + 1) * GROUP] = mixed[
                :, part * GROUP : (part + 1) * GROUP
            ]
    for ctx, target in enumerate((own, near, far, last)):
        write_packed(target, units[meta[1] ^ ctx])


def read_sequence(meta, pieces, targets):
    for ctx, piece in enumerate(pieces):
        value = read_packed(piece)
        for block in range(2):
            place = in_place(meta[1] ^ ctx, block)
            rows = value[block * HALF : (block + 1) * HALF, :]
            for index, target in enumerate(targets):
                target[place, :] = rows[:, index * GROUP : (index + 1) * GROUP]


def write_sequence(meta, pieces, sources):
    for ctx, piece in enumerate(pieces):
        parts = []
        for source in sources:
            blocks = [source[in_place(meta[1] ^ ctx, block), :] for block in range(2)]
            parts.append(jnp.concatenate(blocks, axis=0).astype(LOW))
        write_packed(piece, jnp.concatenate(parts, axis=1))


def head_mask(head, scale=1.0):
    lane = lax.broadcasted_iota(jnp.int32, (1, GROUP), 1)
    inside = (lane >= head * HEAD) & (lane < (head + 1) * HEAD)
    return jnp.where(inside, scale, 0.0).astype(LOW)


def tile_of(index):
    return slice(index * TILE, (index + 1) * TILE)


def weights_of(queries, k_seq, tile, causal, axis):
    keys = [k_seq[tile_of(other), :] for other in range(tile + 1)]
    scores = [mt(queries, key) if axis else mt(key, queries) for key in keys]
    scores[tile] = jnp.where(causal, scores[tile], -1e30)
    top = jnp.max(functools.reduce(jnp.maximum, scores), axis=axis, keepdims=True)
    expo = [jnp.exp(score - top) for score in scores]
    total = jnp.sum(functools.reduce(jnp.add, expo), axis=axis, keepdims=True)
    inverse = 1.0 / total
    return [value * inverse for value in expo]


def causal_tile(axis):
    key = lax.broadcasted_iota(jnp.int32, (TILE, TILE), axis)
    query = lax.broadcasted_iota(jnp.int32, (TILE, TILE), 1 - axis)
    return query >= key


def attend_kernel(meta, *refs):
    pieces, results, (q_seq, k_seq, v_seq, out) = refs[:4], refs[4:8], refs[8:]
    read_sequence(meta, pieces, (q_seq, k_seq, v_seq))
    causal = causal_tile(1)
    scale = 1.0 / math.sqrt(HEAD)
    for tile in range(SPAN // TILE):

        def one_head(head, total, tile=tile):
            mask = head_mask(head)
            queries = q_seq[tile_of(tile), :] * head_mask(head, scale)
            weights = weights_of(queries, k_seq, tile, causal, 1)
            for other, weight in enumerate(weights):
                total = total + mm(weight.astype(LOW), v_seq[tile_of(other), :] * mask)
            return total

        out[tile_of(tile), :] = lax.fori_loop(
            0, GROUP // HEAD, one_head, jnp.zeros((TILE, GROUP), WIDE), unroll=True
        )
    write_sequence(meta, results, (out,))


def attend_back_kernel(meta, *refs):
    pieces, grads, results = refs[:4], refs[4:8], refs[8:12]
    q_seq, k_seq, v_seq, g_seq, dq, dk, dv = refs[12:]
    read_sequence(meta, pieces, (q_seq, k_seq, v_seq))
    read_sequence(meta, grads, (g_seq,))
    causal = causal_tile(0)
    scale = 1.0 / math.sqrt(HEAD)
    dk[...] = jnp.zeros_like(dk)
    dv[...] = jnp.zeros_like(dv)
    for tile in range(SPAN // TILE):

        def one_head(head, total, tile=tile):
            mask = head_mask(head)
            scaled = head_mask(head, scale)
            queries = q_seq[tile_of(tile), :] * scaled
            grad = g_seq[tile_of(tile), :] * mask
            weights = weights_of(queries, k_seq, tile, causal, 0)
            backs = [mt(v_seq[tile_of(other), :], grad) for other in range(tile + 1)]
            products = [weight * back for weight, back in zip(weights, backs)]
            delta = jnp.sum(functools.reduce(jnp.add, products), axis=0, keepdims=True)
            for other, (weight, back) in enumerate(zip(weights, backs)):
                step = (weight * (back - delta)).astype(LOW)
                total = total + tm(step, k_seq[tile_of(other), :] * scaled)
                dk[tile_of(other), :] += mm(step, queries)
                dv[tile_of(other), :] += mm(weight.astype(LOW), grad)
            return total

        dq[tile_of(tile), :] = lax.fori_loop(
            0, GROUP // HEAD, one_head, jnp.zeros((TILE, GROUP), WIDE), unroll=True
        )
    write_sequence(meta, results, (dq, dk, dv))


def middle_kernel(meta, x_ref, dy_ref, h_one_ref, *refs):
    vectors, pieces, parts, refs = refs[:4], refs[4:8], refs[8 : 8 + PARTS], refs[8 + PARTS :]
    (out_ref, pack_ref, mine, theirs, dmid_ref), refs = refs[:5], refs[5:]
    results, (rows_ref, dbias_ref), refs = refs[:4], refs[4:6], refs[6:]
    out_parts, held_out, held_fc, held_proj, units, total, back, chunks, bias, acts, sems = refs
    place = functools.partial(mlp_place, out_parts, held_fc, held_proj)
    copies = load_weight(meta, parts, place, sems)
    vec = read_vectors(meta, vectors, chunks)
    for chunk in range(CTX):
        bias[chunk] = vec[8 + chunk : 9 + chunk]
    for ctx, piece in enumerate(pieces):
        units[meta[1] ^ ctx] = read_packed(piece)
    att = jnp.concatenate([units[index] for index in range(CTX)], axis=1)
    pack_ref[CTX + 1] = att
    pack_ref[CTX + 3] = dy_ref[...]
    pack_ref[CTX + 4] = h_one_ref[...]
    wait_all(copies[0])
    for chunk in range(CTX):
        held_out[:, chunk * GROUP : (chunk + 1) * GROUP] = out_parts[chunk, :, :GROUP]
    mid = x_ref[...].astype(WIDE) + mm(att, held_out[...]) + vec[6:7]
    centred, inverse = moments(mid)
    normed = centred * inverse
    pack_ref[CTX] = (normed * vec[2:3] + vec[3:4]).astype(LOW)
    total[...] = mid + vec[7:8]
    back[...] = jnp.zeros_like(back)
    for group in copies[1:]:
        wait_all(group)
    side = FF_SIDE

    def chunk_step(chunk, carry):
        pre = mm(pack_ref[CTX], held_fc[chunk]) + bias[chunk]
        square = pre * pre
        tanh = jnp.tanh(0.7978845608028654 * (pre + 0.044715 * square * pre))
        act = (0.5 * pre * (1.0 + tanh)).astype(LOW)
        slope = 0.5 * (1.0 + tanh) + 0.5 * pre * (1.0 - tanh * tanh) * (
            0.7978845608028654 * (1.0 + 3.0 * 0.044715 * square)
        )
        grads = []
        for half in range(2):
            weight = held_proj[2 * chunk + half]
            part = act[:, half * side : (half + 1) * side]
            acts[2 * chunk + half] = part
            total[...] += mt(part, weight)
            grads.append(mm(dy_ref[...], weight))
        dpre = (jnp.concatenate(grads, axis=1) * slope).astype(LOW)
        pack_ref[chunk] = dpre
        dbias_ref[chunk] = jnp.sum(dpre.astype(WIDE), axis=0, keepdims=True)
        back[...] += mt(dpre, held_fc[chunk])
        return carry

    lax.fori_loop(0, CTX, chunk_step, 0, unroll=True)
    out_ref[...] = total[...].astype(LOW)
    core = meta[0] & 1
    for chunk in range(CTX):
        mine[chunk] = acts[2 * chunk + core]
        theirs[chunk] = acts[2 * chunk + 1 - core]
    grad = back[...]
    dy = dy_ref[...].astype(WIDE)
    dmid = dy + norm_back(grad, normed, inverse, vec[2:3])
    dmid_ref[...] = dmid
    datt = dmid.astype(LOW)
    pack_ref[CTX + 2] = datt
    rows_ref[0:1] = jnp.sum(grad * normed, axis=0, keepdims=True)
    rows_ref[1:2] = jnp.sum(grad, axis=0, keepdims=True)
    rows_ref[2:3] = jnp.sum(datt.astype(WIDE), axis=0, keepdims=True)
    rows_ref[3:4] = jnp.sum(dy, axis=0, keepdims=True)
    rows_ref[4:8] = jnp.zeros((4, WIDTH), WIDE)
    dout = mt(datt, held_out[...]).astype(LOW)
    for index in range(CTX):
        units[index] = dout[:, index * GROUP : (index + 1) * GROUP]
    for ctx, target in enumerate(results):
        write_packed(target, units[meta[1] ^ ctx])


def mlp_grad_kernel(meta, *refs):
    acts, packs, targets = refs[:2], refs[2:4], refs[4:8]
    held_out, held_fc, held_proj, turn, sems = refs[8:]

    def place(part, ctx):
        ctx = meta[1] ^ ctx
        chunk = (meta[0] ^ (2 * part)) // 2
        rows = pl.ds(part * ROWS, ROWS)
        return [
            (pl.ds(WIDTH + 2 * FF_SIDE, TILE), held_out.at[ctx, rows, :]),
            (pl.ds(0, WIDTH), held_fc.at[ctx, rows, :]),
            (pl.ds(WIDTH, FF_SIDE), held_proj.at[chunk, rows_of(2 * ctx, ROWS), :]),
            (pl.ds(WIDTH + FF_SIDE, FF_SIDE), held_proj.at[chunk, rows_of(2 * ctx + 1, ROWS), :]),
        ]

    dy = [turned(pack[CTX + 3]) for pack in packs]
    for chunk in range(CTX):
        held_proj[chunk] = over_both(dy, [act[chunk] for act in acts]).astype(LOW)
    copies = store_grad(place, targets, sems, (2, 3))
    left = half_rows(meta, [pack[CTX] for pack in packs], turn)
    for chunk in range(CTX):
        held_fc[chunk] = over_both(left, [pack[chunk] for pack in packs]).astype(LOW)
    copies += store_grad(place, targets, sems, (1,))
    left = half_rows(meta, [pack[CTX + 1] for pack in packs], turn)
    grad = over_both(left, [pack[CTX + 2] for pack in packs]).astype(LOW)
    for chunk in range(CTX):
        held_out[chunk, :, :GROUP] = grad[:, chunk * GROUP : (chunk + 1) * GROUP]
        held_out[chunk, :, GROUP:] = jnp.zeros((WIDTH // 2, TILE - GROUP), LOW)

    wait_all(copies + store_grad(place, targets, sems, (0,)))


def qkv_grad_kernel(meta, *refs):
    pack, own, came, targets = refs[:2], refs[2:4], refs[4:6], refs[6:10]
    mixed_ref, dbias_ref, held, units, turn, sems = refs[10:]
    for core in range(2):
        for ctx in range(CTX):
            value = read_packed(own[core] if ctx == 0 else came[core].at[ctx - 1])
            for part in range(3):
                units[core, CTX * part + (meta[1] ^ ctx)] = value[
                    :, part * GROUP : (part + 1) * GROUP
                ]
    left = half_rows(meta, [pack[0][...], pack[1][...]], turn)
    for chunk in range(CTX):
        mixed = [
            jnp.concatenate([units[core, 3 * chunk + part] for part in range(3)], axis=1)
            for core in range(2)
        ]
        mixed_ref[chunk] = mixed[0]
        bias = jnp.sum(mixed[0].astype(WIDE), axis=0, keepdims=True)
        for part in range(3):
            dbias_ref[3 * chunk + part] = bias[:, part * GROUP : (part + 1) * GROUP]
        held[chunk] = over_both(left, mixed).astype(LOW)

    def place(part, ctx):
        return [(pl.ds(0, 3 * GROUP), held.at[meta[1] ^ ctx, pl.ds(part * ROWS, ROWS), :])]

    wait_all(store_grad(place, targets, sems, (0,)))


def input_grad_kernel(meta, x_ref, dmid_ref, mixed_ref, rows_ref, dfc_ref, dqkv_ref, *refs):
    vectors, parts, refs = refs[:4], refs[4 : 4 + PARTS], refs[4 + PARTS :]
    grad_ref, results, (held, chunks, rows, sums, sems) = refs[0], refs[1:5], refs[5:]
    (copies,) = load_weight(meta, parts, functools.partial(qkv_place, held), sems)
    params = read_vectors(meta, vectors, chunks)
    centred, inverse = moments(x_ref[...].astype(WIDE))
    normed = centred * inverse
    wait_all(copies)
    grad = jnp.zeros((TOKENS, WIDTH), WIDE)
    for chunk in range(CTX):
        grad = grad + mt(mixed_ref[chunk], held[chunk])
    grad_ref[...] = dmid_ref[...] + norm_back(grad, normed, inverse, params[0:1])
    rows[0:1] = jnp.sum(grad * normed, axis=0, keepdims=True)
    rows[1:2] = jnp.sum(grad, axis=0, keepdims=True)
    rows[2:4] = rows_ref[0:2]
    for chunk in range(CTX):
        lanes = slice(chunk * GROUP, (chunk + 1) * GROUP)
        rows[4:5, lanes] = dqkv_ref[chunk]
        rows[5:6, lanes] = dqkv_ref[2 * CTX + chunk]
        rows[8 + chunk : 9 + chunk] = dfc_ref[chunk]
    rows[6:8] = rows_ref[2:4]
    rows[12:16] = jnp.zeros((4, WIDTH), WIDE)
    for chunk in range(CTX):
        sums[chunk] = rows[:, chunk * GROUP : (chunk + 1) * GROUP]
    for ctx, target in enumerate(results):
        target[...] = sums[meta[1] ^ ctx]


def sum_kernel(one_kept, one_back, two_kept, two_back, one_keep, one_send, two_keep, two_send):
    pairs = ((one_kept, one_back, one_keep, one_send), (two_kept, two_back, two_keep, two_send))
    for kept, back, keep, send in pairs:
        keep[...] = kept[0].astype(WIDE) + back[0].astype(WIDE)
        send[...] = (kept[1].astype(WIDE) + back[1].astype(WIDE)).astype(LOW)


def near_kernel(one_kept, one_back, two_kept, two_back, one_keep, two_send):
    one_keep[...] = one_kept[...] + one_back[...].astype(WIDE)
    two_send[...] = (two_kept[...] + two_back[...].astype(WIDE)).astype(LOW)


def shape_of(dtype, *dims):
    return jax.ShapeDtypeStruct(dims, dtype)


def call(kernel, arguments, kinds, outputs, out_kinds, scratch, moved=1):
    spec = {
        "v": pl.BlockSpec(memory_space=pltpu.VMEM),
        "s": pl.BlockSpec(memory_space=pltpu.SMEM),
        "a": pl.BlockSpec(memory_space=pl.ANY),
        "h": pl.BlockSpec((None, TOKENS, WIDTH), lambda step: (CTX + 4, 0, 0)),
    }
    return pl.pallas_call(
        kernel,
        grid=(1,),
        out_shape=tuple(outputs),
        in_specs=[spec[kind] for kind in kinds],
        out_specs=tuple(spec[kind] for kind in out_kinds),
        scratch_shapes=scratch,
        cost_estimate=pl.CostEstimate(flops=1, bytes_accessed=moved, transcendentals=0),
        compiler_params=pltpu.CompilerParams(vmem_limit_bytes=VMEM_LIMIT),
    )(*arguments)


def local_fast(
    block_in,
    cotangent,
    w_qkv,
    w_out,
    w_fc,
    w_proj,
    vectors,
    qkv_first,
    qkv_second,
    out_first,
    out_second,
    fc_first,
    fc_second,
    proj_first,
    proj_second,
    vec_first,
    vec_second,
):
    batch, ctx = lax.axis_index("batch"), lax.axis_index("ctx")
    meta = jnp.stack([batch, ctx]).astype(jnp.int32)
    inputs = block_in.reshape(TOKENS, WIDTH)
    grad_low = cotangent.reshape(TOKENS, WIDTH)
    tie = lax.optimization_barrier

    qkv_sems = pltpu.SemaphoreType.DMA((1, BATCH * CTX))
    mlp_sems = pltpu.SemaphoreType.DMA((4, BATCH * CTX))
    qkv_held = pltpu.VMEM((CTX, WIDTH, 3 * GROUP), LOW)
    vec_held = pltpu.VMEM((CTX, 16, GROUP), WIDE)

    low_vec = jnp.pad(vectors.astype(LOW), ((0, 4), (0, 0)))
    low_vec = [low_vec[:, start : start + HEAD] for start in range(0, GROUP, HEAD)]
    low_vec = jnp.concatenate(low_vec + [jnp.zeros((ROWS - 48, HEAD), LOW)], axis=0)
    piece_one = jnp.concatenate([w_qkv.astype(LOW), low_vec], axis=1)
    low_proj = w_proj.astype(LOW).T
    piece_two = jnp.concatenate(
        [
            w_fc.astype(LOW),
            low_proj[:ROWS],
            low_proj[ROWS:],
            w_out.astype(LOW),
            jnp.zeros((ROWS, TILE - GROUP), LOW),
        ],
        axis=1,
    )
    near = jnp.stack([piece_one, swap(piece_one, "ctx", 2)])
    far = swap(near, "ctx", 1)
    own_one = jnp.concatenate([near, far], axis=0)[:, :, : 3 * GROUP]
    piece_two, late = tie((piece_two, far))
    vec_parts = [part[:48, 3 * GROUP :] for part in (near[0], late[0], near[1], late[1])]
    x_one, y_one = gather_first(own_one)
    across_one = gather_second(x_one, y_one)
    near, far = swap(piece_two, "ctx", 1), swap(piece_two, "ctx", 2)
    near, far, across_one = tie((near, far, across_one))
    last = swap(far, "ctx", 1)
    parts_one = [own_one, x_one, y_one, *across_one]
    parts_one = parts_one + to_core(parts_one)

    packed = shape_of(LOW, TOKENS * 3 * GROUP // LANES, LANES)
    single = shape_of(LOW, TOKENS * GROUP // LANES, LANES)
    tokens_low = shape_of(LOW, TOKENS, WIDTH)
    hidden_low = shape_of(LOW, CTX, TOKENS, WIDTH)
    h_one, own, *sent = call(
        qkv_kernel,
        (meta, inputs, *vec_parts, *parts_one),
        "s" + "v" * 5 + "a" * PARTS,
        [tokens_low] + [packed] * 4,
        "v" * 5,
        [qkv_held, pltpu.VMEM((CTX, TOKENS, 3 * GROUP), LOW), vec_held, qkv_sems],
    )
    qkv_pieces = [own] + [swap(part, "ctx", bit) for bit, part in zip((1, 2, 3), sent)]

    last, late_h = tie((last, h_one))
    own_two = jnp.stack([piece_two, far, near, last])
    x_two, y_two = gather_first(own_two)
    qkv_pieces, x_two, y_two = tie((qkv_pieces, x_two, y_two))
    across_two = gather_second(x_two, y_two)
    parts_two = [own_two, x_two, y_two]
    swapped_two = to_core(parts_two)

    sequence_low = pltpu.VMEM((SPAN, GROUP), LOW)
    sequence_wide = pltpu.VMEM((SPAN, GROUP), WIDE)
    own, *sent = call(
        attend_kernel,
        (meta, *qkv_pieces),
        "s" + "v" * 4,
        [single] * 4,
        "v" * 4,
        [sequence_low] * 3 + [sequence_wide],
    )
    sent, swapped_two = tie((sent, swapped_two))
    att_pieces = [own] + [swap(part, "ctx", bit) for bit, part in zip((1, 2, 3), sent)]
    across_two, att_pieces = tie((across_two, att_pieces))
    parts_two = parts_two + list(across_two) + swapped_two + to_core(across_two)

    pack_shape = shape_of(LOW, CTX + 5, TOKENS, WIDTH)
    act_shape = shape_of(LOW, BATCH // 2, TOKENS, FF_SIDE)
    out, pack, act_mine, act_theirs, dmid, own, *sent = call(
        middle_kernel,
        (meta, inputs, grad_low, late_h, *vec_parts, *att_pieces, *parts_two),
        "s" + "v" * 11 + "a" * PARTS,
        [tokens_low, pack_shape, act_shape, act_shape, shape_of(WIDE, TOKENS, WIDTH)]
        + [single] * 4
        + [shape_of(WIDE, 8, WIDTH), shape_of(WIDE, CTX, 1, WIDTH)],
        "v" * 11,
        [
            pltpu.VMEM((CTX, WIDTH, TILE), LOW),
            pltpu.VMEM((WIDTH, WIDTH), LOW),
            pltpu.VMEM((CTX, WIDTH, WIDTH), LOW),
            pltpu.VMEM((BATCH, WIDTH, FF_SIDE), LOW),
            pltpu.VMEM((CTX, TOKENS, GROUP), LOW),
            pltpu.VMEM((TOKENS, WIDTH), WIDE),
            pltpu.VMEM((TOKENS, WIDTH), WIDE),
            vec_held,
            pltpu.VMEM((CTX, 1, WIDTH), WIDE),
            pltpu.VMEM((BATCH, TOKENS, FF_SIDE), LOW),
            mlp_sems,
        ],
    )
    sent, (rows_two, dbias_fc) = sent[:3], sent[3:]
    grad_pieces = [own] + [swap(part, "ctx", bit) for bit, part in zip((1, 2, 3), sent)]
    act_came, pack_came = swap(act_theirs, "batch", CORE), swap(pack, "batch", CORE)

    half_sems = BATCH * CTX // 2
    turn_held = pltpu.VMEM((2, WIDTH, TOKENS), LOW)
    mlp_parts = call(
        mlp_grad_kernel,
        (meta, act_mine, act_came, pack, pack_came),
        "s" + "v" * 4,
        [shape_of(LOW, 2, 2, ROWS, MLP)] * 4,
        "aaaa",
        [
            pltpu.VMEM((CTX, WIDTH // 2, TILE), LOW),
            pltpu.VMEM((CTX, WIDTH // 2, WIDTH), LOW),
            pltpu.VMEM((BATCH // 2, WIDTH, FF_SIDE), LOW),
            turn_held,
            pltpu.SemaphoreType.DMA((4, half_sems)),
        ],
    )
    mlp_parts, grad_pieces = tie((mlp_parts, grad_pieces))
    mlp_kept = mlp_parts[0], mlp_parts[2]
    mlp_back = swap_pair((mlp_parts[1], mlp_parts[3]), YBIT, XBIT)
    own, *sent = call(
        attend_back_kernel,
        (meta, *qkv_pieces, *grad_pieces),
        "s" + "v" * 8,
        [packed] * 4,
        "v" * 4,
        [sequence_low] * 4 + [sequence_wide] * 3,
    )
    own_came = swap(own, "batch", CORE)
    received = [swap(part, "ctx", bit) for bit, part in zip((1, 2, 3), sent)]
    mlp_back, received[0] = tie((mlp_back, received[0]))
    pair = [shape_of(WIDE, 2, ROWS, MLP), shape_of(LOW, 2, ROWS, MLP)]
    one_keep, one_send, two_keep, two_send = call(
        sum_kernel,
        (mlp_kept[0], mlp_back[0], mlp_kept[1], mlp_back[1]),
        "vvvv",
        pair + pair,
        "vvvv",
        [],
    )
    one_keep, received[1], received[2] = tie((one_keep, received[1], received[2]))
    mlp_back = swap_pair((one_send, two_send), XBIT, YBIT)
    received = jnp.stack(received)
    received_came = swap(received, "batch", CORE)

    *qkv_parts, mixed, dbias_qkv = call(
        qkv_grad_kernel,
        (meta, pack, pack_came, own, own_came, received, received_came),
        "shhvvvv",
        [shape_of(LOW, 2, 2, ROWS, 3 * GROUP)] * 4
        + [shape_of(LOW, CTX, TOKENS, 3 * GROUP), shape_of(WIDE, 3 * CTX, 1, GROUP)],
        "aaaavv",
        [
            pltpu.VMEM((CTX, WIDTH // 2, 3 * GROUP), LOW),
            pltpu.VMEM((2, 3 * CTX, TOKENS, GROUP), LOW),
            turn_held,
            pltpu.SemaphoreType.DMA((1, half_sems)),
        ],
    )
    qkv_kept = qkv_parts[0], qkv_parts[2]
    qkv_kept = qkv_parts[0], qkv_parts[2]
    qkv_back = swap_pair((qkv_parts[1], qkv_parts[3]), YBIT, XBIT)
    grad_input, own, *sent = call(
        input_grad_kernel,
        (meta, inputs, dmid, mixed, rows_two, dbias_fc, dbias_qkv, *vec_parts, *parts_one),
        "s" + "v" * 10 + "a" * PARTS,
        [shape_of(WIDE, TOKENS, WIDTH)] + [shape_of(WIDE, 16, GROUP)] * 4,
        "v" * 5,
        [qkv_held, vec_held, pltpu.VMEM((16, WIDTH), WIDE), vec_held, qkv_sems],
        moved=40_000_000,
    )
    mlp_back, own, sent = tie((mlp_back, own, sent))
    vec_grad = own + sum(swap(part, "ctx", bit) for bit, part in zip((1, 2, 3), sent))
    mlp_one, mlp_two = call(
        near_kernel, (one_keep, mlp_back[0], two_keep, mlp_back[1]), "vvvv", pair, "vv", []
    )
    mlp_two, vec_grad = tie((mlp_two, vec_grad))
    mlp_two = swap(mlp_two, "ctx", 1)
    mlp_one, qkv_back = tie((mlp_one, qkv_back))
    qkv_kept, qkv_sent = scatter_second(qkv_kept, qkv_back)
    qkv_back = swap_pair(qkv_sent, XBIT, YBIT)
    qkv_back, vec_grad = tie((qkv_back, vec_grad))
    qkv_one, qkv_two = scatter_near(qkv_kept, qkv_back)
    for bit in (CORE, XBIT, YBIT):
        vec_grad = vec_grad + swap(vec_grad, "batch", bit)
    mlp_two, vec_grad = tie((mlp_two, vec_grad))
    mlp_grad = scatter_far(mlp_one, mlp_two)
    qkv_grad = scatter_far(qkv_one, qkv_two)
    vec_grad = vec_grad[:12]
    fc_grad = mlp_grad[:, :WIDTH]
    proj_grad = jnp.concatenate(
        [mlp_grad[:, WIDTH : WIDTH + FF_SIDE], mlp_grad[:, WIDTH + FF_SIDE : WIDTH + 2 * FF_SIDE]],
        axis=0,
    )
    out_grad = mlp_grad[:, WIDTH + 2 * FF_SIDE : WIDTH + 2 * FF_SIDE + GROUP]

    qkv_m, qkv_s, qkv_w = adamw(w_qkv, qkv_grad, qkv_first, qkv_second, 0.06, 0.1)
    out_m, out_s, out_w = adamw(w_out, out_grad, out_first, out_second, 0.06, 0.1)
    fc_m, fc_s, fc_w = adamw(w_fc, fc_grad, fc_first, fc_second, 0.06, 0.1)
    proj_m, proj_s, proj_w = adamw(w_proj, proj_grad.T, proj_first, proj_second, 0.06, 0.1)
    vec_m, vec_s, vec_w = adamw(vectors, vec_grad, vec_first, vec_second, 0.2, 0.0)
    return (
        out.reshape(block_in.shape),
        grad_input.reshape(block_in.shape),
        qkv_m,
        qkv_s,
        qkv_w,
        out_m,
        out_s,
        out_w,
        fc_m,
        fc_s,
        fc_w,
        proj_m,
        proj_s,
        proj_w,
        vec_m,
        vec_s,
        vec_w,
    )


def solution(mesh):
    in_specs = (
        P("batch", "ctx", None, None),
        P("batch", "ctx", None, None),
        P("batch", "ctx"),
        P("batch", "ctx"),
        P("batch", "ctx"),
        P("batch", "ctx"),
        P(None, "ctx"),
        P("batch", "ctx"),
        P("batch", "ctx"),
        P("batch", "ctx"),
        P("batch", "ctx"),
        P("batch", "ctx"),
        P("batch", "ctx"),
        P("batch", "ctx"),
        P("batch", "ctx"),
        P(None, "ctx"),
        P(None, "ctx"),
    )
    out_specs = (
        P("batch", "ctx", None, None),
        P("batch", "ctx", None, None),
        P("batch", "ctx"),
        P("batch", "ctx"),
        P("batch", "ctx"),
        P("batch", "ctx"),
        P("batch", "ctx"),
        P("batch", "ctx"),
        P("batch", "ctx"),
        P("batch", "ctx"),
        P("batch", "ctx"),
        P("batch", "ctx"),
        P("batch", "ctx"),
        P("batch", "ctx"),
        P(None, "ctx"),
        P(None, "ctx"),
        P(None, "ctx"),
    )
    sizes = (mesh.shape["batch"], mesh.shape["ctx"])
    local = local_fast if sizes == (BATCH, CTX) else local_any
    return jax.shard_map(local, mesh=mesh, in_specs=in_specs, out_specs=out_specs, check_vma=False)
```

```python
import functools
import math

import jax
import jax.numpy as jnp
from jax import lax
from jax.experimental import pallas as pl
from jax.experimental.pallas import tpu as pltpu
from jax.sharding import PartitionSpec as P

HEADS = 12
STEP = 10


def layer_norm(value, gain, shift):
    mean = jnp.mean(value, axis=-1, keepdims=True)
    centred = value - mean
    spread = jnp.mean(centred * centred, axis=-1, keepdims=True)
    return centred * lax.rsqrt(spread + 1e-05) * gain + shift


def gelu_tanh(value):
    return (
        0.5
        * value
        * (1.0 + jnp.tanh(0.7978845608028654 * (value + 0.044715 * value * value * value)))
    )


def block_places(index, count, half):
    offsets = jnp.arange(half, dtype=jnp.int32)
    first = index * half + offsets
    second = (2 * count - 1 - index) * half + offsets
    return jnp.concatenate([first, second])


def scores_of(queries, keys, scale, allowed):
    raw = jnp.einsum("sqhd,skhd->shqk", queries, keys, preferred_element_type=jnp.float32) * scale
    return jnp.where(allowed[None, None], raw, -1e30)


def pair_grads(queries, grads, keys, values, top, total, delta, scale, allowed):
    score = scores_of(queries, keys, scale, allowed)
    weights = jnp.exp(score - top[..., None]) / total[..., None]
    back_weights = jnp.einsum("sqhd,skhd->shqk", grads, values, preferred_element_type=jnp.float32)
    grad_score = (weights * (back_weights - delta[..., None])).astype(jnp.bfloat16)
    return (weights.astype(jnp.bfloat16), grad_score)


def rows_product(left, right):
    return jnp.einsum("ra,rb->ab", left, right, preferred_element_type=jnp.float32)


def back_product(grad, weight):
    return jnp.einsum("rb,ab->ra", grad, weight, preferred_element_type=jnp.float32)


def adamw(weight, grad, first, second, rate, decay):
    first = 0.9 * first + 0.1 * grad
    second = 0.999 * second + 0.001 * grad * grad
    first_hat = first / (1.0 - 0.9**STEP)
    second_hat = second / (1.0 - 0.999**STEP)
    weight = weight - rate * (first_hat / (jnp.sqrt(second_hat) + 1e-08) + decay * weight)
    return (first, second, weight)


def local_any(
    block_in,
    cotangent,
    w_qkv,
    w_out,
    w_fc,
    w_proj,
    vectors,
    qkv_first,
    qkv_second,
    out_first,
    out_second,
    fc_first,
    fc_second,
    proj_first,
    proj_second,
    vec_first,
    vec_second,
):
    low_type = jnp.bfloat16
    wide = jnp.float32
    row_parts = (
        lax.all_gather(w_qkv.astype(low_type), "batch", axis=0, tiled=True),
        lax.all_gather(w_out.astype(low_type), "batch", axis=0, tiled=True),
        lax.all_gather(w_fc.astype(low_type), "batch", axis=0, tiled=True),
        lax.all_gather(w_proj.astype(low_type), "batch", axis=0, tiled=True),
    )
    full_qkv, full_out, full_fc, full_proj, full_vec = (
        lax.all_gather(row_parts[0], "ctx", axis=1, tiled=True),
        lax.all_gather(row_parts[1], "ctx", axis=1, tiled=True),
        lax.all_gather(row_parts[2], "ctx", axis=1, tiled=True),
        lax.all_gather(row_parts[3], "ctx", axis=1, tiled=True),
        lax.all_gather(vectors.astype(low_type), "ctx", axis=1, tiled=True),
    )
    params = full_vec.astype(wide)
    seqs, pair, half, width = block_in.shape
    heads = HEADS
    head = width // heads
    rows = seqs * pair * half
    span = pair * half
    count = lax.axis_size("ctx")
    index = lax.axis_index("ctx")
    scale = 1.0 / math.sqrt(head)
    inputs = block_in.astype(wide).reshape(rows, width)
    normed_one = layer_norm(inputs, params[0], params[1]).astype(low_type)
    mixed = jnp.dot(normed_one, full_qkv, preferred_element_type=wide)
    queries = (mixed[:, :width] + params[4]).astype(low_type)
    keys = mixed[:, width : 2 * width].astype(low_type)
    values = (mixed[:, 2 * width :] + params[5]).astype(low_type)
    key_all, value_all = (
        lax.all_gather(keys.reshape(seqs, pair, half, width), "ctx", axis=1, tiled=True),
        lax.all_gather(values.reshape(seqs, pair, half, width), "ctx", axis=1, tiled=True),
    )
    query_heads = queries.reshape(seqs, span, heads, head)
    own_places = block_places(index, count, half)

    def piece_of(source, piece):
        return lax.dynamic_slice_in_dim(source, 2 * piece, 2, 1).reshape(seqs, span, heads, head)

    def allowed_for(piece):
        return own_places[:, None] >= block_places(piece, count, half)[None, :]

    def stats_step(piece, carry):
        top, total = carry
        score = scores_of(query_heads, piece_of(key_all, piece), scale, allowed_for(piece))
        new_top = jnp.maximum(top, jnp.max(score, axis=-1))
        total = total * jnp.exp(top - new_top) + jnp.sum(
            jnp.exp(score - new_top[..., None]), axis=-1
        )
        return (new_top, total)

    start_stats = (jnp.full((seqs, heads, span), -1e30, wide), jnp.zeros((seqs, heads, span), wide))
    top, total = lax.fori_loop(0, count, stats_step, start_stats)

    def output_step(piece, acc):
        score = scores_of(query_heads, piece_of(key_all, piece), scale, allowed_for(piece))
        weights = (jnp.exp(score - top[..., None]) / total[..., None]).astype(low_type)
        return acc + jnp.einsum(
            "shqk,skhd->sqhd", weights, piece_of(value_all, piece), preferred_element_type=wide
        )

    attended = lax.fori_loop(0, count, output_step, jnp.zeros((seqs, span, heads, head), wide))
    att_low = attended.reshape(rows, width).astype(low_type)
    mid = inputs + jnp.dot(att_low, full_out, preferred_element_type=wide) + params[6]
    normed_two = layer_norm(mid, params[2], params[3]).astype(low_type)
    pre = jnp.dot(normed_two, full_fc, preferred_element_type=wide) + params[8:12].reshape(-1)
    act_low = gelu_tanh(pre).astype(low_type)
    result = mid + jnp.dot(act_low, full_proj, preferred_element_type=wide) + params[7]
    out_block = result.astype(low_type).reshape(block_in.shape)
    grad_low = cotangent.reshape(rows, width)
    grad_out = grad_low.astype(wide)
    grad_wproj = rows_product(act_low, grad_low)
    back_act = back_product(grad_low, full_proj)
    grad_pre = jax.vjp(gelu_tanh, pre)[1](back_act)[0].astype(low_type)
    grad_wfc = rows_product(normed_two, grad_pre)
    back_two = back_product(grad_pre, full_fc)
    back_mid, grad_gain_two, grad_shift_two = jax.vjp(layer_norm, mid, params[2], params[3])[1](
        back_two
    )
    grad_mid = grad_out + back_mid
    grad_att_low = grad_mid.astype(low_type)
    grad_wout = rows_product(att_low, grad_att_low)
    back_att = back_product(grad_att_low, full_out)
    grad_heads = back_att.astype(low_type).reshape(seqs, span, heads, head)
    delta = jnp.einsum("sqhd,sqhd->shq", grad_heads.astype(wide), attended)
    query_all, grad_all = (
        lax.all_gather(queries.reshape(seqs, pair, half, width), "ctx", axis=1, tiled=True),
        lax.all_gather(grad_heads.reshape(seqs, pair, half, width), "ctx", axis=1, tiled=True),
    )
    top_all, total_all, delta_all = (
        lax.all_gather(top.reshape(seqs, heads, pair, half), "ctx", axis=2, tiled=True),
        lax.all_gather(total.reshape(seqs, heads, pair, half), "ctx", axis=2, tiled=True),
        lax.all_gather(delta.reshape(seqs, heads, pair, half), "ctx", axis=2, tiled=True),
    )

    def query_step(piece, grad_query):
        key_part = piece_of(key_all, piece)
        value_part = piece_of(value_all, piece)
        weights_low, grad_score = pair_grads(
            query_heads,
            grad_heads,
            key_part,
            value_part,
            top,
            total,
            delta,
            scale,
            allowed_for(piece),
        )
        return grad_query + jnp.einsum(
            "shqk,skhd->sqhd", grad_score, key_part, preferred_element_type=wide
        )

    grad_query = lax.fori_loop(0, count, query_step, jnp.zeros((seqs, span, heads, head), wide))
    key_heads = keys.reshape(seqs, span, heads, head)
    value_heads = values.reshape(seqs, span, heads, head)

    def stat_piece(source, piece):
        return lax.dynamic_slice_in_dim(source, 2 * piece, 2, 2).reshape(seqs, heads, span)

    def key_step(piece, carry):
        grad_key, grad_value = carry
        query_part = piece_of(query_all, piece)
        grad_part = piece_of(grad_all, piece)
        allowed = block_places(piece, count, half)[:, None] >= own_places[None, :]
        weights_low, grad_score = pair_grads(
            query_part,
            grad_part,
            key_heads,
            value_heads,
            stat_piece(top_all, piece),
            stat_piece(total_all, piece),
            stat_piece(delta_all, piece),
            scale,
            allowed,
        )
        grad_key = grad_key + jnp.einsum(
            "shqk,sqhd->skhd", grad_score, query_part, preferred_element_type=wide
        )
        grad_value = grad_value + jnp.einsum(
            "shqk,sqhd->skhd", weights_low, grad_part, preferred_element_type=wide
        )
        return (grad_key, grad_value)

    start_keys = (
        jnp.zeros((seqs, span, heads, head), wide),
        jnp.zeros((seqs, span, heads, head), wide),
    )
    grad_key, grad_value = lax.fori_loop(0, count, key_step, start_keys)
    grad_keys = (grad_key * scale).reshape(seqs, pair, half, width)
    grad_values = grad_value.reshape(seqs, pair, half, width)
    grad_q_low = (grad_query * scale).reshape(rows, width).astype(low_type)
    grad_k_low = grad_keys.reshape(rows, width).astype(low_type)
    grad_v_low = grad_values.reshape(rows, width).astype(low_type)
    grad_mixed = jnp.concatenate([grad_q_low, grad_k_low, grad_v_low], axis=1)
    grad_wqkv = rows_product(normed_one, grad_mixed)
    back_one = back_product(grad_mixed, full_qkv)
    back_in, grad_gain_one, grad_shift_one = jax.vjp(layer_norm, inputs, params[0], params[1])[1](
        back_one
    )
    grad_input = (grad_mid + back_in).reshape(block_in.shape)
    grad_bias_q = jnp.sum(grad_q_low.astype(wide), axis=0)
    grad_bias_v = jnp.sum(grad_v_low.astype(wide), axis=0)
    grad_bias_out = jnp.sum(grad_att_low.astype(wide), axis=0)
    grad_bias_proj = jnp.sum(grad_out, axis=0)
    grad_bias_fc = jnp.sum(grad_pre.astype(wide), axis=0).reshape(4, width)
    small_rows = jnp.stack(
        [
            grad_gain_one,
            grad_shift_one,
            grad_gain_two,
            grad_shift_two,
            grad_bias_q,
            grad_bias_v,
            grad_bias_out,
            grad_bias_proj,
        ]
    )
    grad_vectors = jnp.concatenate([small_rows, grad_bias_fc], axis=0)
    col_sums = (
        lax.psum_scatter(grad_wqkv, "ctx", scatter_dimension=1, tiled=True),
        lax.psum_scatter(grad_wout, "ctx", scatter_dimension=1, tiled=True),
        lax.psum_scatter(grad_wfc, "ctx", scatter_dimension=1, tiled=True),
        lax.psum_scatter(grad_wproj, "ctx", scatter_dimension=1, tiled=True),
        lax.psum_scatter(grad_vectors, "ctx", scatter_dimension=1, tiled=True),
    )
    qkv_grad, out_grad, fc_grad, proj_grad = (
        lax.psum_scatter(col_sums[0], "batch", scatter_dimension=0, tiled=True),
        lax.psum_scatter(col_sums[1], "batch", scatter_dimension=0, tiled=True),
        lax.psum_scatter(col_sums[2], "batch", scatter_dimension=0, tiled=True),
        lax.psum_scatter(col_sums[3], "batch", scatter_dimension=0, tiled=True),
    )
    vec_grad = lax.psum(col_sums[4], "batch")
    qkv_m, qkv_s, qkv_w = adamw(w_qkv, qkv_grad, qkv_first, qkv_second, 0.06, 0.1)
    out_m, out_s, out_w = adamw(w_out, out_grad, out_first, out_second, 0.06, 0.1)
    fc_m, fc_s, fc_w = adamw(w_fc, fc_grad, fc_first, fc_second, 0.06, 0.1)
    proj_m, proj_s, proj_w = adamw(w_proj, proj_grad, proj_first, proj_second, 0.06, 0.1)
    vec_m, vec_s, vec_w = adamw(vectors, vec_grad, vec_first, vec_second, 0.2, 0.0)
    return (
        out_block,
        grad_input,
        qkv_m,
        qkv_s,
        qkv_w,
        out_m,
        out_s,
        out_w,
        fc_m,
        fc_s,
        fc_w,
        proj_m,
        proj_s,
        proj_w,
        vec_m,
        vec_s,
        vec_w,
    )


BATCH = 8
CTX = 4
WIDTH = 768
HEAD = 64
GROUP = WIDTH // CTX
TOKENS = 256
HALF = 128
FF_SIDE = 384
ROWS = WIDTH // BATCH
MLP = WIDTH + 2 * FF_SIDE + 256
SPAN = TOKENS * CTX
TILE = 256
LOW = jnp.bfloat16
WIDE = jnp.float32
CORE, XBIT, YBIT = 1, 2, 4
PLACES = (0, 2, 1, 3)
SOURCES = (
    (0, PLACES),
    (XBIT, PLACES),
    (YBIT, PLACES),
    (XBIT + YBIT, PLACES[:2]),
    (XBIT + YBIT, PLACES[2:]),
    (CORE, PLACES),
    (CORE + XBIT, PLACES),
    (CORE + YBIT, PLACES),
    (CORE + XBIT + YBIT, PLACES[:2]),
    (CORE + XBIT + YBIT, PLACES[2:]),
)
PARTS = len(SOURCES)
VMEM_LIMIT = 56 * 1024 * 1024


def swap(value, axis, bit):
    size = BATCH if axis == "batch" else CTX
    return lax.ppermute(value, axis, [(i, i ^ bit) for i in range(size)])


def mm(left, right):
    return lax.dot_general(left, right, (((1,), (0,)), ((), ())), preferred_element_type=WIDE)


def mt(left, right):
    return lax.dot_general(left, right, (((1,), (1,)), ((), ())), preferred_element_type=WIDE)


def tm(left, right):
    return lax.dot_general(left, right, (((0,), (0,)), ((), ())), preferred_element_type=WIDE)


def turned(value):
    return value.T


def moments(value):
    mean = jnp.mean(value, axis=-1, keepdims=True)
    centred = value - mean
    spread = jnp.mean(centred * centred, axis=-1, keepdims=True)
    return centred, lax.rsqrt(spread + 1e-05)


def norm_back(grad, normed, inverse, gain):
    part = grad * gain
    mean = jnp.mean(part, axis=-1, keepdims=True)
    cross = jnp.mean(part * normed, axis=-1, keepdims=True)
    return inverse * (part - mean - normed * cross)


def gather_first(own):
    return swap(own, "batch", XBIT), swap(own, "batch", YBIT)


def gather_second(from_x, from_y):
    return swap(from_x[:2], "batch", YBIT), swap(from_y[2:], "batch", XBIT)


def to_core(parts):
    return [swap(part, "batch", CORE) for part in parts]


def swap_pair(pair, first, second):
    return swap(pair[0], "batch", first), swap(pair[1], "batch", second)


def scatter_second(kept, back):
    one = kept[0].astype(WIDE) + back[0].astype(WIDE)
    two = kept[1].astype(WIDE) + back[1].astype(WIDE)
    return (one[0], two[0]), (one[1].astype(LOW), two[1].astype(LOW))


def scatter_near(kept, back):
    one = kept[0].astype(WIDE) + back[0].astype(WIDE)
    two = (kept[1].astype(WIDE) + back[1].astype(WIDE)).astype(LOW)
    return one, swap(two, "ctx", 1)


def scatter_far(one, two):
    one = one + two.astype(WIDE)
    return one[0] + swap(one[1].astype(LOW), "ctx", 2).astype(WIDE)


def rows_of(index, size):
    return pl.ds(pl.multiple_of(index * size, 16), size)


def qkv_place(held, batch, ctx):
    return [(pl.ds(0, 3 * GROUP), held.at[ctx, rows_of(batch, ROWS), :])]


def mlp_place(held_out, held_fc, held_proj, batch, ctx):
    return [
        (pl.ds(WIDTH + 2 * FF_SIDE, TILE), held_out.at[ctx, rows_of(batch, ROWS), :]),
        (pl.ds(0, WIDTH), held_fc.at[ctx, rows_of(batch, ROWS), :]),
        (pl.ds(WIDTH, FF_SIDE), held_proj.at[batch, rows_of(2 * ctx, ROWS), :]),
        (pl.ds(WIDTH + FF_SIDE, FF_SIDE), held_proj.at[batch, rows_of(2 * ctx + 1, ROWS), :]),
    ]


def load_weight(meta, parts, place, sems):
    copies = []
    for part, (source, places) in zip(parts, SOURCES):
        for index, ctx in enumerate(places):
            ranges = place(meta[0] ^ source, meta[1] ^ ctx)
            copies.append([(part.at[index, :, lanes], target) for lanes, target in ranges])
    started = []
    for kind in range(len(copies[0])):
        group = []
        for number, copy in enumerate(copies):
            group.append(pltpu.make_async_copy(*copy[kind], sems.at[kind, number]))
            group[-1].start()
        started.append(group)
    return started


def store_grad(held, targets, sems, kinds):
    one_kept, one_sent, two_kept, two_sent = targets
    copies = []
    for y in range(2):
        for x in range(2):
            for index, ctx in enumerate(PLACES):
                if index < 2:
                    target = (one_sent if y else one_kept).at[x, index]
                else:
                    target = (two_sent if x else two_kept).at[y, index - 2]
                ranges = held(2 * y + x, ctx)
                for kind in kinds:
                    lanes, source = ranges[kind]
                    number = (2 * y + x) * CTX + ctx
                    copies.append(
                        pltpu.make_async_copy(source, target.at[:, lanes], sems.at[kind, number])
                    )
                    copies[-1].start()
    return copies


def half_rows(meta, pair, held):
    for index, value in enumerate(pair):
        held[index] = turned(value)
    parts = []
    for index in range(2):
        rows = [held[index, rows_of(meta[0] ^ (2 * part), ROWS), :] for part in range(BATCH // 2)]
        parts.append(jnp.concatenate(rows, axis=0))
    return parts


def over_both(left, right):
    return mm(left[0], right[0]) + mm(left[1], right[1])


def wait_all(copies):
    for copy in copies:
        copy.wait()


LANES = 128


def write_packed(target, value):
    full = value.shape[1] // LANES
    for index in range(full):
        target[index * TOKENS : (index + 1) * TOKENS, :] = value[
            :, index * LANES : (index + 1) * LANES
        ]
    rest = value[:, full * LANES :]
    target[full * TOKENS :, :] = jnp.concatenate([rest[:HALF], rest[HALF:]], axis=1)


def read_packed(source):
    full = source.shape[0] // TOKENS
    parts = [source[index * TOKENS : (index + 1) * TOKENS, :] for index in range(full)]
    rest = source[full * TOKENS :, :]
    parts.append(jnp.concatenate([rest[:, : LANES // 2], rest[:, LANES // 2 :]], axis=0))
    return jnp.concatenate(parts, axis=1)


def in_place(ctx, block):
    first = ctx if block == 0 else 2 * CTX - 1 - ctx
    return pl.ds(pl.multiple_of(first * HALF, HALF), HALF)


def read_vectors(meta, parts, chunks):
    for ctx, part in enumerate(parts):
        rows = [part[16 * index : 16 * (index + 1), :] for index in range(GROUP // HEAD)]
        chunks[meta[1] ^ ctx] = jnp.concatenate(rows, axis=1).astype(WIDE)
    return jnp.concatenate([chunks[index] for index in range(CTX)], axis=1)


def qkv_kernel(meta, x_ref, *refs):
    vectors, parts, refs = refs[:4], refs[4 : 4 + PARTS], refs[4 + PARTS :]
    h_ref, own, near, far, last, held, units, chunks, sems = refs
    (copies,) = load_weight(meta, parts, functools.partial(qkv_place, held), sems)
    params = read_vectors(meta, vectors, chunks)
    bias = jnp.concatenate([params[4:5], jnp.zeros((1, WIDTH), WIDE), params[5:6]], axis=1)
    centred, inverse = moments(x_ref[...].astype(WIDE))
    normed = (centred * inverse * params[0:1] + params[1:2]).astype(LOW)
    h_ref[...] = normed
    wait_all(copies)
    for chunk in range(CTX):
        mixed = mm(normed, held[chunk]) + bias[:, 3 * GROUP * chunk : 3 * GROUP * (chunk + 1)]
        mixed = mixed.astype(LOW)
        for part in range(3):
            unit = 3 * chunk + part
            units[unit % CTX, :, (unit // CTX) * GROUP : (unit // CTX + 1) * GROUP] = mixed[
                :, part * GROUP : (part + 1) * GROUP
            ]
    for ctx, target in enumerate((own, near, far, last)):
        write_packed(target, units[meta[1] ^ ctx])


def read_sequence(meta, pieces, targets):
    for ctx, piece in enumerate(pieces):
        value = read_packed(piece)
        for block in range(2):
            place = in_place(meta[1] ^ ctx, block)
            rows = value[block * HALF : (block + 1) * HALF, :]
            for index, target in enumerate(targets):
                target[place, :] = rows[:, index * GROUP : (index + 1) * GROUP]


def write_sequence(meta, pieces, sources):
    for ctx, piece in enumerate(pieces):
        parts = []
        for source in sources:
            blocks = [source[in_place(meta[1] ^ ctx, block), :] for block in range(2)]
            parts.append(jnp.concatenate(blocks, axis=0).astype(LOW))
        write_packed(piece, jnp.concatenate(parts, axis=1))


def head_mask(head, scale=1.0):
    lane = lax.broadcasted_iota(jnp.int32, (1, GROUP), 1)
    inside = (lane >= head * HEAD) & (lane < (head + 1) * HEAD)
    return jnp.where(inside, scale, 0.0).astype(LOW)


def tile_of(index):
    return slice(index * TILE, (index + 1) * TILE)


def weights_of(queries, k_seq, tile, causal, axis):
    keys = [k_seq[tile_of(other), :] for other in range(tile + 1)]
    scores = [mt(queries, key) if axis else mt(key, queries) for key in keys]
    scores[tile] = jnp.where(causal, scores[tile], -1e30)
    top = jnp.max(functools.reduce(jnp.maximum, scores), axis=axis, keepdims=True)
    expo = [jnp.exp(score - top) for score in scores]
    total = jnp.sum(functools.reduce(jnp.add, expo), axis=axis, keepdims=True)
    inverse = 1.0 / total
    return [value * inverse for value in expo]


def causal_tile(axis):
    key = lax.broadcasted_iota(jnp.int32, (TILE, TILE), axis)
    query = lax.broadcasted_iota(jnp.int32, (TILE, TILE), 1 - axis)
    return query >= key


def attend_kernel(meta, *refs):
    pieces, results, (q_seq, k_seq, v_seq, out) = refs[:4], refs[4:8], refs[8:]
    read_sequence(meta, pieces, (q_seq, k_seq, v_seq))
    causal = causal_tile(1)
    scale = 1.0 / math.sqrt(HEAD)
    for tile in range(SPAN // TILE):

        def one_head(head, total, tile=tile):
            mask = head_mask(head)
            queries = q_seq[tile_of(tile), :] * head_mask(head, scale)
            weights = weights_of(queries, k_seq, tile, causal, 1)
            for other, weight in enumerate(weights):
                total = total + mm(weight.astype(LOW), v_seq[tile_of(other), :] * mask)
            return total

        out[tile_of(tile), :] = lax.fori_loop(
            0, GROUP // HEAD, one_head, jnp.zeros((TILE, GROUP), WIDE), unroll=True
        )
    write_sequence(meta, results, (out,))


def attend_back_kernel(meta, *refs):
    pieces, grads, results = refs[:4], refs[4:8], refs[8:12]
    q_seq, k_seq, v_seq, g_seq, dq, dk, dv = refs[12:]
    read_sequence(meta, pieces, (q_seq, k_seq, v_seq))
    read_sequence(meta, grads, (g_seq,))
    causal = causal_tile(0)
    scale = 1.0 / math.sqrt(HEAD)
    dk[...] = jnp.zeros_like(dk)
    dv[...] = jnp.zeros_like(dv)
    for tile in range(SPAN // TILE):

        def one_head(head, total, tile=tile):
            mask = head_mask(head)
            scaled = head_mask(head, scale)
            queries = q_seq[tile_of(tile), :] * scaled
            grad = g_seq[tile_of(tile), :] * mask
            weights = weights_of(queries, k_seq, tile, causal, 0)
            backs = [mt(v_seq[tile_of(other), :], grad) for other in range(tile + 1)]
            products = [weight * back for weight, back in zip(weights, backs)]
            delta = jnp.sum(functools.reduce(jnp.add, products), axis=0, keepdims=True)
            for other, (weight, back) in enumerate(zip(weights, backs)):
                step = (weight * (back - delta)).astype(LOW)
                total = total + tm(step, k_seq[tile_of(other), :] * scaled)
                dk[tile_of(other), :] += mm(step, queries)
                dv[tile_of(other), :] += mm(weight.astype(LOW), grad)
            return total

        dq[tile_of(tile), :] = lax.fori_loop(
            0, GROUP // HEAD, one_head, jnp.zeros((TILE, GROUP), WIDE), unroll=True
        )
    write_sequence(meta, results, (dq, dk, dv))


def middle_kernel(meta, x_ref, dy_ref, h_one_ref, *refs):
    vectors, pieces, parts, refs = refs[:4], refs[4:8], refs[8 : 8 + PARTS], refs[8 + PARTS :]
    (out_ref, pack_ref, mine, theirs, dmid_ref), refs = refs[:5], refs[5:]
    results, (rows_ref, dbias_ref), refs = refs[:4], refs[4:6], refs[6:]
    out_parts, held_out, held_fc, held_proj, units, total, back, chunks, bias, acts, sems = refs
    place = functools.partial(mlp_place, out_parts, held_fc, held_proj)
    copies = load_weight(meta, parts, place, sems)
    vec = read_vectors(meta, vectors, chunks)
    for chunk in range(CTX):
        bias[chunk] = vec[8 + chunk : 9 + chunk]
    for ctx, piece in enumerate(pieces):
        units[meta[1] ^ ctx] = read_packed(piece)
    att = jnp.concatenate([units[index] for index in range(CTX)], axis=1)
    pack_ref[CTX + 1] = att
    pack_ref[CTX + 3] = dy_ref[...]
    pack_ref[CTX + 4] = h_one_ref[...]
    wait_all(copies[0])
    for chunk in range(CTX):
        held_out[:, chunk * GROUP : (chunk + 1) * GROUP] = out_parts[chunk, :, :GROUP]
    mid = x_ref[...].astype(WIDE) + mm(att, held_out[...]) + vec[6:7]
    centred, inverse = moments(mid)
    normed = centred * inverse
    pack_ref[CTX] = (normed * vec[2:3] + vec[3:4]).astype(LOW)
    total[...] = mid + vec[7:8]
    back[...] = jnp.zeros_like(back)
    for group in copies[1:]:
        wait_all(group)
    side = FF_SIDE

    def chunk_step(chunk, carry):
        pre = mm(pack_ref[CTX], held_fc[chunk]) + bias[chunk]
        square = pre * pre
        tanh = jnp.tanh(0.7978845608028654 * (pre + 0.044715 * square * pre))
        act = (0.5 * pre * (1.0 + tanh)).astype(LOW)
        slope = 0.5 * (1.0 + tanh) + 0.5 * pre * (1.0 - tanh * tanh) * (
            0.7978845608028654 * (1.0 + 3.0 * 0.044715 * square)
        )
        grads = []
        for half in range(2):
            weight = held_proj[2 * chunk + half]
            part = act[:, half * side : (half + 1) * side]
            acts[2 * chunk + half] = part
            total[...] += mt(part, weight)
            grads.append(mm(dy_ref[...], weight))
        dpre = (jnp.concatenate(grads, axis=1) * slope).astype(LOW)
        pack_ref[chunk] = dpre
        dbias_ref[chunk] = jnp.sum(dpre.astype(WIDE), axis=0, keepdims=True)
        back[...] += mt(dpre, held_fc[chunk])
        return carry

    lax.fori_loop(0, CTX, chunk_step, 0, unroll=True)
    out_ref[...] = total[...].astype(LOW)
    core = meta[0] & 1
    for chunk in range(CTX):
        mine[chunk] = acts[2 * chunk + core]
        theirs[chunk] = acts[2 * chunk + 1 - core]
    grad = back[...]
    dy = dy_ref[...].astype(WIDE)
    dmid = dy + norm_back(grad, normed, inverse, vec[2:3])
    dmid_ref[...] = dmid
    datt = dmid.astype(LOW)
    pack_ref[CTX + 2] = datt
    rows_ref[0:1] = jnp.sum(grad * normed, axis=0, keepdims=True)
    rows_ref[1:2] = jnp.sum(grad, axis=0, keepdims=True)
    rows_ref[2:3] = jnp.sum(datt.astype(WIDE), axis=0, keepdims=True)
    rows_ref[3:4] = jnp.sum(dy, axis=0, keepdims=True)
    rows_ref[4:8] = jnp.zeros((4, WIDTH), WIDE)
    dout = mt(datt, held_out[...]).astype(LOW)
    for index in range(CTX):
        units[index] = dout[:, index * GROUP : (index + 1) * GROUP]
    for ctx, target in enumerate(results):
        write_packed(target, units[meta[1] ^ ctx])


def mlp_grad_kernel(meta, *refs):
    acts, packs, targets = refs[:2], refs[2:4], refs[4:8]
    held_out, held_fc, held_proj, turn, sems = refs[8:]

    def place(part, ctx):
        ctx = meta[1] ^ ctx
        chunk = (meta[0] ^ (2 * part)) // 2
        rows = pl.ds(part * ROWS, ROWS)
        return [
            (pl.ds(WIDTH + 2 * FF_SIDE, TILE), held_out.at[ctx, rows, :]),
            (pl.ds(0, WIDTH), held_fc.at[ctx, rows, :]),
            (pl.ds(WIDTH, FF_SIDE), held_proj.at[chunk, rows_of(2 * ctx, ROWS), :]),
            (pl.ds(WIDTH + FF_SIDE, FF_SIDE), held_proj.at[chunk, rows_of(2 * ctx + 1, ROWS), :]),
        ]

    dy = [turned(pack[CTX + 3]) for pack in packs]
    for chunk in range(CTX):
        held_proj[chunk] = over_both(dy, [act[chunk] for act in acts]).astype(LOW)
    copies = store_grad(place, targets, sems, (2, 3))
    left = half_rows(meta, [pack[CTX] for pack in packs], turn)
    for chunk in range(CTX):
        held_fc[chunk] = over_both(left, [pack[chunk] for pack in packs]).astype(LOW)
    copies += store_grad(place, targets, sems, (1,))
    left = half_rows(meta, [pack[CTX + 1] for pack in packs], turn)
    grad = over_both(left, [pack[CTX + 2] for pack in packs]).astype(LOW)
    for chunk in range(CTX):
        held_out[chunk, :, :GROUP] = grad[:, chunk * GROUP : (chunk + 1) * GROUP]
        held_out[chunk, :, GROUP:] = jnp.zeros((WIDTH // 2, TILE - GROUP), LOW)

    wait_all(copies + store_grad(place, targets, sems, (0,)))


def qkv_grad_kernel(meta, *refs):
    pack, own, came, targets = refs[:2], refs[2:4], refs[4:6], refs[6:10]
    mixed_ref, dbias_ref, held, units, turn, sems = refs[10:]
    for core in range(2):
        for ctx in range(CTX):
            value = read_packed(own[core] if ctx == 0 else came[core].at[ctx - 1])
            for part in range(3):
                units[core, CTX * part + (meta[1] ^ ctx)] = value[
                    :, part * GROUP : (part + 1) * GROUP
                ]
    left = half_rows(meta, [pack[0][...], pack[1][...]], turn)
    for chunk in range(CTX):
        mixed = [
            jnp.concatenate([units[core, 3 * chunk + part] for part in range(3)], axis=1)
            for core in range(2)
        ]
        mixed_ref[chunk] = mixed[0]
        bias = jnp.sum(mixed[0].astype(WIDE), axis=0, keepdims=True)
        for part in range(3):
            dbias_ref[3 * chunk + part] = bias[:, part * GROUP : (part + 1) * GROUP]
        held[chunk] = over_both(left, mixed).astype(LOW)

    def place(part, ctx):
        return [(pl.ds(0, 3 * GROUP), held.at[meta[1] ^ ctx, pl.ds(part * ROWS, ROWS), :])]

    wait_all(store_grad(place, targets, sems, (0,)))


def input_grad_kernel(meta, x_ref, dmid_ref, mixed_ref, rows_ref, dfc_ref, dqkv_ref, *refs):
    vectors, parts, refs = refs[:4], refs[4 : 4 + PARTS], refs[4 + PARTS :]
    grad_ref, results, (held, chunks, rows, sums, sems) = refs[0], refs[1:5], refs[5:]
    (copies,) = load_weight(meta, parts, functools.partial(qkv_place, held), sems)
    params = read_vectors(meta, vectors, chunks)
    centred, inverse = moments(x_ref[...].astype(WIDE))
    normed = centred * inverse
    wait_all(copies)
    grad = jnp.zeros((TOKENS, WIDTH), WIDE)
    for chunk in range(CTX):
        grad = grad + mt(mixed_ref[chunk], held[chunk])
    grad_ref[...] = dmid_ref[...] + norm_back(grad, normed, inverse, params[0:1])
    rows[0:1] = jnp.sum(grad * normed, axis=0, keepdims=True)
    rows[1:2] = jnp.sum(grad, axis=0, keepdims=True)
    rows[2:4] = rows_ref[0:2]
    for chunk in range(CTX):
        lanes = slice(chunk * GROUP, (chunk + 1) * GROUP)
        rows[4:5, lanes] = dqkv_ref[chunk]
        rows[5:6, lanes] = dqkv_ref[2 * CTX + chunk]
        rows[8 + chunk : 9 + chunk] = dfc_ref[chunk]
    rows[6:8] = rows_ref[2:4]
    rows[12:16] = jnp.zeros((4, WIDTH), WIDE)
    for chunk in range(CTX):
        sums[chunk] = rows[:, chunk * GROUP : (chunk + 1) * GROUP]
    for ctx, target in enumerate(results):
        target[...] = sums[meta[1] ^ ctx]


def sum_kernel(one_kept, one_back, two_kept, two_back, one_keep, one_send, two_keep, two_send):
    pairs = ((one_kept, one_back, one_keep, one_send), (two_kept, two_back, two_keep, two_send))
    for kept, back, keep, send in pairs:
        keep[...] = kept[0].astype(WIDE) + back[0].astype(WIDE)
        send[...] = (kept[1].astype(WIDE) + back[1].astype(WIDE)).astype(LOW)


def near_kernel(one_kept, one_back, two_kept, two_back, one_keep, two_send):
    one_keep[...] = one_kept[...] + one_back[...].astype(WIDE)
    two_send[...] = (two_kept[...] + two_back[...].astype(WIDE)).astype(LOW)


def shape_of(dtype, *dims):
    return jax.ShapeDtypeStruct(dims, dtype)


def call(kernel, arguments, kinds, outputs, out_kinds, scratch, moved=1):
    spec = {
        "v": pl.BlockSpec(memory_space=pltpu.VMEM),
        "s": pl.BlockSpec(memory_space=pltpu.SMEM),
        "a": pl.BlockSpec(memory_space=pl.ANY),
        "h": pl.BlockSpec((None, TOKENS, WIDTH), lambda step: (CTX + 4, 0, 0)),
    }
    return pl.pallas_call(
        kernel,
        grid=(1,),
        out_shape=tuple(outputs),
        in_specs=[spec[kind] for kind in kinds],
        out_specs=tuple(spec[kind] for kind in out_kinds),
        scratch_shapes=scratch,
        cost_estimate=pl.CostEstimate(flops=1, bytes_accessed=moved, transcendentals=0),
        compiler_params=pltpu.CompilerParams(vmem_limit_bytes=VMEM_LIMIT),
    )(*arguments)


def local_fast(
    block_in,
    cotangent,
    w_qkv,
    w_out,
    w_fc,
    w_proj,
    vectors,
    qkv_first,
    qkv_second,
    out_first,
    out_second,
    fc_first,
    fc_second,
    proj_first,
    proj_second,
    vec_first,
    vec_second,
):
    batch, ctx = lax.axis_index("batch"), lax.axis_index("ctx")
    meta = jnp.stack([batch, ctx]).astype(jnp.int32)
    inputs = block_in.reshape(TOKENS, WIDTH)
    grad_low = cotangent.reshape(TOKENS, WIDTH)
    tie = lax.optimization_barrier

    qkv_sems = pltpu.SemaphoreType.DMA((1, BATCH * CTX))
    mlp_sems = pltpu.SemaphoreType.DMA((4, BATCH * CTX))
    qkv_held = pltpu.VMEM((CTX, WIDTH, 3 * GROUP), LOW)
    vec_held = pltpu.VMEM((CTX, 16, GROUP), WIDE)

    low_vec = jnp.pad(vectors.astype(LOW), ((0, 4), (0, 0)))
    low_vec = [low_vec[:, start : start + HEAD] for start in range(0, GROUP, HEAD)]
    low_vec = jnp.concatenate(low_vec + [jnp.zeros((ROWS - 48, HEAD), LOW)], axis=0)
    piece_one = jnp.concatenate([w_qkv.astype(LOW), low_vec], axis=1)
    low_proj = w_proj.astype(LOW).T
    piece_two = jnp.concatenate(
        [
            w_fc.astype(LOW),
            low_proj[:ROWS],
            low_proj[ROWS:],
            w_out.astype(LOW),
            jnp.zeros((ROWS, TILE - GROUP), LOW),
        ],
        axis=1,
    )
    near = jnp.stack([piece_one, swap(piece_one, "ctx", 2)])
    far = swap(near, "ctx", 1)
    own_one = jnp.concatenate([near, far], axis=0)[:, :, : 3 * GROUP]
    piece_two, late = tie((piece_two, far))
    vec_parts = [part[:48, 3 * GROUP :] for part in (near[0], late[0], near[1], late[1])]
    x_one, y_one = gather_first(own_one)
    across_one = gather_second(x_one, y_one)
    near, far = swap(piece_two, "ctx", 1), swap(piece_two, "ctx", 2)
    near, far, across_one = tie((near, far, across_one))
    last = swap(far, "ctx", 1)
    parts_one = [own_one, x_one, y_one, *across_one]
    parts_one = parts_one + to_core(parts_one)

    packed = shape_of(LOW, TOKENS * 3 * GROUP // LANES, LANES)
    single = shape_of(LOW, TOKENS * GROUP // LANES, LANES)
    tokens_low = shape_of(LOW, TOKENS, WIDTH)
    hidden_low = shape_of(LOW, CTX, TOKENS, WIDTH)
    h_one, own, *sent = call(
        qkv_kernel,
        (meta, inputs, *vec_parts, *parts_one),
        "s" + "v" * 5 + "a" * PARTS,
        [tokens_low] + [packed] * 4,
        "v" * 5,
        [qkv_held, pltpu.VMEM((CTX, TOKENS, 3 * GROUP), LOW), vec_held, qkv_sems],
    )
    qkv_pieces = [own] + [swap(part, "ctx", bit) for bit, part in zip((1, 2, 3), sent)]

    last, late_h = tie((last, h_one))
    own_two = jnp.stack([piece_two, far, near, last])
    x_two, y_two = gather_first(own_two)
    qkv_pieces, x_two, y_two = tie((qkv_pieces, x_two, y_two))
    across_two = gather_second(x_two, y_two)
    parts_two = [own_two, x_two, y_two]
    swapped_two = to_core(parts_two)

    sequence_low = pltpu.VMEM((SPAN, GROUP), LOW)
    sequence_wide = pltpu.VMEM((SPAN, GROUP), WIDE)
    own, *sent = call(
        attend_kernel,
        (meta, *qkv_pieces),
        "s" + "v" * 4,
        [single] * 4,
        "v" * 4,
        [sequence_low] * 3 + [sequence_wide],
    )
    sent, swapped_two = tie((sent, swapped_two))
    att_pieces = [own] + [swap(part, "ctx", bit) for bit, part in zip((1, 2, 3), sent)]
    across_two, att_pieces = tie((across_two, att_pieces))
    parts_two = parts_two + list(across_two) + swapped_two + to_core(across_two)

    pack_shape = shape_of(LOW, CTX + 5, TOKENS, WIDTH)
    act_shape = shape_of(LOW, BATCH // 2, TOKENS, FF_SIDE)
    out, pack, act_mine, act_theirs, dmid, own, *sent = call(
        middle_kernel,
        (meta, inputs, grad_low, late_h, *vec_parts, *att_pieces, *parts_two),
        "s" + "v" * 11 + "a" * PARTS,
        [tokens_low, pack_shape, act_shape, act_shape, shape_of(WIDE, TOKENS, WIDTH)]
        + [single] * 4
        + [shape_of(WIDE, 8, WIDTH), shape_of(WIDE, CTX, 1, WIDTH)],
        "v" * 11,
        [
            pltpu.VMEM((CTX, WIDTH, TILE), LOW),
            pltpu.VMEM((WIDTH, WIDTH), LOW),
            pltpu.VMEM((CTX, WIDTH, WIDTH), LOW),
            pltpu.VMEM((BATCH, WIDTH, FF_SIDE), LOW),
            pltpu.VMEM((CTX, TOKENS, GROUP), LOW),
            pltpu.VMEM((TOKENS, WIDTH), WIDE),
            pltpu.VMEM((TOKENS, WIDTH), WIDE),
            vec_held,
            pltpu.VMEM((CTX, 1, WIDTH), WIDE),
            pltpu.VMEM((BATCH, TOKENS, FF_SIDE), LOW),
            mlp_sems,
        ],
    )
    sent, (rows_two, dbias_fc) = sent[:3], sent[3:]
    grad_pieces = [own] + [swap(part, "ctx", bit) for bit, part in zip((1, 2, 3), sent)]
    act_came, pack_came = swap(act_theirs, "batch", CORE), swap(pack, "batch", CORE)

    half_sems = BATCH * CTX // 2
    turn_held = pltpu.VMEM((2, WIDTH, TOKENS), LOW)
    mlp_parts = call(
        mlp_grad_kernel,
        (meta, act_mine, act_came, pack, pack_came),
        "s" + "v" * 4,
        [shape_of(LOW, 2, 2, ROWS, MLP)] * 4,
        "aaaa",
        [
            pltpu.VMEM((CTX, WIDTH // 2, TILE), LOW),
            pltpu.VMEM((CTX, WIDTH // 2, WIDTH), LOW),
            pltpu.VMEM((BATCH // 2, WIDTH, FF_SIDE), LOW),
            turn_held,
            pltpu.SemaphoreType.DMA((4, half_sems)),
        ],
    )
    mlp_parts, grad_pieces = tie((mlp_parts, grad_pieces))
    mlp_kept = mlp_parts[0], mlp_parts[2]
    mlp_back = swap_pair((mlp_parts[1], mlp_parts[3]), YBIT, XBIT)
    own, *sent = call(
        attend_back_kernel,
        (meta, *qkv_pieces, *grad_pieces),
        "s" + "v" * 8,
        [packed] * 4,
        "v" * 4,
        [sequence_low] * 4 + [sequence_wide] * 3,
    )
    own_came = swap(own, "batch", CORE)
    received = [swap(part, "ctx", bit) for bit, part in zip((1, 2, 3), sent)]
    mlp_back, received[0] = tie((mlp_back, received[0]))
    pair = [shape_of(WIDE, 2, ROWS, MLP), shape_of(LOW, 2, ROWS, MLP)]
    one_keep, one_send, two_keep, two_send = call(
        sum_kernel,
        (mlp_kept[0], mlp_back[0], mlp_kept[1], mlp_back[1]),
        "vvvv",
        pair + pair,
        "vvvv",
        [],
    )
    one_keep, received[1], received[2] = tie((one_keep, received[1], received[2]))
    mlp_back = swap_pair((one_send, two_send), XBIT, YBIT)
    received = jnp.stack(received)
    received_came = swap(received, "batch", CORE)

    *qkv_parts, mixed, dbias_qkv = call(
        qkv_grad_kernel,
        (meta, pack, pack_came, own, own_came, received, received_came),
        "shhvvvv",
        [shape_of(LOW, 2, 2, ROWS, 3 * GROUP)] * 4
        + [shape_of(LOW, CTX, TOKENS, 3 * GROUP), shape_of(WIDE, 3 * CTX, 1, GROUP)],
        "aaaavv",
        [
            pltpu.VMEM((CTX, WIDTH // 2, 3 * GROUP), LOW),
            pltpu.VMEM((2, 3 * CTX, TOKENS, GROUP), LOW),
            turn_held,
            pltpu.SemaphoreType.DMA((1, half_sems)),
        ],
    )
    qkv_kept = qkv_parts[0], qkv_parts[2]
    qkv_kept = qkv_parts[0], qkv_parts[2]
    qkv_back = swap_pair((qkv_parts[1], qkv_parts[3]), YBIT, XBIT)
    grad_input, own, *sent = call(
        input_grad_kernel,
        (meta, inputs, dmid, mixed, rows_two, dbias_fc, dbias_qkv, *vec_parts, *parts_one),
        "s" + "v" * 10 + "a" * PARTS,
        [shape_of(WIDE, TOKENS, WIDTH)] + [shape_of(WIDE, 16, GROUP)] * 4,
        "v" * 5,
        [qkv_held, vec_held, pltpu.VMEM((16, WIDTH), WIDE), vec_held, qkv_sems],
        moved=40_000_000,
    )
    mlp_back, own, sent = tie((mlp_back, own, sent))
    vec_grad = own + sum(swap(part, "ctx", bit) for bit, part in zip((1, 2, 3), sent))
    mlp_one, mlp_two = call(
        near_kernel, (one_keep, mlp_back[0], two_keep, mlp_back[1]), "vvvv", pair, "vv", []
    )
    mlp_two, vec_grad = tie((mlp_two, vec_grad))
    mlp_two = swap(mlp_two, "ctx", 1)
    mlp_one, qkv_back = tie((mlp_one, qkv_back))
    qkv_kept, qkv_sent = scatter_second(qkv_kept, qkv_back)
    qkv_back = swap_pair(qkv_sent, XBIT, YBIT)
    qkv_back, vec_grad = tie((qkv_back, vec_grad))
    qkv_one, qkv_two = scatter_near(qkv_kept, qkv_back)
    for bit in (CORE, XBIT):
        vec_grad = vec_grad + swap(vec_grad, "batch", bit)
    mlp_two, qkv_two, vec_grad = tie((mlp_two, qkv_two, vec_grad))
    vec_grad = vec_grad + swap(vec_grad, "batch", YBIT)
    mlp_grad = scatter_far(mlp_one, mlp_two)
    qkv_grad = scatter_far(qkv_one, qkv_two)
    vec_grad = vec_grad[:12]
    fc_grad = mlp_grad[:, :WIDTH]
    proj_grad = jnp.concatenate(
        [mlp_grad[:, WIDTH : WIDTH + FF_SIDE], mlp_grad[:, WIDTH + FF_SIDE : WIDTH + 2 * FF_SIDE]],
        axis=0,
    )
    out_grad = mlp_grad[:, WIDTH + 2 * FF_SIDE : WIDTH + 2 * FF_SIDE + GROUP]

    qkv_m, qkv_s, qkv_w = adamw(w_qkv, qkv_grad, qkv_first, qkv_second, 0.06, 0.1)
    out_m, out_s, out_w = adamw(w_out, out_grad, out_first, out_second, 0.06, 0.1)
    fc_m, fc_s, fc_w = adamw(w_fc, fc_grad, fc_first, fc_second, 0.06, 0.1)
    proj_m, proj_s, proj_w = adamw(w_proj, proj_grad.T, proj_first, proj_second, 0.06, 0.1)
    vec_m, vec_s, vec_w = adamw(vectors, vec_grad, vec_first, vec_second, 0.2, 0.0)
    return (
        out.reshape(block_in.shape),
        grad_input.reshape(block_in.shape),
        qkv_m,
        qkv_s,
        qkv_w,
        out_m,
        out_s,
        out_w,
        fc_m,
        fc_s,
        fc_w,
        proj_m,
        proj_s,
        proj_w,
        vec_m,
        vec_s,
        vec_w,
    )


def solution(mesh):
    in_specs = (
        P("batch", "ctx", None, None),
        P("batch", "ctx", None, None),
        P("batch", "ctx"),
        P("batch", "ctx"),
        P("batch", "ctx"),
        P("batch", "ctx"),
        P(None, "ctx"),
        P("batch", "ctx"),
        P("batch", "ctx"),
        P("batch", "ctx"),
        P("batch", "ctx"),
        P("batch", "ctx"),
        P("batch", "ctx"),
        P("batch", "ctx"),
        P("batch", "ctx"),
        P(None, "ctx"),
        P(None, "ctx"),
    )
    out_specs = (
        P("batch", "ctx", None, None),
        P("batch", "ctx", None, None),
        P("batch", "ctx"),
        P("batch", "ctx"),
        P("batch", "ctx"),
        P("batch", "ctx"),
        P("batch", "ctx"),
        P("batch", "ctx"),
        P("batch", "ctx"),
        P("batch", "ctx"),
        P("batch", "ctx"),
        P("batch", "ctx"),
        P("batch", "ctx"),
        P("batch", "ctx"),
        P(None, "ctx"),
        P(None, "ctx"),
        P(None, "ctx"),
    )
    sizes = (mesh.shape["batch"], mesh.shape["ctx"])
    local = local_fast if sizes == (BATCH, CTX) else local_any
    return jax.shard_map(local, mesh=mesh, in_specs=in_specs, out_specs=out_specs, check_vma=False)
```
